32 devices in a mesh: groups: 2 (over x), tensor: 16 (over z, y, core).
Axes of the slice: x: 2, y: 2, z: 4, core: 2. Of those that a mesh axis runs over, the one named last changes fastest.
Arguments:
- tokens: bfloat16 [256, 8192], P('groups', 'tensor'), parts along dimension 0, may hold values from -6 to 6
- weight: bfloat16 [8192, 16384], P('tensor'), may hold values from -0.0625 to 0.0625
- generators: float32 [8, 8192, 32], P('groups', 'tensor'), parts along dimension 0, may hold values from -2 to 2
- orders: int32 [4, 32], replicated, may hold values from 0 to 31, each once within a row
- cotangent: bfloat16 [256, 16384], P('groups', 'tensor'), parts along dimension 0, may hold values from -1.5 to 1.5
Outputs:
- outputs: float32 [256, 16384], P('groups', 'tensor'), parts along dimension 0
- grad_tokens: float32 [256, 8192], P('groups', 'tensor'), parts along dimension 0
- grad_generators: float32 [8, 8192, 32], P('groups', 'tensor'), parts along dimension 0
The draws below stay inside these ranges and needn't reach their ends.
There are 2 independent parts, one for each index of `groups`. The reference program is written for one: setup_inputs(seed, part) draws one part's arguments, and reference() takes and returns one part's arrays. A program takes and returns all parts, laid end to end along the dimension named above; an argument that names none is the same for every part. Nothing has to cross between parts.
Inputs may be any that keep to these rules, and one draw needn't show every extreme that they name: Each row of orders is a permutation of 0 to 31.
All inputs are finite; a program needn't handle non-finite values.
Results may differ from the reference program's by a relative error of at most 0.0003.
Values may be sent and summed in bfloat16 or wider, within the bound.
No kernel may reach another device: no remote copies, remote signals or barrier semaphores. Data moves between devices by JAX's collectives and lax.ppermute only.
A program may use at most 128 MiB of HBM per device.

```python
import jax
import jax.numpy as jnp
from jax import lax

D = 8192
HIDDEN_SIZE = 16384
BLOCK = 32
SECTIONS = 4
TOKENS = 128
HALF = 16


def level_of(key, dims, cuts, smallest, high):
    gain, own = 1.0, jax.random.fold_in(key, 6)
    for axis_at, blocks in cuts:
        heights = jnp.exp(jax.random.uniform(jax.random.fold_in(own, axis_at), (blocks,), jnp.float32, smallest / len(cuts), high / len(cuts)))
        gain = gain * jnp.repeat(heights, dims[axis_at] // blocks).reshape([-1 if axis == axis_at else 1 for axis in range(len(dims))])
    return gain


def bell_draw(rng, dims, deviation, limit, pieces=(), held_as=jnp.bfloat16):
    array = jax.random.normal(rng, dims, jnp.float32) * deviation
    if len(pieces) > 0:
        array = level_of(rng, dims, pieces, -0.22, 0.18) * array
    return jnp.clip(array, min=-limit, max=limit).astype(held_as)


def setup_inputs(seed: int = 0, part: int = 0) -> dict:
    key_list = jax.random.split(jax.random.key(seed), 6)
    part_splits = jax.random.split(jax.random.fold_in(key_list[5], part), 6)
    tokens = bell_draw(part_splits[0], (TOKENS, D), 1.0, 6.0, ((1, 16),))
    weight = bell_draw(key_list[1], (D, HIDDEN_SIZE), D ** -0.5, 0.0625, ((0, 16),))
    generators = bell_draw(part_splits[2], (SECTIONS, D, BLOCK), 0.3, 2.0, ((1, 16),), jnp.float32)
    orders = jax.vmap(lambda own: jax.random.permutation(own, BLOCK))(jax.random.split(key_list[3], SECTIONS)).reshape((SECTIONS, BLOCK)).astype(jnp.int32)
    cotangent = bell_draw(part_splits[4], (TOKENS, HIDDEN_SIZE), 0.25, 1.5, ((1, 16),))
    return dict(tokens=tokens, weight=weight, generators=generators, orders=orders, cotangent=cotangent)


HIGHEST = lax.Precision.HIGHEST

def cayley(gen_blocks, ordering):
    block_size = gen_blocks.shape[-1]
    identity = jnp.eye(block_size, dtype=gen_blocks.dtype)
    skewed = gen_blocks - jnp.swapaxes(gen_blocks, 1, 2)
    shifted = identity + skewed
    numerator = jnp.einsum('bij,bjk->bik', shifted, shifted, precision=HIGHEST)
    metric = identity - jnp.einsum('bij,bjk->bik', skewed, skewed, precision=HIGHEST)
    factor = jnp.linalg.cholesky(metric)
    target = jnp.swapaxes(numerator, 1, 2)
    partly = lax.linalg.triangular_solve(factor, target, left_side=True, lower=True)
    solved = lax.linalg.triangular_solve(factor, partly, left_side=True, lower=True, transpose_a=True)
    rotation = jnp.swapaxes(solved, 1, 2)
    picker = (ordering[:, None] == jnp.arange(block_size, dtype=jnp.int32)[None, :]).astype(rotation.dtype)
    return jnp.einsum('im,bmn,jn->bij', picker, rotation, picker, precision=HIGHEST)

def section_blocks(gen_rows, distance):
    row_count, block_size = gen_rows.shape
    grouped = gen_rows.reshape(row_count // (2 * distance), 2, distance // HALF, HALF, block_size)
    return jnp.transpose(grouped, (0, 2, 1, 3, 4)).reshape(-1, 2 * HALF, block_size)

def section_apply(rows, rotation, distance):
    row_count, columns = rows.shape
    bunches = row_count // (2 * distance)
    spread = distance // HALF
    grouped = rows.reshape(bunches, 2, spread, HALF, columns)
    shaped = rotation.reshape(bunches, spread, 2, HALF, 2, HALF)
    moved = jnp.einsum('gshepf,gpsfc->ghsec', shaped, grouped, precision=HIGHEST)
    return moved.reshape(row_count, columns)

def distance_of(section):
    return D // 2 if section == 0 else HALF * 2 ** (section - 1)

def reference(tokens, weight, generators, orders, cotangent):

    def forward(gen_all, token_values):
        current = weight.astype(jnp.float32)
        for section in range(SECTIONS):
            distance = distance_of(section)
            rotation = cayley(section_blocks(gen_all[section], distance), orders[section])
            current = section_apply(current, rotation, distance)
        return jnp.dot(token_values, current, precision=HIGHEST)
    outputs, pullback = jax.vjp(forward, generators, tokens.astype(jnp.float32))
    grad_generators, grad_tokens = pullback(cotangent.astype(jnp.float32))
    return (outputs, grad_tokens, grad_generators)
```

```python
import functools

import jax
import jax.numpy as jnp
import numpy as np
from jax import lax
from jax.experimental import pallas as pl
from jax.experimental.pallas import tpu as pltpu
from jax.sharding import PartitionSpec as P

HIGHEST = lax.Precision.HIGHEST
VMEM_LIMIT = 48 * 2**20
GROUP = 128
NN = (((1,), (0,)), ((), ()))
NT = (((1,), (1,)), ((), ()))
TN = (((0,), (0,)), ((), ()))
CHUNKS = 2


def exchange(array, bit):
    size = lax.axis_size("tensor")
    return lax.ppermute(array, "tensor", [(i, i ^ (1 << bit)) for i in range(size)])


def dot(a, b, dims=NN):
    return lax.dot_general(a, b, dims, precision=HIGHEST, preferred_element_type=jnp.float32)


def iota(shape, dim):
    return lax.broadcasted_iota(jnp.int32, shape, dim)


def split_halves(rows_ref, lo_ref, hi_ref, section, rows, half):
    step = half << (section - 1)
    base = section * rows
    for start in range(base, base + rows, 2 * step):
        low = rows_ref[start : start + step, :]
        high = rows_ref[start + step : start + 2 * step, :]
        lo_ref[start : start + step, :] = low
        lo_ref[start + step : start + 2 * step, :] = low
        hi_ref[start : start + step, :] = high
        hi_ref[start + step : start + 2 * step, :] = high


def to_lanes(lo_ref, hi_ref, out_ref, lanes, half, block):
    for a in range(half):
        out_ref[a * block : (a + 1) * block, :] = lo_ref[pl.ds(a, lanes, stride=half), :].T
        out_ref[(half + a) * block : (half + a + 1) * block, :] = hi_ref[
            pl.ds(a, lanes, stride=half), :
        ].T


def by_section(parts, section_of):
    out = parts[-1]
    for k in range(len(parts) - 2, -1, -1):
        out = jnp.where(section_of == k, parts[k], out)
    return out


def lane_facts(shape, per_section, high):
    lane = iota(shape, 1)
    section_of = lane // per_section
    part = lane % per_section
    upper = jnp.bitwise_and(jnp.right_shift(part, jnp.maximum(section_of - 1, 0)), 1)
    return section_of, jnp.where(section_of == 0, high, upper) == 1


def block_masks(section, half):
    row = iota((GROUP, GROUP), 0) // half
    col = iota((GROUP, GROUP), 1) // half
    bit = 1 << (section - 1)
    return col == jnp.bitwise_and(row, ~bit), col == jnp.bitwise_or(row, bit)


def same_mask(half):
    return iota((GROUP, GROUP), 0) // half == iota((GROUP, GROUP), 1) // half


def spreader(offset, block, half):
    return (iota((block, GROUP), 0) == offset + iota((block, GROUP), 1) % half).astype(jnp.float32)


def gatherer(offset, block, half):
    return (iota((GROUP, block), 1) == offset + iota((GROUP, block), 0) % half).astype(jnp.float32)


def rotate_kernel(
    orders_ref, high_ref, gen_ref, far_ref, tok_ref,
    inv_ref, near_ref, ffar_ref, bfar_ref, xs_ref,
    lo_ref, hi_ref, a_ref, b_ref, row_ref, rowt_ref,
):
    sections, block = orders_ref.shape
    half = block // 2
    rows = far_ref.shape[0]
    per_section = rows // half
    lanes = sections * per_section
    high = high_ref[0]
    own = gen_ref[0:rows, :]
    other = far_ref[...]
    lo_ref[0:rows, :] = jnp.where(high == 1, other, own)
    hi_ref[0:rows, :] = jnp.where(high == 1, own, other)
    for k in range(1, sections):
        split_halves(gen_ref, lo_ref, hi_ref, k, rows, half)
    to_lanes(lo_ref, hi_ref, a_ref, lanes, half, block)
    section_of, upper = lane_facts((block, lanes), per_section, high)

    def permute_rows(i, _):
        parts = [
            a_ref[pl.ds(pl.multiple_of(orders_ref[k, i] * block, block), block), :]
            for k in range(sections)
        ]
        b_ref[pl.ds(pl.multiple_of(i * block, block), block), :] = by_section(parts, section_of)
        return 0

    lax.fori_loop(0, block, permute_rows, 0, unroll=4)

    def permute_cols(j, _):
        parts = [
            b_ref[pl.ds(orders_ref[k, j], block, stride=block), :] for k in range(sections)
        ]
        a_ref[pl.ds(pl.multiple_of(j * block, block), block), :] = by_section(parts, section_of)
        return 0

    lax.fori_loop(0, block, permute_cols, 0, unroll=4)
    sub = iota((block, lanes), 0)
    for j in range(block):
        inv_ref[j * block : (j + 1) * block, :] = (
            a_ref[j * block : (j + 1) * block, :]
            - a_ref[pl.ds(j, block, stride=block), :]
            + (sub == j).astype(jnp.float32)
        )

    def eliminate(k, _):
        at = pl.multiple_of(k * block, block)
        here = sub == k
        inverse = 1.0 / inv_ref[pl.ds(at + k, 1), :]
        pivot = jnp.where(here, inverse, inv_ref[pl.ds(at, block), :] * inverse)
        for i in range(block):
            factor = inv_ref[pl.ds(i * block + k, 1), :]
            row = inv_ref[i * block : (i + 1) * block, :]
            inv_ref[i * block : (i + 1) * block, :] = jnp.where(here, 0.0, row) - factor * pivot
        inv_ref[pl.ds(at, block), :] = pivot
        return 0

    lax.fori_loop(0, block, eliminate, 0)

    for a in range(half):
        low = 2.0 * inv_ref[a * block : (a + 1) * block, :] - (sub == a).astype(jnp.float32)
        top = 2.0 * inv_ref[(half + a) * block : (half + a + 1) * block, :] - (
            sub == half + a
        ).astype(jnp.float32)
        row_ref[pl.ds(a, lanes, stride=half), :] = jnp.where(upper, top, low).T
        low = 2.0 * inv_ref[pl.ds(a, block, stride=block), :] - (sub == a).astype(jnp.float32)
        top = 2.0 * inv_ref[pl.ds(half + a, block, stride=block), :] - (sub == half + a).astype(
            jnp.float32
        )
        rowt_ref[pl.ds(a, lanes, stride=half), :] = jnp.where(upper, top, low).T
    spread_lo = spreader(0, block, half)
    spread_hi = spreader(half, block, half)
    spread_own = spreader(half * high, block, half)
    spread_oth = spreader(half * (1 - high), block, half)
    same = same_mask(half)
    for start in range(0, rows, GROUP):
        stop = start + GROUP
        part = rowt_ref[start:stop, :]
        ffar_ref[0, start:stop, :] = jnp.where(same, dot(part, spread_own), 0.0)
        ffar_ref[1, start:stop, :] = jnp.where(same, dot(part, spread_oth), 0.0)
        part = row_ref[start:stop, :]
        bfar_ref[0, start:stop, :] = jnp.where(same, dot(part, spread_own), 0.0)
        bfar_ref[1, start:stop, :] = jnp.where(same, dot(part, spread_oth), 0.0)
        value = tok_ref[:, start:stop].astype(jnp.float32)
        for k in range(sections - 1, 0, -1):
            lo_mask, hi_mask = block_masks(k, half)
            part = row_ref[k * rows + start : k * rows + stop, :]
            matrix = jnp.where(lo_mask, dot(part, spread_lo), 0.0) + jnp.where(
                hi_mask, dot(part, spread_hi), 0.0
            )
            near_ref[k - 1, start:stop, :] = matrix
            value = dot(value, matrix)
            xs_ref[k - 1, :, start:stop] = value


def far_kernel(own_ref, oth_ref, far_ref, out_ref):
    count, rows = own_ref.shape[1:]
    for start in range(0, rows, GROUP):
        stop = start + GROUP
        value = dot(own_ref[0, :, start:stop], far_ref[0, start:stop, :], NT) + dot(
            oth_ref[:, start:stop], far_ref[1, start:stop, :], NT
        )
        first = value.astype(jnp.bfloat16)
        out_ref[0:count, start:stop] = first
        out_ref[count : 2 * count, start:stop] = (value - first.astype(jnp.float32)).astype(
            jnp.bfloat16
        )


def project_kernel(places_ref, x_ref, w_ref, out_ref):
    count = out_ref.shape[1]
    both = jnp.dot(x_ref[...], w_ref[...], preferred_element_type=jnp.float32)
    out_ref[0] = both[:count] + both[count:]


def project(x_both, weight, places, chunk, chunks):
    pieces = places.shape[0]
    count2, rows = x_both.shape
    count = count2 // 2
    width = weight.shape[1] // lax.axis_size("tensor") // chunks
    return pl.pallas_call(
        project_kernel,
        out_shape=jax.ShapeDtypeStruct((pieces, count, width), jnp.float32),
        grid_spec=pltpu.PrefetchScalarGridSpec(
            num_scalar_prefetch=1,
            grid=(pieces,),
            in_specs=[
                pl.BlockSpec((count2, rows), lambda p, places: (0, 0)),
                pl.BlockSpec((rows, width), lambda p, places: (0, places[p] * chunks + chunk)),
            ],
            out_specs=pl.BlockSpec((1, count, width), lambda p, places: (p, 0, 0)),
        ),
        compiler_params=pltpu.CompilerParams(vmem_limit_bytes=VMEM_LIMIT),
        cost_estimate=pl.CostEstimate(
            flops=2 * count2 * rows * width * pieces,
            bytes_accessed=pieces * width * (2 * rows + 4 * count),
            transcendentals=0,
        ),
        name="project",
    )(places, x_both, weight)


def back_kernel(cot_ref, w_ref, out_ref):
    @pl.when(pl.program_id(0) == 0)
    def _():
        out_ref[...] = jnp.zeros_like(out_ref)

    out_ref[...] += lax.dot_general(
        cot_ref[0], w_ref[...], NT, preferred_element_type=jnp.float32
    )


def project_back(gathered, weight):
    pieces, count, width = gathered.shape
    rows = weight.shape[0]
    return pl.pallas_call(
        back_kernel,
        out_shape=jax.ShapeDtypeStruct((count, rows), jnp.float32),
        grid=(pieces,),
        in_specs=[
            pl.BlockSpec((1, count, width), lambda p: (p, 0, 0)),
            pl.BlockSpec((rows, width), lambda p: (0, p)),
        ],
        out_specs=pl.BlockSpec((count, rows), lambda p: (0, 0)),
        compiler_params=pltpu.CompilerParams(vmem_limit_bytes=VMEM_LIMIT),
        cost_estimate=pl.CostEstimate(
            flops=2 * count * rows * width * pieces,
            bytes_accessed=pieces * width * 2 * (rows + count),
            transcendentals=0,
        ),
        name="project_back",
    )(gathered, weight)


def lane_matmul(left_ref, right_ref, out_ref, block, lanes):
    step = 4

    def body(t, _):
        first = t * step
        totals = [jnp.zeros((block, lanes), jnp.float32) for _ in range(step)]
        for j in range(block):
            right = right_ref[j * block : (j + 1) * block, :]
            for s in range(step):
                totals[s] += left_ref[pl.ds((first + s) * block + j, 1), :] * right
        for s in range(step):
            out_ref[pl.ds(pl.multiple_of((first + s) * block, block), block), :] = totals[s]
        return 0

    lax.fori_loop(0, block // step, body, 0)


def grads_kernel(
    inverse_ref, high_ref, own_ref, oth_ref, x_oth_ref, tok_ref, xs_ref, near_ref, bfar_ref, inv_ref,
    gtok_ref, ggen_ref,
    row_ref, lo_ref, hi_ref, a_ref, b_ref, c_ref,
):
    sections, block = inverse_ref.shape
    half = block // 2
    count, rows = own_ref.shape
    per_section = rows // half
    lanes = sections * per_section
    high = high_ref[0]
    gather_lo = gatherer(0, block, half)
    gather_hi = gatherer(half, block, half)
    gather_own = gatherer(half * high, block, half)
    gather_oth = gatherer(half * (1 - high), block, half)
    same = same_mask(half)
    for start in range(0, rows, GROUP):
        stop = start + GROUP
        x_own = xs_ref[0, :, start:stop]
        x_oth = x_oth_ref[:, start:stop]
        g_own = own_ref[:, start:stop]
        g_oth = oth_ref[:, start:stop]

        def far_rows(x):
            return dot(jnp.where(same, dot(x, g_own, TN), 0.0), gather_own) + dot(
                jnp.where(same, dot(x, g_oth, TN), 0.0), gather_oth
            )

        mine, theirs = far_rows(x_own), far_rows(x_oth)
        lo_ref[start:stop, :] = jnp.where(high == 1, theirs, mine)
        hi_ref[start:stop, :] = jnp.where(high == 1, mine, theirs)
        grad = dot(g_own, bfar_ref[0, start:stop, :], NT) + dot(g_oth, bfar_ref[1, start:stop, :], NT)
        for k in range(1, sections):
            lo_mask, hi_mask = block_masks(k, half)
            if k < sections - 1:
                x = xs_ref[k, :, start:stop]
            else:
                x = tok_ref[:, start:stop].astype(jnp.float32)
            outer = dot(x, grad, TN)
            row_ref[k * rows + start : k * rows + stop, :] = dot(
                jnp.where(lo_mask, outer, 0.0), gather_lo
            ) + dot(jnp.where(hi_mask, outer, 0.0), gather_hi)
            grad = dot(grad, near_ref[k - 1, start:stop, :], NT)
        gtok_ref[:, start:stop] = grad
    for k in range(1, sections):
        split_halves(row_ref, lo_ref, hi_ref, k, rows, half)
    to_lanes(lo_ref, hi_ref, a_ref, lanes, half, block)
    for j in range(block):
        b_ref[j * block : (j + 1) * block, :] = inv_ref[pl.ds(j, block, stride=block), :]
    lane_matmul(a_ref, b_ref, c_ref, block, lanes)
    lane_matmul(b_ref, c_ref, a_ref, block, lanes)
    for j in range(block):
        c_ref[j * block : (j + 1) * block, :] = 2.0 * (
            a_ref[j * block : (j + 1) * block, :] - a_ref[pl.ds(j, block, stride=block), :]
        )
    section_of, upper = lane_facts((block, lanes), per_section, high)

    def permute_cols(j, _):
        parts = [
            c_ref[pl.ds(inverse_ref[k, j], block, stride=block), :] for k in range(sections)
        ]
        b_ref[pl.ds(pl.multiple_of(j * block, block), block), :] = by_section(parts, section_of)
        return 0

    lax.fori_loop(0, block, permute_cols, 0, unroll=4)
    for a in range(half):
        low, top = [
            by_section(
                [
                    b_ref[pl.ds(inverse_ref[k, at], block, stride=block), :]
                    for k in range(sections)
                ],
                section_of,
            )
            for at in (a, half + a)
        ]
        ggen_ref[pl.ds(a, lanes, stride=half), :] = jnp.where(upper, top, low).T


def local(tokens, weight, generators, orders, cotangent):
    sections, rows, block = generators.shape
    half = block // 2
    count = tokens.shape[0]
    size = lax.axis_size("tensor")
    bits = size.bit_length() - 1
    here = lax.axis_index("tensor")
    pair_bit = bits - 1
    high = jnp.bitwise_and(jnp.right_shift(here, pair_bit), 1).astype(jnp.int32).reshape(1)
    lanes = sections * (rows // half)
    f32 = jnp.float32
    full = pl.BlockSpec(memory_space=pltpu.VMEM)
    scalars = pl.BlockSpec(memory_space=pltpu.SMEM)
    params = pltpu.CompilerParams(vmem_limit_bytes=VMEM_LIMIT)

    far_gen = exchange(generators[0], pair_bit)
    gathered = lax.all_gather(cotangent, "tensor", axis=0, tiled=False)
    flat = generators.reshape(sections * rows, block)
    square = (block * block, lanes)
    inv, near, ffar, bfar, xs = pl.pallas_call(
        rotate_kernel,
        out_shape=(
            jax.ShapeDtypeStruct(square, f32),
            jax.ShapeDtypeStruct((sections - 1, rows, GROUP), f32),
            jax.ShapeDtypeStruct((2, rows, GROUP), f32),
            jax.ShapeDtypeStruct((2, rows, GROUP), f32),
            jax.ShapeDtypeStruct((sections - 1, count, rows), f32),
        ),
        in_specs=[scalars, scalars, full, full, full],
        out_specs=(full,) * 5,
        scratch_shapes=[
            pltpu.VMEM((sections * rows, block), f32),
            pltpu.VMEM((sections * rows, block), f32),
            pltpu.VMEM(square, f32),
            pltpu.VMEM(square, f32),
            pltpu.VMEM((sections * rows, block), f32),
            pltpu.VMEM((sections * rows, block), f32),
        ],
        compiler_params=params,
        name="rotations",
    )(orders, high, flat, far_gen, tokens)
    x_other = exchange(xs[0], pair_bit)
    x_both = pl.pallas_call(
        far_kernel,
        out_shape=jax.ShapeDtypeStruct((2 * count, rows), jnp.bfloat16),
        in_specs=[full] * 3,
        out_specs=full,
        compiler_params=params,
        name="far_apply",
    )(xs, x_other, ffar)

    reverse = np.array(
        [sum(((p >> b) & 1) << (bits - 1 - b) for b in range(bits)) for p in range(size)], np.int32
    )
    places = jnp.bitwise_xor(here.astype(jnp.int32), jnp.asarray(reverse))
    outs = []
    for chunk in range(CHUNKS):
        send = project(x_both, weight, places[size // 2 :], chunk, CHUNKS)
        keep = project(x_both, weight, places[: size // 2], chunk, CHUNKS)
        outs.append((send, keep))
    done = []
    for send, keep in outs:
        for bit in range(bits):
            got = exchange(send, bit)
            if bit < bits - 1:
                mid = keep.shape[0] // 2
                send, keep = keep[mid:] + got[mid:], keep[:mid] + got[:mid]
            else:
                keep = keep + got
        done.append(keep[0])
    outputs = jnp.concatenate(done, axis=1)

    grad_cols = project_back(gathered, weight)
    grad_other = exchange(grad_cols, pair_bit)
    numbers = jnp.arange(block, dtype=jnp.int32)
    inverse = jnp.sum(
        jnp.where(orders[:, :, None] == numbers[None, None, :], numbers[None, :, None], 0), axis=1
    ).astype(jnp.int32)
    grad_tokens, grad_gens = pl.pallas_call(
        grads_kernel,
        out_shape=(
            jax.ShapeDtypeStruct((count, rows), f32),
            jax.ShapeDtypeStruct((sections * rows, block), f32),
        ),
        in_specs=[scalars, scalars] + [full] * 8,
        out_specs=(full,) * 2,
        scratch_shapes=[
            pltpu.VMEM((sections * rows, block), f32),
            pltpu.VMEM((sections * rows, block), f32),
            pltpu.VMEM((sections * rows, block), f32),
            pltpu.VMEM(square, f32),
            pltpu.VMEM(square, f32),
            pltpu.VMEM(square, f32),
        ],
        compiler_params=params,
        name="gradients",
    )(inverse, high, grad_cols, grad_other, x_other, tokens, xs, near, bfar, inv)
    return outputs, grad_tokens, grad_gens.reshape(sections, rows, block)


def solution(mesh):
    placed = (
        P("groups", "tensor"),
        P("tensor", None),
        P("groups", "tensor", None),
        P(),
        P("groups", "tensor"),
    )
    return jax.shard_map(
        local,
        mesh=mesh,
        in_specs=placed,
        out_specs=(P("groups", "tensor"), P("groups", "tensor"), P("groups", "tensor", None)),
        check_vma=False,
    )
```

```python
import functools

import jax
import jax.numpy as jnp
import numpy as np
from jax import lax
from jax.experimental import pallas as pl
from jax.experimental.pallas import tpu as pltpu
from jax.sharding import PartitionSpec as P

VMEM_LIMIT = 16 * 2**20
WIDE_LIMIT = 40 * 2**20
GROUP = 128
NN = (((1,), (0,)), ((), ()))
NT = (((1,), (1,)), ((), ()))
TN = (((0,), (0,)), ((), ()))
CHUNKS = 2


def exchange(array, bit):
    size = lax.axis_size("tensor")
    return lax.ppermute(array, "tensor", [(i, i ^ (1 << bit)) for i in range(size)])


def parts_of(x):
    first = x.astype(jnp.bfloat16)
    return first, (x - first.astype(jnp.float32)).astype(jnp.bfloat16)


def one_dot(a, b, dims=NN):
    return lax.dot_general(a, b, dims, preferred_element_type=jnp.float32)


def dot(a, b, dims=NN):
    a_first, a_rest = parts_of(a)
    b_first, b_rest = parts_of(b)
    return (
        one_dot(a_first, b_first, dims) + one_dot(a_rest, b_first, dims) + one_dot(a_first, b_rest, dims)
    )


def pick(a, chooser):
    first, rest = parts_of(a)
    return one_dot(first, chooser) + one_dot(rest, chooser)


def iota(shape, dim):
    return lax.broadcasted_iota(jnp.int32, shape, dim)


def split_halves(rows_ref, lo_ref, hi_ref, section, rows, half):
    step = half << (section - 1)
    base = section * rows
    for start in range(base, base + rows, 2 * step):
        low = rows_ref[start : start + step, :]
        high = rows_ref[start + step : start + 2 * step, :]
        lo_ref[start : start + step, :] = low
        lo_ref[start + step : start + 2 * step, :] = low
        hi_ref[start : start + step, :] = high
        hi_ref[start + step : start + 2 * step, :] = high


def to_lanes(lo_ref, hi_ref, out_ref, lanes, half, block):
    for a in range(half):
        out_ref[a * block : (a + 1) * block, :] = lo_ref[pl.ds(a, lanes, stride=half), :].T
        out_ref[(half + a) * block : (half + a + 1) * block, :] = hi_ref[
            pl.ds(a, lanes, stride=half), :
        ].T


def by_section(parts, section_of):
    out = parts[-1]
    for k in range(len(parts) - 2, -1, -1):
        out = jnp.where(section_of == k, parts[k], out)
    return out


def lane_facts(shape, per_section, high):
    lane = iota(shape, 1)
    section_of = lane // per_section
    part = lane % per_section
    upper = jnp.bitwise_and(jnp.right_shift(part, jnp.maximum(section_of - 1, 0)), 1)
    return section_of, jnp.where(section_of == 0, high, upper) == 1


def block_masks(section, half):
    row = iota((GROUP, GROUP), 0) // half
    col = iota((GROUP, GROUP), 1) // half
    bit = 1 << (section - 1)
    return col == jnp.bitwise_and(row, ~bit), col == jnp.bitwise_or(row, bit)


def same_mask(half):
    return iota((GROUP, GROUP), 0) // half == iota((GROUP, GROUP), 1) // half


def spreader(offsets, block, half):
    row, col = iota((block, GROUP), 0), iota((block, GROUP), 1) % half
    return jnp.concatenate([(row == at + col).astype(jnp.bfloat16) for at in offsets], axis=1)


def gatherer(offset, block, half):
    row, col = iota((GROUP, block), 0) % half, iota((GROUP, block), 1)
    return (col == offset + row).astype(jnp.bfloat16)


def invert_blocks(orders_ref, lo_ref, hi_ref, inv_ref, a_ref, b_ref, section_of):
    sections, block = orders_ref.shape
    half = block // 2
    lanes = inv_ref.shape[1]
    to_lanes(lo_ref, hi_ref, a_ref, lanes, half, block)

    def permute_rows(i, _):
        parts = [
            a_ref[pl.ds(pl.multiple_of(orders_ref[k, i] * block, block), block), :]
            for k in range(sections)
        ]
        b_ref[pl.ds(pl.multiple_of(i * block, block), block), :] = by_section(parts, section_of)
        return 0

    lax.fori_loop(0, block, permute_rows, 0, unroll=4)

    def permute_cols(j, _):
        parts = [
            b_ref[pl.ds(orders_ref[k, j], block, stride=block), :] for k in range(sections)
        ]
        a_ref[pl.ds(pl.multiple_of(j * block, block), block), :] = by_section(parts, section_of)
        return 0

    lax.fori_loop(0, block, permute_cols, 0, unroll=4)
    sub = iota((block, lanes), 0)
    for j in range(block):
        inv_ref[j * block : (j + 1) * block, :] = (
            a_ref[j * block : (j + 1) * block, :]
            - a_ref[pl.ds(j, block, stride=block), :]
            + (sub == j).astype(jnp.float32)
        )

    def eliminate(k, _):
        at = pl.multiple_of(k * block, block)
        here = sub == k
        inverse = 1.0 / inv_ref[pl.ds(at + k, 1), :]
        factors = inv_ref[pl.ds(k, block, stride=block), :]
        pivot = jnp.where(here, inverse, inv_ref[pl.ds(at, block), :] * inverse)
        for i in range(block):
            row = inv_ref[i * block : (i + 1) * block, :]
            inv_ref[i * block : (i + 1) * block, :] = (
                jnp.where(here, 0.0, row) - factors[i : i + 1, :] * pivot
            )
        inv_ref[pl.ds(at, block), :] = pivot
        return 0

    lax.fori_loop(0, block, eliminate, 0)


def own_rows(inv_ref, out_ref, half, block, upper):
    lanes = inv_ref.shape[1]
    sub = iota((block, lanes), 0)
    for a in range(half):
        low = 2.0 * inv_ref[a * block : (a + 1) * block, :] - (sub == a).astype(jnp.float32)
        top = 2.0 * inv_ref[(half + a) * block : (half + a + 1) * block, :] - (
            sub == half + a
        ).astype(jnp.float32)
        out_ref[pl.ds(a, lanes, stride=half), :] = jnp.where(upper, top, low).T


def own_cols(inv_ref, out_ref, half, block, upper):
    lanes = inv_ref.shape[1]
    sub = iota((block, lanes), 0)
    for a in range(half):
        low = 2.0 * inv_ref[pl.ds(a, block, stride=block), :] - (sub == a).astype(jnp.float32)
        top = 2.0 * inv_ref[pl.ds(half + a, block, stride=block), :] - (sub == half + a).astype(
            jnp.float32
        )
        out_ref[pl.ds(a, lanes, stride=half), :] = jnp.where(upper, top, low).T


def near_kernel(
    orders_ref, gen_ref, tok_ref, inv_ref, near_ref, xs_ref, lo_ref, hi_ref, a_ref, b_ref, row_ref
):
    sections, block = orders_ref.shape
    half = block // 2
    rows = tok_ref.shape[1]
    lanes = sections * rows // half
    lo_ref[0:rows, :] = gen_ref[0:rows, :]
    hi_ref[0:rows, :] = gen_ref[0:rows, :]
    for k in range(1, sections):
        split_halves(gen_ref, lo_ref, hi_ref, k, rows, half)
    section_of, upper = lane_facts((block, lanes), rows // half, 0)
    invert_blocks(orders_ref, lo_ref, hi_ref, inv_ref, a_ref, b_ref, section_of)
    own_rows(inv_ref, row_ref, half, block, upper)
    spread = spreader((0, half), block, half)
    for k in range(1, sections):
        lo_mask, hi_mask = block_masks(k, half)
        wide = pick(row_ref[k * rows : (k + 1) * rows, :], spread)
        for start in range(0, rows, GROUP):
            part = wide[start : start + GROUP]
            near_ref[k - 1, start : start + GROUP, :] = jnp.where(
                lo_mask, part[:, :GROUP], jnp.where(hi_mask, part[:, GROUP:], 0.0)
            )
    for start in range(0, rows, GROUP):
        stop = start + GROUP
        value = tok_ref[:, start:stop].astype(jnp.float32)
        for k in range(sections - 1, 0, -1):
            value = dot(value, near_ref[k - 1, start:stop, :])
            xs_ref[k - 1, :, start:stop] = value


def far_rotations_kernel(
    orders_ref, high_ref, own_ref, far_ref, inv_ref, ffar_ref, bfar_ref,
    lo_ref, hi_ref, a_ref, b_ref, row_ref, col_ref,
):
    block = orders_ref.shape[1]
    half = block // 2
    rows = far_ref.shape[0]
    high = high_ref[0]
    own = own_ref[...]
    other = far_ref[...]
    lo_ref[...] = jnp.where(high == 1, other, own)
    hi_ref[...] = jnp.where(high == 1, own, other)
    invert_blocks(orders_ref, lo_ref, hi_ref, inv_ref, a_ref, b_ref, None)
    upper = high == 1
    own_rows(inv_ref, row_ref, half, block, upper)
    own_cols(inv_ref, col_ref, half, block, upper)
    spread = spreader((half * high, half * (1 - high)), block, half)
    same = same_mask(half)
    for source, target in ((col_ref, ffar_ref), (row_ref, bfar_ref)):
        wide = pick(source[...], spread)
        for start in range(0, rows, GROUP):
            part = wide[start : start + GROUP]
            target[0, start : start + GROUP, :] = jnp.where(same, part[:, :GROUP], 0.0)
            target[1, start : start + GROUP, :] = jnp.where(same, part[:, GROUP:], 0.0)


def far_kernel(own_ref, oth_ref, far_ref, out_ref):
    count, rows = own_ref.shape[1:]
    for start in range(0, rows, GROUP):
        stop = start + GROUP
        value = dot(own_ref[0, :, start:stop], far_ref[0, start:stop, :], NT) + dot(
            oth_ref[:, start:stop], far_ref[1, start:stop, :], NT
        )
        first = value.astype(jnp.bfloat16)
        out_ref[0:count, start:stop] = first
        out_ref[count : 2 * count, start:stop] = (value - first.astype(jnp.float32)).astype(
            jnp.bfloat16
        )


def project_kernel(chunk, places_ref, x_ref, w_ref, out_ref):
    pieces, count, width = out_ref.shape

    def body(p, _):
        at = pl.multiple_of((places_ref[p] * CHUNKS + chunk) * width, width)
        both = one_dot(x_ref[...], w_ref[:, pl.ds(at, width)])
        out_ref[p] = both[:count] + both[count:]
        return 0

    lax.fori_loop(0, pieces, body, 0)


def project(x_both, weight, places, chunk):
    pieces = places.shape[0]
    count2, rows = x_both.shape
    count = count2 // 2
    width = weight.shape[1] // lax.axis_size("tensor") // CHUNKS
    return pl.pallas_call(
        functools.partial(project_kernel, chunk),
        out_shape=jax.ShapeDtypeStruct((pieces, count, width), jnp.float32),
        in_specs=[pl.BlockSpec(memory_space=pltpu.SMEM)] + [pl.BlockSpec(memory_space=pltpu.VMEM)] * 2,
        out_specs=pl.BlockSpec(memory_space=pltpu.VMEM),
        compiler_params=pltpu.CompilerParams(vmem_limit_bytes=WIDE_LIMIT),
        cost_estimate=pl.CostEstimate(
            flops=2 * count2 * rows * width * pieces,
            bytes_accessed=pieces * width * 4 * count,
            transcendentals=0,
        ),
        name="project",
    )(places, x_both, weight)


def back_kernel(cot_ref, w_ref, out_ref):
    pieces, count, width = cot_ref.shape
    total = jnp.zeros(out_ref.shape, jnp.float32)
    for p in range(pieces):
        total += one_dot(cot_ref[p], w_ref[:, p * width : (p + 1) * width], NT)
    out_ref[...] = total


def project_back(gathered, weight):
    pieces, count, width = gathered.shape
    rows = weight.shape[0]
    return pl.pallas_call(
        back_kernel,
        out_shape=jax.ShapeDtypeStruct((count, rows), jnp.float32),
        in_specs=[pl.BlockSpec(memory_space=pltpu.VMEM)] * 2,
        out_specs=pl.BlockSpec(memory_space=pltpu.VMEM),
        compiler_params=pltpu.CompilerParams(vmem_limit_bytes=WIDE_LIMIT),
        cost_estimate=pl.CostEstimate(
            flops=2 * count * rows * width * pieces,
            bytes_accessed=pieces * width * 2 * (rows + count),
            transcendentals=0,
        ),
        name="project_back",
    )(gathered, weight)


def lane_matmul(left_ref, right_ref, out_ref, block, lanes):
    step = 4

    def body(t, _):
        first = t * step
        totals = [jnp.zeros((block, lanes), jnp.float32) for _ in range(step)]
        for j in range(block):
            right = right_ref[j * block : (j + 1) * block, :]
            for s in range(step):
                totals[s] += left_ref[pl.ds((first + s) * block + j, 1), :] * right
        for s in range(step):
            out_ref[pl.ds(pl.multiple_of((first + s) * block, block), block), :] = totals[s]
        return 0

    lax.fori_loop(0, block // step, body, 0)


def grads_kernel(
    inverse_ref, high_ref, own_ref, oth_ref, x_oth_ref, tok_ref, xs_ref, near_ref, bfar_ref, inv_far_ref, inv_ref,
    gtok_ref, ggen_ref,
    row_ref, lo_ref, hi_ref, a_ref, b_ref, c_ref,
):
    sections, block = inverse_ref.shape
    half = block // 2
    count, rows = own_ref.shape
    per_section = rows // half
    lanes = sections * per_section
    high = high_ref[0]
    gather_lo = gatherer(0, block, half)
    gather_hi = gatherer(half, block, half)
    gather_own = gatherer(half * high, block, half)
    gather_oth = gatherer(half * (1 - high), block, half)
    same = same_mask(half)
    for start in range(0, rows, GROUP):
        stop = start + GROUP
        x_own = xs_ref[0, :, start:stop]
        x_oth = x_oth_ref[:, start:stop]
        g_own = own_ref[:, start:stop]
        g_oth = oth_ref[:, start:stop]

        def far_rows(x):
            return pick(jnp.where(same, dot(x, g_own, TN), 0.0), gather_own) + pick(
                jnp.where(same, dot(x, g_oth, TN), 0.0), gather_oth
            )

        mine, theirs = far_rows(x_own), far_rows(x_oth)
        lo_ref[start:stop, :] = jnp.where(high == 1, theirs, mine)
        hi_ref[start:stop, :] = jnp.where(high == 1, mine, theirs)
        grad = dot(g_own, bfar_ref[0, start:stop, :], NT) + dot(g_oth, bfar_ref[1, start:stop, :], NT)
        for k in range(1, sections):
            lo_mask, hi_mask = block_masks(k, half)
            if k < sections - 1:
                x = xs_ref[k, :, start:stop]
            else:
                x = tok_ref[:, start:stop].astype(jnp.float32)
            outer = dot(x, grad, TN)
            row_ref[k * rows + start : k * rows + stop, :] = pick(
                jnp.where(lo_mask, outer, 0.0), gather_lo
            ) + pick(jnp.where(hi_mask, outer, 0.0), gather_hi)
            grad = dot(grad, near_ref[k - 1, start:stop, :], NT)
        gtok_ref[:, start:stop] = grad
    for k in range(1, sections):
        split_halves(row_ref, lo_ref, hi_ref, k, rows, half)
    to_lanes(lo_ref, hi_ref, a_ref, lanes, half, block)
    for j in range(block):
        b_ref[j * block : (j + 1) * block, :] = inv_ref[pl.ds(j, block, stride=block), :]
        b_ref[j * block : (j + 1) * block, 0:per_section] = inv_far_ref[
            pl.ds(j, block, stride=block), :
        ]
    lane_matmul(a_ref, b_ref, c_ref, block, lanes)
    lane_matmul(b_ref, c_ref, a_ref, block, lanes)
    for j in range(block):
        c_ref[j * block : (j + 1) * block, :] = 2.0 * (
            a_ref[j * block : (j + 1) * block, :] - a_ref[pl.ds(j, block, stride=block), :]
        )
    section_of, upper = lane_facts((block, lanes), per_section, high)

    def permute_cols(j, _):
        parts = [
            c_ref[pl.ds(inverse_ref[k, j], block, stride=block), :] for k in range(sections)
        ]
        b_ref[pl.ds(pl.multiple_of(j * block, block), block), :] = by_section(parts, section_of)
        return 0

    lax.fori_loop(0, block, permute_cols, 0, unroll=4)
    for a in range(half):
        low, top = [
            by_section(
                [
                    b_ref[pl.ds(inverse_ref[k, at], block, stride=block), :]
                    for k in range(sections)
                ],
                section_of,
            )
            for at in (a, half + a)
        ]
        ggen_ref[pl.ds(a, lanes, stride=half), :] = jnp.where(upper, top, low).T


def local(tokens, weight, generators, orders, cotangent):
    sections, rows, block = generators.shape
    half = block // 2
    count = tokens.shape[0]
    size = lax.axis_size("tensor")
    bits = size.bit_length() - 1
    here = lax.axis_index("tensor")
    pair_bit = bits - 1
    high = jnp.bitwise_and(jnp.right_shift(here, pair_bit), 1).astype(jnp.int32).reshape(1)
    lanes = sections * (rows // half)
    f32 = jnp.float32
    full = pl.BlockSpec(memory_space=pltpu.VMEM)
    scalars = pl.BlockSpec(memory_space=pltpu.SMEM)
    params = pltpu.CompilerParams(vmem_limit_bytes=VMEM_LIMIT)

    far_gen = exchange(generators[0], pair_bit)
    gathered = lax.all_gather(cotangent, "tensor", axis=0, tiled=False)
    flat = generators.reshape(sections * rows, block)
    square = (block * block, lanes)
    far_square = (block * block, lanes // sections)
    inv, near, xs = pl.pallas_call(
        near_kernel,
        out_shape=(
            jax.ShapeDtypeStruct(square, f32),
            jax.ShapeDtypeStruct((sections - 1, rows, GROUP), f32),
            jax.ShapeDtypeStruct((sections - 1, count, rows), f32),
        ),
        in_specs=[scalars, full, full],
        out_specs=(full,) * 3,
        scratch_shapes=[
            pltpu.VMEM((sections * rows, block), f32),
            pltpu.VMEM((sections * rows, block), f32),
            pltpu.VMEM(square, f32),
            pltpu.VMEM(square, f32),
            pltpu.VMEM((sections * rows, block), f32),
        ],
        compiler_params=params,
        name="near_rotations",
    )(orders, flat, tokens)
    x_other = exchange(xs[0], pair_bit)
    inv_far, ffar, bfar = pl.pallas_call(
        far_rotations_kernel,
        out_shape=(
            jax.ShapeDtypeStruct(far_square, f32),
            jax.ShapeDtypeStruct((2, rows, GROUP), f32),
            jax.ShapeDtypeStruct((2, rows, GROUP), f32),
        ),
        in_specs=[scalars, scalars, full, full],
        out_specs=(full,) * 3,
        scratch_shapes=[
            pltpu.VMEM((rows, block), f32),
            pltpu.VMEM((rows, block), f32),
            pltpu.VMEM(far_square, f32),
            pltpu.VMEM(far_square, f32),
            pltpu.VMEM((rows, block), f32),
            pltpu.VMEM((rows, block), f32),
        ],
        compiler_params=params,
        cost_estimate=pl.CostEstimate(flops=10**7, bytes_accessed=10**7, transcendentals=0),
        name="far_rotations",
    )(orders[:1], high, generators[0], far_gen)
    x_both = pl.pallas_call(
        far_kernel,
        out_shape=jax.ShapeDtypeStruct((2 * count, rows), jnp.bfloat16),
        in_specs=[full] * 3,
        out_specs=full,
        compiler_params=params,
        name="far_apply",
    )(xs, x_other, ffar)

    reverse = np.array(
        [sum(((p >> b) & 1) << (bits - 1 - b) for b in range(bits)) for p in range(size)], np.int32
    )
    places = jnp.bitwise_xor(here.astype(jnp.int32), jnp.asarray(reverse))
    outs = []
    for chunk in range(CHUNKS):
        send = project(x_both, weight, places[size // 2 :], chunk)
        keep = project(x_both, weight, places[: size // 2], chunk)
        outs.append((send, keep))
    def stage(pair, got):
        send, keep = pair
        if keep.shape[0] == 1:
            return None, keep + got
        mid = keep.shape[0] // 2
        return keep[mid:] + got[mid:], keep[:mid] + got[:mid]

    for bit in range(bits):
        gots = [exchange(send, bit) for send, _ in outs]
        if bit == min(1, bits - 1):
            grad_cols = project_back(gathered, weight)
            grad_cols, *gots = lax.optimization_barrier([grad_cols] + gots)
            grad_other = exchange(grad_cols, pair_bit)
        outs = [stage(pair, got) for pair, got in zip(outs, gots)]
    outputs = jnp.concatenate([keep[0] for _, keep in outs], axis=1)

    numbers = jnp.arange(block, dtype=jnp.int32)
    inverse = jnp.sum(
        jnp.where(orders[:, :, None] == numbers[None, None, :], numbers[None, :, None], 0), axis=1
    ).astype(jnp.int32)
    grad_tokens, grad_gens = pl.pallas_call(
        grads_kernel,
        out_shape=(
            jax.ShapeDtypeStruct((count, rows), f32),
            jax.ShapeDtypeStruct((sections * rows, block), f32),
        ),
        in_specs=[scalars, scalars] + [full] * 9,
        out_specs=(full,) * 2,
        scratch_shapes=[
            pltpu.VMEM((sections * rows, block), f32),
            pltpu.VMEM((sections * rows, block), f32),
            pltpu.VMEM((sections * rows, block), f32),
            pltpu.VMEM(square, f32),
            pltpu.VMEM(square, f32),
            pltpu.VMEM(square, f32),
        ],
        compiler_params=params,
        name="gradients",
    )(inverse, high, grad_cols, grad_other, x_other, tokens, xs, near, bfar, inv_far, inv)
    return outputs, grad_tokens, grad_gens.reshape(sections, rows, block)


def solution(mesh):
    placed = (
        P("groups", "tensor"),
        P("tensor", None),
        P("groups", "tensor", None),
        P(),
        P("groups", "tensor"),
    )
    return jax.shard_map(
        local,
        mesh=mesh,
        in_specs=placed,
        out_specs=(P("groups", "tensor"), P("groups", "tensor"), P("groups", "tensor", None)),
        check_vma=False,
    )
```

```python
import functools

import jax
import jax.numpy as jnp
import numpy as np
from jax import lax
from jax.experimental import pallas as pl
from jax.experimental.pallas import tpu as pltpu
from jax.sharding import PartitionSpec as P

VMEM_LIMIT = 16 * 2**20
WIDE_LIMIT = 50 * 2**20
GROUP = 128
NN = (((1,), (0,)), ((), ()))
NT = (((1,), (1,)), ((), ()))
TN = (((0,), (0,)), ((), ()))
CHUNKS = 2


def exchange(array, bit):
    size = lax.axis_size("tensor")
    return lax.ppermute(array, "tensor", [(i, i ^ (1 << bit)) for i in range(size)])


def parts_of(x):
    first = x.astype(jnp.bfloat16)
    return first, (x - first.astype(jnp.float32)).astype(jnp.bfloat16)


def one_dot(a, b, dims=NN):
    return lax.dot_general(a, b, dims, preferred_element_type=jnp.float32)


def dot(a, b, dims=NN):
    a_first, a_rest = parts_of(a)
    b_first, b_rest = parts_of(b)
    return (
        one_dot(a_first, b_first, dims) + one_dot(a_rest, b_first, dims) + one_dot(a_first, b_rest, dims)
    )


def pick(a, chooser):
    first, rest = parts_of(a)
    return one_dot(first, chooser) + one_dot(rest, chooser)


def iota(shape, dim):
    return lax.broadcasted_iota(jnp.int32, shape, dim)


def split_halves(rows_ref, lo_ref, hi_ref, section, rows, half):
    step = half << (section - 1)
    base = section * rows
    for start in range(base, base + rows, 2 * step):
        low = rows_ref[start : start + step, :]
        high = rows_ref[start + step : start + 2 * step, :]
        lo_ref[start : start + step, :] = low
        lo_ref[start + step : start + 2 * step, :] = low
        hi_ref[start : start + step, :] = high
        hi_ref[start + step : start + 2 * step, :] = high


def to_lanes(lo_ref, hi_ref, out_ref, lanes, half, block):
    for a in range(half):
        out_ref[a * block : (a + 1) * block, :] = lo_ref[pl.ds(a, lanes, stride=half), :].T
        out_ref[(half + a) * block : (half + a + 1) * block, :] = hi_ref[
            pl.ds(a, lanes, stride=half), :
        ].T


def by_section(parts, section_of):
    out = parts[-1]
    for k in range(len(parts) - 2, -1, -1):
        out = jnp.where(section_of == k, parts[k], out)
    return out


def lane_facts(shape, per_section, high):
    lane = iota(shape, 1)
    section_of = lane // per_section
    part = lane % per_section
    upper = jnp.bitwise_and(jnp.right_shift(part, jnp.maximum(section_of - 1, 0)), 1)
    return section_of, jnp.where(section_of == 0, high, upper) == 1


def block_masks(section, half):
    row = iota((GROUP, GROUP), 0) // half
    col = iota((GROUP, GROUP), 1) // half
    bit = 1 << (section - 1)
    return col == jnp.bitwise_and(row, ~bit), col == jnp.bitwise_or(row, bit)


def same_mask(half):
    return iota((GROUP, GROUP), 0) // half == iota((GROUP, GROUP), 1) // half


def spreader(offsets, block, half):
    row, col = iota((block, GROUP), 0), iota((block, GROUP), 1) % half
    return jnp.concatenate([(row == at + col).astype(jnp.bfloat16) for at in offsets], axis=1)


def gatherer(offset, block, half):
    row, col = iota((GROUP, block), 0) % half, iota((GROUP, block), 1)
    return (col == offset + row).astype(jnp.bfloat16)


def invert_blocks(orders_ref, lo_ref, hi_ref, inv_ref, a_ref, b_ref, section_of):
    sections, block = orders_ref.shape
    half = block // 2
    lanes = inv_ref.shape[1]
    to_lanes(lo_ref, hi_ref, a_ref, lanes, half, block)

    def permute_rows(i, _):
        parts = [
            a_ref[pl.ds(pl.multiple_of(orders_ref[k, i] * block, block), block), :]
            for k in range(sections)
        ]
        b_ref[pl.ds(pl.multiple_of(i * block, block), block), :] = by_section(parts, section_of)
        return 0

    lax.fori_loop(0, block, permute_rows, 0, unroll=4)

    def permute_cols(j, _):
        parts = [
            b_ref[pl.ds(orders_ref[k, j], block, stride=block), :] for k in range(sections)
        ]
        a_ref[pl.ds(pl.multiple_of(j * block, block), block), :] = by_section(parts, section_of)
        return 0

    lax.fori_loop(0, block, permute_cols, 0, unroll=4)
    sub = iota((block, lanes), 0)
    for j in range(block):
        inv_ref[j * block : (j + 1) * block, :] = (
            a_ref[j * block : (j + 1) * block, :]
            - a_ref[pl.ds(j, block, stride=block), :]
            + (sub == j).astype(jnp.float32)
        )

    def eliminate(k, _):
        at = pl.multiple_of(k * block, block)
        here = sub == k
        inverse = 1.0 / inv_ref[pl.ds(at + k, 1), :]
        factors = inv_ref[pl.ds(k, block, stride=block), :]
        pivot = jnp.where(here, inverse, inv_ref[pl.ds(at, block), :] * inverse)
        for i in range(block):
            row = inv_ref[i * block : (i + 1) * block, :]
            inv_ref[i * block : (i + 1) * block, :] = (
                jnp.where(here, 0.0, row) - factors[i : i + 1, :] * pivot
            )
        inv_ref[pl.ds(at, block), :] = pivot
        return 0

    lax.fori_loop(0, block, eliminate, 0)


def own_rows(inv_ref, out_ref, half, block, upper):
    lanes = inv_ref.shape[1]
    sub = iota((block, lanes), 0)
    for a in range(half):
        low = 2.0 * inv_ref[a * block : (a + 1) * block, :] - (sub == a).astype(jnp.float32)
        top = 2.0 * inv_ref[(half + a) * block : (half + a + 1) * block, :] - (
            sub == half + a
        ).astype(jnp.float32)
        out_ref[pl.ds(a, lanes, stride=half), :] = jnp.where(upper, top, low).T


def own_cols(inv_ref, out_ref, half, block, upper):
    lanes = inv_ref.shape[1]
    sub = iota((block, lanes), 0)
    for a in range(half):
        low = 2.0 * inv_ref[pl.ds(a, block, stride=block), :] - (sub == a).astype(jnp.float32)
        top = 2.0 * inv_ref[pl.ds(half + a, block, stride=block), :] - (sub == half + a).astype(
            jnp.float32
        )
        out_ref[pl.ds(a, lanes, stride=half), :] = jnp.where(upper, top, low).T


def near_kernel(
    orders_ref, gen_ref, tok_ref, inv_ref, near_ref, xs_ref, lo_ref, hi_ref, a_ref, b_ref, row_ref
):
    sections, block = orders_ref.shape
    half = block // 2
    rows = tok_ref.shape[1]
    lanes = sections * rows // half
    lo_ref[0:rows, :] = gen_ref[0:rows, :]
    hi_ref[0:rows, :] = gen_ref[0:rows, :]
    for k in range(1, sections):
        split_halves(gen_ref, lo_ref, hi_ref, k, rows, half)
    section_of, upper = lane_facts((block, lanes), rows // half, 0)
    invert_blocks(orders_ref, lo_ref, hi_ref, inv_ref, a_ref, b_ref, section_of)
    own_rows(inv_ref, row_ref, half, block, upper)
    spread = spreader((0, half), block, half)
    for k in range(1, sections):
        lo_mask, hi_mask = block_masks(k, half)
        wide = pick(row_ref[k * rows : (k + 1) * rows, :], spread)
        for start in range(0, rows, GROUP):
            part = wide[start : start + GROUP]
            near_ref[k - 1, start : start + GROUP, :] = jnp.where(
                lo_mask, part[:, :GROUP], jnp.where(hi_mask, part[:, GROUP:], 0.0)
            )
    for start in range(0, rows, GROUP):
        stop = start + GROUP
        value = tok_ref[:, start:stop].astype(jnp.float32)
        for k in range(sections - 1, 0, -1):
            value = dot(value, near_ref[k - 1, start:stop, :])
            xs_ref[k - 1, :, start:stop] = value


def far_rotations_kernel(
    orders_ref, high_ref, own_ref, far_ref, inv_ref, ffar_ref, bfar_ref,
    lo_ref, hi_ref, a_ref, b_ref, row_ref, col_ref,
):
    block = orders_ref.shape[1]
    half = block // 2
    rows = far_ref.shape[0]
    high = high_ref[0]
    own = own_ref[...]
    other = far_ref[...]
    lo_ref[...] = jnp.where(high == 1, other, own)
    hi_ref[...] = jnp.where(high == 1, own, other)
    invert_blocks(orders_ref, lo_ref, hi_ref, inv_ref, a_ref, b_ref, None)
    upper = high == 1
    own_rows(inv_ref, row_ref, half, block, upper)
    own_cols(inv_ref, col_ref, half, block, upper)
    spread = spreader((half * high, half * (1 - high)), block, half)
    same = same_mask(half)
    for source, target in ((col_ref, ffar_ref), (row_ref, bfar_ref)):
        wide = pick(source[...], spread)
        for start in range(0, rows, GROUP):
            part = wide[start : start + GROUP]
            target[0, start : start + GROUP, :] = jnp.where(same, part[:, :GROUP], 0.0)
            target[1, start : start + GROUP, :] = jnp.where(same, part[:, GROUP:], 0.0)


def far_kernel(own_ref, oth_ref, far_ref, out_ref):
    count, rows = own_ref.shape[1:]
    for start in range(0, rows, GROUP):
        stop = start + GROUP
        value = dot(own_ref[0, :, start:stop], far_ref[0, start:stop, :], NT) + dot(
            oth_ref[:, start:stop], far_ref[1, start:stop, :], NT
        )
        first = value.astype(jnp.bfloat16)
        out_ref[0:count, start:stop] = first
        out_ref[count : 2 * count, start:stop] = (value - first.astype(jnp.float32)).astype(
            jnp.bfloat16
        )


def project_kernel(chunk, places_ref, x_ref, w_ref, out_ref, held_ref, sems):
    pieces, count, width = out_ref.shape

    def fetch(p):
        at = pl.multiple_of((places_ref[p] * CHUNKS + chunk) * width, width)
        return pltpu.make_async_copy(w_ref.at[:, pl.ds(at, width)], held_ref.at[p], sems.at[p])

    for p in range(pieces):
        fetch(p).start()
    for p in range(pieces):
        fetch(p).wait()
        both = one_dot(x_ref[...], held_ref[p])
        out_ref[p] = both[:count] + both[count:]


def project(x_both, weight, places, chunk):
    pieces = places.shape[0]
    count2, rows = x_both.shape
    count = count2 // 2
    width = weight.shape[1] // lax.axis_size("tensor") // CHUNKS
    return pl.pallas_call(
        functools.partial(project_kernel, chunk),
        out_shape=jax.ShapeDtypeStruct((pieces, count, width), jnp.float32),
        in_specs=[
            pl.BlockSpec(memory_space=pltpu.SMEM),
            pl.BlockSpec(memory_space=pltpu.VMEM),
            pl.BlockSpec(memory_space=pl.ANY),
        ],
        out_specs=pl.BlockSpec(memory_space=pltpu.VMEM),
        scratch_shapes=[
            pltpu.VMEM((pieces, rows, width), weight.dtype),
            pltpu.SemaphoreType.DMA((pieces,)),
        ],
        compiler_params=pltpu.CompilerParams(vmem_limit_bytes=WIDE_LIMIT),
        cost_estimate=pl.CostEstimate(
            flops=2 * count2 * rows * width * pieces,
            bytes_accessed=pieces * width * (2 * rows + 4 * count),
            transcendentals=0,
        ),
        name="project",
    )(places, x_both, weight)


def back_kernel(cot_ref, w_ref, out_ref, cots_ref, held_ref, cot_sems, sems):
    pieces, _, width = cot_ref.shape

    def fetches(p):
        return (
            pltpu.make_async_copy(cot_ref.at[p], cots_ref.at[p], cot_sems.at[p]),
            pltpu.make_async_copy(
                w_ref.at[:, pl.ds(p * width, width)], held_ref.at[p], sems.at[p]
            ),
        )

    for p in range(pieces):
        for copy in fetches(p):
            copy.start()
    total = jnp.zeros(out_ref.shape, jnp.float32)
    for p in range(pieces):
        for copy in fetches(p):
            copy.wait()
        total += one_dot(cots_ref[p], held_ref[p], NT)
    out_ref[...] = total


def project_back(gathered, weight):
    pieces, count, width = gathered.shape
    rows = weight.shape[0]
    return pl.pallas_call(
        back_kernel,
        out_shape=jax.ShapeDtypeStruct((count, rows), jnp.float32),
        in_specs=[pl.BlockSpec(memory_space=pl.ANY)] * 2,
        out_specs=pl.BlockSpec(memory_space=pltpu.VMEM),
        scratch_shapes=[
            pltpu.VMEM((pieces, count, width), gathered.dtype),
            pltpu.VMEM((pieces, rows, width), weight.dtype),
            pltpu.SemaphoreType.DMA((pieces,)),
            pltpu.SemaphoreType.DMA((pieces,)),
        ],
        compiler_params=pltpu.CompilerParams(vmem_limit_bytes=WIDE_LIMIT),
        cost_estimate=pl.CostEstimate(
            flops=2 * count * rows * width * pieces,
            bytes_accessed=pieces * width * 2 * (rows + count),
            transcendentals=0,
        ),
        name="project_back",
    )(gathered, weight)


def lane_matmul(left_ref, right_ref, out_ref, block, lanes):
    step = 4

    def body(t, _):
        first = t * step
        totals = [jnp.zeros((block, lanes), jnp.float32) for _ in range(step)]
        for j in range(block):
            right = right_ref[j * block : (j + 1) * block, :]
            for s in range(step):
                totals[s] += left_ref[pl.ds((first + s) * block + j, 1), :] * right
        for s in range(step):
            out_ref[pl.ds(pl.multiple_of((first + s) * block, block), block), :] = totals[s]
        return 0

    lax.fori_loop(0, block // step, body, 0)


def grads_kernel(
    inverse_ref, high_ref, own_ref, oth_ref, x_oth_ref, tok_ref, xs_ref, near_ref, bfar_ref, inv_far_ref, inv_ref,
    gtok_ref, ggen_ref,
    row_ref, lo_ref, hi_ref, a_ref, b_ref, c_ref,
):
    sections, block = inverse_ref.shape
    half = block // 2
    count, rows = own_ref.shape
    per_section = rows // half
    lanes = sections * per_section
    high = high_ref[0]
    gather_lo = gatherer(0, block, half)
    gather_hi = gatherer(half, block, half)
    gather_own = gatherer(half * high, block, half)
    gather_oth = gatherer(half * (1 - high), block, half)
    same = same_mask(half)
    for start in range(0, rows, GROUP):
        stop = start + GROUP
        x_own = xs_ref[0, :, start:stop]
        x_oth = x_oth_ref[:, start:stop]
        g_own = own_ref[:, start:stop]
        g_oth = oth_ref[:, start:stop]

        def far_rows(x):
            return pick(jnp.where(same, dot(x, g_own, TN), 0.0), gather_own) + pick(
                jnp.where(same, dot(x, g_oth, TN), 0.0), gather_oth
            )

        mine, theirs = far_rows(x_own), far_rows(x_oth)
        lo_ref[start:stop, :] = jnp.where(high == 1, theirs, mine)
        hi_ref[start:stop, :] = jnp.where(high == 1, mine, theirs)
        grad = dot(g_own, bfar_ref[0, start:stop, :], NT) + dot(g_oth, bfar_ref[1, start:stop, :], NT)
        for k in range(1, sections):
            lo_mask, hi_mask = block_masks(k, half)
            if k < sections - 1:
                x = xs_ref[k, :, start:stop]
            else:
                x = tok_ref[:, start:stop].astype(jnp.float32)
            outer = dot(x, grad, TN)
            row_ref[k * rows + start : k * rows + stop, :] = pick(
                jnp.where(lo_mask, outer, 0.0), gather_lo
            ) + pick(jnp.where(hi_mask, outer, 0.0), gather_hi)
            grad = dot(grad, near_ref[k - 1, start:stop, :], NT)
        gtok_ref[:, start:stop] = grad
    for k in range(1, sections):
        split_halves(row_ref, lo_ref, hi_ref, k, rows, half)
    to_lanes(lo_ref, hi_ref, a_ref, lanes, half, block)
    for j in range(block):
        b_ref[j * block : (j + 1) * block, :] = inv_ref[pl.ds(j, block, stride=block), :]
        b_ref[j * block : (j + 1) * block, 0:per_section] = inv_far_ref[
            pl.ds(j, block, stride=block), :
        ]
    lane_matmul(a_ref, b_ref, c_ref, block, lanes)
    lane_matmul(b_ref, c_ref, a_ref, block, lanes)
    for j in range(block):
        c_ref[j * block : (j + 1) * block, :] = 2.0 * (
            a_ref[j * block : (j + 1) * block, :] - a_ref[pl.ds(j, block, stride=block), :]
        )
    section_of, upper = lane_facts((block, lanes), per_section, high)

    def permute_cols(j, _):
        parts = [
            c_ref[pl.ds(inverse_ref[k, j], block, stride=block), :] for k in range(sections)
        ]
        b_ref[pl.ds(pl.multiple_of(j * block, block), block), :] = by_section(parts, section_of)
        return 0

    lax.fori_loop(0, block, permute_cols, 0, unroll=4)
    for a in range(half):
        low, top = [
            by_section(
                [
                    b_ref[pl.ds(inverse_ref[k, at], block, stride=block), :]
                    for k in range(sections)
                ],
                section_of,
            )
            for at in (a, half + a)
        ]
        ggen_ref[pl.ds(a, lanes, stride=half), :] = jnp.where(upper, top, low).T


def local(tokens, weight, generators, orders, cotangent):
    sections, rows, block = generators.shape
    half = block // 2
    count = tokens.shape[0]
    size = lax.axis_size("tensor")
    bits = size.bit_length() - 1
    here = lax.axis_index("tensor")
    pair_bit = bits - 1
    high = jnp.bitwise_and(jnp.right_shift(here, pair_bit), 1).astype(jnp.int32).reshape(1)
    lanes = sections * (rows // half)
    f32 = jnp.float32
    full = pl.BlockSpec(memory_space=pltpu.VMEM)
    scalars = pl.BlockSpec(memory_space=pltpu.SMEM)
    params = pltpu.CompilerParams(vmem_limit_bytes=VMEM_LIMIT)

    far_gen = exchange(generators[0], pair_bit)
    gathered = lax.all_gather(cotangent, "tensor", axis=0, tiled=False)
    flat = generators.reshape(sections * rows, block)
    square = (block * block, lanes)
    far_square = (block * block, lanes // sections)
    inv, near, xs = pl.pallas_call(
        near_kernel,
        out_shape=(
            jax.ShapeDtypeStruct(square, f32),
            jax.ShapeDtypeStruct((sections - 1, rows, GROUP), f32),
            jax.ShapeDtypeStruct((sections - 1, count, rows), f32),
        ),
        in_specs=[scalars, full, full],
        out_specs=(full,) * 3,
        scratch_shapes=[
            pltpu.VMEM((sections * rows, block), f32),
            pltpu.VMEM((sections * rows, block), f32),
            pltpu.VMEM(square, f32),
            pltpu.VMEM(square, f32),
            pltpu.VMEM((sections * rows, block), f32),
        ],
        compiler_params=params,
        name="near_rotations",
    )(orders, flat, tokens)
    x_other = exchange(xs[0], pair_bit)
    inv_far, ffar, bfar = pl.pallas_call(
        far_rotations_kernel,
        out_shape=(
            jax.ShapeDtypeStruct(far_square, f32),
            jax.ShapeDtypeStruct((2, rows, GROUP), f32),
            jax.ShapeDtypeStruct((2, rows, GROUP), f32),
        ),
        in_specs=[scalars, scalars, full, full],
        out_specs=(full,) * 3,
        scratch_shapes=[
            pltpu.VMEM((rows, block), f32),
            pltpu.VMEM((rows, block), f32),
            pltpu.VMEM(far_square, f32),
            pltpu.VMEM(far_square, f32),
            pltpu.VMEM((rows, block), f32),
            pltpu.VMEM((rows, block), f32),
        ],
        compiler_params=params,
        cost_estimate=pl.CostEstimate(flops=10**7, bytes_accessed=10**7, transcendentals=0),
        name="far_rotations",
    )(orders[:1], high, generators[0], far_gen)
    x_both = pl.pallas_call(
        far_kernel,
        out_shape=jax.ShapeDtypeStruct((2 * count, rows), jnp.bfloat16),
        in_specs=[full] * 3,
        out_specs=full,
        compiler_params=params,
        name="far_apply",
    )(xs, x_other, ffar)

    reverse = np.array(
        [sum(((p >> b) & 1) << (bits - 1 - b) for b in range(bits)) for p in range(size)], np.int32
    )
    places = jnp.bitwise_xor(here.astype(jnp.int32), jnp.asarray(reverse))
    outs = []
    for chunk in range(CHUNKS):
        send = project(x_both, weight, places[size // 2 :], chunk)
        keep = project(x_both, weight, places[: size // 2], chunk)
        outs.append((send, keep))
    def stage(pair, got):
        send, keep = pair
        if keep.shape[0] == 1:
            return None, keep + got
        mid = keep.shape[0] // 2
        return keep[mid:] + got[mid:], keep[:mid] + got[:mid]

    numbers = jnp.arange(block, dtype=jnp.int32)
    inverse = jnp.sum(
        jnp.where(orders[:, :, None] == numbers[None, None, :], numbers[None, :, None], 0), axis=1
    ).astype(jnp.int32)
    for bit in range(bits):
        gots = [exchange(send, bit) for send, _ in outs]
        if bit == min(1, bits - 1):
            grad_cols = project_back(gathered, weight)
            grad_cols, gots[0] = lax.optimization_barrier((grad_cols, gots[0]))
            grad_other = exchange(grad_cols, pair_bit)
            grad_tokens, grad_gens = pl.pallas_call(
                grads_kernel,
                out_shape=(
                    jax.ShapeDtypeStruct((count, rows), f32),
                    jax.ShapeDtypeStruct((sections * rows, block), f32),
                ),
                in_specs=[scalars, scalars] + [full] * 9,
                out_specs=(full,) * 2,
                scratch_shapes=[
                    pltpu.VMEM((sections * rows, block), f32),
                    pltpu.VMEM((sections * rows, block), f32),
                    pltpu.VMEM((sections * rows, block), f32),
                    pltpu.VMEM(square, f32),
                    pltpu.VMEM(square, f32),
                    pltpu.VMEM(square, f32),
                ],
                compiler_params=params,
                name="gradients",
            )(inverse, high, grad_cols, grad_other, x_other, tokens, xs, near, bfar, inv_far, inv)
            grad_tokens, grad_gens, gots[-1] = lax.optimization_barrier(
                (grad_tokens, grad_gens, gots[-1])
            )
        outs = [stage(pair, got) for pair, got in zip(outs, gots)]
    outputs = jnp.concatenate([keep[0] for _, keep in outs], axis=1)
    return outputs, grad_tokens, grad_gens.reshape(sections, rows, block)


def solution(mesh):
    placed = (
        P("groups", "tensor"),
        P("tensor", None),
        P("groups", "tensor", None),
        P(),
        P("groups", "tensor"),
    )
    return jax.shard_map(
        local,
        mesh=mesh,
        in_specs=placed,
        out_specs=(P("groups", "tensor"), P("groups", "tensor"), P("groups", "tensor", None)),
        check_vma=False,
    )
```

```python
import functools

import jax
import jax.numpy as jnp
import numpy as np
from jax import lax
from jax.experimental import pallas as pl
from jax.experimental.pallas import tpu as pltpu
from jax.sharding import PartitionSpec as P

VMEM_LIMIT = 16 * 2**20
WIDE_LIMIT = 50 * 2**20
GROUP = 128
NN = (((1,), (0,)), ((), ()))
NT = (((1,), (1,)), ((), ()))
TN = (((0,), (0,)), ((), ()))
CHUNKS = 2


def exchange(array, bit):
    size = lax.axis_size("tensor")
    return lax.ppermute(array, "tensor", [(i, i ^ (1 << bit)) for i in range(size)])


def parts_of(x):
    first = x.astype(jnp.bfloat16)
    return first, (x - first.astype(jnp.float32)).astype(jnp.bfloat16)


def one_dot(a, b, dims=NN):
    return lax.dot_general(a, b, dims, preferred_element_type=jnp.float32)


def dot(a, b, dims=NN):
    a_first, a_rest = parts_of(a)
    b_first, b_rest = parts_of(b)
    return (
        one_dot(a_first, b_first, dims) + one_dot(a_rest, b_first, dims) + one_dot(a_first, b_rest, dims)
    )


def pick(a, chooser):
    first, rest = parts_of(a)
    return one_dot(first, chooser) + one_dot(rest, chooser)


def iota(shape, dim):
    return lax.broadcasted_iota(jnp.int32, shape, dim)


def split_halves(rows_ref, lo_ref, hi_ref, section, rows, half):
    step = half << (section - 1)
    base = section * rows
    for start in range(base, base + rows, 2 * step):
        low = rows_ref[start : start + step, :]
        high = rows_ref[start + step : start + 2 * step, :]
        lo_ref[start : start + step, :] = low
        lo_ref[start + step : start + 2 * step, :] = low
        hi_ref[start : start + step, :] = high
        hi_ref[start + step : start + 2 * step, :] = high


def to_lanes(lo_ref, hi_ref, out_ref, lanes, half, block):
    for a in range(half):
        out_ref[a * block : (a + 1) * block, :] = lo_ref[pl.ds(a, lanes, stride=half), :].T
        out_ref[(half + a) * block : (half + a + 1) * block, :] = hi_ref[
            pl.ds(a, lanes, stride=half), :
        ].T


def by_section(parts, section_of):
    out = parts[-1]
    for k in range(len(parts) - 2, -1, -1):
        out = jnp.where(section_of == k, parts[k], out)
    return out


def lane_facts(shape, per_section, high):
    lane = iota(shape, 1)
    section_of = lane // per_section
    part = lane % per_section
    upper = jnp.bitwise_and(jnp.right_shift(part, jnp.maximum(section_of - 1, 0)), 1)
    return section_of, jnp.where(section_of == 0, high, upper) == 1


def block_masks(section, half):
    row = iota((GROUP, GROUP), 0) // half
    col = iota((GROUP, GROUP), 1) // half
    bit = 1 << (section - 1)
    return col == jnp.bitwise_and(row, ~bit), col == jnp.bitwise_or(row, bit)


def same_mask(half):
    return iota((GROUP, GROUP), 0) // half == iota((GROUP, GROUP), 1) // half


def spreader(offsets, block, half):
    row, col = iota((block, GROUP), 0), iota((block, GROUP), 1) % half
    return jnp.concatenate([(row == at + col).astype(jnp.bfloat16) for at in offsets], axis=1)


def gatherer(offset, block, half):
    row, col = iota((GROUP, block), 0) % half, iota((GROUP, block), 1)
    return (col == offset + row).astype(jnp.bfloat16)


def invert_blocks(orders_ref, lo_ref, hi_ref, inv_ref, a_ref, b_ref, section_of):
    sections, block = orders_ref.shape
    half = block // 2
    lanes = inv_ref.shape[1]
    to_lanes(lo_ref, hi_ref, a_ref, lanes, half, block)

    def permute_rows(i, _):
        parts = [
            a_ref[pl.ds(pl.multiple_of(orders_ref[k, i] * block, block), block), :]
            for k in range(sections)
        ]
        b_ref[pl.ds(pl.multiple_of(i * block, block), block), :] = by_section(parts, section_of)
        return 0

    lax.fori_loop(0, block, permute_rows, 0, unroll=4)

    def permute_cols(j, _):
        parts = [
            b_ref[pl.ds(orders_ref[k, j], block, stride=block), :] for k in range(sections)
        ]
        a_ref[pl.ds(pl.multiple_of(j * block, block), block), :] = by_section(parts, section_of)
        return 0

    lax.fori_loop(0, block, permute_cols, 0, unroll=4)
    sub = iota((block, lanes), 0)
    for j in range(block):
        inv_ref[j * block : (j + 1) * block, :] = (
            a_ref[j * block : (j + 1) * block, :]
            - a_ref[pl.ds(j, block, stride=block), :]
            + (sub == j).astype(jnp.float32)
        )

    def eliminate(k, _):
        at = pl.multiple_of(k * block, block)
        here = sub == k
        inverse = 1.0 / inv_ref[pl.ds(at + k, 1), :]
        factors = inv_ref[pl.ds(k, block, stride=block), :]
        pivot = jnp.where(here, inverse, inv_ref[pl.ds(at, block), :] * inverse)
        for i in range(block):
            row = inv_ref[i * block : (i + 1) * block, :]
            inv_ref[i * block : (i + 1) * block, :] = (
                jnp.where(here, 0.0, row) - factors[i : i + 1, :] * pivot
            )
        inv_ref[pl.ds(at, block), :] = pivot
        return 0

    lax.fori_loop(0, block, eliminate, 0)


def own_rows(inv_ref, out_ref, half, block, upper):
    lanes = inv_ref.shape[1]
    sub = iota((block, lanes), 0)
    for a in range(half):
        low = 2.0 * inv_ref[a * block : (a + 1) * block, :] - (sub == a).astype(jnp.float32)
        top = 2.0 * inv_ref[(half + a) * block : (half + a + 1) * block, :] - (
            sub == half + a
        ).astype(jnp.float32)
        out_ref[pl.ds(a, lanes, stride=half), :] = jnp.where(upper, top, low).T


def own_cols(inv_ref, out_ref, half, block, upper):
    lanes = inv_ref.shape[1]
    sub = iota((block, lanes), 0)
    for a in range(half):
        low = 2.0 * inv_ref[pl.ds(a, block, stride=block), :] - (sub == a).astype(jnp.float32)
        top = 2.0 * inv_ref[pl.ds(half + a, block, stride=block), :] - (sub == half + a).astype(
            jnp.float32
        )
        out_ref[pl.ds(a, lanes, stride=half), :] = jnp.where(upper, top, low).T


def near_kernel(
    orders_ref, gen_ref, tok_ref, inv_ref, near_ref, xs_ref, lo_ref, hi_ref, a_ref, b_ref, row_ref
):
    sections, block = orders_ref.shape
    half = block // 2
    rows = tok_ref.shape[1]
    lanes = sections * rows // half
    lo_ref[0:rows, :] = gen_ref[0:rows, :]
    hi_ref[0:rows, :] = gen_ref[0:rows, :]
    for k in range(1, sections):
        split_halves(gen_ref, lo_ref, hi_ref, k, rows, half)
    section_of, upper = lane_facts((block, lanes), rows // half, 0)
    invert_blocks(orders_ref, lo_ref, hi_ref, inv_ref, a_ref, b_ref, section_of)
    own_rows(inv_ref, row_ref, half, block, upper)
    spread = spreader((0, half), block, half)
    for k in range(1, sections):
        lo_mask, hi_mask = block_masks(k, half)
        wide = pick(row_ref[k * rows : (k + 1) * rows, :], spread)
        for start in range(0, rows, GROUP):
            part = wide[start : start + GROUP]
            near_ref[k - 1, start : start + GROUP, :] = jnp.where(
                lo_mask, part[:, :GROUP], jnp.where(hi_mask, part[:, GROUP:], 0.0)
            )
    for start in range(0, rows, GROUP):
        stop = start + GROUP
        value = tok_ref[:, start:stop].astype(jnp.float32)
        for k in range(sections - 1, 0, -1):
            value = dot(value, near_ref[k - 1, start:stop, :])
            xs_ref[k - 1, :, start:stop] = value


def far_rotations_kernel(
    orders_ref, high_ref, own_ref, far_ref, inv_ref, ffar_ref, bfar_ref,
    lo_ref, hi_ref, a_ref, b_ref, row_ref, col_ref,
):
    block = orders_ref.shape[1]
    half = block // 2
    rows = far_ref.shape[0]
    high = high_ref[0]
    own = own_ref[...]
    other = far_ref[...]
    lo_ref[...] = jnp.where(high == 1, other, own)
    hi_ref[...] = jnp.where(high == 1, own, other)
    invert_blocks(orders_ref, lo_ref, hi_ref, inv_ref, a_ref, b_ref, None)
    upper = high == 1
    own_rows(inv_ref, row_ref, half, block, upper)
    own_cols(inv_ref, col_ref, half, block, upper)
    spread = spreader((half * high, half * (1 - high)), block, half)
    same = same_mask(half)
    for source, target in ((col_ref, ffar_ref), (row_ref, bfar_ref)):
        wide = pick(source[...], spread)
        for start in range(0, rows, GROUP):
            part = wide[start : start + GROUP]
            target[0, start : start + GROUP, :] = jnp.where(same, part[:, :GROUP], 0.0)
            target[1, start : start + GROUP, :] = jnp.where(same, part[:, GROUP:], 0.0)


def far_kernel(own_ref, oth_ref, far_ref, out_ref):
    count, rows = own_ref.shape
    for start in range(0, rows, GROUP):
        stop = start + GROUP
        value = dot(own_ref[:, start:stop], far_ref[0, start:stop, :], NT) + dot(
            oth_ref[:, start:stop], far_ref[1, start:stop, :], NT
        )
        first = value.astype(jnp.bfloat16)
        out_ref[0:count, start:stop] = first
        out_ref[count : 2 * count, start:stop] = (value - first.astype(jnp.float32)).astype(
            jnp.bfloat16
        )


def project_kernel(chunk, places_ref, x_ref, w_ref, send_ref, keep_ref, held_ref, sems):
    pieces, count, width = send_ref.shape

    def fetch(p):
        at = pl.multiple_of((places_ref[p] * CHUNKS + chunk) * width, width)
        return pltpu.make_async_copy(w_ref.at[:, pl.ds(at, width)], held_ref.at[p], sems.at[p])

    for p in range(2 * pieces):
        fetch(p).start()
    for p in range(2 * pieces):
        fetch(p).wait()
        both = one_dot(x_ref[...], held_ref[p])
        target = send_ref if p < pieces else keep_ref
        target[p % pieces] = both[:count] + both[count:]


def project(x_both, weight, places, chunk):
    pieces = places.shape[0]
    count2, rows = x_both.shape
    count = count2 // 2
    width = weight.shape[1] // lax.axis_size("tensor") // CHUNKS
    return pl.pallas_call(
        functools.partial(project_kernel, chunk),
        out_shape=(jax.ShapeDtypeStruct((pieces // 2, count, width), jnp.float32),) * 2,
        in_specs=[
            pl.BlockSpec(memory_space=pltpu.SMEM),
            pl.BlockSpec(memory_space=pltpu.VMEM),
            pl.BlockSpec(memory_space=pl.ANY),
        ],
        out_specs=(pl.BlockSpec(memory_space=pltpu.VMEM),) * 2,
        scratch_shapes=[
            pltpu.VMEM((pieces, rows, width), weight.dtype),
            pltpu.SemaphoreType.DMA((pieces,)),
        ],
        compiler_params=pltpu.CompilerParams(vmem_limit_bytes=WIDE_LIMIT),
        cost_estimate=pl.CostEstimate(
            flops=2 * count2 * rows * width * pieces,
            bytes_accessed=pieces * width * (2 * rows + 4 * count),
            transcendentals=0,
        ),
        name="project",
    )(places, x_both, weight)


def back_kernel(orders, places_ref, *refs):
    cots = refs[: 2 * len(orders)]
    w_ref, out_ref, cots_ref, held_ref, cot_sems, sems = refs[2 * len(orders) :]
    half, _, width = cots[0].shape
    todo = []
    for part, order in enumerate(orders):
        for n, offset in enumerate(order):
            todo.append((len(todo), cots[2 * part + n // half].at[n % half], offset, part))

    def fetches(slot, cot, offset, part):
        at = pl.multiple_of((places_ref[offset] * len(orders) + part) * width, width)
        return (
            pltpu.make_async_copy(cot, cots_ref.at[slot], cot_sems.at[slot]),
            pltpu.make_async_copy(
                w_ref.at[:, pl.ds(at, width)], held_ref.at[slot], sems.at[slot]
            ),
        )

    for item in todo:
        for copy in fetches(*item):
            copy.start()
    total = jnp.zeros(out_ref.shape, jnp.float32)
    for item in todo:
        for copy in fetches(*item):
            copy.wait()
        total += one_dot(cots_ref[item[0]], held_ref[item[0]], NT)
    out_ref[...] = total


def project_back(places, gathered, orders, weight):
    half, count, width = gathered[0].shape
    steps = half * len(gathered)
    rows = weight.shape[0]
    return pl.pallas_call(
        functools.partial(back_kernel, orders),
        out_shape=jax.ShapeDtypeStruct((count, rows), jnp.float32),
        in_specs=[pl.BlockSpec(memory_space=pltpu.SMEM)]
        + [pl.BlockSpec(memory_space=pl.ANY)] * (len(gathered) + 1),
        out_specs=pl.BlockSpec(memory_space=pltpu.VMEM),
        scratch_shapes=[
            pltpu.VMEM((steps, count, width), weight.dtype),
            pltpu.VMEM((steps, rows, width), weight.dtype),
            pltpu.SemaphoreType.DMA((steps,)),
            pltpu.SemaphoreType.DMA((steps,)),
        ],
        compiler_params=pltpu.CompilerParams(vmem_limit_bytes=WIDE_LIMIT),
        cost_estimate=pl.CostEstimate(
            flops=2 * count * rows * width * steps,
            bytes_accessed=steps * width * 2 * (rows + count),
            transcendentals=0,
        ),
        name="project_back",
    )(places, *gathered, weight)


def grow(array, bit):
    return jnp.concatenate([array, exchange(array, bit)], axis=0)


def gather_order(stages):
    order = [0]
    for bit in stages:
        order = order + [n ^ (1 << bit) for n in order]
    return tuple(order)


def lane_matmul(left_ref, right_ref, out_ref, block, lanes):
    step = 4

    def body(t, _):
        first = t * step
        totals = [jnp.zeros((block, lanes), jnp.float32) for _ in range(step)]
        for j in range(block):
            right = right_ref[j * block : (j + 1) * block, :]
            for s in range(step):
                totals[s] += left_ref[pl.ds((first + s) * block + j, 1), :] * right
        for s in range(step):
            out_ref[pl.ds(pl.multiple_of((first + s) * block, block), block), :] = totals[s]
        return 0

    lax.fori_loop(0, block // step, body, 0)


def grads_kernel(
    inverse_ref, high_ref, own_ref, oth_ref, x_oth_ref, tok_ref, xs_ref, near_ref, bfar_ref, inv_far_ref, inv_ref,
    gtok_ref, ggen_ref,
    row_ref, lo_ref, hi_ref, a_ref, b_ref, c_ref,
):
    sections, block = inverse_ref.shape
    half = block // 2
    count, rows = own_ref.shape
    per_section = rows // half
    lanes = sections * per_section
    high = high_ref[0]
    gather_lo = gatherer(0, block, half)
    gather_hi = gatherer(half, block, half)
    gather_own = gatherer(half * high, block, half)
    gather_oth = gatherer(half * (1 - high), block, half)
    same = same_mask(half)
    for start in range(0, rows, GROUP):
        stop = start + GROUP
        x_own = xs_ref[0, :, start:stop]
        x_oth = x_oth_ref[:, start:stop]
        g_own = own_ref[:, start:stop]
        g_oth = oth_ref[:, start:stop]

        def far_rows(x):
            return pick(jnp.where(same, dot(x, g_own, TN), 0.0), gather_own) + pick(
                jnp.where(same, dot(x, g_oth, TN), 0.0), gather_oth
            )

        mine, theirs = far_rows(x_own), far_rows(x_oth)
        lo_ref[start:stop, :] = jnp.where(high == 1, theirs, mine)
        hi_ref[start:stop, :] = jnp.where(high == 1, mine, theirs)
        grad = dot(g_own, bfar_ref[0, start:stop, :], NT) + dot(g_oth, bfar_ref[1, start:stop, :], NT)
        for k in range(1, sections):
            lo_mask, hi_mask = block_masks(k, half)
            if k < sections - 1:
                x = xs_ref[k, :, start:stop]
            else:
                x = tok_ref[:, start:stop].astype(jnp.float32)
            outer = dot(x, grad, TN)
            row_ref[k * rows + start : k * rows + stop, :] = pick(
                jnp.where(lo_mask, outer, 0.0), gather_lo
            ) + pick(jnp.where(hi_mask, outer, 0.0), gather_hi)
            grad = dot(grad, near_ref[k - 1, start:stop, :], NT)
        gtok_ref[:, start:stop] = grad
    for k in range(1, sections):
        split_halves(row_ref, lo_ref, hi_ref, k, rows, half)
    to_lanes(lo_ref, hi_ref, a_ref, lanes, half, block)
    for j in range(block):
        b_ref[j * block : (j + 1) * block, :] = inv_ref[pl.ds(j, block, stride=block), :]
        b_ref[j * block : (j + 1) * block, 0:per_section] = inv_far_ref[
            pl.ds(j, block, stride=block), :
        ]
    lane_matmul(a_ref, b_ref, c_ref, block, lanes)
    lane_matmul(b_ref, c_ref, a_ref, block, lanes)
    for j in range(block):
        c_ref[j * block : (j + 1) * block, :] = 2.0 * (
            a_ref[j * block : (j + 1) * block, :] - a_ref[pl.ds(j, block, stride=block), :]
        )
    section_of, upper = lane_facts((block, lanes), per_section, high)

    def permute_cols(j, _):
        parts = [
            c_ref[pl.ds(inverse_ref[k, j], block, stride=block), :] for k in range(sections)
        ]
        b_ref[pl.ds(pl.multiple_of(j * block, block), block), :] = by_section(parts, section_of)
        return 0

    lax.fori_loop(0, block, permute_cols, 0, unroll=4)
    for a in range(half):
        low, top = [
            by_section(
                [
                    b_ref[pl.ds(inverse_ref[k, at], block, stride=block), :]
                    for k in range(sections)
                ],
                section_of,
            )
            for at in (a, half + a)
        ]
        ggen_ref[pl.ds(a, lanes, stride=half), :] = jnp.where(upper, top, low).T


def local(tokens, weight, generators, orders, cotangent):
    sections, rows, block = generators.shape
    half = block // 2
    count = tokens.shape[0]
    size = lax.axis_size("tensor")
    bits = size.bit_length() - 1
    here = lax.axis_index("tensor")
    pair_bit = bits - 1
    high = jnp.bitwise_and(jnp.right_shift(here, pair_bit), 1).astype(jnp.int32).reshape(1)
    lanes = sections * (rows // half)
    f32 = jnp.float32
    full = pl.BlockSpec(memory_space=pltpu.VMEM)
    scalars = pl.BlockSpec(memory_space=pltpu.SMEM)
    params = pltpu.CompilerParams(vmem_limit_bytes=VMEM_LIMIT)

    far_gen = exchange(generators[0], pair_bit)
    wide = cotangent.shape[1] // 2
    first, second = cotangent[None, :, :wide], cotangent[None, :, wide:]
    order_first = list(range(bits - 1, -1, -1))
    order_second = [1] + list(range(bits - 1, 1, -1)) + [0]
    first = grow(first, order_first[0])
    second = grow(second, order_second[0])
    flat = generators.reshape(sections * rows, block)
    square = (block * block, lanes)
    far_square = (block * block, lanes // sections)
    inv, near, xs = pl.pallas_call(
        near_kernel,
        out_shape=(
            jax.ShapeDtypeStruct(square, f32),
            jax.ShapeDtypeStruct((sections - 1, rows, GROUP), f32),
            jax.ShapeDtypeStruct((sections - 1, count, rows), f32),
        ),
        in_specs=[scalars, full, full],
        out_specs=(full,) * 3,
        scratch_shapes=[
            pltpu.VMEM((sections * rows, block), f32),
            pltpu.VMEM((sections * rows, block), f32),
            pltpu.VMEM(square, f32),
            pltpu.VMEM(square, f32),
            pltpu.VMEM((sections * rows, block), f32),
        ],
        compiler_params=params,
        name="near_rotations",
    )(orders, flat, tokens)
    x_last, first, second, far_gen = lax.optimization_barrier((xs[0], first, second, far_gen))
    for bit in order_first[1:-2]:
        first = grow(first, bit)
    x_other = exchange(x_last, pair_bit)
    inv_far, ffar, bfar = pl.pallas_call(
        far_rotations_kernel,
        out_shape=(
            jax.ShapeDtypeStruct(far_square, f32),
            jax.ShapeDtypeStruct((2, rows, GROUP), f32),
            jax.ShapeDtypeStruct((2, rows, GROUP), f32),
        ),
        in_specs=[scalars, scalars, full, full],
        out_specs=(full,) * 3,
        scratch_shapes=[
            pltpu.VMEM((rows, block), f32),
            pltpu.VMEM((rows, block), f32),
            pltpu.VMEM(far_square, f32),
            pltpu.VMEM(far_square, f32),
            pltpu.VMEM((rows, block), f32),
            pltpu.VMEM((rows, block), f32),
        ],
        compiler_params=params,
        cost_estimate=pl.CostEstimate(flops=10**7, bytes_accessed=10**7, transcendentals=0),
        name="far_rotations",
    )(orders[:1], high, generators[0], far_gen)
    ffar, first = lax.optimization_barrier((ffar, first))
    first = grow(first, order_first[-2])
    x_other, second = lax.optimization_barrier((x_other, second))
    second = grow(second, order_second[1])
    x_both = pl.pallas_call(
        far_kernel,
        out_shape=jax.ShapeDtypeStruct((2 * count, rows), jnp.bfloat16),
        in_specs=[full] * 3,
        out_specs=full,
        compiler_params=params,
        name="far_apply",
    )(x_last, x_other, ffar)

    reverse = np.array(
        [sum(((p >> b) & 1) << (bits - 1 - b) for b in range(bits)) for p in range(size)], np.int32
    )
    fixed = here.astype(jnp.int32)
    places = jnp.bitwise_xor(fixed, jnp.asarray(np.roll(reverse, size // 2)))
    back_places = jnp.bitwise_xor(fixed, jnp.arange(size, dtype=jnp.int32))
    outs = [project(x_both, weight, places, chunk) for chunk in range(CHUNKS)]
    keep, first, second = lax.optimization_barrier((outs[-1][1], first, second))
    outs[-1] = (outs[-1][0], keep)
    for bit in order_second[2:-1]:
        second = grow(second, bit)
    gathered = [first, exchange(first, 0), second, exchange(second, 0)]
    gather_orders = (gather_order(order_first), gather_order(order_second))

    def stage(pair, got):
        send, keep = pair
        if keep.shape[0] == 1:
            return None, keep + got
        mid = keep.shape[0] // 2
        return keep[mid:] + got[mid:], keep[:mid] + got[:mid]

    numbers = jnp.arange(block, dtype=jnp.int32)
    inverse = jnp.sum(
        jnp.where(orders[:, :, None] == numbers[None, None, :], numbers[None, :, None], 0), axis=1
    ).astype(jnp.int32)
    for bit in range(bits):
        gots = [exchange(send, bit) for send, _ in outs]
        if bit == min(1, bits - 1):
            grad_cols = project_back(back_places, gathered, gather_orders, weight)
            grad_cols, gots[0] = lax.optimization_barrier((grad_cols, gots[0]))
            grad_other = exchange(grad_cols, pair_bit)
            grad_tokens, grad_gens = pl.pallas_call(
                grads_kernel,
                out_shape=(
                    jax.ShapeDtypeStruct((count, rows), f32),
                    jax.ShapeDtypeStruct((sections * rows, block), f32),
                ),
                in_specs=[scalars, scalars] + [full] * 9,
                out_specs=(full,) * 2,
                scratch_shapes=[
                    pltpu.VMEM((sections * rows, block), f32),
                    pltpu.VMEM((sections * rows, block), f32),
                    pltpu.VMEM((sections * rows, block), f32),
                    pltpu.VMEM(square, f32),
                    pltpu.VMEM(square, f32),
                    pltpu.VMEM(square, f32),
                ],
                compiler_params=params,
                name="gradients",
            )(inverse, high, grad_cols, grad_other, x_other, tokens, xs, near, bfar, inv_far, inv)
            grad_tokens, grad_gens, gots[-1] = lax.optimization_barrier(
                (grad_tokens, grad_gens, gots[-1])
            )
        outs = [stage(pair, got) for pair, got in zip(outs, gots)]
    outputs = jnp.concatenate([keep[0] for _, keep in outs], axis=1)
    return outputs, grad_tokens, grad_gens.reshape(sections, rows, block)


def solution(mesh):
    placed = (
        P("groups", "tensor"),
        P("tensor", None),
        P("groups", "tensor", None),
        P(),
        P("groups", "tensor"),
    )
    return jax.shard_map(
        local,
        mesh=mesh,
        in_specs=placed,
        out_specs=(P("groups", "tensor"), P("groups", "tensor"), P("groups", "tensor", None)),
        check_vma=False,
    )
```

```python
import functools

import jax
import jax.numpy as jnp
import numpy as np
from jax import lax
from jax.experimental import pallas as pl
from jax.experimental.pallas import tpu as pltpu
from jax.sharding import PartitionSpec as P

VMEM_LIMIT = 16 * 2**20
WIDE_LIMIT = 50 * 2**20
GROUP = 128
NN = (((1,), (0,)), ((), ()))
NT = (((1,), (1,)), ((), ()))
TN = (((0,), (0,)), ((), ()))
CHUNKS = 2


def exchange(array, bit):
    size = lax.axis_size("tensor")
    return lax.ppermute(array, "tensor", [(i, i ^ (1 << bit)) for i in range(size)])


def parts_of(x):
    first = x.astype(jnp.bfloat16)
    return first, (x - first.astype(jnp.float32)).astype(jnp.bfloat16)


def one_dot(a, b, dims=NN):
    return lax.dot_general(a, b, dims, preferred_element_type=jnp.float32)


def after(value, *earlier):
    return lax.optimization_barrier((value, *earlier))[0]


def dot(a, b, dims=NN):
    a_first, a_rest = parts_of(a)
    b_first, b_rest = parts_of(b)
    return (
        one_dot(a_first, b_first, dims) + one_dot(a_rest, b_first, dims) + one_dot(a_first, b_rest, dims)
    )


def pick(a, chooser):
    first, rest = parts_of(a)
    return one_dot(first, chooser) + one_dot(rest, chooser)


def iota(shape, dim):
    return lax.broadcasted_iota(jnp.int32, shape, dim)


def split_halves(rows_ref, lo_ref, hi_ref, section, rows, half):
    step = half << (section - 1)
    base = section * rows
    for start in range(base, base + rows, 2 * step):
        low = rows_ref[start : start + step, :]
        high = rows_ref[start + step : start + 2 * step, :]
        lo_ref[start : start + step, :] = low
        lo_ref[start + step : start + 2 * step, :] = low
        hi_ref[start : start + step, :] = high
        hi_ref[start + step : start + 2 * step, :] = high


def to_lanes(lo_ref, hi_ref, out_ref, lanes, half, block):
    for a in range(half):
        out_ref[a * block : (a + 1) * block, :] = lo_ref[pl.ds(a, lanes, stride=half), :].T
        out_ref[(half + a) * block : (half + a + 1) * block, :] = hi_ref[
            pl.ds(a, lanes, stride=half), :
        ].T


def by_section(parts, section_of):
    out = parts[-1]
    for k in range(len(parts) - 2, -1, -1):
        out = jnp.where(section_of == k, parts[k], out)
    return out


def lane_facts(shape, per_section, high):
    lane = iota(shape, 1)
    section_of = lane // per_section
    part = lane % per_section
    upper = jnp.bitwise_and(jnp.right_shift(part, jnp.maximum(section_of - 1, 0)), 1)
    return section_of, jnp.where(section_of == 0, high, upper) == 1


def block_masks(section, half):
    row = iota((GROUP, GROUP), 0) // half
    col = iota((GROUP, GROUP), 1) // half
    bit = 1 << (section - 1)
    return col == jnp.bitwise_and(row, ~bit), col == jnp.bitwise_or(row, bit)


def same_mask(half):
    return iota((GROUP, GROUP), 0) // half == iota((GROUP, GROUP), 1) // half


def spreader(offsets, block, half):
    row, col = iota((block, GROUP), 0), iota((block, GROUP), 1) % half
    return jnp.concatenate([(row == at + col).astype(jnp.bfloat16) for at in offsets], axis=1)


def gatherer(offset, block, half):
    row, col = iota((GROUP, block), 0) % half, iota((GROUP, block), 1)
    return (col == offset + row).astype(jnp.bfloat16)


def invert_blocks(orders_ref, lo_ref, hi_ref, inv_ref, a_ref, b_ref, section_of):
    sections, block = orders_ref.shape
    half = block // 2
    lanes = inv_ref.shape[1]
    to_lanes(lo_ref, hi_ref, a_ref, lanes, half, block)

    def permute_rows(i, _):
        parts = [
            a_ref[pl.ds(pl.multiple_of(orders_ref[k, i] * block, block), block), :]
            for k in range(sections)
        ]
        b_ref[pl.ds(pl.multiple_of(i * block, block), block), :] = by_section(parts, section_of)
        return 0

    lax.fori_loop(0, block, permute_rows, 0, unroll=4)

    def permute_cols(j, _):
        parts = [
            b_ref[pl.ds(orders_ref[k, j], block, stride=block), :] for k in range(sections)
        ]
        a_ref[pl.ds(pl.multiple_of(j * block, block), block), :] = by_section(parts, section_of)
        return 0

    lax.fori_loop(0, block, permute_cols, 0, unroll=4)
    sub = iota((block, lanes), 0)
    for j in range(block):
        inv_ref[j * block : (j + 1) * block, :] = (
            a_ref[j * block : (j + 1) * block, :]
            - a_ref[pl.ds(j, block, stride=block), :]
            + (sub == j).astype(jnp.float32)
        )

    def eliminate(k, _):
        at = pl.multiple_of(k * block, block)
        here = sub == k
        inverse = 1.0 / inv_ref[pl.ds(at + k, 1), :]
        factors = inv_ref[pl.ds(k, block, stride=block), :]
        pivot = jnp.where(here, inverse, inv_ref[pl.ds(at, block), :] * inverse)
        for i in range(block):
            row = inv_ref[i * block : (i + 1) * block, :]
            inv_ref[i * block : (i + 1) * block, :] = (
                jnp.where(here, 0.0, row) - factors[i : i + 1, :] * pivot
            )
        inv_ref[pl.ds(at, block), :] = pivot
        return 0

    lax.fori_loop(0, block, eliminate, 0)


def own_rows(inv_ref, out_ref, half, block, upper):
    lanes = inv_ref.shape[1]
    sub = iota((block, lanes), 0)
    for a in range(half):
        low = 2.0 * inv_ref[a * block : (a + 1) * block, :] - (sub == a).astype(jnp.float32)
        top = 2.0 * inv_ref[(half + a) * block : (half + a + 1) * block, :] - (
            sub == half + a
        ).astype(jnp.float32)
        out_ref[pl.ds(a, lanes, stride=half), :] = jnp.where(upper, top, low).T


def own_cols(inv_ref, out_ref, half, block, upper):
    lanes = inv_ref.shape[1]
    sub = iota((block, lanes), 0)
    for a in range(half):
        low = 2.0 * inv_ref[pl.ds(a, block, stride=block), :] - (sub == a).astype(jnp.float32)
        top = 2.0 * inv_ref[pl.ds(half + a, block, stride=block), :] - (sub == half + a).astype(
            jnp.float32
        )
        out_ref[pl.ds(a, lanes, stride=half), :] = jnp.where(upper, top, low).T


def near_kernel(
    orders_ref, gen_ref, tok_ref, inv_ref, near_ref, xs_ref, lo_ref, hi_ref, a_ref, b_ref, row_ref
):
    sections, block = orders_ref.shape
    half = block // 2
    rows = tok_ref.shape[1]
    lanes = sections * rows // half
    lo_ref[0:rows, :] = gen_ref[0:rows, :]
    hi_ref[0:rows, :] = gen_ref[0:rows, :]
    for k in range(1, sections):
        split_halves(gen_ref, lo_ref, hi_ref, k, rows, half)
    section_of, upper = lane_facts((block, lanes), rows // half, 0)
    invert_blocks(orders_ref, lo_ref, hi_ref, inv_ref, a_ref, b_ref, section_of)
    own_rows(inv_ref, row_ref, half, block, upper)
    spread = spreader((0, half), block, half)
    for k in range(1, sections):
        lo_mask, hi_mask = block_masks(k, half)
        wide = pick(row_ref[k * rows : (k + 1) * rows, :], spread)
        for start in range(0, rows, GROUP):
            part = wide[start : start + GROUP]
            near_ref[k - 1, start : start + GROUP, :] = jnp.where(
                lo_mask, part[:, :GROUP], jnp.where(hi_mask, part[:, GROUP:], 0.0)
            )
    for start in range(0, rows, GROUP):
        stop = start + GROUP
        value = tok_ref[:, start:stop].astype(jnp.float32)
        for k in range(sections - 1, 0, -1):
            value = dot(value, near_ref[k - 1, start:stop, :])
            xs_ref[k - 1, :, start:stop] = value


def far_rotations_kernel(
    orders_ref, high_ref, own_ref, far_ref, inv_ref, ffar_ref, bfar_ref,
    lo_ref, hi_ref, a_ref, b_ref, row_ref, col_ref,
):
    block = orders_ref.shape[1]
    half = block // 2
    rows = far_ref.shape[0]
    high = high_ref[0]
    own = own_ref[...]
    other = far_ref[...]
    lo_ref[...] = jnp.where(high == 1, other, own)
    hi_ref[...] = jnp.where(high == 1, own, other)
    invert_blocks(orders_ref, lo_ref, hi_ref, inv_ref, a_ref, b_ref, None)
    upper = high == 1
    own_rows(inv_ref, row_ref, half, block, upper)
    own_cols(inv_ref, col_ref, half, block, upper)
    spread = spreader((half * high, half * (1 - high)), block, half)
    same = same_mask(half)
    for source, target in ((col_ref, ffar_ref), (row_ref, bfar_ref)):
        wide = pick(source[...], spread)
        for start in range(0, rows, GROUP):
            part = wide[start : start + GROUP]
            target[0, start : start + GROUP, :] = jnp.where(same, part[:, :GROUP], 0.0)
            target[1, start : start + GROUP, :] = jnp.where(same, part[:, GROUP:], 0.0)


def far_kernel(own_ref, oth_ref, far_ref, out_ref):
    count, rows = own_ref.shape
    for start in range(0, rows, GROUP):
        stop = start + GROUP
        value = dot(own_ref[:, start:stop], far_ref[0, start:stop, :], NT) + dot(
            oth_ref[:, start:stop], far_ref[1, start:stop, :], NT
        )
        first = value.astype(jnp.bfloat16)
        out_ref[0:count, start:stop] = first
        out_ref[count : 2 * count, start:stop] = (value - first.astype(jnp.float32)).astype(
            jnp.bfloat16
        )


def project_kernel(
    chunk, places_ref, x_ref, w_ref, send_ref, keep_ref, held_ref, made_ref, sems, out_sems
):
    pieces, count, width = send_ref.shape

    def leave(p):
        target = send_ref if p < pieces else keep_ref
        return pltpu.make_async_copy(made_ref.at[p], target.at[p % pieces], out_sems.at[p])

    def fetch(p):
        at = pl.multiple_of((places_ref[p] * CHUNKS + chunk) * width, width)
        return pltpu.make_async_copy(w_ref.at[:, pl.ds(at, width)], held_ref.at[p], sems.at[p])

    for p in range(2 * pieces):
        fetch(p).start()
    for p in range(2 * pieces):
        fetch(p).wait()
        both = one_dot(x_ref[...], held_ref[p])
        made_ref[p] = both[:count] + both[count:]
        leave(p).start()
    for p in range(2 * pieces):
        leave(p).wait()


def project(x_both, weight, places, chunk):
    pieces = places.shape[0]
    count2, rows = x_both.shape
    count = count2 // 2
    width = weight.shape[1] // lax.axis_size("tensor") // CHUNKS
    return pl.pallas_call(
        functools.partial(project_kernel, chunk),
        out_shape=(jax.ShapeDtypeStruct((pieces // 2, count, width), jnp.float32),) * 2,
        in_specs=[
            pl.BlockSpec(memory_space=pltpu.SMEM),
            pl.BlockSpec(memory_space=pltpu.VMEM),
            pl.BlockSpec(memory_space=pl.ANY),
        ],
        out_specs=(pl.BlockSpec(memory_space=pl.ANY),) * 2,
        scratch_shapes=[
            pltpu.VMEM((pieces, rows, width), weight.dtype),
            pltpu.VMEM((pieces, count, width), jnp.float32),
            pltpu.SemaphoreType.DMA((pieces,)),
            pltpu.SemaphoreType.DMA((pieces,)),
        ],
        compiler_params=pltpu.CompilerParams(vmem_limit_bytes=WIDE_LIMIT),
        cost_estimate=pl.CostEstimate(
            flops=2 * count2 * rows * width * pieces,
            bytes_accessed=pieces * width * (2 * rows + 4 * count),
            transcendentals=0,
        ),
        name="project",
    )(places, x_both, weight)


def back_kernel(orders, places_ref, *refs):
    cots = refs[: 2 * len(orders)]
    w_ref, out_ref, cots_ref, held_ref, cot_sems, sems = refs[2 * len(orders) :]
    half, _, width = cots[0].shape
    todo = []
    for part, order in enumerate(orders):
        for n, offset in enumerate(order):
            todo.append((len(todo), cots[2 * part + n // half].at[n % half], offset, part))

    def fetches(slot, cot, offset, part):
        at = pl.multiple_of((places_ref[offset] * len(orders) + part) * width, width)
        here = pl.ds(slot * width, width)
        return (
            pltpu.make_async_copy(cot, cots_ref.at[:, here], cot_sems.at[slot]),
            pltpu.make_async_copy(w_ref.at[:, pl.ds(at, width)], held_ref.at[:, here], sems.at[slot]),
        )

    for item in todo:
        for copy in fetches(*item):
            copy.start()
    for first in range(0, len(todo), 2):
        for item in todo[first : first + 2]:
            for copy in fetches(*item):
                copy.wait()
        here = slice(first * width, (first + 2) * width)
        product = one_dot(cots_ref[:, here], held_ref[:, here], NT)
        if first == 0:
            out_ref[...] = product
        else:
            out_ref[...] += product


def project_back(places, gathered, orders, weight):
    half, count, width = gathered[0].shape
    steps = half * len(gathered)
    rows = weight.shape[0]
    return pl.pallas_call(
        functools.partial(back_kernel, orders),
        out_shape=jax.ShapeDtypeStruct((count, rows), jnp.float32),
        in_specs=[pl.BlockSpec(memory_space=pltpu.SMEM)]
        + [pl.BlockSpec(memory_space=pl.ANY)] * (len(gathered) + 1),
        out_specs=pl.BlockSpec(memory_space=pltpu.VMEM),
        scratch_shapes=[
            pltpu.VMEM((count, steps * width), weight.dtype),
            pltpu.VMEM((rows, steps * width), weight.dtype),
            pltpu.SemaphoreType.DMA((steps,)),
            pltpu.SemaphoreType.DMA((steps,)),
        ],
        compiler_params=pltpu.CompilerParams(vmem_limit_bytes=WIDE_LIMIT),
        cost_estimate=pl.CostEstimate(
            flops=2 * count * rows * width * steps,
            bytes_accessed=steps * width * 2 * (rows + count),
            transcendentals=0,
        ),
        name="project_back",
    )(places, *gathered, weight)


def grow(array, bit):
    return jnp.concatenate([array, exchange(array, bit)], axis=0)


def narrow(values):
    rows = values.reshape(-1, values.shape[-1])
    exponent = jnp.ceil(jnp.log2(jnp.maximum(jnp.max(jnp.abs(rows)), 1e-30))) - 15.0
    tag = jnp.full((16, rows.shape[1]), exponent)
    return jnp.concatenate([rows * jnp.exp2(-exponent), tag], axis=0).astype(jnp.float16)


def widen(packed, shape):
    rows = packed.astype(jnp.float32)
    return (rows[:-16] * jnp.exp2(rows[-16, 0])).reshape(shape)


def gather_order(stages):
    order = [0]
    for bit in stages:
        order = order + [n ^ (1 << bit) for n in order]
    return tuple(order)


def lane_matmul(left_ref, right_ref, out_ref, block, lanes):
    step = 4

    def body(t, _):
        first = t * step
        totals = [jnp.zeros((block, lanes), jnp.float32) for _ in range(step)]
        for j in range(block):
            right = right_ref[j * block : (j + 1) * block, :]
            for s in range(step):
                totals[s] += left_ref[pl.ds((first + s) * block + j, 1), :] * right
        for s in range(step):
            out_ref[pl.ds(pl.multiple_of((first + s) * block, block), block), :] = totals[s]
        return 0

    lax.fori_loop(0, block // step, body, 0)


def grads_kernel(
    inverse_ref, high_ref, own_ref, oth_ref, x_oth_ref, tok_ref, xs_ref, near_ref, bfar_ref, inv_far_ref, inv_ref,
    gtok_ref, ggen_ref,
    row_ref, lo_ref, hi_ref, a_ref, b_ref, c_ref,
):
    sections, block = inverse_ref.shape
    half = block // 2
    count, rows = own_ref.shape
    per_section = rows // half
    lanes = sections * per_section
    high = high_ref[0]
    gather_lo = gatherer(0, block, half)
    gather_hi = gatherer(half, block, half)
    gather_own = gatherer(half * high, block, half)
    gather_oth = gatherer(half * (1 - high), block, half)
    same = same_mask(half)
    for start in range(0, rows, GROUP):
        stop = start + GROUP
        x_own = xs_ref[0, :, start:stop]
        x_oth = x_oth_ref[:, start:stop]
        g_own = own_ref[:, start:stop]
        g_oth = oth_ref[:, start:stop]

        def far_rows(x):
            return pick(jnp.where(same, dot(x, g_own, TN), 0.0), gather_own) + pick(
                jnp.where(same, dot(x, g_oth, TN), 0.0), gather_oth
            )

        mine, theirs = far_rows(x_own), far_rows(x_oth)
        lo_ref[start:stop, :] = jnp.where(high == 1, theirs, mine)
        hi_ref[start:stop, :] = jnp.where(high == 1, mine, theirs)
        grad = dot(g_own, bfar_ref[0, start:stop, :], NT) + dot(g_oth, bfar_ref[1, start:stop, :], NT)
        for k in range(1, sections):
            lo_mask, hi_mask = block_masks(k, half)
            if k < sections - 1:
                x = xs_ref[k, :, start:stop]
            else:
                x = tok_ref[:, start:stop].astype(jnp.float32)
            outer = dot(x, grad, TN)
            row_ref[k * rows + start : k * rows + stop, :] = pick(
                jnp.where(lo_mask, outer, 0.0), gather_lo
            ) + pick(jnp.where(hi_mask, outer, 0.0), gather_hi)
            grad = dot(grad, near_ref[k - 1, start:stop, :], NT)
        gtok_ref[:, start:stop] = grad
    for k in range(1, sections):
        split_halves(row_ref, lo_ref, hi_ref, k, rows, half)
    to_lanes(lo_ref, hi_ref, a_ref, lanes, half, block)
    for j in range(block):
        b_ref[j * block : (j + 1) * block, :] = inv_ref[pl.ds(j, block, stride=block), :]
        b_ref[j * block : (j + 1) * block, 0:per_section] = inv_far_ref[
            pl.ds(j, block, stride=block), :
        ]
    lane_matmul(a_ref, b_ref, c_ref, block, lanes)
    lane_matmul(b_ref, c_ref, a_ref, block, lanes)
    for j in range(block):
        c_ref[j * block : (j + 1) * block, :] = 2.0 * (
            a_ref[j * block : (j + 1) * block, :] - a_ref[pl.ds(j, block, stride=block), :]
        )
    section_of, upper = lane_facts((block, lanes), per_section, high)

    def permute_cols(j, _):
        parts = [
            c_ref[pl.ds(inverse_ref[k, j], block, stride=block), :] for k in range(sections)
        ]
        b_ref[pl.ds(pl.multiple_of(j * block, block), block), :] = by_section(parts, section_of)
        return 0

    lax.fori_loop(0, block, permute_cols, 0, unroll=4)
    for a in range(half):
        low, top = [
            by_section(
                [
                    b_ref[pl.ds(inverse_ref[k, at], block, stride=block), :]
                    for k in range(sections)
                ],
                section_of,
            )
            for at in (a, half + a)
        ]
        ggen_ref[pl.ds(a, lanes, stride=half), :] = jnp.where(upper, top, low).T


def local(tokens, weight, generators, orders, cotangent):
    sections, rows, block = generators.shape
    half = block // 2
    count = tokens.shape[0]
    size = lax.axis_size("tensor")
    bits = size.bit_length() - 1
    here = lax.axis_index("tensor")
    pair_bit = bits - 1
    high = jnp.bitwise_and(jnp.right_shift(here, pair_bit), 1).astype(jnp.int32).reshape(1)
    lanes = sections * (rows // half)
    f32 = jnp.float32
    full = pl.BlockSpec(memory_space=pltpu.VMEM)
    scalars = pl.BlockSpec(memory_space=pltpu.SMEM)
    params = pltpu.CompilerParams(vmem_limit_bytes=VMEM_LIMIT)

    far_gen = exchange(generators[0], pair_bit)
    wide = cotangent.shape[1] // 2
    first, second = cotangent[None, :, :wide], cotangent[None, :, wide:]
    order_first = list(range(bits - 1, -1, -1))
    order_second = [1] + list(range(bits - 1, 1, -1)) + [0]
    first = grow(first, order_first[0])
    second = grow(second, order_second[0])
    flat = generators.reshape(sections * rows, block)
    square = (block * block, lanes)
    far_square = (block * block, lanes // sections)
    inv, near, xs = pl.pallas_call(
        near_kernel,
        out_shape=(
            jax.ShapeDtypeStruct(square, f32),
            jax.ShapeDtypeStruct((sections - 1, rows, GROUP), f32),
            jax.ShapeDtypeStruct((sections - 1, count, rows), f32),
        ),
        in_specs=[scalars, full, full],
        out_specs=(full,) * 3,
        scratch_shapes=[
            pltpu.VMEM((sections * rows, block), f32),
            pltpu.VMEM((sections * rows, block), f32),
            pltpu.VMEM(square, f32),
            pltpu.VMEM(square, f32),
            pltpu.VMEM((sections * rows, block), f32),
        ],
        compiler_params=params,
        name="near_rotations",
    )(orders, flat, tokens)
    x_last, first, second, far_gen = lax.optimization_barrier((xs[0], first, second, far_gen))
    for bit in order_first[1:-2]:
        first = grow(first, bit)
    x_other = exchange(x_last, pair_bit)
    inv_far, ffar, bfar = pl.pallas_call(
        far_rotations_kernel,
        out_shape=(
            jax.ShapeDtypeStruct(far_square, f32),
            jax.ShapeDtypeStruct((2, rows, GROUP), f32),
            jax.ShapeDtypeStruct((2, rows, GROUP), f32),
        ),
        in_specs=[scalars, scalars, full, full],
        out_specs=(full,) * 3,
        scratch_shapes=[
            pltpu.VMEM((rows, block), f32),
            pltpu.VMEM((rows, block), f32),
            pltpu.VMEM(far_square, f32),
            pltpu.VMEM(far_square, f32),
            pltpu.VMEM((rows, block), f32),
            pltpu.VMEM((rows, block), f32),
        ],
        compiler_params=params,
        cost_estimate=pl.CostEstimate(flops=10**7, bytes_accessed=10**7, transcendentals=0),
        name="far_rotations",
    )(orders[:1], high, generators[0], far_gen)
    ffar, first = lax.optimization_barrier((ffar, first))
    first = grow(first, order_first[-2])
    x_other, second = lax.optimization_barrier((x_other, second))
    second = grow(second, order_second[1])
    x_both = pl.pallas_call(
        far_kernel,
        out_shape=jax.ShapeDtypeStruct((2 * count, rows), jnp.bfloat16),
        in_specs=[full] * 3,
        out_specs=full,
        compiler_params=params,
        name="far_apply",
    )(x_last, x_other, ffar)

    reverse = np.array(
        [sum(((p >> b) & 1) << (bits - 1 - b) for b in range(bits)) for p in range(size)], np.int32
    )
    fixed = here.astype(jnp.int32)
    places = jnp.bitwise_xor(fixed, jnp.asarray(np.roll(reverse, size // 2)))
    back_places = jnp.bitwise_xor(fixed, jnp.arange(size, dtype=jnp.int32))
    outs = []
    for chunk in range(CHUNKS):
        outs.append(project(x_both, weight, places, chunk))
        if chunk == 0:
            x_both = after(x_both, outs[0][0], first, second)

    def stage(pair, got):
        send, keep = pair
        if keep.shape[0] == 1:
            return None, keep + got
        mid = keep.shape[0] // 2
        return keep[mid:] + got[mid:], keep[:mid] + got[:mid]

    def advance(outs, gots):
        return [stage(pair, got) for pair, got in zip(outs, gots)]

    outs = advance(outs, [exchange(send, 0) for send, _ in outs])
    shapes = [send.shape for send, _ in outs]
    sends = [narrow(send) for send, _ in outs]
    gots = [exchange(send, 1) for send in sends]
    for bit in order_second[2:-1]:
        second = jnp.concatenate([second, after(exchange(second, bit), *sends)], axis=0)
    gathered = [first, exchange(first, 0), second, exchange(second, 0)]
    gather_orders = (gather_order(order_first), gather_order(order_second))
    numbers = jnp.arange(block, dtype=jnp.int32)
    inverse = jnp.sum(
        jnp.where(orders[:, :, None] == numbers[None, None, :], numbers[None, :, None], 0), axis=1
    ).astype(jnp.int32)
    grad_cols = project_back(back_places, gathered, gather_orders, weight)
    gots[-1] = after(gots[-1], grad_cols)
    grad_other = exchange(grad_cols, pair_bit)
    grad_tokens, grad_gens = pl.pallas_call(
        grads_kernel,
        out_shape=(
            jax.ShapeDtypeStruct((count, rows), f32),
            jax.ShapeDtypeStruct((sections * rows, block), f32),
        ),
        in_specs=[scalars, scalars] + [full] * 9,
        out_specs=(full,) * 2,
        scratch_shapes=[
            pltpu.VMEM((sections * rows, block), f32),
            pltpu.VMEM((sections * rows, block), f32),
            pltpu.VMEM((sections * rows, block), f32),
            pltpu.VMEM(square, f32),
            pltpu.VMEM(square, f32),
            pltpu.VMEM(square, f32),
        ],
        compiler_params=params,
        name="gradients",
    )(inverse, high, grad_cols, grad_other, x_other, tokens, xs, near, bfar, inv_far, inv)
    outs = advance(outs, [widen(got, shape) for got, shape in zip(gots, shapes)])
    for bit in range(2, bits):
        gots = [exchange(send, bit) for send, _ in outs]
        if bit == 2:
            gots[-1] = after(gots[-1], grad_tokens, grad_gens)
        outs = advance(outs, gots)
    outputs = jnp.concatenate([keep[0] for _, keep in outs], axis=1)
    return outputs, grad_tokens, grad_gens.reshape(sections, rows, block)


def solution(mesh):
    placed = (
        P("groups", "tensor"),
        P("tensor", None),
        P("groups", "tensor", None),
        P(),
        P("groups", "tensor"),
    )
    return jax.shard_map(
        local,
        mesh=mesh,
        in_specs=placed,
        out_specs=(P("groups", "tensor"), P("groups", "tensor"), P("groups", "tensor", None)),
        check_vma=False,
    )
```

```python
import functools

import jax
import jax.numpy as jnp
import numpy as np
from jax import lax
from jax.experimental import pallas as pl
from jax.experimental.pallas import tpu as pltpu
from jax.sharding import PartitionSpec as P

VMEM_LIMIT = 16 * 2**20
WIDE_LIMIT = 50 * 2**20
GROUP = 128
NN = (((1,), (0,)), ((), ()))
NT = (((1,), (1,)), ((), ()))
TN = (((0,), (0,)), ((), ()))
CHUNKS = 2


def exchange(array, bit):
    size = lax.axis_size("tensor")
    return lax.ppermute(array, "tensor", [(i, i ^ (1 << bit)) for i in range(size)])


def parts_of(x):
    first = x.astype(jnp.bfloat16)
    return first, (x - first.astype(jnp.float32)).astype(jnp.bfloat16)


def one_dot(a, b, dims=NN):
    return lax.dot_general(a, b, dims, preferred_element_type=jnp.float32)


def after(value, *earlier):
    return lax.optimization_barrier((value, *earlier))[0]


def dot(a, b, dims=NN):
    a_first, a_rest = parts_of(a)
    b_first, b_rest = parts_of(b)
    return (
        one_dot(a_first, b_first, dims) + one_dot(a_rest, b_first, dims) + one_dot(a_first, b_rest, dims)
    )


def pick(a, chooser):
    first, rest = parts_of(a)
    return one_dot(first, chooser) + one_dot(rest, chooser)


def iota(shape, dim):
    return lax.broadcasted_iota(jnp.int32, shape, dim)


def split_halves(rows_ref, lo_ref, hi_ref, section, rows, half):
    step = half << (section - 1)
    base = section * rows
    for start in range(base, base + rows, 2 * step):
        low = rows_ref[start : start + step, :]
        high = rows_ref[start + step : start + 2 * step, :]
        lo_ref[start : start + step, :] = low
        lo_ref[start + step : start + 2 * step, :] = low
        hi_ref[start : start + step, :] = high
        hi_ref[start + step : start + 2 * step, :] = high


def to_lanes(lo_ref, hi_ref, out_ref, lanes, half, block):
    for a in range(half):
        out_ref[a * block : (a + 1) * block, :] = lo_ref[pl.ds(a, lanes, stride=half), :].T
        out_ref[(half + a) * block : (half + a + 1) * block, :] = hi_ref[
            pl.ds(a, lanes, stride=half), :
        ].T


def by_section(parts, section_of):
    out = parts[-1]
    for k in range(len(parts) - 2, -1, -1):
        out = jnp.where(section_of == k, parts[k], out)
    return out


def lane_facts(shape, per_section, high):
    lane = iota(shape, 1)
    section_of = lane // per_section
    part = lane % per_section
    upper = jnp.bitwise_and(jnp.right_shift(part, jnp.maximum(section_of - 1, 0)), 1)
    return section_of, jnp.where(section_of == 0, high, upper) == 1


def block_masks(section, half):
    row = iota((GROUP, GROUP), 0) // half
    col = iota((GROUP, GROUP), 1) // half
    bit = 1 << (section - 1)
    return col == jnp.bitwise_and(row, ~bit), col == jnp.bitwise_or(row, bit)


def same_mask(half):
    return iota((GROUP, GROUP), 0) // half == iota((GROUP, GROUP), 1) // half


def spreader(offsets, block, half):
    row, col = iota((block, GROUP), 0), iota((block, GROUP), 1) % half
    return jnp.concatenate([(row == at + col).astype(jnp.bfloat16) for at in offsets], axis=1)


def gatherer(offset, block, half):
    row, col = iota((GROUP, block), 0) % half, iota((GROUP, block), 1)
    return (col == offset + row).astype(jnp.bfloat16)


def transpose_to(out_ref, in_ref, block, change=lambda j, t: t):
    for j in range(block):
        out_ref[j * block : (j + 1) * block, :] = change(j, in_ref[pl.ds(j, block, stride=block), :])


def permuted_row(orders_ref, in_ref, i, section_of):
    sections, block = orders_ref.shape
    return by_section(
        [
            in_ref[pl.ds(pl.multiple_of(orders_ref[k, i] * block, block), block), :]
            for k in range(sections)
        ],
        section_of,
    )


def permute_rows(orders_ref, in_ref, out_ref, section_of):
    block = orders_ref.shape[1]
    for i in range(block):
        out_ref[i * block : (i + 1) * block, :] = permuted_row(orders_ref, in_ref, i, section_of)


def invert_blocks(orders_ref, lo_ref, hi_ref, inv_ref, a_ref, b_ref, section_of):
    sections, block = orders_ref.shape
    half = block // 2
    lanes = inv_ref.shape[1]
    to_lanes(lo_ref, hi_ref, a_ref, lanes, half, block)

    transpose_to(b_ref, a_ref, block, lambda j, t: a_ref[j * block : (j + 1) * block, :] - t)
    permute_rows(orders_ref, b_ref, a_ref, section_of)
    transpose_to(b_ref, a_ref, block)
    permute_rows(orders_ref, b_ref, inv_ref, section_of)
    sub = iota((block, lanes), 0)
    for j in range(block):
        inv_ref[j * block : (j + 1) * block, :] += (sub == j).astype(jnp.float32)

    def eliminate(k, _):
        at = pl.multiple_of(k * block, block)
        here = sub == k
        inverse = 1.0 / inv_ref[pl.ds(at + k, 1), :]
        factors = inv_ref[pl.ds(k, block, stride=block), :]
        pivot = jnp.where(here, inverse, inv_ref[pl.ds(at, block), :] * inverse)
        for i in range(block):
            row = inv_ref[i * block : (i + 1) * block, :]
            inv_ref[i * block : (i + 1) * block, :] = (
                jnp.where(here, 0.0, row) - factors[i : i + 1, :] * pivot
            )
        inv_ref[pl.ds(at, block), :] = pivot
        return 0

    lax.fori_loop(0, block, eliminate, 0)


def own_rows(inv_ref, out_ref, half, block, upper):
    lanes = inv_ref.shape[1]
    sub = iota((block, lanes), 0)
    for a in range(half):
        low = 2.0 * inv_ref[a * block : (a + 1) * block, :] - (sub == a).astype(jnp.float32)
        top = 2.0 * inv_ref[(half + a) * block : (half + a + 1) * block, :] - (
            sub == half + a
        ).astype(jnp.float32)
        out_ref[pl.ds(a, lanes, stride=half), :] = jnp.where(upper, top, low).T


def own_cols(inv_ref, out_ref, half, block, upper):
    lanes = inv_ref.shape[1]
    sub = iota((block, lanes), 0)
    for a in range(half):
        low = 2.0 * inv_ref[pl.ds(a, block, stride=block), :] - (sub == a).astype(jnp.float32)
        top = 2.0 * inv_ref[pl.ds(half + a, block, stride=block), :] - (sub == half + a).astype(
            jnp.float32
        )
        out_ref[pl.ds(a, lanes, stride=half), :] = jnp.where(upper, top, low).T


def near_kernel(
    orders_ref, gen_ref, tok_ref, inv_ref, near_ref, xs_ref, lo_ref, hi_ref, a_ref, b_ref, row_ref
):
    sections, block = orders_ref.shape
    half = block // 2
    rows = tok_ref.shape[1]
    lanes = sections * rows // half
    for k in range(sections):
        row_ref[k * rows : (k + 1) * rows, :] = gen_ref[k * block : (k + 1) * block, :].T
    lo_ref[0:rows, :] = row_ref[0:rows, :]
    hi_ref[0:rows, :] = row_ref[0:rows, :]
    for k in range(1, sections):
        split_halves(row_ref, lo_ref, hi_ref, k, rows, half)
    section_of, upper = lane_facts((block, lanes), rows // half, 0)
    invert_blocks(orders_ref, lo_ref, hi_ref, inv_ref, a_ref, b_ref, section_of)
    own_rows(inv_ref, row_ref, half, block, upper)
    spread = spreader((0, half), block, half)
    for k in range(1, sections):
        lo_mask, hi_mask = block_masks(k, half)
        wide = pick(row_ref[k * rows : (k + 1) * rows, :], spread)
        for start in range(0, rows, GROUP):
            part = wide[start : start + GROUP]
            near_ref[k - 1, start : start + GROUP, :] = jnp.where(
                lo_mask, part[:, :GROUP], jnp.where(hi_mask, part[:, GROUP:], 0.0)
            )
    for start in range(0, rows, GROUP):
        stop = start + GROUP
        value = tok_ref[:, start:stop].astype(jnp.float32)
        for k in range(sections - 1, 0, -1):
            value = dot(value, near_ref[k - 1, start:stop, :])
            xs_ref[k - 1, :, start:stop] = value


def far_rotations_kernel(
    orders_ref, high_ref, own_ref, far_ref, inv_ref, ffar_ref, bfar_ref,
    lo_ref, hi_ref, a_ref, b_ref, row_ref, col_ref,
):
    block = orders_ref.shape[1]
    half = block // 2
    rows = far_ref.shape[1]
    high = high_ref[0]
    own = own_ref[...].T
    other = far_ref[...].T
    lo_ref[...] = jnp.where(high == 1, other, own)
    hi_ref[...] = jnp.where(high == 1, own, other)
    invert_blocks(orders_ref, lo_ref, hi_ref, inv_ref, a_ref, b_ref, None)
    upper = high == 1
    own_rows(inv_ref, row_ref, half, block, upper)
    own_cols(inv_ref, col_ref, half, block, upper)
    spread = spreader((half * high, half * (1 - high)), block, half)
    same = same_mask(half)
    for source, target in ((col_ref, ffar_ref), (row_ref, bfar_ref)):
        wide = pick(source[...], spread)
        for start in range(0, rows, GROUP):
            part = wide[start : start + GROUP]
            target[0, start : start + GROUP, :] = jnp.where(same, part[:, :GROUP], 0.0)
            target[1, start : start + GROUP, :] = jnp.where(same, part[:, GROUP:], 0.0)


def beside(a, b):
    return jnp.concatenate([a, b], axis=1)


def far_kernel(own_ref, oth_ref, far_ref, out_ref):
    count, rows = own_ref.shape
    for start in range(0, rows, GROUP):
        stop = start + GROUP
        value = dot(
            beside(own_ref[:, start:stop], oth_ref[:, start:stop]),
            beside(far_ref[0, start:stop, :], far_ref[1, start:stop, :]),
            NT,
        )
        first = value.astype(jnp.bfloat16)
        out_ref[0:count, start:stop] = first
        out_ref[count : 2 * count, start:stop] = (value - first.astype(jnp.float32)).astype(
            jnp.bfloat16
        )


def project_kernel(
    chunk, places_ref, x_ref, w_ref, send_ref, keep_ref, held_ref, made_ref, sems, out_sems
):
    pieces, count, width = send_ref.shape

    def leave(p):
        target = send_ref if p < pieces else keep_ref
        return pltpu.make_async_copy(made_ref.at[p], target.at[p % pieces], out_sems.at[p])

    def fetch(p):
        at = pl.multiple_of((places_ref[p] * CHUNKS + chunk) * width, width)
        return pltpu.make_async_copy(w_ref.at[:, pl.ds(at, width)], held_ref.at[p], sems.at[p])

    for p in range(2 * pieces):
        fetch(p).start()
    for p in range(2 * pieces):
        fetch(p).wait()
        both = one_dot(x_ref[...], held_ref[p])
        made_ref[p] = both[:count] + both[count:]
        leave(p).start()
    for p in range(2 * pieces):
        leave(p).wait()


def project(x_both, weight, places, chunk):
    pieces = places.shape[0]
    count2, rows = x_both.shape
    count = count2 // 2
    width = weight.shape[1] // lax.axis_size("tensor") // CHUNKS
    return pl.pallas_call(
        functools.partial(project_kernel, chunk),
        out_shape=(jax.ShapeDtypeStruct((pieces // 2, count, width), jnp.float32),) * 2,
        in_specs=[
            pl.BlockSpec(memory_space=pltpu.SMEM),
            pl.BlockSpec(memory_space=pltpu.VMEM),
            pl.BlockSpec(memory_space=pl.ANY),
        ],
        out_specs=(pl.BlockSpec(memory_space=pl.ANY),) * 2,
        scratch_shapes=[
            pltpu.VMEM((pieces, rows, width), weight.dtype),
            pltpu.VMEM((pieces, count, width), jnp.float32),
            pltpu.SemaphoreType.DMA((pieces,)),
            pltpu.SemaphoreType.DMA((pieces,)),
        ],
        compiler_params=pltpu.CompilerParams(vmem_limit_bytes=WIDE_LIMIT),
        cost_estimate=pl.CostEstimate(
            flops=2 * count2 * rows * width * pieces,
            bytes_accessed=pieces * width * (2 * rows + 4 * count),
            transcendentals=0,
        ),
        name="project",
    )(places, x_both, weight)


def back_kernel(order, places_ref, low_ref, high_ref, w_ref, out_ref, cots_ref, held_ref, cot_sems, sems):
    half, _, width = low_ref.shape

    def fetches(slot):
        at = pl.multiple_of(places_ref[order[slot]] * width, width)
        here = pl.ds(slot * width, width)
        cot = (low_ref if slot < half else high_ref).at[slot % half]
        return (
            pltpu.make_async_copy(cot, cots_ref.at[:, here], cot_sems.at[slot]),
            pltpu.make_async_copy(w_ref.at[:, pl.ds(at, width)], held_ref.at[:, here], sems.at[slot]),
        )

    for slot in range(2 * half):
        for copy in fetches(slot):
            copy.start()
    for slot in range(2 * half):
        for copy in fetches(slot):
            copy.wait()
        here = slice(slot * width, (slot + 1) * width)
        product = one_dot(cots_ref[:, here], held_ref[:, here], NT)
        if slot == 0:
            out_ref[...] = product
        else:
            out_ref[...] += product


def project_back(places, gathered, order, weight):
    half, count, width = gathered[0].shape
    steps = half * len(gathered)
    rows = weight.shape[0]
    return pl.pallas_call(
        functools.partial(back_kernel, order),
        out_shape=jax.ShapeDtypeStruct((count, rows), jnp.float32),
        in_specs=[pl.BlockSpec(memory_space=pltpu.SMEM)]
        + [pl.BlockSpec(memory_space=pl.ANY)] * (len(gathered) + 1),
        out_specs=pl.BlockSpec(memory_space=pltpu.VMEM),
        scratch_shapes=[
            pltpu.VMEM((count, steps * width), weight.dtype),
            pltpu.VMEM((rows, steps * width), weight.dtype),
            pltpu.SemaphoreType.DMA((steps,)),
            pltpu.SemaphoreType.DMA((steps,)),
        ],
        compiler_params=pltpu.CompilerParams(vmem_limit_bytes=WIDE_LIMIT),
        cost_estimate=pl.CostEstimate(
            flops=2 * count * rows * width * steps,
            bytes_accessed=steps * width * 2 * (rows + count),
            transcendentals=0,
        ),
        name="project_back",
    )(places, *gathered, weight)


def grow(array, bit):
    return jnp.concatenate([array, exchange(array, bit)], axis=0)


def gather_order(stages):
    order = [0]
    for bit in stages:
        order = order + [n ^ (1 << bit) for n in order]
    return tuple(order)


def lane_matmul(left_ref, right_ref, out_ref, block, lanes):
    step = 4

    def body(t, _):
        first = t * step
        totals = [jnp.zeros((block, lanes), jnp.float32) for _ in range(step)]
        for j in range(block):
            right = right_ref[j * block : (j + 1) * block, :]
            for s in range(step):
                totals[s] += left_ref[pl.ds((first + s) * block + j, 1), :] * right
        for s in range(step):
            out_ref[pl.ds(pl.multiple_of((first + s) * block, block), block), :] = totals[s]
        return 0

    lax.fori_loop(0, block // step, body, 0)


def grads_kernel(
    inverse_ref, high_ref, own_ref, oth_ref, x_oth_ref, tok_ref, xs_ref, near_ref, bfar_ref, inv_far_ref, inv_ref,
    gtok_ref, ggen_ref,
    row_ref, lo_ref, hi_ref, a_ref, b_ref, c_ref,
):
    sections, block = inverse_ref.shape
    half = block // 2
    count, rows = own_ref.shape
    per_section = rows // half
    lanes = sections * per_section
    high = high_ref[0]
    gather_lo = gatherer(0, block, half)
    gather_hi = gatherer(half, block, half)
    gather_own = gatherer(half * high, block, half)
    gather_oth = gatherer(half * (1 - high), block, half)
    same = same_mask(half)
    for start in range(0, rows, GROUP):
        stop = start + GROUP
        x_own = xs_ref[0, :, start:stop]
        x_oth = x_oth_ref[:, start:stop]
        g_own = own_ref[:, start:stop]
        g_oth = oth_ref[:, start:stop]

        def far_rows(x):
            return pick(jnp.where(same, dot(x, g_own, TN), 0.0), gather_own) + pick(
                jnp.where(same, dot(x, g_oth, TN), 0.0), gather_oth
            )

        mine, theirs = far_rows(x_own), far_rows(x_oth)
        lo_ref[start:stop, :] = jnp.where(high == 1, theirs, mine)
        hi_ref[start:stop, :] = jnp.where(high == 1, mine, theirs)
        grad = dot(g_own, bfar_ref[0, start:stop, :], NT) + dot(g_oth, bfar_ref[1, start:stop, :], NT)
        for k in range(1, sections):
            lo_mask, hi_mask = block_masks(k, half)
            if k < sections - 1:
                x = xs_ref[k, :, start:stop]
            else:
                x = tok_ref[:, start:stop].astype(jnp.float32)
            outer = dot(x, grad, TN)
            row_ref[k * rows + start : k * rows + stop, :] = pick(
                jnp.where(lo_mask, outer, 0.0), gather_lo
            ) + pick(jnp.where(hi_mask, outer, 0.0), gather_hi)
            grad = dot(grad, near_ref[k - 1, start:stop, :], NT)
        gtok_ref[:, start:stop] = grad
    for k in range(1, sections):
        split_halves(row_ref, lo_ref, hi_ref, k, rows, half)
    to_lanes(lo_ref, hi_ref, a_ref, lanes, half, block)
    for j in range(block):
        b_ref[j * block : (j + 1) * block, :] = inv_ref[pl.ds(j, block, stride=block), :]
        b_ref[j * block : (j + 1) * block, 0:per_section] = inv_far_ref[
            pl.ds(j, block, stride=block), :
        ]
    lane_matmul(a_ref, b_ref, c_ref, block, lanes)
    lane_matmul(b_ref, c_ref, a_ref, block, lanes)
    section_of, upper = lane_facts((block, lanes), per_section, high)
    transpose_to(c_ref, a_ref, block, lambda j, t: 2.0 * (t - a_ref[j * block : (j + 1) * block, :]))
    permute_rows(inverse_ref, c_ref, b_ref, section_of)
    transpose_to(a_ref, b_ref, block)
    for a in range(half):
        low = permuted_row(inverse_ref, a_ref, a, section_of)
        top = permuted_row(inverse_ref, a_ref, half + a, section_of)
        row_ref[pl.ds(a, lanes, stride=half), :] = jnp.where(upper, top, low).T
    for k in range(sections):
        ggen_ref[k * block : (k + 1) * block, :] = row_ref[k * rows : (k + 1) * rows, :].T


def pack_kernel(keep_ref, got_ref, packed_ref, out_ref):
    half, count, width = out_ref.shape
    largest = jnp.zeros((count, width), jnp.float32)
    for p in range(half):
        total = keep_ref[half + p] + got_ref[half + p]
        packed_ref[p * count : (p + 1) * count, :] = total
        largest = jnp.maximum(largest, jnp.abs(total))
        out_ref[p] = keep_ref[p] + got_ref[p]
    peak = jnp.max(largest, axis=(0, 1), keepdims=True)
    exponent = jnp.ceil(jnp.log2(jnp.maximum(peak, 1e-30))) - 15.0
    scale = jnp.exp2(-exponent)
    for p in range(half):
        packed_ref[p * count : (p + 1) * count, :] *= scale
    packed_ref[half * count :, :] = jnp.broadcast_to(exponent, (16, width))


def unpack_kernel(keep_ref, got_ref, send_ref, out_ref):
    half, count, width = out_ref.shape
    scale = jnp.exp2(got_ref[2 * half * count : 2 * half * count + 1, 0:1])
    for p in range(half):
        low, top = p * count, (half + p) * count
        out_ref[p] = keep_ref[p] + got_ref[low : low + count, :] * scale
        send_ref[p] = keep_ref[half + p] + got_ref[top : top + count, :] * scale


def summed(kernel, name, keep, got, first):
    pieces, count, width = keep.shape
    full = pl.BlockSpec(memory_space=pltpu.VMEM)
    return pl.pallas_call(
        kernel,
        out_shape=(first, jax.ShapeDtypeStruct((pieces // 2, count, width), jnp.float32)),
        in_specs=[full] * 2,
        out_specs=(full,) * 2,
        compiler_params=pltpu.CompilerParams(vmem_limit_bytes=VMEM_LIMIT),
        name=name,
    )(keep, got)


def pack(keep, got):
    pieces, count, width = keep.shape
    first = jax.ShapeDtypeStruct((pieces // 2 * count + 16, width), jnp.float32)
    packed, keep = summed(pack_kernel, "sum_pack", keep, got, first)
    return packed.astype(jnp.float16), keep


def unpack(keep, got):
    pieces, count, width = keep.shape
    first = jax.ShapeDtypeStruct((pieces // 2, count, width), jnp.float32)
    return summed(unpack_kernel, "sum_unpack", keep, got.astype(jnp.float32), first)


def local(tokens, weight, generators, orders, cotangent):
    sections, rows, block = generators.shape
    half = block // 2
    count = tokens.shape[0]
    size = lax.axis_size("tensor")
    bits = size.bit_length() - 1
    here = lax.axis_index("tensor")
    pair_bit = bits - 1
    high = jnp.bitwise_and(jnp.right_shift(here, pair_bit), 1).astype(jnp.int32).reshape(1)
    lanes = sections * (rows // half)
    f32 = jnp.float32
    full = pl.BlockSpec(memory_space=pltpu.VMEM)
    scalars = pl.BlockSpec(memory_space=pltpu.SMEM)
    params = pltpu.CompilerParams(vmem_limit_bytes=VMEM_LIMIT)

    stored = jnp.swapaxes(generators, 1, 2)
    far_gen = exchange(stored[0], pair_bit)
    order = list(range(bits - 1, -1, -1))
    pieces = grow(cotangent[None], order[0])
    flat = stored.reshape(sections * block, rows)
    square = (block * block, lanes)
    far_square = (block * block, lanes // sections)
    inv, near, xs = pl.pallas_call(
        near_kernel,
        out_shape=(
            jax.ShapeDtypeStruct(square, f32),
            jax.ShapeDtypeStruct((sections - 1, rows, GROUP), f32),
            jax.ShapeDtypeStruct((sections - 1, count, rows), f32),
        ),
        in_specs=[scalars, full, full],
        out_specs=(full,) * 3,
        scratch_shapes=[
            pltpu.VMEM((sections * rows, block), f32),
            pltpu.VMEM((sections * rows, block), f32),
            pltpu.VMEM(square, f32),
            pltpu.VMEM(square, f32),
            pltpu.VMEM((sections * rows, block), f32),
        ],
        compiler_params=params,
        name="near_rotations",
    )(orders, flat, tokens)
    x_last, pieces, far_gen = lax.optimization_barrier((xs[0], pieces, far_gen))
    news = exchange(pieces, order[1])
    x_other = exchange(x_last, pair_bit)
    inv_far, ffar, bfar = pl.pallas_call(
        far_rotations_kernel,
        out_shape=(
            jax.ShapeDtypeStruct(far_square, f32),
            jax.ShapeDtypeStruct((2, rows, GROUP), f32),
            jax.ShapeDtypeStruct((2, rows, GROUP), f32),
        ),
        in_specs=[scalars, scalars, full, full],
        out_specs=(full,) * 3,
        scratch_shapes=[
            pltpu.VMEM((rows, block), f32),
            pltpu.VMEM((rows, block), f32),
            pltpu.VMEM(far_square, f32),
            pltpu.VMEM(far_square, f32),
            pltpu.VMEM((rows, block), f32),
            pltpu.VMEM((rows, block), f32),
        ],
        compiler_params=params,
        cost_estimate=pl.CostEstimate(flops=10**7, bytes_accessed=10**7, transcendentals=0),
        name="far_rotations",
    )(orders[:1], high, stored[0], far_gen)
    pieces = jnp.concatenate([pieces, after(news, ffar)], axis=0)
    for bit in order[2:-1]:
        pieces = grow(pieces, bit)
    x_both = pl.pallas_call(
        far_kernel,
        out_shape=jax.ShapeDtypeStruct((2 * count, rows), jnp.bfloat16),
        in_specs=[full] * 3,
        out_specs=full,
        compiler_params=params,
        name="far_apply",
    )(x_last, x_other, ffar)

    reverse = np.array(
        [sum(((p >> b) & 1) << (bits - 1 - b) for b in range(bits)) for p in range(size)], np.int32
    )
    fixed = here.astype(jnp.int32)
    places = jnp.bitwise_xor(fixed, jnp.asarray(np.roll(reverse, size // 2)))
    back_places = jnp.bitwise_xor(fixed, jnp.arange(size, dtype=jnp.int32))
    outs = []
    for chunk in range(CHUNKS):
        outs.append(project(x_both, weight, places, chunk))
        x_both = after(x_both, outs[-1][0])

    def stage(pair, got):
        send, keep = pair
        if keep.shape[0] == 1:
            return None, keep + got
        mid = keep.shape[0] // 2
        return keep[mid:] + got[mid:], keep[:mid] + got[:mid]

    outs = [pack(keep, exchange(send, 0)) for send, keep in outs]
    gots = [exchange(send, 1) for send, _ in outs]
    gathered = [after(pieces, *[send for send, _ in outs]), exchange(pieces, 0)]
    numbers = jnp.arange(block, dtype=jnp.int32)
    inverse = jnp.sum(
        jnp.where(orders[:, :, None] == numbers[None, None, :], numbers[None, :, None], 0), axis=1
    ).astype(jnp.int32)
    grad_cols = project_back(back_places, gathered, gather_order(order), weight)
    grad_other = exchange(grad_cols, pair_bit)
    gots[0] = after(gots[0], grad_cols)
    gots[-1] = after(gots[-1], grad_other)
    grad_tokens, grad_gens = pl.pallas_call(
        grads_kernel,
        out_shape=(
            jax.ShapeDtypeStruct((count, rows), f32),
            jax.ShapeDtypeStruct((sections * block, rows), f32),
        ),
        in_specs=[scalars, scalars] + [full] * 9,
        out_specs=(full,) * 2,
        scratch_shapes=[
            pltpu.VMEM((sections * rows, block), f32),
            pltpu.VMEM((sections * rows, block), f32),
            pltpu.VMEM((sections * rows, block), f32),
            pltpu.VMEM(square, f32),
            pltpu.VMEM(square, f32),
            pltpu.VMEM(square, f32),
        ],
        compiler_params=params,
        name="gradients",
    )(inverse, high, grad_cols, grad_other, x_other, tokens, xs, near, bfar, inv_far, inv)
    outs = [unpack(keep, got) for (_, keep), got in zip(outs, gots)]
    for bit in range(2, bits):
        gots = [exchange(send, bit) for send, _ in outs]
        if bit == bits - 1:
            gots[-1] = after(gots[-1], grad_tokens, grad_gens)
        outs = [stage(pair, got) for pair, got in zip(outs, gots)]
    outputs = jnp.concatenate([keep[0] for _, keep in outs], axis=1)
    return outputs, grad_tokens, jnp.swapaxes(grad_gens.reshape(sections, block, rows), 1, 2)


def solution(mesh):
    placed = (
        P("groups", "tensor"),
        P("tensor", None),
        P("groups", "tensor", None),
        P(),
        P("groups", "tensor"),
    )
    return jax.shard_map(
        local,
        mesh=mesh,
        in_specs=placed,
        out_specs=(P("groups", "tensor"), P("groups", "tensor"), P("groups", "tensor", None)),
        check_vma=False,
    )
```

```python
import functools

import jax
import jax.numpy as jnp
import numpy as np
from jax import lax
from jax.experimental import pallas as pl
from jax.experimental.pallas import tpu as pltpu
from jax.sharding import PartitionSpec as P

VMEM_LIMIT = 16 * 2**20
WIDE_LIMIT = 50 * 2**20
GROUP = 128
NN = (((1,), (0,)), ((), ()))
NT = (((1,), (1,)), ((), ()))
TN = (((0,), (0,)), ((), ()))
CHUNKS = 2


def exchange(array, bit):
    size = lax.axis_size("tensor")
    return lax.ppermute(array, "tensor", [(i, i ^ (1 << bit)) for i in range(size)])


def parts_of(x):
    first = x.astype(jnp.bfloat16)
    return first, (x - first.astype(jnp.float32)).astype(jnp.bfloat16)


def one_dot(a, b, dims=NN):
    return lax.dot_general(a, b, dims, preferred_element_type=jnp.float32)


def after(value, *earlier):
    return lax.optimization_barrier((value, *earlier))[0]


def dot(a, b, dims=NN):
    a_first, a_rest = parts_of(a)
    b_first, b_rest = parts_of(b)
    return (
        one_dot(a_first, b_first, dims) + one_dot(a_rest, b_first, dims) + one_dot(a_first, b_rest, dims)
    )


def pick(a, chooser):
    first, rest = parts_of(a)
    return one_dot(first, chooser) + one_dot(rest, chooser)


def iota(shape, dim):
    return lax.broadcasted_iota(jnp.int32, shape, dim)


def split_halves(rows_ref, lo_ref, hi_ref, section, rows, half):
    step = half << (section - 1)
    base = section * rows
    for start in range(base, base + rows, 2 * step):
        low = rows_ref[start : start + step, :]
        high = rows_ref[start + step : start + 2 * step, :]
        lo_ref[start : start + step, :] = low
        lo_ref[start + step : start + 2 * step, :] = low
        hi_ref[start : start + step, :] = high
        hi_ref[start + step : start + 2 * step, :] = high


def to_lanes(lo_ref, hi_ref, out_ref, lanes, half, block):
    for a in range(half):
        out_ref[a * block : (a + 1) * block, :] = lo_ref[pl.ds(a, lanes, stride=half), :].T
        out_ref[(half + a) * block : (half + a + 1) * block, :] = hi_ref[
            pl.ds(a, lanes, stride=half), :
        ].T


def by_section(parts, section_of):
    out = parts[-1]
    for k in range(len(parts) - 2, -1, -1):
        out = jnp.where(section_of == k, parts[k], out)
    return out


def lane_facts(shape, per_section, high):
    lane = iota(shape, 1)
    section_of = lane // per_section
    part = lane % per_section
    upper = jnp.bitwise_and(jnp.right_shift(part, jnp.maximum(section_of - 1, 0)), 1)
    return section_of, jnp.where(section_of == 0, high, upper) == 1


def block_masks(section, half):
    row = iota((GROUP, GROUP), 0) // half
    col = iota((GROUP, GROUP), 1) // half
    bit = 1 << (section - 1)
    return col == jnp.bitwise_and(row, ~bit), col == jnp.bitwise_or(row, bit)


def same_mask(half):
    return iota((GROUP, GROUP), 0) // half == iota((GROUP, GROUP), 1) // half


def spreader(offsets, block, half):
    row, col = iota((block, GROUP), 0), iota((block, GROUP), 1) % half
    return jnp.concatenate([(row == at + col).astype(jnp.bfloat16) for at in offsets], axis=1)


def gatherer(offset, block, half):
    row, col = iota((GROUP, block), 0) % half, iota((GROUP, block), 1)
    return (col == offset + row).astype(jnp.bfloat16)


def transpose_to(out_ref, in_ref, block, change=lambda j, t: t):
    for j in range(block):
        out_ref[j * block : (j + 1) * block, :] = change(j, in_ref[pl.ds(j, block, stride=block), :])


def permuted_row(orders_ref, in_ref, i, section_of):
    sections, block = orders_ref.shape
    return by_section(
        [
            in_ref[pl.ds(pl.multiple_of(orders_ref[k, i] * block, block), block), :]
            for k in range(sections)
        ],
        section_of,
    )


def permute_rows(orders_ref, in_ref, out_ref, section_of):
    block = orders_ref.shape[1]
    for i in range(block):
        out_ref[i * block : (i + 1) * block, :] = permuted_row(orders_ref, in_ref, i, section_of)


def invert_blocks(orders_ref, lo_ref, hi_ref, inv_ref, a_ref, b_ref, section_of):
    sections, block = orders_ref.shape
    half = block // 2
    lanes = inv_ref.shape[1]
    to_lanes(lo_ref, hi_ref, a_ref, lanes, half, block)

    transpose_to(b_ref, a_ref, block, lambda j, t: a_ref[j * block : (j + 1) * block, :] - t)
    permute_rows(orders_ref, b_ref, a_ref, section_of)
    transpose_to(b_ref, a_ref, block)
    permute_rows(orders_ref, b_ref, inv_ref, section_of)
    sub = iota((block, lanes), 0)
    for j in range(block):
        inv_ref[j * block : (j + 1) * block, :] += (sub == j).astype(jnp.float32)

    def eliminate(k, _):
        at = pl.multiple_of(k * block, block)
        here = sub == k
        inverse = 1.0 / inv_ref[pl.ds(at + k, 1), :]
        factors = inv_ref[pl.ds(k, block, stride=block), :]
        pivot = jnp.where(here, inverse, inv_ref[pl.ds(at, block), :] * inverse)
        for i in range(block):
            row = inv_ref[i * block : (i + 1) * block, :]
            inv_ref[i * block : (i + 1) * block, :] = (
                jnp.where(here, 0.0, row) - factors[i : i + 1, :] * pivot
            )
        inv_ref[pl.ds(at, block), :] = pivot
        return 0

    lax.fori_loop(0, block, eliminate, 0)


def own_rows(inv_ref, out_ref, half, block, upper):
    lanes = inv_ref.shape[1]
    sub = iota((block, lanes), 0)
    for a in range(half):
        low = 2.0 * inv_ref[a * block : (a + 1) * block, :] - (sub == a).astype(jnp.float32)
        top = 2.0 * inv_ref[(half + a) * block : (half + a + 1) * block, :] - (
            sub == half + a
        ).astype(jnp.float32)
        out_ref[pl.ds(a, lanes, stride=half), :] = jnp.where(upper, top, low).T


def own_cols(inv_ref, out_ref, half, block, upper):
    lanes = inv_ref.shape[1]
    sub = iota((block, lanes), 0)
    for a in range(half):
        low = 2.0 * inv_ref[pl.ds(a, block, stride=block), :] - (sub == a).astype(jnp.float32)
        top = 2.0 * inv_ref[pl.ds(half + a, block, stride=block), :] - (sub == half + a).astype(
            jnp.float32
        )
        out_ref[pl.ds(a, lanes, stride=half), :] = jnp.where(upper, top, low).T


def near_kernel(
    orders_ref, gen_ref, tok_ref, inv_ref, near_ref, xs_ref, lo_ref, hi_ref, a_ref, b_ref, row_ref
):
    sections, block = orders_ref.shape
    half = block // 2
    rows = tok_ref.shape[1]
    lanes = sections * rows // half
    for k in range(sections):
        row_ref[k * rows : (k + 1) * rows, :] = gen_ref[k * block : (k + 1) * block, :].T
    lo_ref[0:rows, :] = row_ref[0:rows, :]
    hi_ref[0:rows, :] = row_ref[0:rows, :]
    for k in range(1, sections):
        split_halves(row_ref, lo_ref, hi_ref, k, rows, half)
    section_of, upper = lane_facts((block, lanes), rows // half, 0)
    invert_blocks(orders_ref, lo_ref, hi_ref, inv_ref, a_ref, b_ref, section_of)
    own_rows(inv_ref, row_ref, half, block, upper)
    spread = spreader((0, half), block, half)
    for k in range(1, sections):
        lo_mask, hi_mask = block_masks(k, half)
        wide = pick(row_ref[k * rows : (k + 1) * rows, :], spread)
        for start in range(0, rows, GROUP):
            part = wide[start : start + GROUP]
            near_ref[k - 1, start : start + GROUP, :] = jnp.where(
                lo_mask, part[:, :GROUP], jnp.where(hi_mask, part[:, GROUP:], 0.0)
            )
    for start in range(0, rows, GROUP):
        stop = start + GROUP
        value = tok_ref[:, start:stop].astype(jnp.float32)
        for k in range(sections - 1, 0, -1):
            value = dot(value, near_ref[k - 1, start:stop, :])
            xs_ref[k - 1, :, start:stop] = value


def far_rotations_kernel(
    orders_ref, high_ref, own_ref, far_ref, inv_ref, ffar_ref, bfar_ref,
    lo_ref, hi_ref, a_ref, b_ref, row_ref, col_ref,
):
    block = orders_ref.shape[1]
    half = block // 2
    rows = far_ref.shape[1]
    high = high_ref[0]
    own = own_ref[...].T
    other = far_ref[...].T
    lo_ref[...] = jnp.where(high == 1, other, own)
    hi_ref[...] = jnp.where(high == 1, own, other)
    invert_blocks(orders_ref, lo_ref, hi_ref, inv_ref, a_ref, b_ref, None)
    upper = high == 1
    own_rows(inv_ref, row_ref, half, block, upper)
    own_cols(inv_ref, col_ref, half, block, upper)
    spread = spreader((half * high, half * (1 - high)), block, half)
    same = same_mask(half)
    for source, target in ((col_ref, ffar_ref), (row_ref, bfar_ref)):
        wide = pick(source[...], spread)
        for start in range(0, rows, GROUP):
            part = wide[start : start + GROUP]
            target[0, start : start + GROUP, :] = jnp.where(same, part[:, :GROUP], 0.0)
            target[1, start : start + GROUP, :] = jnp.where(same, part[:, GROUP:], 0.0)


def beside(a, b):
    return jnp.concatenate([a, b], axis=1)


def far_kernel(own_ref, oth_ref, far_ref, out_ref):
    count, rows = own_ref.shape
    for start in range(0, rows, GROUP):
        stop = start + GROUP
        value = dot(
            beside(own_ref[:, start:stop], oth_ref[:, start:stop]),
            beside(far_ref[0, start:stop, :], far_ref[1, start:stop, :]),
            NT,
        )
        first = value.astype(jnp.bfloat16)
        out_ref[0:count, start:stop] = first
        out_ref[count : 2 * count, start:stop] = (value - first.astype(jnp.float32)).astype(
            jnp.bfloat16
        )


def project_kernel(places_ref, x_ref, w_ref, *refs):
    *out_refs, held_ref, made_ref, sems, out_sems = refs
    pieces, count, width = made_ref.shape
    half = pieces // 2
    part = width // CHUNKS

    def fetch(p):
        at = pl.multiple_of(places_ref[p] * width, width)
        return pltpu.make_async_copy(w_ref.at[:, pl.ds(at, width)], held_ref.at[p], sems.at[p])

    def leave(p, chunk):
        return pltpu.make_async_copy(
            made_ref.at[p, :, pl.ds(chunk * part, part)],
            out_refs[2 * chunk + p // half].at[p % half],
            out_sems.at[chunk, p],
        )

    for p in range(pieces):
        fetch(p).start()
    for p in range(pieces):
        fetch(p).wait()
        both = one_dot(x_ref[...], held_ref[p])
        made_ref[p] = both[:count] + both[count:]
        for chunk in range(CHUNKS):
            leave(p, chunk).start()
    for p in range(pieces):
        for chunk in range(CHUNKS):
            leave(p, chunk).wait()


def project(x_both, weight, places):
    pieces = places.shape[0]
    count2, rows = x_both.shape
    count = count2 // 2
    width = weight.shape[1] // lax.axis_size("tensor")
    outs = pl.pallas_call(
        project_kernel,
        out_shape=(jax.ShapeDtypeStruct((pieces // 2, count, width // CHUNKS), jnp.float32),)
        * (2 * CHUNKS),
        in_specs=[
            pl.BlockSpec(memory_space=pltpu.SMEM),
            pl.BlockSpec(memory_space=pltpu.VMEM),
            pl.BlockSpec(memory_space=pl.ANY),
        ],
        out_specs=(pl.BlockSpec(memory_space=pl.ANY),) * (2 * CHUNKS),
        scratch_shapes=[
            pltpu.VMEM((pieces, rows, width), weight.dtype),
            pltpu.VMEM((pieces, count, width), jnp.float32),
            pltpu.SemaphoreType.DMA((pieces,)),
            pltpu.SemaphoreType.DMA((CHUNKS, pieces)),
        ],
        compiler_params=pltpu.CompilerParams(vmem_limit_bytes=WIDE_LIMIT),
        cost_estimate=pl.CostEstimate(
            flops=2 * count2 * rows * width * pieces,
            bytes_accessed=pieces * width * (2 * rows + 4 * count),
            transcendentals=0,
        ),
        name="project",
    )(places, x_both, weight)
    return [outs[2 * chunk : 2 * chunk + 2] for chunk in range(CHUNKS)]


def back_kernel(order, places_ref, low_ref, high_ref, w_ref, out_ref, cots_ref, held_ref, cot_sems, sems):
    half, _, width = low_ref.shape

    def fetches(slot):
        at = pl.multiple_of(places_ref[order[slot]] * width, width)
        here = pl.ds(slot * width, width)
        cot = (low_ref if slot < half else high_ref).at[slot % half]
        return (
            pltpu.make_async_copy(cot, cots_ref.at[:, here], cot_sems.at[slot]),
            pltpu.make_async_copy(w_ref.at[:, pl.ds(at, width)], held_ref.at[:, here], sems.at[slot]),
        )

    for slot in range(2 * half):
        for copy in fetches(slot):
            copy.start()
    for slot in range(2 * half):
        for copy in fetches(slot):
            copy.wait()
        here = slice(slot * width, (slot + 1) * width)
        product = one_dot(cots_ref[:, here], held_ref[:, here], NT)
        if slot == 0:
            out_ref[...] = product
        else:
            out_ref[...] += product


def project_back(places, gathered, order, weight):
    half, count, width = gathered[0].shape
    steps = half * len(gathered)
    rows = weight.shape[0]
    return pl.pallas_call(
        functools.partial(back_kernel, order),
        out_shape=jax.ShapeDtypeStruct((count, rows), jnp.float32),
        in_specs=[pl.BlockSpec(memory_space=pltpu.SMEM)]
        + [pl.BlockSpec(memory_space=pl.ANY)] * (len(gathered) + 1),
        out_specs=pl.BlockSpec(memory_space=pltpu.VMEM),
        scratch_shapes=[
            pltpu.VMEM((count, steps * width), weight.dtype),
            pltpu.VMEM((rows, steps * width), weight.dtype),
            pltpu.SemaphoreType.DMA((steps,)),
            pltpu.SemaphoreType.DMA((steps,)),
        ],
        compiler_params=pltpu.CompilerParams(vmem_limit_bytes=WIDE_LIMIT),
        cost_estimate=pl.CostEstimate(
            flops=2 * count * rows * width * steps,
            bytes_accessed=steps * width * 2 * (rows + count),
            transcendentals=0,
        ),
        name="project_back",
    )(places, *gathered, weight)


def grow(array, bit):
    return jnp.concatenate([array, exchange(array, bit)], axis=0)


def gather_order(stages):
    order = [0]
    for bit in stages:
        order = order + [n ^ (1 << bit) for n in order]
    return tuple(order)


def lane_matmul(left_ref, right_ref, out_ref, block, lanes):
    step = 4

    def body(t, _):
        first = t * step
        totals = [jnp.zeros((block, lanes), jnp.float32) for _ in range(step)]
        for j in range(block):
            right = right_ref[j * block : (j + 1) * block, :]
            for s in range(step):
                totals[s] += left_ref[pl.ds((first + s) * block + j, 1), :] * right
        for s in range(step):
            out_ref[pl.ds(pl.multiple_of((first + s) * block, block), block), :] = totals[s]
        return 0

    lax.fori_loop(0, block // step, body, 0)


def grads_kernel(
    inverse_ref, high_ref, own_ref, oth_ref, x_oth_ref, tok_ref, xs_ref, near_ref, bfar_ref, inv_far_ref, inv_ref,
    gtok_ref, ggen_ref,
    row_ref, lo_ref, hi_ref, a_ref, b_ref, c_ref,
):
    sections, block = inverse_ref.shape
    half = block // 2
    count, rows = own_ref.shape
    per_section = rows // half
    lanes = sections * per_section
    high = high_ref[0]
    gather_lo = gatherer(0, block, half)
    gather_hi = gatherer(half, block, half)
    gather_own = gatherer(half * high, block, half)
    gather_oth = gatherer(half * (1 - high), block, half)
    same = same_mask(half)
    for start in range(0, rows, GROUP):
        stop = start + GROUP
        x_own = xs_ref[0, :, start:stop]
        x_oth = x_oth_ref[:, start:stop]
        g_own = own_ref[:, start:stop]
        g_oth = oth_ref[:, start:stop]

        def far_rows(x):
            return pick(jnp.where(same, dot(x, g_own, TN), 0.0), gather_own) + pick(
                jnp.where(same, dot(x, g_oth, TN), 0.0), gather_oth
            )

        mine, theirs = far_rows(x_own), far_rows(x_oth)
        lo_ref[start:stop, :] = jnp.where(high == 1, theirs, mine)
        hi_ref[start:stop, :] = jnp.where(high == 1, mine, theirs)
        grad = dot(g_own, bfar_ref[0, start:stop, :], NT) + dot(g_oth, bfar_ref[1, start:stop, :], NT)
        for k in range(1, sections):
            lo_mask, hi_mask = block_masks(k, half)
            if k < sections - 1:
                x = xs_ref[k, :, start:stop]
            else:
                x = tok_ref[:, start:stop].astype(jnp.float32)
            outer = dot(x, grad, TN)
            row_ref[k * rows + start : k * rows + stop, :] = pick(
                jnp.where(lo_mask, outer, 0.0), gather_lo
            ) + pick(jnp.where(hi_mask, outer, 0.0), gather_hi)
            grad = dot(grad, near_ref[k - 1, start:stop, :], NT)
        gtok_ref[:, start:stop] = grad
    for k in range(1, sections):
        split_halves(row_ref, lo_ref, hi_ref, k, rows, half)
    to_lanes(lo_ref, hi_ref, a_ref, lanes, half, block)
    for j in range(block):
        b_ref[j * block : (j + 1) * block, :] = inv_ref[pl.ds(j, block, stride=block), :]
        b_ref[j * block : (j + 1) * block, 0:per_section] = inv_far_ref[
            pl.ds(j, block, stride=block), :
        ]
    lane_matmul(a_ref, b_ref, c_ref, block, lanes)
    lane_matmul(b_ref, c_ref, a_ref, block, lanes)
    section_of, upper = lane_facts((block, lanes), per_section, high)
    transpose_to(c_ref, a_ref, block, lambda j, t: 2.0 * (t - a_ref[j * block : (j + 1) * block, :]))
    permute_rows(inverse_ref, c_ref, b_ref, section_of)
    transpose_to(a_ref, b_ref, block)
    for a in range(half):
        low = permuted_row(inverse_ref, a_ref, a, section_of)
        top = permuted_row(inverse_ref, a_ref, half + a, section_of)
        row_ref[pl.ds(a, lanes, stride=half), :] = jnp.where(upper, top, low).T
    for k in range(sections):
        ggen_ref[k * block : (k + 1) * block, :] = row_ref[k * rows : (k + 1) * rows, :].T


def pack_kernel(keep_ref, got_ref, packed_ref, out_ref):
    half, count, width = out_ref.shape
    largest = jnp.zeros((count, width), jnp.float32)
    for p in range(half):
        total = keep_ref[half + p] + got_ref[half + p]
        packed_ref[p * count : (p + 1) * count, :] = total
        largest = jnp.maximum(largest, jnp.abs(total))
        out_ref[p] = keep_ref[p] + got_ref[p]
    peak = jnp.max(largest, axis=(0, 1), keepdims=True)
    exponent = jnp.ceil(jnp.log2(jnp.maximum(peak, 1e-30))) - 15.0
    scale = jnp.exp2(-exponent)
    for p in range(half):
        packed_ref[p * count : (p + 1) * count, :] *= scale
    packed_ref[half * count :, :] = jnp.broadcast_to(exponent, (16, width))


def unpack_kernel(keep_ref, got_ref, send_ref, out_ref):
    half, count, width = out_ref.shape
    scale = jnp.exp2(got_ref[2 * half * count : 2 * half * count + 1, 0:1])
    for p in range(half):
        low, top = p * count, (half + p) * count
        out_ref[p] = keep_ref[p] + got_ref[low : low + count, :] * scale
        send_ref[p] = keep_ref[half + p] + got_ref[top : top + count, :] * scale


def summed(kernel, name, keep, got, first):
    pieces, count, width = keep.shape
    full = pl.BlockSpec(memory_space=pltpu.VMEM)
    return pl.pallas_call(
        kernel,
        out_shape=(first, jax.ShapeDtypeStruct((pieces // 2, count, width), jnp.float32)),
        in_specs=[full] * 2,
        out_specs=(full,) * 2,
        compiler_params=pltpu.CompilerParams(vmem_limit_bytes=VMEM_LIMIT),
        name=name,
    )(keep, got)


def pack(keep, got):
    pieces, count, width = keep.shape
    first = jax.ShapeDtypeStruct((pieces // 2 * count + 16, width), jnp.float32)
    packed, keep = summed(pack_kernel, "sum_pack", keep, got, first)
    return packed.astype(jnp.float16), keep


def unpack(keep, got):
    pieces, count, width = keep.shape
    first = jax.ShapeDtypeStruct((pieces // 2, count, width), jnp.float32)
    return summed(unpack_kernel, "sum_unpack", keep, got.astype(jnp.float32), first)


def local(tokens, weight, generators, orders, cotangent):
    sections, rows, block = generators.shape
    half = block // 2
    count = tokens.shape[0]
    size = lax.axis_size("tensor")
    bits = size.bit_length() - 1
    here = lax.axis_index("tensor")
    pair_bit = bits - 1
    high = jnp.bitwise_and(jnp.right_shift(here, pair_bit), 1).astype(jnp.int32).reshape(1)
    lanes = sections * (rows // half)
    f32 = jnp.float32
    full = pl.BlockSpec(memory_space=pltpu.VMEM)
    scalars = pl.BlockSpec(memory_space=pltpu.SMEM)
    params = pltpu.CompilerParams(vmem_limit_bytes=VMEM_LIMIT)

    stored = jnp.swapaxes(generators, 1, 2)
    far_gen = exchange(stored[0], pair_bit)
    order = list(range(bits - 1, -1, -1))
    pieces = grow(cotangent[None], order[0])
    flat = stored.reshape(sections * block, rows)
    square = (block * block, lanes)
    far_square = (block * block, lanes // sections)
    inv, near, xs = pl.pallas_call(
        near_kernel,
        out_shape=(
            jax.ShapeDtypeStruct(square, f32),
            jax.ShapeDtypeStruct((sections - 1, rows, GROUP), f32),
            jax.ShapeDtypeStruct((sections - 1, count, rows), f32),
        ),
        in_specs=[scalars, full, full],
        out_specs=(full,) * 3,
        scratch_shapes=[
            pltpu.VMEM((sections * rows, block), f32),
            pltpu.VMEM((sections * rows, block), f32),
            pltpu.VMEM(square, f32),
            pltpu.VMEM(square, f32),
            pltpu.VMEM((sections * rows, block), f32),
        ],
        compiler_params=params,
        name="near_rotations",
    )(orders, flat, tokens)
    x_last, pieces, far_gen = lax.optimization_barrier((xs[0], pieces, far_gen))
    news = exchange(pieces, order[1])
    x_other = exchange(x_last, pair_bit)
    inv_far, ffar, bfar = pl.pallas_call(
        far_rotations_kernel,
        out_shape=(
            jax.ShapeDtypeStruct(far_square, f32),
            jax.ShapeDtypeStruct((2, rows, GROUP), f32),
            jax.ShapeDtypeStruct((2, rows, GROUP), f32),
        ),
        in_specs=[scalars, scalars, full, full],
        out_specs=(full,) * 3,
        scratch_shapes=[
            pltpu.VMEM((rows, block), f32),
            pltpu.VMEM((rows, block), f32),
            pltpu.VMEM(far_square, f32),
            pltpu.VMEM(far_square, f32),
            pltpu.VMEM((rows, block), f32),
            pltpu.VMEM((rows, block), f32),
        ],
        compiler_params=params,
        cost_estimate=pl.CostEstimate(flops=10**7, bytes_accessed=10**7, transcendentals=0),
        name="far_rotations",
    )(orders[:1], high, stored[0], far_gen)
    pieces = jnp.concatenate([pieces, after(news, ffar, x_other)], axis=0)
    for bit in order[2:-1]:
        pieces = grow(pieces, bit)
    x_both = pl.pallas_call(
        far_kernel,
        out_shape=jax.ShapeDtypeStruct((2 * count, rows), jnp.bfloat16),
        in_specs=[full] * 3,
        out_specs=full,
        compiler_params=params,
        name="far_apply",
    )(x_last, x_other, ffar)

    reverse = np.array(
        [sum(((p >> b) & 1) << (bits - 1 - b) for b in range(bits)) for p in range(size)], np.int32
    )
    fixed = here.astype(jnp.int32)
    places = jnp.bitwise_xor(fixed, jnp.asarray(np.roll(reverse, size // 2)))
    back_places = jnp.bitwise_xor(fixed, jnp.arange(size, dtype=jnp.int32))
    outs = project(x_both, weight, places)

    def stage(pair, got):
        send, keep = pair
        if keep.shape[0] == 1:
            return None, keep + got
        mid = keep.shape[0] // 2
        return keep[mid:] + got[mid:], keep[:mid] + got[:mid]

    outs = [pack(keep, exchange(send, 0)) for send, keep in outs]
    gots = [exchange(send, 1) for send, _ in outs]
    gathered = [after(pieces, *[send for send, _ in outs]), exchange(pieces, 0)]
    numbers = jnp.arange(block, dtype=jnp.int32)
    inverse = jnp.sum(
        jnp.where(orders[:, :, None] == numbers[None, None, :], numbers[None, :, None], 0), axis=1
    ).astype(jnp.int32)
    grad_cols = project_back(back_places, gathered, gather_order(order), weight)
    grad_other = exchange(grad_cols, pair_bit)
    gots[0] = after(gots[0], grad_cols)
    gots[-1] = after(gots[-1], grad_other)
    grad_tokens, grad_gens = pl.pallas_call(
        grads_kernel,
        out_shape=(
            jax.ShapeDtypeStruct((count, rows), f32),
            jax.ShapeDtypeStruct((sections * block, rows), f32),
        ),
        in_specs=[scalars, scalars] + [full] * 9,
        out_specs=(full,) * 2,
        scratch_shapes=[
            pltpu.VMEM((sections * rows, block), f32),
            pltpu.VMEM((sections * rows, block), f32),
            pltpu.VMEM((sections * rows, block), f32),
            pltpu.VMEM(square, f32),
            pltpu.VMEM(square, f32),
            pltpu.VMEM(square, f32),
        ],
        compiler_params=params,
        name="gradients",
    )(inverse, high, grad_cols, grad_other, x_other, tokens, xs, near, bfar, inv_far, inv)
    outs = [unpack(keep, got) for (_, keep), got in zip(outs, gots)]
    for bit in range(2, bits):
        gots = [exchange(send, bit) for send, _ in outs]
        if bit == 2:
            gots[-1] = after(gots[-1], grad_tokens, grad_gens)
        outs = [stage(pair, got) for pair, got in zip(outs, gots)]
    outputs = jnp.concatenate([keep[0] for _, keep in outs], axis=1)
    return outputs, grad_tokens, jnp.swapaxes(grad_gens.reshape(sections, block, rows), 1, 2)


def solution(mesh):
    placed = (
        P("groups", "tensor"),
        P("tensor", None),
        P("groups", "tensor", None),
        P(),
        P("groups", "tensor"),
    )
    return jax.shard_map(
        local,
        mesh=mesh,
        in_specs=placed,
        out_specs=(P("groups", "tensor"), P("groups", "tensor"), P("groups", "tensor", None)),
        check_vma=False,
    )
```

```python
import functools

import jax
import jax.numpy as jnp
import numpy as np
from jax import lax
from jax.experimental import pallas as pl
from jax.experimental.pallas import tpu as pltpu
from jax.sharding import PartitionSpec as P

VMEM_LIMIT = 16 * 2**20
WIDE_LIMIT = 50 * 2**20
GROUP = 128
NN = (((1,), (0,)), ((), ()))
NT = (((1,), (1,)), ((), ()))
TN = (((0,), (0,)), ((), ()))
CHUNKS = 2


def exchange(array, bit):
    size = lax.axis_size("tensor")
    return lax.ppermute(array, "tensor", [(i, i ^ (1 << bit)) for i in range(size)])


def parts_of(x):
    first = x.astype(jnp.bfloat16)
    return first, (x - first.astype(jnp.float32)).astype(jnp.bfloat16)


def one_dot(a, b, dims=NN):
    return lax.dot_general(a, b, dims, preferred_element_type=jnp.float32)


def after(value, *earlier):
    return lax.optimization_barrier((value, *earlier))[0]


def dot(a, b, dims=NN):
    a_first, a_rest = parts_of(a)
    b_first, b_rest = parts_of(b)
    return (
        one_dot(a_first, b_first, dims) + one_dot(a_rest, b_first, dims) + one_dot(a_first, b_rest, dims)
    )


def pick(a, chooser):
    first, rest = parts_of(a)
    return one_dot(first, chooser) + one_dot(rest, chooser)


def iota(shape, dim):
    return lax.broadcasted_iota(jnp.int32, shape, dim)


def split_halves(rows_ref, lo_ref, hi_ref, section, rows, half):
    step = half << (section - 1)
    base = section * rows
    for start in range(base, base + rows, 2 * step):
        low = rows_ref[start : start + step, :]
        high = rows_ref[start + step : start + 2 * step, :]
        lo_ref[start : start + step, :] = low
        lo_ref[start + step : start + 2 * step, :] = low
        hi_ref[start : start + step, :] = high
        hi_ref[start + step : start + 2 * step, :] = high


def to_lanes(lo_ref, hi_ref, out_ref, lanes, half, block):
    for a in range(half):
        out_ref[a * block : (a + 1) * block, :] = lo_ref[pl.ds(a, lanes, stride=half), :].T
        out_ref[(half + a) * block : (half + a + 1) * block, :] = hi_ref[
            pl.ds(a, lanes, stride=half), :
        ].T


def by_section(parts, section_of):
    out = parts[-1]
    for k in range(len(parts) - 2, -1, -1):
        out = jnp.where(section_of == k, parts[k], out)
    return out


def lane_facts(shape, per_section, high):
    lane = iota(shape, 1)
    section_of = lane // per_section
    part = lane % per_section
    upper = jnp.bitwise_and(jnp.right_shift(part, jnp.maximum(section_of - 1, 0)), 1)
    return section_of, jnp.where(section_of == 0, high, upper) == 1


def block_masks(section, half):
    row = iota((GROUP, GROUP), 0) // half
    col = iota((GROUP, GROUP), 1) // half
    bit = 1 << (section - 1)
    return col == jnp.bitwise_and(row, ~bit), col == jnp.bitwise_or(row, bit)


def same_mask(half):
    return iota((GROUP, GROUP), 0) // half == iota((GROUP, GROUP), 1) // half


def spreader(offsets, block, half):
    row, col = iota((block, GROUP), 0), iota((block, GROUP), 1) % half
    return jnp.concatenate([(row == at + col).astype(jnp.bfloat16) for at in offsets], axis=1)


def gatherer(offset, block, half):
    row, col = iota((GROUP, block), 0) % half, iota((GROUP, block), 1)
    return (col == offset + row).astype(jnp.bfloat16)


def transpose_to(out_ref, in_ref, block, change=lambda j, t: t):
    for j in range(block):
        out_ref[j * block : (j + 1) * block, :] = change(j, in_ref[pl.ds(j, block, stride=block), :])


def permuted_row(orders_ref, in_ref, i, section_of):
    sections, block = orders_ref.shape
    return by_section(
        [
            in_ref[pl.ds(pl.multiple_of(orders_ref[k, i] * block, block), block), :]
            for k in range(sections)
        ],
        section_of,
    )


def permute_rows(orders_ref, in_ref, out_ref, section_of):
    block = orders_ref.shape[1]
    for i in range(block):
        out_ref[i * block : (i + 1) * block, :] = permuted_row(orders_ref, in_ref, i, section_of)


def invert_blocks(orders_ref, lo_ref, hi_ref, inv_ref, a_ref, b_ref, section_of):
    sections, block = orders_ref.shape
    half = block // 2
    lanes = inv_ref.shape[1]
    to_lanes(lo_ref, hi_ref, a_ref, lanes, half, block)

    transpose_to(b_ref, a_ref, block, lambda j, t: a_ref[j * block : (j + 1) * block, :] - t)
    permute_rows(orders_ref, b_ref, a_ref, section_of)
    transpose_to(b_ref, a_ref, block)
    permute_rows(orders_ref, b_ref, inv_ref, section_of)
    sub = iota((block, lanes), 0)
    for j in range(block):
        inv_ref[j * block : (j + 1) * block, :] += (sub == j).astype(jnp.float32)

    def eliminate(k, _):
        at = pl.multiple_of(k * block, block)
        here = sub == k
        inverse = 1.0 / inv_ref[pl.ds(at + k, 1), :]
        factors = inv_ref[pl.ds(k, block, stride=block), :]
        pivot = jnp.where(here, inverse, inv_ref[pl.ds(at, block), :] * inverse)
        for i in range(block):
            row = inv_ref[i * block : (i + 1) * block, :]
            inv_ref[i * block : (i + 1) * block, :] = (
                jnp.where(here, 0.0, row) - factors[i : i + 1, :] * pivot
            )
        inv_ref[pl.ds(at, block), :] = pivot
        return 0

    lax.fori_loop(0, block, eliminate, 0)


def own_rows(inv_ref, out_ref, half, block, upper):
    lanes = inv_ref.shape[1]
    sub = iota((block, lanes), 0)
    for a in range(half):
        low = 2.0 * inv_ref[a * block : (a + 1) * block, :] - (sub == a).astype(jnp.float32)
        top = 2.0 * inv_ref[(half + a) * block : (half + a + 1) * block, :] - (
            sub == half + a
        ).astype(jnp.float32)
        out_ref[pl.ds(a, lanes, stride=half), :] = jnp.where(upper, top, low).T


def own_cols(inv_ref, out_ref, half, block, upper):
    lanes = inv_ref.shape[1]
    sub = iota((block, lanes), 0)
    for a in range(half):
        low = 2.0 * inv_ref[pl.ds(a, block, stride=block), :] - (sub == a).astype(jnp.float32)
        top = 2.0 * inv_ref[pl.ds(half + a, block, stride=block), :] - (sub == half + a).astype(
            jnp.float32
        )
        out_ref[pl.ds(a, lanes, stride=half), :] = jnp.where(upper, top, low).T


def near_kernel(
    orders_ref, gen_ref, tok_ref, inv_ref, near_ref, xs_ref, packed_ref,
    lo_ref, hi_ref, a_ref, b_ref, row_ref,
):
    sections, block = orders_ref.shape
    half = block // 2
    rows = tok_ref.shape[1]
    lanes = sections * rows // half
    for k in range(sections):
        row_ref[k * rows : (k + 1) * rows, :] = gen_ref[k * block : (k + 1) * block, :].T
    lo_ref[0:rows, :] = row_ref[0:rows, :]
    hi_ref[0:rows, :] = row_ref[0:rows, :]
    for k in range(1, sections):
        split_halves(row_ref, lo_ref, hi_ref, k, rows, half)
    section_of, upper = lane_facts((block, lanes), rows // half, 0)
    invert_blocks(orders_ref, lo_ref, hi_ref, inv_ref, a_ref, b_ref, section_of)
    own_rows(inv_ref, row_ref, half, block, upper)
    spread = spreader((0, half), block, half)
    for k in range(1, sections):
        lo_mask, hi_mask = block_masks(k, half)
        wide = pick(row_ref[k * rows : (k + 1) * rows, :], spread)
        for start in range(0, rows, GROUP):
            part = wide[start : start + GROUP]
            near_ref[k - 1, start : start + GROUP, :] = jnp.where(
                lo_mask, part[:, :GROUP], jnp.where(hi_mask, part[:, GROUP:], 0.0)
            )
    for start in range(0, rows, GROUP):
        stop = start + GROUP
        value = tok_ref[:, start:stop].astype(jnp.float32)
        for k in range(sections - 1, 0, -1):
            value = dot(value, near_ref[k - 1, start:stop, :])
            xs_ref[k - 1, :, start:stop] = value
    write_packed(packed_ref, xs_ref[0])


def far_rotations_kernel(
    orders_ref, high_ref, own_ref, far_ref, inv_ref, ffar_ref, bfar_ref,
    lo_ref, hi_ref, a_ref, b_ref, row_ref, col_ref,
):
    block = orders_ref.shape[1]
    half = block // 2
    rows = far_ref.shape[1]
    high = high_ref[0]
    own = own_ref[...].T
    other = far_ref[...].T
    lo_ref[...] = jnp.where(high == 1, other, own)
    hi_ref[...] = jnp.where(high == 1, own, other)
    invert_blocks(orders_ref, lo_ref, hi_ref, inv_ref, a_ref, b_ref, None)
    upper = high == 1
    own_rows(inv_ref, row_ref, half, block, upper)
    own_cols(inv_ref, col_ref, half, block, upper)
    spread = spreader((half * high, half * (1 - high)), block, half)
    same = same_mask(half)
    for source, target in ((col_ref, ffar_ref), (row_ref, bfar_ref)):
        wide = pick(source[...], spread)
        for start in range(0, rows, GROUP):
            part = wide[start : start + GROUP]
            target[0, start : start + GROUP, :] = jnp.where(same, part[:, :GROUP], 0.0)
            target[1, start : start + GROUP, :] = jnp.where(same, part[:, GROUP:], 0.0)


def write_packed(packed_ref, value):
    count, width = value.shape
    peak = jnp.max(jnp.abs(value), axis=(0, 1), keepdims=True)
    exponent = jnp.ceil(jnp.log2(jnp.maximum(peak, 1e-30))) - 15.0
    packed_ref[0:count, :] = value * jnp.exp2(-exponent)
    packed_ref[count:, :] = jnp.broadcast_to(exponent, (16, width))


def read_packed(packed_ref, start, stop):
    count = packed_ref.shape[0] - 16
    return packed_ref[0:count, start:stop] * jnp.exp2(packed_ref[count : count + 1, 0:1])


def exchange_packed(packed, bit):
    return exchange(packed.astype(jnp.float16), bit).astype(jnp.float32)


def beside(a, b):
    return jnp.concatenate([a, b], axis=1)


def far_kernel(own_ref, oth_ref, far_ref, out_ref):
    count, rows = own_ref.shape[1:]
    for start in range(0, rows, GROUP):
        stop = start + GROUP
        value = dot(
            beside(own_ref[0, :, start:stop], read_packed(oth_ref, start, stop)),
            beside(far_ref[0, start:stop, :], far_ref[1, start:stop, :]),
            NT,
        )
        first = value.astype(jnp.bfloat16)
        out_ref[0:count, start:stop] = first
        out_ref[count : 2 * count, start:stop] = (value - first.astype(jnp.float32)).astype(
            jnp.bfloat16
        )


def project_kernel(places_ref, x_ref, w_ref, *refs):
    *out_refs, held_ref, made_ref, sems, out_sems = refs
    pieces, count, width = made_ref.shape
    half = pieces // 2
    part = width // CHUNKS

    def fetch(p):
        at = pl.multiple_of(places_ref[p] * width, width)
        return pltpu.make_async_copy(w_ref.at[:, pl.ds(at, width)], held_ref.at[p], sems.at[p])

    def leave(p, chunk):
        return pltpu.make_async_copy(
            made_ref.at[p, :, pl.ds(chunk * part, part)],
            out_refs[2 * chunk + p // half].at[p % half],
            out_sems.at[chunk, p],
        )

    for p in range(pieces):
        fetch(p).start()
    for p in range(pieces):
        fetch(p).wait()
        both = one_dot(x_ref[...], held_ref[p])
        made_ref[p] = both[:count] + both[count:]
        for chunk in range(CHUNKS):
            leave(p, chunk).start()
    for p in range(pieces):
        for chunk in range(CHUNKS):
            leave(p, chunk).wait()


def project(x_both, weight, places):
    pieces = places.shape[0]
    count2, rows = x_both.shape
    count = count2 // 2
    width = weight.shape[1] // lax.axis_size("tensor")
    outs = pl.pallas_call(
        project_kernel,
        out_shape=(jax.ShapeDtypeStruct((pieces // 2, count, width // CHUNKS), jnp.float32),)
        * (2 * CHUNKS),
        in_specs=[
            pl.BlockSpec(memory_space=pltpu.SMEM),
            pl.BlockSpec(memory_space=pltpu.VMEM),
            pl.BlockSpec(memory_space=pl.ANY),
        ],
        out_specs=(pl.BlockSpec(memory_space=pl.ANY),) * (2 * CHUNKS),
        scratch_shapes=[
            pltpu.VMEM((pieces, rows, width), weight.dtype),
            pltpu.VMEM((pieces, count, width), jnp.float32),
            pltpu.SemaphoreType.DMA((pieces,)),
            pltpu.SemaphoreType.DMA((CHUNKS, pieces)),
        ],
        compiler_params=pltpu.CompilerParams(vmem_limit_bytes=WIDE_LIMIT),
        cost_estimate=pl.CostEstimate(
            flops=2 * count2 * rows * width * pieces,
            bytes_accessed=pieces * width * (2 * rows + 4 * count),
            transcendentals=0,
        ),
        name="project",
    )(places, x_both, weight)
    return [outs[2 * chunk : 2 * chunk + 2] for chunk in range(CHUNKS)]


def back_kernel(order, places_ref, low_ref, high_ref, w_ref, out_ref, packed_ref, cots_ref, held_ref, cot_sems, sems):
    half, _, width = low_ref.shape

    def fetches(slot):
        at = pl.multiple_of(places_ref[order[slot]] * width, width)
        here = pl.ds(slot * width, width)
        cot = (low_ref if slot < half else high_ref).at[slot % half]
        return (
            pltpu.make_async_copy(cot, cots_ref.at[:, here], cot_sems.at[slot]),
            pltpu.make_async_copy(w_ref.at[:, pl.ds(at, width)], held_ref.at[:, here], sems.at[slot]),
        )

    for slot in range(2 * half):
        for copy in fetches(slot):
            copy.start()
    for slot in range(2 * half):
        for copy in fetches(slot):
            copy.wait()
        here = slice(slot * width, (slot + 1) * width)
        product = one_dot(cots_ref[:, here], held_ref[:, here], NT)
        if slot == 0:
            out_ref[...] = product
        else:
            out_ref[...] += product
    write_packed(packed_ref, out_ref[...])


def project_back(places, gathered, order, weight):
    half, count, width = gathered[0].shape
    steps = half * len(gathered)
    rows = weight.shape[0]
    return pl.pallas_call(
        functools.partial(back_kernel, order),
        out_shape=(
            jax.ShapeDtypeStruct((count, rows), jnp.float32),
            jax.ShapeDtypeStruct((count + 16, rows), jnp.float32),
        ),
        in_specs=[pl.BlockSpec(memory_space=pltpu.SMEM)]
        + [pl.BlockSpec(memory_space=pl.ANY)] * (len(gathered) + 1),
        out_specs=(pl.BlockSpec(memory_space=pltpu.VMEM),) * 2,
        scratch_shapes=[
            pltpu.VMEM((count, steps * width), weight.dtype),
            pltpu.VMEM((rows, steps * width), weight.dtype),
            pltpu.SemaphoreType.DMA((steps,)),
            pltpu.SemaphoreType.DMA((steps,)),
        ],
        compiler_params=pltpu.CompilerParams(vmem_limit_bytes=WIDE_LIMIT),
        cost_estimate=pl.CostEstimate(
            flops=2 * count * rows * width * steps,
            bytes_accessed=steps * width * 2 * (rows + count),
            transcendentals=0,
        ),
        name="project_back",
    )(places, *gathered, weight)


def grow(array, bit):
    return jnp.concatenate([array, exchange(array, bit)], axis=0)


def gather_order(stages):
    order = [0]
    for bit in stages:
        order = order + [n ^ (1 << bit) for n in order]
    return tuple(order)


def lane_matmul(left_ref, right_ref, out_ref, block, lanes):
    step = 4

    def body(t, _):
        first = t * step
        totals = [jnp.zeros((block, lanes), jnp.float32) for _ in range(step)]
        for j in range(block):
            right = right_ref[j * block : (j + 1) * block, :]
            for s in range(step):
                totals[s] += left_ref[pl.ds((first + s) * block + j, 1), :] * right
        for s in range(step):
            out_ref[pl.ds(pl.multiple_of((first + s) * block, block), block), :] = totals[s]
        return 0

    lax.fori_loop(0, block // step, body, 0)


def grads_kernel(
    inverse_ref, high_ref, own_ref, oth_ref, x_oth_ref, tok_ref, xs_ref, near_ref, bfar_ref, inv_far_ref, inv_ref,
    gtok_ref, ggen_ref,
    row_ref, lo_ref, hi_ref, a_ref, b_ref, c_ref,
):
    sections, block = inverse_ref.shape
    half = block // 2
    count, rows = own_ref.shape
    per_section = rows // half
    lanes = sections * per_section
    high = high_ref[0]
    chooser = jnp.concatenate([gatherer(0, block, half), gatherer(half, block, half)], axis=0)
    far_chooser = jnp.concatenate(
        [gatherer(half * high, block, half), gatherer(half * (1 - high), block, half)], axis=0
    )
    same = same_mask(half)
    same = jnp.concatenate([beside(same, same)] * 2, axis=0)
    for start in range(0, rows, GROUP):
        stop = start + GROUP
        x_pair = beside(xs_ref[0, :, start:stop], read_packed(x_oth_ref, start, stop))
        g_pair = beside(own_ref[:, start:stop], read_packed(oth_ref, start, stop))
        both = pick(jnp.where(same, dot(x_pair, g_pair, TN), 0.0), far_chooser)
        mine, theirs = both[:GROUP], both[GROUP:]
        lo_ref[start:stop, :] = jnp.where(high == 1, theirs, mine)
        hi_ref[start:stop, :] = jnp.where(high == 1, mine, theirs)
        grad = dot(g_pair, beside(bfar_ref[0, start:stop, :], bfar_ref[1, start:stop, :]), NT)
        for k in range(1, sections):
            lo_mask, hi_mask = block_masks(k, half)
            if k < sections - 1:
                x = xs_ref[k, :, start:stop]
            else:
                x = tok_ref[:, start:stop].astype(jnp.float32)
            outer = dot(x, grad, TN)
            row_ref[k * rows + start : k * rows + stop, :] = pick(
                beside(jnp.where(lo_mask, outer, 0.0), jnp.where(hi_mask, outer, 0.0)), chooser
            )
            grad = dot(grad, near_ref[k - 1, start:stop, :], NT)
        gtok_ref[:, start:stop] = grad
    for k in range(1, sections):
        split_halves(row_ref, lo_ref, hi_ref, k, rows, half)
    to_lanes(lo_ref, hi_ref, a_ref, lanes, half, block)
    for j in range(block):
        b_ref[j * block : (j + 1) * block, :] = inv_ref[pl.ds(j, block, stride=block), :]
        b_ref[j * block : (j + 1) * block, 0:per_section] = inv_far_ref[
            pl.ds(j, block, stride=block), :
        ]
    lane_matmul(a_ref, b_ref, c_ref, block, lanes)
    lane_matmul(b_ref, c_ref, a_ref, block, lanes)
    section_of, upper = lane_facts((block, lanes), per_section, high)
    transpose_to(c_ref, a_ref, block, lambda j, t: 2.0 * (t - a_ref[j * block : (j + 1) * block, :]))
    permute_rows(inverse_ref, c_ref, b_ref, section_of)
    transpose_to(a_ref, b_ref, block)
    for a in range(half):
        low = permuted_row(inverse_ref, a_ref, a, section_of)
        top = permuted_row(inverse_ref, a_ref, half + a, section_of)
        row_ref[pl.ds(a, lanes, stride=half), :] = jnp.where(upper, top, low).T
    for k in range(sections):
        ggen_ref[k * block : (k + 1) * block, :] = row_ref[k * rows : (k + 1) * rows, :].T


def pack_kernel(keep_ref, got_ref, packed_ref, out_ref):
    half, count, width = out_ref.shape
    largest = jnp.zeros((count, width), jnp.float32)
    for p in range(half):
        total = keep_ref[half + p] + got_ref[half + p]
        packed_ref[p * count : (p + 1) * count, :] = total
        largest = jnp.maximum(largest, jnp.abs(total))
        out_ref[p] = keep_ref[p] + got_ref[p]
    peak = jnp.max(largest, axis=(0, 1), keepdims=True)
    exponent = jnp.ceil(jnp.log2(jnp.maximum(peak, 1e-30))) - 15.0
    scale = jnp.exp2(-exponent)
    for p in range(half):
        packed_ref[p * count : (p + 1) * count, :] *= scale
    packed_ref[half * count :, :] = jnp.broadcast_to(exponent, (16, width))


def unpack_kernel(keep_ref, got_ref, send_ref, out_ref):
    half, count, width = out_ref.shape
    scale = jnp.exp2(got_ref[2 * half * count : 2 * half * count + 1, 0:1])
    for p in range(half):
        low, top = p * count, (half + p) * count
        out_ref[p] = keep_ref[p] + got_ref[low : low + count, :] * scale
        send_ref[p] = keep_ref[half + p] + got_ref[top : top + count, :] * scale


def summed(kernel, name, keep, got, first):
    pieces, count, width = keep.shape
    full = pl.BlockSpec(memory_space=pltpu.VMEM)
    return pl.pallas_call(
        kernel,
        out_shape=(first, jax.ShapeDtypeStruct((pieces // 2, count, width), jnp.float32)),
        in_specs=[full] * 2,
        out_specs=(full,) * 2,
        compiler_params=pltpu.CompilerParams(vmem_limit_bytes=VMEM_LIMIT),
        name=name,
    )(keep, got)


def pack(keep, got):
    pieces, count, width = keep.shape
    first = jax.ShapeDtypeStruct((pieces // 2 * count + 16, width), jnp.float32)
    packed, keep = summed(pack_kernel, "sum_pack", keep, got, first)
    return packed.astype(jnp.float16), keep


def unpack(keep, got):
    pieces, count, width = keep.shape
    first = jax.ShapeDtypeStruct((pieces // 2, count, width), jnp.float32)
    return summed(unpack_kernel, "sum_unpack", keep, got.astype(jnp.float32), first)


def local(tokens, weight, generators, orders, cotangent):
    sections, rows, block = generators.shape
    half = block // 2
    count = tokens.shape[0]
    size = lax.axis_size("tensor")
    bits = size.bit_length() - 1
    here = lax.axis_index("tensor")
    pair_bit = bits - 1
    high = jnp.bitwise_and(jnp.right_shift(here, pair_bit), 1).astype(jnp.int32).reshape(1)
    lanes = sections * (rows // half)
    f32 = jnp.float32
    full = pl.BlockSpec(memory_space=pltpu.VMEM)
    scalars = pl.BlockSpec(memory_space=pltpu.SMEM)
    params = pltpu.CompilerParams(vmem_limit_bytes=VMEM_LIMIT)

    stored = jnp.swapaxes(generators, 1, 2)
    far_gen = exchange(stored[0], pair_bit)
    order = list(range(bits - 1, -1, -1))
    pieces = cotangent[None]
    for bit in order[:-3]:
        pieces = grow(pieces, bit)
    flat = stored.reshape(sections * block, rows)
    square = (block * block, lanes)
    far_square = (block * block, lanes // sections)
    inv, near, xs, x_packed = pl.pallas_call(
        near_kernel,
        out_shape=(
            jax.ShapeDtypeStruct(square, f32),
            jax.ShapeDtypeStruct((sections - 1, rows, GROUP), f32),
            jax.ShapeDtypeStruct((sections - 1, count, rows), f32),
            jax.ShapeDtypeStruct((count + 16, rows), f32),
        ),
        in_specs=[scalars, full, full],
        out_specs=(full,) * 4,
        scratch_shapes=[
            pltpu.VMEM((sections * rows, block), f32),
            pltpu.VMEM((sections * rows, block), f32),
            pltpu.VMEM(square, f32),
            pltpu.VMEM(square, f32),
            pltpu.VMEM((sections * rows, block), f32),
        ],
        compiler_params=params,
        name="near_rotations",
    )(orders, flat, tokens)
    x_packed, pieces, far_gen = lax.optimization_barrier((x_packed, pieces, far_gen))
    near_news, side_news = exchange(pieces, order[-3]), exchange(pieces, order[-2])
    x_other = exchange_packed(x_packed, pair_bit)
    inv_far, ffar, bfar = pl.pallas_call(
        far_rotations_kernel,
        out_shape=(
            jax.ShapeDtypeStruct(far_square, f32),
            jax.ShapeDtypeStruct((2, rows, GROUP), f32),
            jax.ShapeDtypeStruct((2, rows, GROUP), f32),
        ),
        in_specs=[scalars, scalars, full, full],
        out_specs=(full,) * 3,
        scratch_shapes=[
            pltpu.VMEM((rows, block), f32),
            pltpu.VMEM((rows, block), f32),
            pltpu.VMEM(far_square, f32),
            pltpu.VMEM(far_square, f32),
            pltpu.VMEM((rows, block), f32),
            pltpu.VMEM((rows, block), f32),
        ],
        compiler_params=params,
        cost_estimate=pl.CostEstimate(flops=10**7, bytes_accessed=10**7, transcendentals=0),
        name="far_rotations",
    )(orders[:1], high, stored[0], far_gen)
    near_news = after(near_news, ffar, x_other)
    last_news = exchange(near_news, order[-2])
    x_both = pl.pallas_call(
        far_kernel,
        out_shape=jax.ShapeDtypeStruct((2 * count, rows), jnp.bfloat16),
        in_specs=[full] * 3,
        out_specs=full,
        compiler_params=params,
        name="far_apply",
    )(xs, x_other, ffar)

    reverse = np.array(
        [sum(((p >> b) & 1) << (bits - 1 - b) for b in range(bits)) for p in range(size)], np.int32
    )
    fixed = here.astype(jnp.int32)
    places = jnp.bitwise_xor(fixed, jnp.asarray(np.roll(reverse, size // 2)))
    back_places = jnp.bitwise_xor(fixed, jnp.arange(size, dtype=jnp.int32))
    outs = project(after(x_both, near_news, side_news), weight, places)

    def stage(pair, got):
        send, keep = pair
        if keep.shape[0] == 1:
            return None, keep + got
        mid = keep.shape[0] // 2
        return keep[mid:] + got[mid:], keep[:mid] + got[:mid]

    outs = [pack(keep, exchange(send, 0)) for send, keep in outs]
    gots = [exchange(send, 1) for send, _ in outs]
    last_news = after(last_news, *[send for send, _ in outs])
    pieces = jnp.concatenate([pieces, near_news, side_news, last_news], axis=0)
    gathered = [pieces, exchange(pieces, 0)]
    numbers = jnp.arange(block, dtype=jnp.int32)
    inverse = jnp.sum(
        jnp.where(orders[:, :, None] == numbers[None, None, :], numbers[None, :, None], 0), axis=1
    ).astype(jnp.int32)
    grad_cols, grad_packed = project_back(back_places, gathered, gather_order(order), weight)
    grad_other = exchange_packed(grad_packed, pair_bit)
    gots[0] = after(gots[0], grad_cols)
    gots[-1] = after(gots[-1], grad_other)
    grad_tokens, grad_gens = pl.pallas_call(
        grads_kernel,
        out_shape=(
            jax.ShapeDtypeStruct((count, rows), f32),
            jax.ShapeDtypeStruct((sections * block, rows), f32),
        ),
        in_specs=[scalars, scalars] + [full] * 9,
        out_specs=(full,) * 2,
        scratch_shapes=[
            pltpu.VMEM((sections * rows, block), f32),
            pltpu.VMEM((sections * rows, block), f32),
            pltpu.VMEM((sections * rows, block), f32),
            pltpu.VMEM(square, f32),
            pltpu.VMEM(square, f32),
            pltpu.VMEM(square, f32),
        ],
        compiler_params=params,
        name="gradients",
    )(inverse, high, grad_cols, grad_other, x_other, tokens, xs, near, bfar, inv_far, inv)
    outs = [unpack(keep, got) for (_, keep), got in zip(outs, gots)]
    for bit in range(2, bits):
        gots = [exchange(send, bit) for send, _ in outs]
        if bit == 2:
            gots[-1] = after(gots[-1], grad_tokens, grad_gens)
        outs = [stage(pair, got) for pair, got in zip(outs, gots)]
    outputs = jnp.concatenate([keep[0] for _, keep in outs], axis=1)
    return outputs, grad_tokens, jnp.swapaxes(grad_gens.reshape(sections, block, rows), 1, 2)


def solution(mesh):
    placed = (
        P("groups", "tensor"),
        P("tensor", None),
        P("groups", "tensor", None),
        P(),
        P("groups", "tensor"),
    )
    return jax.shard_map(
        local,
        mesh=mesh,
        in_specs=placed,
        out_specs=(P("groups", "tensor"), P("groups", "tensor"), P("groups", "tensor", None)),
        check_vma=False,
    )
```

```python
import functools

import jax
import jax.numpy as jnp
import numpy as np
from jax import lax
from jax.experimental import pallas as pl
from jax.experimental.pallas import tpu as pltpu
from jax.sharding import PartitionSpec as P

VMEM_LIMIT = 16 * 2**20
WIDE_LIMIT = 50 * 2**20
GROUP = 128
NN = (((1,), (0,)), ((), ()))
NT = (((1,), (1,)), ((), ()))
TN = (((0,), (0,)), ((), ()))
CHUNKS = 2


def exchange(array, bit):
    size = lax.axis_size("tensor")
    return lax.ppermute(array, "tensor", [(i, i ^ (1 << bit)) for i in range(size)])


def parts_of(x):
    first = x.astype(jnp.bfloat16)
    return first, (x - first.astype(jnp.float32)).astype(jnp.bfloat16)


def one_dot(a, b, dims=NN):
    return lax.dot_general(a, b, dims, preferred_element_type=jnp.float32)


def after(value, *earlier):
    return lax.optimization_barrier((value, *earlier))[0]


def dot(a, b, dims=NN):
    a_first, a_rest = parts_of(a)
    b_first, b_rest = parts_of(b)
    return (
        one_dot(a_first, b_first, dims) + one_dot(a_rest, b_first, dims) + one_dot(a_first, b_rest, dims)
    )


def pick(a, chooser):
    first, rest = parts_of(a)
    return one_dot(first, chooser) + one_dot(rest, chooser)


def iota(shape, dim):
    return lax.broadcasted_iota(jnp.int32, shape, dim)


def split_halves(rows_ref, lo_ref, hi_ref, section, rows, half):
    step = half << (section - 1)
    base = section * rows
    for start in range(base, base + rows, 2 * step):
        low = rows_ref[start : start + step, :]
        high = rows_ref[start + step : start + 2 * step, :]
        lo_ref[start : start + step, :] = low
        lo_ref[start + step : start + 2 * step, :] = low
        hi_ref[start : start + step, :] = high
        hi_ref[start + step : start + 2 * step, :] = high


def to_lanes(lo_ref, hi_ref, out_ref, lanes, half, block):
    for a in range(half):
        out_ref[a * block : (a + 1) * block, :] = lo_ref[pl.ds(a, lanes, stride=half), :].T
        out_ref[(half + a) * block : (half + a + 1) * block, :] = hi_ref[
            pl.ds(a, lanes, stride=half), :
        ].T


def by_section(parts, section_of):
    out = parts[-1]
    for k in range(len(parts) - 2, -1, -1):
        out = jnp.where(section_of == k, parts[k], out)
    return out


def lane_facts(shape, per_section, high):
    lane = iota(shape, 1)
    section_of = lane // per_section
    part = lane % per_section
    upper = jnp.bitwise_and(jnp.right_shift(part, jnp.maximum(section_of - 1, 0)), 1)
    return section_of, jnp.where(section_of == 0, high, upper) == 1


def block_masks(section, half):
    row = iota((GROUP, GROUP), 0) // half
    col = iota((GROUP, GROUP), 1) // half
    bit = 1 << (section - 1)
    return col == jnp.bitwise_and(row, ~bit), col == jnp.bitwise_or(row, bit)


def same_mask(half):
    return iota((GROUP, GROUP), 0) // half == iota((GROUP, GROUP), 1) // half


def spreader(offsets, block, half):
    row, col = iota((block, GROUP), 0), iota((block, GROUP), 1) % half
    return jnp.concatenate([(row == at + col).astype(jnp.bfloat16) for at in offsets], axis=1)


def gatherer(offset, block, half):
    row, col = iota((GROUP, block), 0) % half, iota((GROUP, block), 1)
    return (col == offset + row).astype(jnp.bfloat16)


def transpose_to(out_ref, in_ref, block, change=lambda j, t: t):
    for j in range(block):
        out_ref[j * block : (j + 1) * block, :] = change(j, in_ref[pl.ds(j, block, stride=block), :])


def permuted_row(orders_ref, in_ref, i, section_of):
    sections, block = orders_ref.shape
    return by_section(
        [
            in_ref[pl.ds(pl.multiple_of(orders_ref[k, i] * block, block), block), :]
            for k in range(sections)
        ],
        section_of,
    )


def permute_rows(orders_ref, in_ref, out_ref, section_of):
    block = orders_ref.shape[1]
    for i in range(block):
        out_ref[i * block : (i + 1) * block, :] = permuted_row(orders_ref, in_ref, i, section_of)


def invert_blocks(orders_ref, lo_ref, hi_ref, inv_ref, a_ref, b_ref, section_of):
    sections, block = orders_ref.shape
    half = block // 2
    lanes = inv_ref.shape[1]
    to_lanes(lo_ref, hi_ref, a_ref, lanes, half, block)

    transpose_to(b_ref, a_ref, block, lambda j, t: a_ref[j * block : (j + 1) * block, :] - t)
    permute_rows(orders_ref, b_ref, a_ref, section_of)
    transpose_to(b_ref, a_ref, block)
    permute_rows(orders_ref, b_ref, inv_ref, section_of)
    sub = iota((block, lanes), 0)
    for j in range(block):
        inv_ref[j * block : (j + 1) * block, :] += (sub == j).astype(jnp.float32)

    def eliminate(k, _):
        at = pl.multiple_of(k * block, block)
        here = sub == k
        inverse = 1.0 / inv_ref[pl.ds(at + k, 1), :]
        factors = inv_ref[pl.ds(k, block, stride=block), :]
        pivot = jnp.where(here, inverse, inv_ref[pl.ds(at, block), :] * inverse)
        for i in range(block):
            row = inv_ref[i * block : (i + 1) * block, :]
            inv_ref[i * block : (i + 1) * block, :] = (
                jnp.where(here, 0.0, row) - factors[i : i + 1, :] * pivot
            )
        inv_ref[pl.ds(at, block), :] = pivot
        return 0

    lax.fori_loop(0, block, eliminate, 0)


def own_rows(inv_ref, out_ref, half, block, upper):
    lanes = inv_ref.shape[1]
    sub = iota((block, lanes), 0)
    for a in range(half):
        low = 2.0 * inv_ref[a * block : (a + 1) * block, :] - (sub == a).astype(jnp.float32)
        top = 2.0 * inv_ref[(half + a) * block : (half + a + 1) * block, :] - (
            sub == half + a
        ).astype(jnp.float32)
        out_ref[pl.ds(a, lanes, stride=half), :] = jnp.where(upper, top, low).T


def own_cols(inv_ref, out_ref, half, block, upper):
    lanes = inv_ref.shape[1]
    sub = iota((block, lanes), 0)
    for a in range(half):
        low = 2.0 * inv_ref[pl.ds(a, block, stride=block), :] - (sub == a).astype(jnp.float32)
        top = 2.0 * inv_ref[pl.ds(half + a, block, stride=block), :] - (sub == half + a).astype(
            jnp.float32
        )
        out_ref[pl.ds(a, lanes, stride=half), :] = jnp.where(upper, top, low).T


def near_kernel(
    orders_ref, gen_ref, tok_ref, inv_ref, near_ref, xs_ref,
    lo_ref, hi_ref, a_ref, b_ref, row_ref,
):
    sections, block = orders_ref.shape
    half = block // 2
    rows = tok_ref.shape[1]
    lanes = sections * rows // half
    for k in range(sections):
        row_ref[k * rows : (k + 1) * rows, :] = gen_ref[k * block : (k + 1) * block, :].T
    lo_ref[0:rows, :] = row_ref[0:rows, :]
    hi_ref[0:rows, :] = row_ref[0:rows, :]
    for k in range(1, sections):
        split_halves(row_ref, lo_ref, hi_ref, k, rows, half)
    section_of, upper = lane_facts((block, lanes), rows // half, 0)
    invert_blocks(orders_ref, lo_ref, hi_ref, inv_ref, a_ref, b_ref, section_of)
    own_rows(inv_ref, row_ref, half, block, upper)
    spread = spreader((0, half), block, half)
    for k in range(1, sections):
        lo_mask, hi_mask = block_masks(k, half)
        wide = pick(row_ref[k * rows : (k + 1) * rows, :], spread)
        for start in range(0, rows, GROUP):
            part = wide[start : start + GROUP]
            near_ref[k - 1, start : start + GROUP, :] = jnp.where(
                lo_mask, part[:, :GROUP], jnp.where(hi_mask, part[:, GROUP:], 0.0)
            )
    for start in range(0, rows, GROUP):
        stop = start + GROUP
        value = tok_ref[:, start:stop].astype(jnp.float32)
        for k in range(sections - 1, 0, -1):
            value = dot(value, near_ref[k - 1, start:stop, :])
            xs_ref[k - 1, :, start:stop] = value


def far_rotations_kernel(
    orders_ref, high_ref, own_ref, far_ref, inv_ref, ffar_ref, bfar_ref,
    lo_ref, hi_ref, a_ref, b_ref, row_ref, col_ref,
):
    block = orders_ref.shape[1]
    half = block // 2
    rows = far_ref.shape[1]
    high = high_ref[0]
    own = own_ref[...].T
    other = far_ref[...].T
    lo_ref[...] = jnp.where(high == 1, other, own)
    hi_ref[...] = jnp.where(high == 1, own, other)
    invert_blocks(orders_ref, lo_ref, hi_ref, inv_ref, a_ref, b_ref, None)
    upper = high == 1
    own_rows(inv_ref, row_ref, half, block, upper)
    own_cols(inv_ref, col_ref, half, block, upper)
    spread = spreader((half * high, half * (1 - high)), block, half)
    same = same_mask(half)
    for source, target in ((col_ref, ffar_ref), (row_ref, bfar_ref)):
        wide = pick(source[...], spread)
        for start in range(0, rows, GROUP):
            part = wide[start : start + GROUP]
            target[0, start : start + GROUP, :] = jnp.where(same, part[:, :GROUP], 0.0)
            target[1, start : start + GROUP, :] = jnp.where(same, part[:, GROUP:], 0.0)


def write_packed(packed_ref, value):
    count, width = value.shape
    peak = jnp.max(jnp.abs(value), axis=(0, 1), keepdims=True)
    exponent = jnp.ceil(jnp.log2(jnp.maximum(peak, 1e-30))) - 15.0
    packed_ref[0:count, :] = value * jnp.exp2(-exponent)
    packed_ref[count:, :] = jnp.broadcast_to(exponent, (16, width))


def read_packed(packed_ref, start, stop):
    count = packed_ref.shape[0] - 16
    return packed_ref[0:count, start:stop] * jnp.exp2(packed_ref[count : count + 1, 0:1])


def exchange_packed(packed, bit):
    return exchange(packed.astype(jnp.float16), bit).astype(jnp.float32)


def beside(a, b):
    return jnp.concatenate([a, b], axis=1)


def far_kernel(own_ref, oth_ref, far_ref, out_ref):
    count, rows = own_ref.shape[1:]
    for start in range(0, rows, GROUP):
        stop = start + GROUP
        value = dot(
            beside(own_ref[0, :, start:stop], oth_ref[:, start:stop]),
            beside(far_ref[0, start:stop, :], far_ref[1, start:stop, :]),
            NT,
        )
        first = value.astype(jnp.bfloat16)
        out_ref[0:count, start:stop] = first
        out_ref[count : 2 * count, start:stop] = (value - first.astype(jnp.float32)).astype(
            jnp.bfloat16
        )


def project_kernel(slots, places_ref, x_ref, w_ref, *refs):
    *out_refs, held_ref, made_ref, sems, out_sems = refs
    pieces, count, width = made_ref.shape
    half = pieces // 2
    part = width // CHUNKS

    def fetch(p):
        at = pl.multiple_of(places_ref[p] * width, width)
        return pltpu.make_async_copy(w_ref.at[:, pl.ds(at, width)], held_ref.at[p], sems.at[p])

    def leave(p, chunk):
        return pltpu.make_async_copy(
            made_ref.at[p, :, pl.ds(chunk * part, part)],
            out_refs[2 * chunk + p // half].at[slots[chunk][p]],
            out_sems.at[chunk, p],
        )

    for p in range(pieces):
        fetch(p).start()
    for p in range(pieces):
        fetch(p).wait()
        both = one_dot(x_ref[...], held_ref[p])
        made_ref[p] = both[:count] + both[count:]
        for chunk in range(CHUNKS):
            leave(p, chunk).start()
    for p in range(pieces):
        for chunk in range(CHUNKS):
            leave(p, chunk).wait()


def project(x_both, weight, places, slots):
    pieces = places.shape[0]
    count2, rows = x_both.shape
    count = count2 // 2
    width = weight.shape[1] // lax.axis_size("tensor")
    outs = pl.pallas_call(
        functools.partial(project_kernel, slots),
        out_shape=(jax.ShapeDtypeStruct((pieces // 2, count, width // CHUNKS), jnp.float32),)
        * (2 * CHUNKS),
        in_specs=[
            pl.BlockSpec(memory_space=pltpu.SMEM),
            pl.BlockSpec(memory_space=pltpu.VMEM),
            pl.BlockSpec(memory_space=pl.ANY),
        ],
        out_specs=(pl.BlockSpec(memory_space=pl.ANY),) * (2 * CHUNKS),
        scratch_shapes=[
            pltpu.VMEM((pieces, rows, width), weight.dtype),
            pltpu.VMEM((pieces, count, width), jnp.float32),
            pltpu.SemaphoreType.DMA((pieces,)),
            pltpu.SemaphoreType.DMA((CHUNKS, pieces)),
        ],
        compiler_params=pltpu.CompilerParams(vmem_limit_bytes=WIDE_LIMIT),
        cost_estimate=pl.CostEstimate(
            flops=2 * count2 * rows * width * pieces,
            bytes_accessed=pieces * width * (2 * rows + 4 * count),
            transcendentals=0,
        ),
        name="project",
    )(places, x_both, weight)
    return [outs[2 * chunk : 2 * chunk + 2] for chunk in range(CHUNKS)]


def back_kernel(order, places_ref, low_ref, high_ref, w_ref, out_ref, packed_ref, cots_ref, held_ref, cot_sems, sems):
    half, _, width = low_ref.shape

    def fetches(slot):
        at = pl.multiple_of(places_ref[order[slot]] * width, width)
        here = pl.ds(slot * width, width)
        cot = (low_ref if slot < half else high_ref).at[slot % half]
        return (
            pltpu.make_async_copy(cot, cots_ref.at[:, here], cot_sems.at[slot]),
            pltpu.make_async_copy(w_ref.at[:, pl.ds(at, width)], held_ref.at[:, here], sems.at[slot]),
        )

    for slot in range(2 * half):
        for copy in fetches(slot):
            copy.start()
    for slot in range(2 * half):
        for copy in fetches(slot):
            copy.wait()
        here = slice(slot * width, (slot + 1) * width)
        product = one_dot(cots_ref[:, here], held_ref[:, here], NT)
        if slot == 0:
            out_ref[...] = product
        else:
            out_ref[...] += product
    write_packed(packed_ref, out_ref[...])


def project_back(places, gathered, order, weight):
    half, count, width = gathered[0].shape
    steps = half * len(gathered)
    rows = weight.shape[0]
    return pl.pallas_call(
        functools.partial(back_kernel, order),
        out_shape=(
            jax.ShapeDtypeStruct((count, rows), jnp.float32),
            jax.ShapeDtypeStruct((count + 16, rows), jnp.float32),
        ),
        in_specs=[pl.BlockSpec(memory_space=pltpu.SMEM)]
        + [pl.BlockSpec(memory_space=pl.ANY)] * (len(gathered) + 1),
        out_specs=(pl.BlockSpec(memory_space=pltpu.VMEM),) * 2,
        scratch_shapes=[
            pltpu.VMEM((count, steps * width), weight.dtype),
            pltpu.VMEM((rows, steps * width), weight.dtype),
            pltpu.SemaphoreType.DMA((steps,)),
            pltpu.SemaphoreType.DMA((steps,)),
        ],
        compiler_params=pltpu.CompilerParams(vmem_limit_bytes=WIDE_LIMIT),
        cost_estimate=pl.CostEstimate(
            flops=2 * count * rows * width * steps,
            bytes_accessed=steps * width * 2 * (rows + count),
            transcendentals=0,
        ),
        name="project_back",
    )(places, *gathered, weight)


def grow(array, bit):
    return jnp.concatenate([array, exchange(array, bit)], axis=0)


def gather_order(stages):
    order = [0]
    for bit in stages:
        order = order + [n ^ (1 << bit) for n in order]
    return tuple(order)


def lane_matmul(left_ref, right_ref, out_ref, block, lanes):
    step = 4

    def body(t, _):
        first = t * step
        totals = [jnp.zeros((block, lanes), jnp.float32) for _ in range(step)]
        for j in range(block):
            right = right_ref[j * block : (j + 1) * block, :]
            for s in range(step):
                totals[s] += left_ref[pl.ds((first + s) * block + j, 1), :] * right
        for s in range(step):
            out_ref[pl.ds(pl.multiple_of((first + s) * block, block), block), :] = totals[s]
        return 0

    lax.fori_loop(0, block // step, body, 0)


def grads_kernel(
    inverse_ref, high_ref, own_ref, oth_ref, x_oth_ref, tok_ref, xs_ref, near_ref, bfar_ref, inv_far_ref, inv_ref,
    gtok_ref, ggen_ref,
    row_ref, lo_ref, hi_ref, a_ref, b_ref, c_ref,
):
    sections, block = inverse_ref.shape
    half = block // 2
    count, rows = own_ref.shape
    per_section = rows // half
    lanes = sections * per_section
    high = high_ref[0]
    chooser = jnp.concatenate([gatherer(0, block, half), gatherer(half, block, half)], axis=0)
    far_chooser = jnp.concatenate(
        [gatherer(half * high, block, half), gatherer(half * (1 - high), block, half)], axis=0
    )
    same = same_mask(half)
    same = jnp.concatenate([beside(same, same)] * 2, axis=0)
    for start in range(0, rows, GROUP):
        stop = start + GROUP
        x_pair = beside(xs_ref[0, :, start:stop], x_oth_ref[:, start:stop])
        g_pair = beside(own_ref[:, start:stop], read_packed(oth_ref, start, stop))
        both = pick(jnp.where(same, dot(x_pair, g_pair, TN), 0.0), far_chooser)
        mine, theirs = both[:GROUP], both[GROUP:]
        lo_ref[start:stop, :] = jnp.where(high == 1, theirs, mine)
        hi_ref[start:stop, :] = jnp.where(high == 1, mine, theirs)
        grad = dot(g_pair, beside(bfar_ref[0, start:stop, :], bfar_ref[1, start:stop, :]), NT)
        for k in range(1, sections):
            lo_mask, hi_mask = block_masks(k, half)
            if k < sections - 1:
                x = xs_ref[k, :, start:stop]
            else:
                x = tok_ref[:, start:stop].astype(jnp.float32)
            outer = dot(x, grad, TN)
            row_ref[k * rows + start : k * rows + stop, :] = pick(
                beside(jnp.where(lo_mask, outer, 0.0), jnp.where(hi_mask, outer, 0.0)), chooser
            )
            grad = dot(grad, near_ref[k - 1, start:stop, :], NT)
        gtok_ref[:, start:stop] = grad
    for k in range(1, sections):
        split_halves(row_ref, lo_ref, hi_ref, k, rows, half)
    to_lanes(lo_ref, hi_ref, a_ref, lanes, half, block)
    for j in range(block):
        b_ref[j * block : (j + 1) * block, :] = inv_ref[pl.ds(j, block, stride=block), :]
        b_ref[j * block : (j + 1) * block, 0:per_section] = inv_far_ref[
            pl.ds(j, block, stride=block), :
        ]
    lane_matmul(a_ref, b_ref, c_ref, block, lanes)
    lane_matmul(b_ref, c_ref, a_ref, block, lanes)
    section_of, upper = lane_facts((block, lanes), per_section, high)
    transpose_to(c_ref, a_ref, block, lambda j, t: 2.0 * (t - a_ref[j * block : (j + 1) * block, :]))
    permute_rows(inverse_ref, c_ref, b_ref, section_of)
    transpose_to(a_ref, b_ref, block)
    for a in range(half):
        low = permuted_row(inverse_ref, a_ref, a, section_of)
        top = permuted_row(inverse_ref, a_ref, half + a, section_of)
        row_ref[pl.ds(a, lanes, stride=half), :] = jnp.where(upper, top, low).T
    for k in range(sections):
        ggen_ref[k * block : (k + 1) * block, :] = row_ref[k * rows : (k + 1) * rows, :].T


def pack_kernel(keep_ref, got_ref, packed_ref, out_ref):
    half, count, width = out_ref.shape
    largest = jnp.zeros((count, width), jnp.float32)
    for p in range(half):
        total = keep_ref[half + p] + got_ref[half + p]
        packed_ref[p * count : (p + 1) * count, :] = total
        largest = jnp.maximum(largest, jnp.abs(total))
        out_ref[p] = keep_ref[p] + got_ref[p]
    peak = jnp.max(largest, axis=(0, 1), keepdims=True)
    exponent = jnp.ceil(jnp.log2(jnp.maximum(peak, 1e-30))) - 15.0
    scale = jnp.exp2(-exponent)
    for p in range(half):
        packed_ref[p * count : (p + 1) * count, :] *= scale
    packed_ref[half * count :, :] = jnp.broadcast_to(exponent, (16, width))


def unpack_kernel(keep_ref, got_ref, send_ref, out_ref):
    half, count, width = out_ref.shape
    scale = jnp.exp2(got_ref[2 * half * count : 2 * half * count + 1, 0:1])
    for p in range(half):
        low, top = p * count, (half + p) * count
        out_ref[p] = keep_ref[p] + got_ref[low : low + count, :] * scale
        send_ref[p] = keep_ref[half + p] + got_ref[top : top + count, :] * scale


def last_kernel(*refs):
    *in_refs, out_ref = refs
    chunks = len(in_refs) // 2
    width = in_refs[0].shape[2]
    for chunk in range(chunks):
        out_ref[:, chunk * width : (chunk + 1) * width] = in_refs[chunk][0] + read_packed(
            in_refs[chunks + chunk], 0, width
        )


def summed(kernel, name, keep, got, first):
    pieces, count, width = keep.shape
    full = pl.BlockSpec(memory_space=pltpu.VMEM)
    return pl.pallas_call(
        kernel,
        out_shape=(first, jax.ShapeDtypeStruct((pieces // 2, count, width), jnp.float32)),
        in_specs=[full] * 2,
        out_specs=(full,) * 2,
        compiler_params=pltpu.CompilerParams(vmem_limit_bytes=VMEM_LIMIT),
        name=name,
    )(keep, got)


def pack(keep, got):
    pieces, count, width = keep.shape
    first = jax.ShapeDtypeStruct((pieces // 2 * count + 16, width), jnp.float32)
    packed, keep = summed(pack_kernel, "sum_pack", keep, got, first)
    return packed.astype(jnp.float16), keep


def unpack(keep, got):
    pieces, count, width = keep.shape
    first = jax.ShapeDtypeStruct((pieces // 2, count, width), jnp.float32)
    return summed(unpack_kernel, "sum_unpack", keep, got.astype(jnp.float32), first)


def local(tokens, weight, generators, orders, cotangent):
    sections, rows, block = generators.shape
    half = block // 2
    count = tokens.shape[0]
    size = lax.axis_size("tensor")
    bits = size.bit_length() - 1
    here = lax.axis_index("tensor")
    pair_bit = bits - 1
    high = jnp.bitwise_and(jnp.right_shift(here, pair_bit), 1).astype(jnp.int32).reshape(1)
    lanes = sections * (rows // half)
    f32 = jnp.float32
    full = pl.BlockSpec(memory_space=pltpu.VMEM)
    scalars = pl.BlockSpec(memory_space=pltpu.SMEM)
    params = pltpu.CompilerParams(vmem_limit_bytes=VMEM_LIMIT)

    stored = jnp.swapaxes(generators, 1, 2)
    far_gen = exchange(stored[0], pair_bit)
    order = list(range(bits - 1, -1, -1))
    pieces = cotangent[None]
    for bit in order[:-3]:
        pieces = grow(pieces, bit)
    flat = stored.reshape(sections * block, rows)
    square = (block * block, lanes)
    far_square = (block * block, lanes // sections)
    inv, near, xs = pl.pallas_call(
        near_kernel,
        out_shape=(
            jax.ShapeDtypeStruct(square, f32),
            jax.ShapeDtypeStruct((sections - 1, rows, GROUP), f32),
            jax.ShapeDtypeStruct((sections - 1, count, rows), f32),
        ),
        in_specs=[scalars, full, full],
        out_specs=(full,) * 3,
        scratch_shapes=[
            pltpu.VMEM((sections * rows, block), f32),
            pltpu.VMEM((sections * rows, block), f32),
            pltpu.VMEM(square, f32),
            pltpu.VMEM(square, f32),
            pltpu.VMEM((sections * rows, block), f32),
        ],
        compiler_params=params,
        name="near_rotations",
    )(orders, flat, tokens)
    x_last, pieces, far_gen = lax.optimization_barrier((xs[0], pieces, far_gen))
    near_news, side_news = exchange(pieces, order[-3]), exchange(pieces, order[-2])
    x_other = exchange(x_last, pair_bit)
    inv_far, ffar, bfar = pl.pallas_call(
        far_rotations_kernel,
        out_shape=(
            jax.ShapeDtypeStruct(far_square, f32),
            jax.ShapeDtypeStruct((2, rows, GROUP), f32),
            jax.ShapeDtypeStruct((2, rows, GROUP), f32),
        ),
        in_specs=[scalars, scalars, full, full],
        out_specs=(full,) * 3,
        scratch_shapes=[
            pltpu.VMEM((rows, block), f32),
            pltpu.VMEM((rows, block), f32),
            pltpu.VMEM(far_square, f32),
            pltpu.VMEM(far_square, f32),
            pltpu.VMEM((rows, block), f32),
            pltpu.VMEM((rows, block), f32),
        ],
        compiler_params=params,
        cost_estimate=pl.CostEstimate(flops=10**7, bytes_accessed=10**7, transcendentals=0),
        name="far_rotations",
    )(orders[:1], high, stored[0], far_gen)
    near_news = after(near_news, ffar, x_other)
    last_news = exchange(near_news, order[-2])
    x_both = pl.pallas_call(
        far_kernel,
        out_shape=jax.ShapeDtypeStruct((2 * count, rows), jnp.bfloat16),
        in_specs=[full] * 3,
        out_specs=full,
        compiler_params=params,
        name="far_apply",
    )(xs, x_other, ffar)

    stages = [tuple(range(bits)), (0, 2, 1) + tuple(range(3, bits))]

    def slot_of(offset, bits_in_order):
        return sum(((offset >> bit) & 1) << (bits - 1 - n) for n, bit in enumerate(bits_in_order))

    offsets = sorted(range(size), key=lambda o: (1 - (o & 1), slot_of(o, stages[0])))
    slots = [[slot_of(o, bits_in_order) % (size // 2) for o in offsets] for bits_in_order in stages]
    fixed = here.astype(jnp.int32)
    places = jnp.bitwise_xor(fixed, jnp.asarray(np.array(offsets, np.int32)))
    back_places = jnp.bitwise_xor(fixed, jnp.arange(size, dtype=jnp.int32))
    outs = project(after(x_both, near_news, side_news), weight, places, slots)

    def stage(keep, got):
        mid = keep.shape[0] // 2
        return keep[mid:] + got[mid:], keep[:mid] + got[:mid]

    outs = [pack(keep, exchange(send, 0)) for send, keep in outs]
    gots = [exchange(send, order_[1]) for (send, _), order_ in zip(outs, stages)]
    last_news = after(last_news, *[send for send, _ in outs])
    pieces = jnp.concatenate([pieces, near_news, side_news, last_news], axis=0)
    gathered = [pieces, exchange(pieces, 0)]
    numbers = jnp.arange(block, dtype=jnp.int32)
    inverse = jnp.sum(
        jnp.where(orders[:, :, None] == numbers[None, None, :], numbers[None, :, None], 0), axis=1
    ).astype(jnp.int32)
    grad_cols, grad_packed = project_back(back_places, gathered, gather_order(order), weight)
    grad_other = exchange_packed(grad_packed, pair_bit)
    gots[0] = after(gots[0], grad_cols)
    gots[-1] = after(gots[-1], grad_other)
    grad_tokens, grad_gens = pl.pallas_call(
        grads_kernel,
        out_shape=(
            jax.ShapeDtypeStruct((count, rows), f32),
            jax.ShapeDtypeStruct((sections * block, rows), f32),
        ),
        in_specs=[scalars, scalars] + [full] * 9,
        out_specs=(full,) * 2,
        scratch_shapes=[
            pltpu.VMEM((sections * rows, block), f32),
            pltpu.VMEM((sections * rows, block), f32),
            pltpu.VMEM((sections * rows, block), f32),
            pltpu.VMEM(square, f32),
            pltpu.VMEM(square, f32),
            pltpu.VMEM(square, f32),
        ],
        compiler_params=params,
        name="gradients",
    )(inverse, high, grad_cols, grad_other, x_other, tokens, xs, near, bfar, inv_far, inv)
    outs = [unpack(keep, got) for (_, keep), got in zip(outs, gots)]
    for n in range(2, bits - 1):
        gots = [exchange(send, order_[n]) for (send, _), order_ in zip(outs, stages)]
        merge = pack if n == bits - 2 else stage
        outs = [merge(keep, got) for (_, keep), got in zip(outs, gots)]
    lasts = [exchange(send, bits - 1).astype(f32) for send, _ in outs]
    lasts[-1] = after(lasts[-1], grad_tokens, grad_gens)
    outputs = pl.pallas_call(
        last_kernel,
        out_shape=jax.ShapeDtypeStruct((count, cotangent.shape[1]), f32),
        in_specs=[full] * (2 * CHUNKS),
        out_specs=full,
        compiler_params=params,
        name="last_sums",
    )(*[keep for _, keep in outs], *lasts)
    return outputs, grad_tokens, jnp.swapaxes(grad_gens.reshape(sections, block, rows), 1, 2)


def solution(mesh):
    placed = (
        P("groups", "tensor"),
        P("tensor", None),
        P("groups", "tensor", None),
        P(),
        P("groups", "tensor"),
    )
    return jax.shard_map(
        local,
        mesh=mesh,
        in_specs=placed,
        out_specs=(P("groups", "tensor"), P("groups", "tensor"), P("groups", "tensor", None)),
        check_vma=False,
    )
```

```python
import functools

import jax
import jax.numpy as jnp
import numpy as np
from jax import lax
from jax.experimental import pallas as pl
from jax.experimental.pallas import tpu as pltpu
from jax.sharding import PartitionSpec as P

VMEM_LIMIT = 16 * 2**20
WIDE_LIMIT = 50 * 2**20
GROUP = 128
NN = (((1,), (0,)), ((), ()))
NT = (((1,), (1,)), ((), ()))
TN = (((0,), (0,)), ((), ()))
CHUNKS = 2


def exchange(array, bit):
    size = lax.axis_size("tensor")
    return lax.ppermute(array, "tensor", [(i, i ^ (1 << bit)) for i in range(size)])


def parts_of(x):
    first = x.astype(jnp.bfloat16)
    return first, (x - first.astype(jnp.float32)).astype(jnp.bfloat16)


def one_dot(a, b, dims=NN):
    return lax.dot_general(a, b, dims, preferred_element_type=jnp.float32)


def after(value, *earlier):
    return lax.optimization_barrier((value, *earlier))[0]


def dot(a, b, dims=NN):
    a_first, a_rest = parts_of(a)
    b_first, b_rest = parts_of(b)
    return (
        one_dot(a_first, b_first, dims) + one_dot(a_rest, b_first, dims) + one_dot(a_first, b_rest, dims)
    )


def pick(a, chooser):
    first, rest = parts_of(a)
    return one_dot(first, chooser) + one_dot(rest, chooser)


def iota(shape, dim):
    return lax.broadcasted_iota(jnp.int32, shape, dim)


def split_halves(rows_ref, lo_ref, hi_ref, section, rows, half):
    step = half << (section - 1)
    base = section * rows
    for start in range(base, base + rows, 2 * step):
        low = rows_ref[start : start + step, :]
        high = rows_ref[start + step : start + 2 * step, :]
        lo_ref[start : start + step, :] = low
        lo_ref[start + step : start + 2 * step, :] = low
        hi_ref[start : start + step, :] = high
        hi_ref[start + step : start + 2 * step, :] = high


def to_lanes(lo_ref, hi_ref, out_ref, lanes, half, block):
    for a in range(half):
        out_ref[a * block : (a + 1) * block, :] = lo_ref[pl.ds(a, lanes, stride=half), :].T
        out_ref[(half + a) * block : (half + a + 1) * block, :] = hi_ref[
            pl.ds(a, lanes, stride=half), :
        ].T


def by_section(parts, section_of):
    out = parts[-1]
    for k in range(len(parts) - 2, -1, -1):
        out = jnp.where(section_of == k, parts[k], out)
    return out


def lane_facts(shape, per_section, high):
    lane = iota(shape, 1)
    section_of = lane // per_section
    part = lane % per_section
    upper = jnp.bitwise_and(jnp.right_shift(part, jnp.maximum(section_of - 1, 0)), 1)
    return section_of, jnp.where(section_of == 0, high, upper) == 1


def block_masks(section, half):
    row = iota((GROUP, GROUP), 0) // half
    col = iota((GROUP, GROUP), 1) // half
    bit = 1 << (section - 1)
    return col == jnp.bitwise_and(row, ~bit), col == jnp.bitwise_or(row, bit)


def same_mask(half):
    return iota((GROUP, GROUP), 0) // half == iota((GROUP, GROUP), 1) // half


def spreader(offsets, block, half):
    row, col = iota((block, GROUP), 0), iota((block, GROUP), 1) % half
    return jnp.concatenate([(row == at + col).astype(jnp.bfloat16) for at in offsets], axis=1)


def gatherer(offset, block, half):
    row, col = iota((GROUP, block), 0) % half, iota((GROUP, block), 1)
    return (col == offset + row).astype(jnp.bfloat16)


def transpose_to(out_ref, in_ref, block, change=lambda j, t: t):
    for j in range(block):
        out_ref[j * block : (j + 1) * block, :] = change(j, in_ref[pl.ds(j, block, stride=block), :])


def permuted_row(orders_ref, in_ref, i, section_of):
    sections, block = orders_ref.shape
    return by_section(
        [
            in_ref[pl.ds(pl.multiple_of(orders_ref[k, i] * block, block), block), :]
            for k in range(sections)
        ],
        section_of,
    )


def permute_rows(orders_ref, in_ref, out_ref, section_of):
    block = orders_ref.shape[1]
    for i in range(block):
        out_ref[i * block : (i + 1) * block, :] = permuted_row(orders_ref, in_ref, i, section_of)


def invert_blocks(orders_ref, lo_ref, hi_ref, inv_ref, a_ref, b_ref, section_of):
    sections, block = orders_ref.shape
    half = block // 2
    lanes = inv_ref.shape[1]
    to_lanes(lo_ref, hi_ref, a_ref, lanes, half, block)

    transpose_to(b_ref, a_ref, block, lambda j, t: a_ref[j * block : (j + 1) * block, :] - t)
    permute_rows(orders_ref, b_ref, a_ref, section_of)
    transpose_to(b_ref, a_ref, block)
    permute_rows(orders_ref, b_ref, inv_ref, section_of)
    sub = iota((block, lanes), 0)
    for j in range(block):
        inv_ref[j * block : (j + 1) * block, :] += (sub == j).astype(jnp.float32)

    def eliminate(k, _):
        at = pl.multiple_of(k * block, block)
        here = sub == k
        inverse = 1.0 / inv_ref[pl.ds(at + k, 1), :]
        factors = inv_ref[pl.ds(k, block, stride=block), :]
        pivot = jnp.where(here, inverse, inv_ref[pl.ds(at, block), :] * inverse)
        for i in range(block):
            row = inv_ref[i * block : (i + 1) * block, :]
            inv_ref[i * block : (i + 1) * block, :] = (
                jnp.where(here, 0.0, row) - factors[i : i + 1, :] * pivot
            )
        inv_ref[pl.ds(at, block), :] = pivot
        return 0

    lax.fori_loop(0, block, eliminate, 0)


def own_rows(inv_ref, out_ref, half, block, upper):
    lanes = inv_ref.shape[1]
    sub = iota((block, lanes), 0)
    for a in range(half):
        low = 2.0 * inv_ref[a * block : (a + 1) * block, :] - (sub == a).astype(jnp.float32)
        top = 2.0 * inv_ref[(half + a) * block : (half + a + 1) * block, :] - (
            sub == half + a
        ).astype(jnp.float32)
        out_ref[pl.ds(a, lanes, stride=half), :] = jnp.where(upper, top, low).T


def own_cols(inv_ref, out_ref, half, block, upper):
    lanes = inv_ref.shape[1]
    sub = iota((block, lanes), 0)
    for a in range(half):
        low = 2.0 * inv_ref[pl.ds(a, block, stride=block), :] - (sub == a).astype(jnp.float32)
        top = 2.0 * inv_ref[pl.ds(half + a, block, stride=block), :] - (sub == half + a).astype(
            jnp.float32
        )
        out_ref[pl.ds(a, lanes, stride=half), :] = jnp.where(upper, top, low).T


def near_kernel(
    orders_ref, gen_ref, tok_ref, inv_ref, near_ref, xs_ref,
    lo_ref, hi_ref, a_ref, b_ref, row_ref,
):
    sections, block = orders_ref.shape
    half = block // 2
    rows = tok_ref.shape[1]
    lanes = sections * rows // half
    for k in range(sections):
        row_ref[k * rows : (k + 1) * rows, :] = gen_ref[k * block : (k + 1) * block, :].T
    lo_ref[0:rows, :] = row_ref[0:rows, :]
    hi_ref[0:rows, :] = row_ref[0:rows, :]
    for k in range(1, sections):
        split_halves(row_ref, lo_ref, hi_ref, k, rows, half)
    section_of, upper = lane_facts((block, lanes), rows // half, 0)
    invert_blocks(orders_ref, lo_ref, hi_ref, inv_ref, a_ref, b_ref, section_of)
    own_rows(inv_ref, row_ref, half, block, upper)
    spread = spreader((0, half), block, half)
    for k in range(1, sections):
        lo_mask, hi_mask = block_masks(k, half)
        wide = pick(row_ref[k * rows : (k + 1) * rows, :], spread)
        for start in range(0, rows, GROUP):
            part = wide[start : start + GROUP]
            near_ref[k - 1, start : start + GROUP, :] = jnp.where(
                lo_mask, part[:, :GROUP], jnp.where(hi_mask, part[:, GROUP:], 0.0)
            )
    for start in range(0, rows, GROUP):
        stop = start + GROUP
        value = tok_ref[:, start:stop].astype(jnp.float32)
        for k in range(sections - 1, 0, -1):
            value = dot(value, near_ref[k - 1, start:stop, :])
            xs_ref[k - 1, :, start:stop] = value


def far_rotations_kernel(
    orders_ref, high_ref, own_ref, far_ref, inv_ref, ffar_ref, bfar_ref,
    lo_ref, hi_ref, a_ref, b_ref, row_ref, col_ref,
):
    block = orders_ref.shape[1]
    half = block // 2
    rows = far_ref.shape[1]
    high = high_ref[0]
    own = own_ref[...].T
    other = far_ref[...].T
    lo_ref[...] = jnp.where(high == 1, other, own)
    hi_ref[...] = jnp.where(high == 1, own, other)
    invert_blocks(orders_ref, lo_ref, hi_ref, inv_ref, a_ref, b_ref, None)
    upper = high == 1
    own_rows(inv_ref, row_ref, half, block, upper)
    own_cols(inv_ref, col_ref, half, block, upper)
    spread = spreader((half * high, half * (1 - high)), block, half)
    same = same_mask(half)
    for source, target in ((col_ref, ffar_ref), (row_ref, bfar_ref)):
        wide = pick(source[...], spread)
        for start in range(0, rows, GROUP):
            part = wide[start : start + GROUP]
            target[0, start : start + GROUP, :] = jnp.where(same, part[:, :GROUP], 0.0)
            target[1, start : start + GROUP, :] = jnp.where(same, part[:, GROUP:], 0.0)


def write_packed(packed_ref, value):
    count, width = value.shape
    peak = jnp.max(jnp.abs(value), axis=(0, 1), keepdims=True)
    exponent = jnp.ceil(jnp.log2(jnp.maximum(peak, 1e-30))) - 15.0
    packed_ref[0:count, :] = value * jnp.exp2(-exponent)
    packed_ref[count:, :] = jnp.broadcast_to(exponent, (16, width))


def read_packed(packed_ref, start, stop):
    count = packed_ref.shape[0] - 16
    return packed_ref[0:count, start:stop] * jnp.exp2(packed_ref[count : count + 1, 0:1])


def exchange_packed(packed, bit):
    return exchange(packed.astype(jnp.float16), bit).astype(jnp.float32)


def beside(a, b):
    return jnp.concatenate([a, b], axis=1)


def far_kernel(own_ref, oth_ref, far_ref, out_ref):
    count, rows = own_ref.shape[1:]
    for start in range(0, rows, GROUP):
        stop = start + GROUP
        value = dot(
            beside(own_ref[0, :, start:stop], oth_ref[:, start:stop]),
            beside(far_ref[0, start:stop, :], far_ref[1, start:stop, :]),
            NT,
        )
        first = value.astype(jnp.bfloat16)
        out_ref[0:count, start:stop] = first
        out_ref[count : 2 * count, start:stop] = (value - first.astype(jnp.float32)).astype(
            jnp.bfloat16
        )


def project_kernel(slots, places_ref, x_ref, w_ref, *refs):
    *out_refs, held_ref, made_ref, sems, out_sems = refs
    pieces, count, width = made_ref.shape
    half = pieces // 2
    part = width // CHUNKS

    def fetch(p):
        at = pl.multiple_of(places_ref[p] * width, width)
        return pltpu.make_async_copy(w_ref.at[:, pl.ds(at, width)], held_ref.at[p], sems.at[p])

    def leave(p, chunk):
        return pltpu.make_async_copy(
            made_ref.at[p, :, pl.ds(chunk * part, part)],
            out_refs[2 * chunk + p // half].at[slots[chunk][p]],
            out_sems.at[chunk, p],
        )

    for p in range(pieces):
        fetch(p).start()
    for p in range(pieces):
        fetch(p).wait()
        both = one_dot(x_ref[...], held_ref[p])
        made_ref[p] = both[:count] + both[count:]
        for chunk in range(CHUNKS):
            leave(p, chunk).start()
    for p in range(pieces):
        for chunk in range(CHUNKS):
            leave(p, chunk).wait()


def project(x_both, weight, places, slots):
    pieces = places.shape[0]
    count2, rows = x_both.shape
    count = count2 // 2
    width = weight.shape[1] // lax.axis_size("tensor")
    outs = pl.pallas_call(
        functools.partial(project_kernel, slots),
        out_shape=(jax.ShapeDtypeStruct((pieces // 2, count, width // CHUNKS), jnp.float32),)
        * (2 * CHUNKS),
        in_specs=[
            pl.BlockSpec(memory_space=pltpu.SMEM),
            pl.BlockSpec(memory_space=pltpu.VMEM),
            pl.BlockSpec(memory_space=pl.ANY),
        ],
        out_specs=(pl.BlockSpec(memory_space=pl.ANY),) * (2 * CHUNKS),
        scratch_shapes=[
            pltpu.VMEM((pieces, rows, width), weight.dtype),
            pltpu.VMEM((pieces, count, width), jnp.float32),
            pltpu.SemaphoreType.DMA((pieces,)),
            pltpu.SemaphoreType.DMA((CHUNKS, pieces)),
        ],
        compiler_params=pltpu.CompilerParams(vmem_limit_bytes=WIDE_LIMIT),
        cost_estimate=pl.CostEstimate(
            flops=2 * count2 * rows * width * pieces,
            bytes_accessed=pieces * width * (2 * rows + 4 * count),
            transcendentals=0,
        ),
        name="project",
    )(places, x_both, weight)
    return [outs[2 * chunk : 2 * chunk + 2] for chunk in range(CHUNKS)]


def back_kernel(order, places_ref, low_ref, high_ref, w_ref, out_ref, packed_ref, cots_ref, held_ref, cot_sems, sems):
    half, _, width = low_ref.shape

    def fetches(slot):
        at = pl.multiple_of(places_ref[order[slot]] * width, width)
        here = pl.ds(slot * width, width)
        cot = (low_ref if slot < half else high_ref).at[slot % half]
        return (
            pltpu.make_async_copy(cot, cots_ref.at[:, here], cot_sems.at[slot]),
            pltpu.make_async_copy(w_ref.at[:, pl.ds(at, width)], held_ref.at[:, here], sems.at[slot]),
        )

    for slot in range(2 * half):
        for copy in fetches(slot):
            copy.start()
    for slot in range(2 * half):
        for copy in fetches(slot):
            copy.wait()
        here = slice(slot * width, (slot + 1) * width)
        product = one_dot(cots_ref[:, here], held_ref[:, here], NT)
        if slot == 0:
            out_ref[...] = product
        else:
            out_ref[...] += product
    write_packed(packed_ref, out_ref[...])


def project_back(places, gathered, order, weight):
    half, count, width = gathered[0].shape
    steps = half * len(gathered)
    rows = weight.shape[0]
    return pl.pallas_call(
        functools.partial(back_kernel, order),
        out_shape=(
            jax.ShapeDtypeStruct((count, rows), jnp.float32),
            jax.ShapeDtypeStruct((count + 16, rows), jnp.float32),
        ),
        in_specs=[pl.BlockSpec(memory_space=pltpu.SMEM)]
        + [pl.BlockSpec(memory_space=pl.ANY)] * (len(gathered) + 1),
        out_specs=(pl.BlockSpec(memory_space=pltpu.VMEM),) * 2,
        scratch_shapes=[
            pltpu.VMEM((count, steps * width), weight.dtype),
            pltpu.VMEM((rows, steps * width), weight.dtype),
            pltpu.SemaphoreType.DMA((steps,)),
            pltpu.SemaphoreType.DMA((steps,)),
        ],
        compiler_params=pltpu.CompilerParams(vmem_limit_bytes=WIDE_LIMIT),
        cost_estimate=pl.CostEstimate(
            flops=2 * count * rows * width * steps,
            bytes_accessed=steps * width * 2 * (rows + count),
            transcendentals=0,
        ),
        name="project_back",
    )(places, *gathered, weight)


def grow(array, bit):
    return jnp.concatenate([array, exchange(array, bit)], axis=0)


def gather_order(stages):
    order = [0]
    for bit in stages:
        order = order + [n ^ (1 << bit) for n in order]
    return tuple(order)


def lane_matmul(left_ref, right_ref, out_ref, block, lanes):
    step = 4

    def body(t, _):
        first = t * step
        totals = [jnp.zeros((block, lanes), jnp.float32) for _ in range(step)]
        for j in range(block):
            right = right_ref[j * block : (j + 1) * block, :]
            for s in range(step):
                totals[s] += left_ref[pl.ds((first + s) * block + j, 1), :] * right
        for s in range(step):
            out_ref[pl.ds(pl.multiple_of((first + s) * block, block), block), :] = totals[s]
        return 0

    lax.fori_loop(0, block // step, body, 0)


def grads_kernel(
    inverse_ref, high_ref, own_ref, oth_ref, x_oth_ref, tok_ref, xs_ref, near_ref, bfar_ref, inv_far_ref, inv_ref,
    gtok_ref, ggen_ref,
    row_ref, lo_ref, hi_ref, a_ref, b_ref, c_ref,
):
    sections, block = inverse_ref.shape
    half = block // 2
    count, rows = own_ref.shape
    per_section = rows // half
    lanes = sections * per_section
    high = high_ref[0]
    chooser = jnp.concatenate([gatherer(0, block, half), gatherer(half, block, half)], axis=0)
    far_chooser = jnp.concatenate(
        [gatherer(half * high, block, half), gatherer(half * (1 - high), block, half)], axis=0
    )
    same = same_mask(half)
    same = jnp.concatenate([beside(same, same)] * 2, axis=0)
    for start in range(0, rows, GROUP):
        stop = start + GROUP
        x_pair = beside(xs_ref[0, :, start:stop], x_oth_ref[:, start:stop])
        g_pair = beside(own_ref[:, start:stop], read_packed(oth_ref, start, stop))
        both = pick(jnp.where(same, dot(x_pair, g_pair, TN), 0.0), far_chooser)
        mine, theirs = both[:GROUP], both[GROUP:]
        lo_ref[start:stop, :] = jnp.where(high == 1, theirs, mine)
        hi_ref[start:stop, :] = jnp.where(high == 1, mine, theirs)
        grad = dot(g_pair, beside(bfar_ref[0, start:stop, :], bfar_ref[1, start:stop, :]), NT)
        for k in range(1, sections):
            lo_mask, hi_mask = block_masks(k, half)
            if k < sections - 1:
                x = xs_ref[k, :, start:stop]
            else:
                x = tok_ref[:, start:stop].astype(jnp.float32)
            outer = dot(x, grad, TN)
            row_ref[k * rows + start : k * rows + stop, :] = pick(
                beside(jnp.where(lo_mask, outer, 0.0), jnp.where(hi_mask, outer, 0.0)), chooser
            )
            grad = dot(grad, near_ref[k - 1, start:stop, :], NT)
        gtok_ref[:, start:stop] = grad
    for k in range(1, sections):
        split_halves(row_ref, lo_ref, hi_ref, k, rows, half)
    to_lanes(lo_ref, hi_ref, a_ref, lanes, half, block)
    for j in range(block):
        b_ref[j * block : (j + 1) * block, :] = inv_ref[pl.ds(j, block, stride=block), :]
        b_ref[j * block : (j + 1) * block, 0:per_section] = inv_far_ref[
            pl.ds(j, block, stride=block), :
        ]
    lane_matmul(a_ref, b_ref, c_ref, block, lanes)
    lane_matmul(b_ref, c_ref, a_ref, block, lanes)
    section_of, upper = lane_facts((block, lanes), per_section, high)
    transpose_to(c_ref, a_ref, block, lambda j, t: 2.0 * (t - a_ref[j * block : (j + 1) * block, :]))
    permute_rows(inverse_ref, c_ref, b_ref, section_of)
    transpose_to(a_ref, b_ref, block)
    for a in range(half):
        low = permuted_row(inverse_ref, a_ref, a, section_of)
        top = permuted_row(inverse_ref, a_ref, half + a, section_of)
        row_ref[pl.ds(a, lanes, stride=half), :] = jnp.where(upper, top, low).T
    for k in range(sections):
        ggen_ref[k * block : (k + 1) * block, :] = row_ref[k * rows : (k + 1) * rows, :].T


def pack_kernel(keep_ref, got_ref, packed_ref, out_ref):
    half, count, width = out_ref.shape
    largest = jnp.zeros((count, width), jnp.float32)
    for p in range(half):
        total = keep_ref[half + p] + got_ref[half + p]
        packed_ref[p * count : (p + 1) * count, :] = total
        largest = jnp.maximum(largest, jnp.abs(total))
        out_ref[p] = keep_ref[p] + got_ref[p]
    peak = jnp.max(largest, axis=(0, 1), keepdims=True)
    exponent = jnp.ceil(jnp.log2(jnp.maximum(peak, 1e-30))) - 15.0
    scale = jnp.exp2(-exponent)
    for p in range(half):
        packed_ref[p * count : (p + 1) * count, :] *= scale
    packed_ref[half * count :, :] = jnp.broadcast_to(exponent, (16, width))


def unpack_kernel(keep_ref, got_ref, send_ref, out_ref):
    half, count, width = out_ref.shape
    scale = jnp.exp2(got_ref[2 * half * count : 2 * half * count + 1, 0:1])
    for p in range(half):
        low, top = p * count, (half + p) * count
        out_ref[p] = keep_ref[p] + got_ref[low : low + count, :] * scale
        send_ref[p] = keep_ref[half + p] + got_ref[top : top + count, :] * scale


def last_kernel(*refs):
    *in_refs, out_ref = refs
    chunks = len(in_refs) // 2
    width = in_refs[0].shape[2]
    for chunk in range(chunks):
        out_ref[:, chunk * width : (chunk + 1) * width] = in_refs[chunk][0] + read_packed(
            in_refs[chunks + chunk], 0, width
        )


def summed(kernel, name, keep, got, first):
    pieces, count, width = keep.shape
    full = pl.BlockSpec(memory_space=pltpu.VMEM)
    return pl.pallas_call(
        kernel,
        out_shape=(first, jax.ShapeDtypeStruct((pieces // 2, count, width), jnp.float32)),
        in_specs=[full] * 2,
        out_specs=(full,) * 2,
        compiler_params=pltpu.CompilerParams(vmem_limit_bytes=VMEM_LIMIT),
        name=name,
    )(keep, got)


def pack(keep, got):
    pieces, count, width = keep.shape
    first = jax.ShapeDtypeStruct((pieces // 2 * count + 16, width), jnp.float32)
    packed, keep = summed(pack_kernel, "sum_pack", keep, got, first)
    return packed.astype(jnp.float16), keep


def unpack(keep, got):
    pieces, count, width = keep.shape
    first = jax.ShapeDtypeStruct((pieces // 2, count, width), jnp.float32)
    return summed(unpack_kernel, "sum_unpack", keep, got.astype(jnp.float32), first)


def local(tokens, weight, generators, orders, cotangent):
    sections, rows, block = generators.shape
    half = block // 2
    count = tokens.shape[0]
    size = lax.axis_size("tensor")
    bits = size.bit_length() - 1
    here = lax.axis_index("tensor")
    pair_bit = bits - 1
    high = jnp.bitwise_and(jnp.right_shift(here, pair_bit), 1).astype(jnp.int32).reshape(1)
    lanes = sections * (rows // half)
    f32 = jnp.float32
    full = pl.BlockSpec(memory_space=pltpu.VMEM)
    scalars = pl.BlockSpec(memory_space=pltpu.SMEM)
    params = pltpu.CompilerParams(vmem_limit_bytes=VMEM_LIMIT)

    stored = jnp.swapaxes(generators, 1, 2)
    far_gen = exchange(stored[0], pair_bit)
    order = list(range(bits - 1, -1, -1))
    pieces = cotangent[None]
    for bit in order[:-3]:
        pieces = grow(pieces, bit)
    flat = stored.reshape(sections * block, rows)
    square = (block * block, lanes)
    far_square = (block * block, lanes // sections)
    inv, near, xs = pl.pallas_call(
        near_kernel,
        out_shape=(
            jax.ShapeDtypeStruct(square, f32),
            jax.ShapeDtypeStruct((sections - 1, rows, GROUP), f32),
            jax.ShapeDtypeStruct((sections - 1, count, rows), f32),
        ),
        in_specs=[scalars, full, full],
        out_specs=(full,) * 3,
        scratch_shapes=[
            pltpu.VMEM((sections * rows, block), f32),
            pltpu.VMEM((sections * rows, block), f32),
            pltpu.VMEM(square, f32),
            pltpu.VMEM(square, f32),
            pltpu.VMEM((sections * rows, block), f32),
        ],
        compiler_params=params,
        name="near_rotations",
    )(orders, flat, tokens)
    pieces, far_gen = after(pieces, xs), after(far_gen, xs)
    x_other = exchange(xs[0], pair_bit)
    inv_far, ffar, bfar = pl.pallas_call(
        far_rotations_kernel,
        out_shape=(
            jax.ShapeDtypeStruct(far_square, f32),
            jax.ShapeDtypeStruct((2, rows, GROUP), f32),
            jax.ShapeDtypeStruct((2, rows, GROUP), f32),
        ),
        in_specs=[scalars, scalars, full, full],
        out_specs=(full,) * 3,
        scratch_shapes=[
            pltpu.VMEM((rows, block), f32),
            pltpu.VMEM((rows, block), f32),
            pltpu.VMEM(far_square, f32),
            pltpu.VMEM(far_square, f32),
            pltpu.VMEM((rows, block), f32),
            pltpu.VMEM((rows, block), f32),
        ],
        compiler_params=params,
        cost_estimate=pl.CostEstimate(flops=10**7, bytes_accessed=10**7, transcendentals=0),
        name="far_rotations",
    )(orders[:1], high, stored[0], far_gen)
    pieces = after(pieces, ffar)
    near_news, side_news = exchange(pieces, order[-3]), exchange(pieces, order[-2])
    last_news = exchange(near_news, order[-2])
    x_both = pl.pallas_call(
        far_kernel,
        out_shape=jax.ShapeDtypeStruct((2 * count, rows), jnp.bfloat16),
        in_specs=[full] * 3,
        out_specs=full,
        compiler_params=params,
        name="far_apply",
    )(xs, x_other, ffar)

    stages = [tuple(range(bits)), (0, 2, 1) + tuple(range(3, bits))]

    def slot_of(offset, bits_in_order):
        return sum(((offset >> bit) & 1) << (bits - 1 - n) for n, bit in enumerate(bits_in_order))

    offsets = sorted(range(size), key=lambda o: (1 - (o & 1), slot_of(o, stages[0])))
    slots = [[slot_of(o, bits_in_order) % (size // 2) for o in offsets] for bits_in_order in stages]
    fixed = here.astype(jnp.int32)
    places = jnp.bitwise_xor(fixed, jnp.asarray(np.array(offsets, np.int32)))
    back_places = jnp.bitwise_xor(fixed, jnp.arange(size, dtype=jnp.int32))
    outs = project(x_both, weight, places, slots)

    def stage(keep, got):
        mid = keep.shape[0] // 2
        return keep[mid:] + got[mid:], keep[:mid] + got[:mid]

    outs = [pack(keep, exchange(after(send, near_news, side_news), 0)) for send, keep in outs]
    gots = [exchange(send, order_[1]) for (send, _), order_ in zip(outs, stages)]
    last_news = after(last_news, *[send for send, _ in outs])
    pieces = jnp.concatenate([pieces, near_news, side_news, last_news], axis=0)
    gathered = [pieces, exchange(pieces, 0)]
    numbers = jnp.arange(block, dtype=jnp.int32)
    inverse = jnp.sum(
        jnp.where(orders[:, :, None] == numbers[None, None, :], numbers[None, :, None], 0), axis=1
    ).astype(jnp.int32)
    grad_cols, grad_packed = project_back(back_places, gathered, gather_order(order), weight)
    grad_other = exchange_packed(grad_packed, pair_bit)
    gots[0] = after(gots[0], grad_cols)
    gots[-1] = after(gots[-1], grad_other)
    grad_tokens, grad_gens = pl.pallas_call(
        grads_kernel,
        out_shape=(
            jax.ShapeDtypeStruct((count, rows), f32),
            jax.ShapeDtypeStruct((sections * block, rows), f32),
        ),
        in_specs=[scalars, scalars] + [full] * 9,
        out_specs=(full,) * 2,
        scratch_shapes=[
            pltpu.VMEM((sections * rows, block), f32),
            pltpu.VMEM((sections * rows, block), f32),
            pltpu.VMEM((sections * rows, block), f32),
            pltpu.VMEM(square, f32),
            pltpu.VMEM(square, f32),
            pltpu.VMEM(square, f32),
        ],
        compiler_params=params,
        name="gradients",
    )(inverse, high, grad_cols, grad_other, x_other, tokens, xs, near, bfar, inv_far, inv)
    outs = [unpack(keep, got) for (_, keep), got in zip(outs, gots)]
    for n in range(2, bits - 1):
        gots = [exchange(send, order_[n]) for (send, _), order_ in zip(outs, stages)]
        merge = pack if n == bits - 2 else stage
        outs = [merge(keep, got) for (_, keep), got in zip(outs, gots)]
    lasts = [exchange(send, bits - 1).astype(f32) for send, _ in outs]
    lasts[-1] = after(lasts[-1], grad_tokens, grad_gens)
    outputs = pl.pallas_call(
        last_kernel,
        out_shape=jax.ShapeDtypeStruct((count, cotangent.shape[1]), f32),
        in_specs=[full] * (2 * CHUNKS),
        out_specs=full,
        compiler_params=params,
        name="last_sums",
    )(*[keep for _, keep in outs], *lasts)
    return outputs, grad_tokens, jnp.swapaxes(grad_gens.reshape(sections, block, rows), 1, 2)


def solution(mesh):
    placed = (
        P("groups", "tensor"),
        P("tensor", None),
        P("groups", "tensor", None),
        P(),
        P("groups", "tensor"),
    )
    return jax.shard_map(
        local,
        mesh=mesh,
        in_specs=placed,
        out_specs=(P("groups", "tensor"), P("groups", "tensor"), P("groups", "tensor", None)),
        check_vma=False,
    )
```

```python
import functools

import jax
import jax.numpy as jnp
import numpy as np
from jax import lax
from jax.experimental import pallas as pl
from jax.experimental.pallas import tpu as pltpu
from jax.sharding import PartitionSpec as P

VMEM_LIMIT = 16 * 2**20
WIDE_LIMIT = 50 * 2**20
GROUP = 128
NN = (((1,), (0,)), ((), ()))
NT = (((1,), (1,)), ((), ()))
TN = (((0,), (0,)), ((), ()))
CHUNKS = 2


def exchange(array, bit):
    size = lax.axis_size("tensor")
    return lax.ppermute(array, "tensor", [(i, i ^ (1 << bit)) for i in range(size)])


def parts_of(x):
    first = x.astype(jnp.bfloat16)
    return first, (x - first.astype(jnp.float32)).astype(jnp.bfloat16)


def one_dot(a, b, dims=NN):
    return lax.dot_general(a, b, dims, preferred_element_type=jnp.float32)


def after(value, *earlier):
    return lax.optimization_barrier((value, *earlier))[0]


def dot(a, b, dims=NN):
    a_first, a_rest = parts_of(a)
    b_first, b_rest = parts_of(b)
    return (
        one_dot(a_first, b_first, dims) + one_dot(a_rest, b_first, dims) + one_dot(a_first, b_rest, dims)
    )


def pick(a, chooser):
    first, rest = parts_of(a)
    return one_dot(first, chooser) + one_dot(rest, chooser)


def iota(shape, dim):
    return lax.broadcasted_iota(jnp.int32, shape, dim)


def split_halves(rows_ref, lo_ref, hi_ref, section, rows, half):
    step = half << (section - 1)
    base = section * rows
    for start in range(base, base + rows, 2 * step):
        low = rows_ref[start : start + step, :]
        high = rows_ref[start + step : start + 2 * step, :]
        lo_ref[start : start + step, :] = low
        lo_ref[start + step : start + 2 * step, :] = low
        hi_ref[start : start + step, :] = high
        hi_ref[start + step : start + 2 * step, :] = high


def to_lanes(lo_ref, hi_ref, out_ref, lanes, half, block):
    for a in range(half):
        out_ref[a * block : (a + 1) * block, :] = lo_ref[pl.ds(a, lanes, stride=half), :].T
        out_ref[(half + a) * block : (half + a + 1) * block, :] = hi_ref[
            pl.ds(a, lanes, stride=half), :
        ].T


def by_section(parts, section_of):
    out = parts[-1]
    for k in range(len(parts) - 2, -1, -1):
        out = jnp.where(section_of == k, parts[k], out)
    return out


def lane_facts(shape, per_section, high):
    lane = iota(shape, 1)
    section_of = lane // per_section
    part = lane % per_section
    upper = jnp.bitwise_and(jnp.right_shift(part, jnp.maximum(section_of - 1, 0)), 1)
    return section_of, jnp.where(section_of == 0, high, upper) == 1


def block_masks(section, half):
    row = iota((GROUP, GROUP), 0) // half
    col = iota((GROUP, GROUP), 1) // half
    bit = 1 << (section - 1)
    return col == jnp.bitwise_and(row, ~bit), col == jnp.bitwise_or(row, bit)


def same_mask(half):
    return iota((GROUP, GROUP), 0) // half == iota((GROUP, GROUP), 1) // half


def spreader(offsets, block, half):
    row, col = iota((block, GROUP), 0), iota((block, GROUP), 1) % half
    return jnp.concatenate([(row == at + col).astype(jnp.bfloat16) for at in offsets], axis=1)


def gatherer(offset, block, half):
    row, col = iota((GROUP, block), 0) % half, iota((GROUP, block), 1)
    return (col == offset + row).astype(jnp.bfloat16)


def transpose_to(out_ref, in_ref, block, change=lambda j, t: t):
    for j in range(block):
        out_ref[j * block : (j + 1) * block, :] = change(j, in_ref[pl.ds(j, block, stride=block), :])


def permuted_row(orders_ref, in_ref, i, section_of):
    sections, block = orders_ref.shape
    return by_section(
        [
            in_ref[pl.ds(pl.multiple_of(orders_ref[k, i] * block, block), block), :]
            for k in range(sections)
        ],
        section_of,
    )


def permute_rows(orders_ref, in_ref, out_ref, section_of):
    block = orders_ref.shape[1]
    for i in range(block):
        out_ref[i * block : (i + 1) * block, :] = permuted_row(orders_ref, in_ref, i, section_of)


def invert_blocks(orders_ref, lo_ref, hi_ref, inv_ref, a_ref, b_ref, section_of):
    sections, block = orders_ref.shape
    half = block // 2
    lanes = inv_ref.shape[1]
    to_lanes(lo_ref, hi_ref, a_ref, lanes, half, block)

    transpose_to(b_ref, a_ref, block, lambda j, t: a_ref[j * block : (j + 1) * block, :] - t)
    permute_rows(orders_ref, b_ref, a_ref, section_of)
    transpose_to(b_ref, a_ref, block)
    permute_rows(orders_ref, b_ref, inv_ref, section_of)
    sub = iota((block, lanes), 0)
    for j in range(block):
        inv_ref[j * block : (j + 1) * block, :] += (sub == j).astype(jnp.float32)

    def eliminate(k, _):
        at = pl.multiple_of(k * block, block)
        here = sub == k
        inverse = 1.0 / inv_ref[pl.ds(at + k, 1), :]
        factors = inv_ref[pl.ds(k, block, stride=block), :]
        pivot = jnp.where(here, inverse, inv_ref[pl.ds(at, block), :] * inverse)
        for i in range(block):
            row = inv_ref[i * block : (i + 1) * block, :]
            inv_ref[i * block : (i + 1) * block, :] = (
                jnp.where(here, 0.0, row) - factors[i : i + 1, :] * pivot
            )
        inv_ref[pl.ds(at, block), :] = pivot
        return 0

    lax.fori_loop(0, block, eliminate, 0)


def own_rows(inv_ref, out_ref, half, block, upper):
    lanes = inv_ref.shape[1]
    sub = iota((block, lanes), 0)
    for a in range(half):
        low = 2.0 * inv_ref[a * block : (a + 1) * block, :] - (sub == a).astype(jnp.float32)
        top = 2.0 * inv_ref[(half + a) * block : (half + a + 1) * block, :] - (
            sub == half + a
        ).astype(jnp.float32)
        out_ref[pl.ds(a, lanes, stride=half), :] = jnp.where(upper, top, low).T


def own_cols(inv_ref, out_ref, half, block, upper):
    lanes = inv_ref.shape[1]
    sub = iota((block, lanes), 0)
    for a in range(half):
        low = 2.0 * inv_ref[pl.ds(a, block, stride=block), :] - (sub == a).astype(jnp.float32)
        top = 2.0 * inv_ref[pl.ds(half + a, block, stride=block), :] - (sub == half + a).astype(
            jnp.float32
        )
        out_ref[pl.ds(a, lanes, stride=half), :] = jnp.where(upper, top, low).T


def near_kernel(
    orders_ref, gen_ref, tok_ref, inv_ref, near_ref, xs_ref,
    lo_ref, hi_ref, a_ref, b_ref, row_ref,
):
    sections, block = orders_ref.shape
    half = block // 2
    rows = tok_ref.shape[1]
    lanes = sections * rows // half
    for k in range(sections):
        row_ref[k * rows : (k + 1) * rows, :] = gen_ref[k * block : (k + 1) * block, :].T
    lo_ref[0:rows, :] = row_ref[0:rows, :]
    hi_ref[0:rows, :] = row_ref[0:rows, :]
    for k in range(1, sections):
        split_halves(row_ref, lo_ref, hi_ref, k, rows, half)
    section_of, upper = lane_facts((block, lanes), rows // half, 0)
    invert_blocks(orders_ref, lo_ref, hi_ref, inv_ref, a_ref, b_ref, section_of)
    own_rows(inv_ref, row_ref, half, block, upper)
    spread = spreader((0, half), block, half)
    for k in range(1, sections):
        lo_mask, hi_mask = block_masks(k, half)
        wide = pick(row_ref[k * rows : (k + 1) * rows, :], spread)
        for start in range(0, rows, GROUP):
            part = wide[start : start + GROUP]
            near_ref[k - 1, start : start + GROUP, :] = jnp.where(
                lo_mask, part[:, :GROUP], jnp.where(hi_mask, part[:, GROUP:], 0.0)
            )
    for start in range(0, rows, GROUP):
        stop = start + GROUP
        value = tok_ref[:, start:stop].astype(jnp.float32)
        for k in range(sections - 1, 0, -1):
            value = dot(value, near_ref[k - 1, start:stop, :])
            xs_ref[k - 1, :, start:stop] = value


def far_rotations_kernel(
    orders_ref, high_ref, own_ref, far_ref, inv_ref, ffar_ref, bfar_ref,
    lo_ref, hi_ref, a_ref, b_ref, row_ref, col_ref,
):
    block = orders_ref.shape[1]
    half = block // 2
    rows = far_ref.shape[1]
    high = high_ref[0]
    own = own_ref[...].T
    other = far_ref[...].T
    lo_ref[...] = jnp.where(high == 1, other, own)
    hi_ref[...] = jnp.where(high == 1, own, other)
    invert_blocks(orders_ref, lo_ref, hi_ref, inv_ref, a_ref, b_ref, None)
    upper = high == 1
    own_rows(inv_ref, row_ref, half, block, upper)
    own_cols(inv_ref, col_ref, half, block, upper)
    spread = spreader((half * high, half * (1 - high)), block, half)
    same = same_mask(half)
    for source, target in ((col_ref, ffar_ref), (row_ref, bfar_ref)):
        wide = pick(source[...], spread)
        for start in range(0, rows, GROUP):
            part = wide[start : start + GROUP]
            target[0, start : start + GROUP, :] = jnp.where(same, part[:, :GROUP], 0.0)
            target[1, start : start + GROUP, :] = jnp.where(same, part[:, GROUP:], 0.0)


def write_packed(packed_ref, value):
    count, width = value.shape
    peak = jnp.max(jnp.abs(value), axis=(0, 1), keepdims=True)
    exponent = jnp.ceil(jnp.log2(jnp.maximum(peak, 1e-30))) - 15.0
    packed_ref[0:count, :] = value * jnp.exp2(-exponent)
    packed_ref[count:, :] = jnp.broadcast_to(exponent, (16, width))


def read_packed(packed_ref, start, stop):
    count = packed_ref.shape[0] - 16
    return packed_ref[0:count, start:stop] * jnp.exp2(packed_ref[count : count + 1, 0:1])


def exchange_packed(packed, bit):
    return exchange(packed.astype(jnp.float16), bit).astype(jnp.float32)


def beside(a, b):
    return jnp.concatenate([a, b], axis=1)


def far_kernel(own_ref, oth_ref, far_ref, out_ref):
    count, rows = own_ref.shape[1:]
    for start in range(0, rows, GROUP):
        stop = start + GROUP
        value = dot(
            beside(own_ref[0, :, start:stop], oth_ref[:, start:stop]),
            beside(far_ref[0, start:stop, :], far_ref[1, start:stop, :]),
            NT,
        )
        first = value.astype(jnp.bfloat16)
        out_ref[0:count, start:stop] = first
        out_ref[count : 2 * count, start:stop] = (value - first.astype(jnp.float32)).astype(
            jnp.bfloat16
        )


def project_kernel(slots, places_ref, x_ref, w_ref, *refs):
    *out_refs, held_ref, made_ref, sems, out_sems = refs
    pieces, count, width = made_ref.shape
    half = pieces // 2
    part = width // CHUNKS

    def fetch(p):
        at = pl.multiple_of(places_ref[p] * width, width)
        return pltpu.make_async_copy(w_ref.at[:, pl.ds(at, width)], held_ref.at[p], sems.at[p])

    def leave(p, chunk):
        return pltpu.make_async_copy(
            made_ref.at[p, :, pl.ds(chunk * part, part)],
            out_refs[2 * chunk + p // half].at[slots[chunk][p]],
            out_sems.at[chunk, p],
        )

    for p in range(pieces):
        fetch(p).start()
    for p in range(pieces):
        fetch(p).wait()
        both = one_dot(x_ref[...], held_ref[p])
        made_ref[p] = both[:count] + both[count:]
        for chunk in range(CHUNKS):
            leave(p, chunk).start()
    for p in range(pieces):
        for chunk in range(CHUNKS):
            leave(p, chunk).wait()


def project(x_both, weight, places, slots):
    pieces = places.shape[0]
    count2, rows = x_both.shape
    count = count2 // 2
    width = weight.shape[1] // lax.axis_size("tensor")
    outs = pl.pallas_call(
        functools.partial(project_kernel, slots),
        out_shape=(jax.ShapeDtypeStruct((pieces // 2, count, width // CHUNKS), jnp.float32),)
        * (2 * CHUNKS),
        in_specs=[
            pl.BlockSpec(memory_space=pltpu.SMEM),
            pl.BlockSpec(memory_space=pltpu.VMEM),
            pl.BlockSpec(memory_space=pl.ANY),
        ],
        out_specs=(pl.BlockSpec(memory_space=pl.ANY),) * (2 * CHUNKS),
        scratch_shapes=[
            pltpu.VMEM((pieces, rows, width), weight.dtype),
            pltpu.VMEM((pieces, count, width), jnp.float32),
            pltpu.SemaphoreType.DMA((pieces,)),
            pltpu.SemaphoreType.DMA((CHUNKS, pieces)),
        ],
        compiler_params=pltpu.CompilerParams(vmem_limit_bytes=WIDE_LIMIT),
        cost_estimate=pl.CostEstimate(
            flops=2 * count2 * rows * width * pieces,
            bytes_accessed=pieces * width * (2 * rows + 4 * count),
            transcendentals=0,
        ),
        name="project",
    )(places, x_both, weight)
    return [outs[2 * chunk : 2 * chunk + 2] for chunk in range(CHUNKS)]


def back_kernel(order, places_ref, low_ref, high_ref, w_ref, out_ref, packed_ref, cots_ref, held_ref, cot_sems, sems):
    half, _, width = low_ref.shape

    def fetches(slot):
        at = pl.multiple_of(places_ref[order[slot]] * width, width)
        here = pl.ds(slot * width, width)
        cot = (low_ref if slot < half else high_ref).at[slot % half]
        return (
            pltpu.make_async_copy(cot, cots_ref.at[:, here], cot_sems.at[slot]),
            pltpu.make_async_copy(w_ref.at[:, pl.ds(at, width)], held_ref.at[:, here], sems.at[slot]),
        )

    for slot in range(2 * half):
        for copy in fetches(slot):
            copy.start()
    for slot in range(2 * half):
        for copy in fetches(slot):
            copy.wait()
        here = slice(slot * width, (slot + 1) * width)
        product = one_dot(cots_ref[:, here], held_ref[:, here], NT)
        if slot == 0:
            out_ref[...] = product
        else:
            out_ref[...] += product
    write_packed(packed_ref, out_ref[...])


def project_back(places, gathered, order, weight):
    half, count, width = gathered[0].shape
    steps = half * len(gathered)
    rows = weight.shape[0]
    return pl.pallas_call(
        functools.partial(back_kernel, order),
        out_shape=(
            jax.ShapeDtypeStruct((count, rows), jnp.float32),
            jax.ShapeDtypeStruct((count + 16, rows), jnp.float32),
        ),
        in_specs=[pl.BlockSpec(memory_space=pltpu.SMEM)]
        + [pl.BlockSpec(memory_space=pl.ANY)] * (len(gathered) + 1),
        out_specs=(pl.BlockSpec(memory_space=pltpu.VMEM),) * 2,
        scratch_shapes=[
            pltpu.VMEM((count, steps * width), weight.dtype),
            pltpu.VMEM((rows, steps * width), weight.dtype),
            pltpu.SemaphoreType.DMA((steps,)),
            pltpu.SemaphoreType.DMA((steps,)),
        ],
        compiler_params=pltpu.CompilerParams(vmem_limit_bytes=WIDE_LIMIT),
        cost_estimate=pl.CostEstimate(
            flops=2 * count * rows * width * steps,
            bytes_accessed=steps * width * 2 * (rows + count),
            transcendentals=0,
        ),
        name="project_back",
    )(places, *gathered, weight)


def grow(array, bit):
    return jnp.concatenate([array, exchange(array, bit)], axis=0)


def gather_order(stages):
    order = [0]
    for bit in stages:
        order = order + [n ^ (1 << bit) for n in order]
    return tuple(order)


def lane_matmul(left_ref, right_ref, out_ref, block, lanes):
    step = 4

    def body(t, _):
        first = t * step
        totals = [jnp.zeros((block, lanes), jnp.float32) for _ in range(step)]
        for j in range(block):
            right = right_ref[j * block : (j + 1) * block, :]
            for s in range(step):
                totals[s] += left_ref[pl.ds((first + s) * block + j, 1), :] * right
        for s in range(step):
            out_ref[pl.ds(pl.multiple_of((first + s) * block, block), block), :] = totals[s]
        return 0

    lax.fori_loop(0, block // step, body, 0)


def grads_kernel(
    inverse_ref, high_ref, own_ref, oth_ref, x_oth_ref, tok_ref, xs_ref, near_ref, bfar_ref, inv_far_ref, inv_ref,
    gtok_ref, ggen_ref,
    row_ref, lo_ref, hi_ref, a_ref, b_ref, c_ref,
):
    sections, block = inverse_ref.shape
    half = block // 2
    count, rows = own_ref.shape
    per_section = rows // half
    lanes = sections * per_section
    high = high_ref[0]
    chooser = jnp.concatenate([gatherer(0, block, half), gatherer(half, block, half)], axis=0)
    far_chooser = jnp.concatenate(
        [gatherer(half * high, block, half), gatherer(half * (1 - high), block, half)], axis=0
    )
    same = same_mask(half)
    same = jnp.concatenate([beside(same, same)] * 2, axis=0)
    for start in range(0, rows, GROUP):
        stop = start + GROUP
        x_pair = beside(xs_ref[0, :, start:stop], x_oth_ref[:, start:stop])
        g_pair = beside(own_ref[:, start:stop], read_packed(oth_ref, start, stop))
        both = pick(jnp.where(same, dot(x_pair, g_pair, TN), 0.0), far_chooser)
        mine, theirs = both[:GROUP], both[GROUP:]
        lo_ref[start:stop, :] = jnp.where(high == 1, theirs, mine)
        hi_ref[start:stop, :] = jnp.where(high == 1, mine, theirs)
        grad = dot(g_pair, beside(bfar_ref[0, start:stop, :], bfar_ref[1, start:stop, :]), NT)
        for k in range(1, sections):
            lo_mask, hi_mask = block_masks(k, half)
            if k < sections - 1:
                x = xs_ref[k, :, start:stop]
            else:
                x = tok_ref[:, start:stop].astype(jnp.float32)
            outer = dot(x, grad, TN)
            row_ref[k * rows + start : k * rows + stop, :] = pick(
                beside(jnp.where(lo_mask, outer, 0.0), jnp.where(hi_mask, outer, 0.0)), chooser
            )
            grad = dot(grad, near_ref[k - 1, start:stop, :], NT)
        gtok_ref[:, start:stop] = grad
    for k in range(1, sections):
        split_halves(row_ref, lo_ref, hi_ref, k, rows, half)
    to_lanes(lo_ref, hi_ref, a_ref, lanes, half, block)
    for j in range(block):
        b_ref[j * block : (j + 1) * block, :] = inv_ref[pl.ds(j, block, stride=block), :]
        b_ref[j * block : (j + 1) * block, 0:per_section] = inv_far_ref[
            pl.ds(j, block, stride=block), :
        ]
    lane_matmul(a_ref, b_ref, c_ref, block, lanes)
    lane_matmul(b_ref, c_ref, a_ref, block, lanes)
    section_of, upper = lane_facts((block, lanes), per_section, high)
    transpose_to(c_ref, a_ref, block, lambda j, t: 2.0 * (t - a_ref[j * block : (j + 1) * block, :]))
    permute_rows(inverse_ref, c_ref, b_ref, section_of)
    transpose_to(a_ref, b_ref, block)
    for a in range(half):
        low = permuted_row(inverse_ref, a_ref, a, section_of)
        top = permuted_row(inverse_ref, a_ref, half + a, section_of)
        row_ref[pl.ds(a, lanes, stride=half), :] = jnp.where(upper, top, low).T
    for k in range(sections):
        ggen_ref[k * block : (k + 1) * block, :] = row_ref[k * rows : (k + 1) * rows, :].T


def pack_kernel(keep_ref, got_ref, packed_ref, out_ref):
    half, count, width = out_ref.shape
    largest = jnp.zeros((count, width), jnp.float32)
    for p in range(half):
        total = keep_ref[half + p] + got_ref[half + p]
        packed_ref[p * count : (p + 1) * count, :] = total
        largest = jnp.maximum(largest, jnp.abs(total))
        out_ref[p] = keep_ref[p] + got_ref[p]
    peak = jnp.max(largest, axis=(0, 1), keepdims=True)
    exponent = jnp.ceil(jnp.log2(jnp.maximum(peak, 1e-30))) - 15.0
    scale = jnp.exp2(-exponent)
    for p in range(half):
        packed_ref[p * count : (p + 1) * count, :] *= scale
    packed_ref[half * count :, :] = jnp.broadcast_to(exponent, (16, width))


def unpack_kernel(keep_ref, got_ref, send_ref, out_ref):
    half, count, width = out_ref.shape
    scale = jnp.exp2(got_ref[2 * half * count : 2 * half * count + 1, 0:1])
    for p in range(half):
        low, top = p * count, (half + p) * count
        out_ref[p] = keep_ref[p] + got_ref[low : low + count, :] * scale
        send_ref[p] = keep_ref[half + p] + got_ref[top : top + count, :] * scale


def last_kernel(*refs):
    *in_refs, out_ref = refs
    chunks = len(in_refs) // 2
    width = in_refs[0].shape[2]
    for chunk in range(chunks):
        out_ref[:, chunk * width : (chunk + 1) * width] = in_refs[chunk][0] + read_packed(
            in_refs[chunks + chunk], 0, width
        )


def summed(kernel, name, keep, got, first):
    pieces, count, width = keep.shape
    full = pl.BlockSpec(memory_space=pltpu.VMEM)
    return pl.pallas_call(
        kernel,
        out_shape=(first, jax.ShapeDtypeStruct((pieces // 2, count, width), jnp.float32)),
        in_specs=[full] * 2,
        out_specs=(full,) * 2,
        compiler_params=pltpu.CompilerParams(vmem_limit_bytes=VMEM_LIMIT),
        name=name,
    )(keep, got)


def pack(keep, got):
    pieces, count, width = keep.shape
    first = jax.ShapeDtypeStruct((pieces // 2 * count + 16, width), jnp.float32)
    packed, keep = summed(pack_kernel, "sum_pack", keep, got, first)
    return packed.astype(jnp.float16), keep


def unpack(keep, got):
    pieces, count, width = keep.shape
    first = jax.ShapeDtypeStruct((pieces // 2, count, width), jnp.float32)
    return summed(unpack_kernel, "sum_unpack", keep, got.astype(jnp.float32), first)


def local(tokens, weight, generators, orders, cotangent):
    sections, rows, block = generators.shape
    half = block // 2
    count = tokens.shape[0]
    size = lax.axis_size("tensor")
    bits = size.bit_length() - 1
    here = lax.axis_index("tensor")
    pair_bit = bits - 1
    high = jnp.bitwise_and(jnp.right_shift(here, pair_bit), 1).astype(jnp.int32).reshape(1)
    lanes = sections * (rows // half)
    f32 = jnp.float32
    full = pl.BlockSpec(memory_space=pltpu.VMEM)
    scalars = pl.BlockSpec(memory_space=pltpu.SMEM)
    params = pltpu.CompilerParams(vmem_limit_bytes=VMEM_LIMIT)

    stored = jnp.swapaxes(generators, 1, 2)
    far_gen = exchange(stored[0], pair_bit)
    order = list(range(bits - 1, -1, -1))
    pieces = cotangent[None]
    for bit in order[:-4]:
        pieces = grow(pieces, bit)
    firsts = [exchange(pieces, bit) for bit in order[-4:-1]]
    flat = stored.reshape(sections * block, rows)
    square = (block * block, lanes)
    far_square = (block * block, lanes // sections)
    inv, near, xs = pl.pallas_call(
        near_kernel,
        out_shape=(
            jax.ShapeDtypeStruct(square, f32),
            jax.ShapeDtypeStruct((sections - 1, rows, GROUP), f32),
            jax.ShapeDtypeStruct((sections - 1, count, rows), f32),
        ),
        in_specs=[scalars, full, full],
        out_specs=(full,) * 3,
        scratch_shapes=[
            pltpu.VMEM((sections * rows, block), f32),
            pltpu.VMEM((sections * rows, block), f32),
            pltpu.VMEM(square, f32),
            pltpu.VMEM(square, f32),
            pltpu.VMEM((sections * rows, block), f32),
        ],
        compiler_params=params,
        name="near_rotations",
    )(orders, flat, tokens)
    by_far, by_mid, by_side = [after(first, xs) for first in firsts]
    far_gen = after(far_gen, xs, by_side)
    x_other = exchange(xs[0], pair_bit)
    inv_far, ffar, bfar = pl.pallas_call(
        far_rotations_kernel,
        out_shape=(
            jax.ShapeDtypeStruct(far_square, f32),
            jax.ShapeDtypeStruct((2, rows, GROUP), f32),
            jax.ShapeDtypeStruct((2, rows, GROUP), f32),
        ),
        in_specs=[scalars, scalars, full, full],
        out_specs=(full,) * 3,
        scratch_shapes=[
            pltpu.VMEM((rows, block), f32),
            pltpu.VMEM((rows, block), f32),
            pltpu.VMEM(far_square, f32),
            pltpu.VMEM(far_square, f32),
            pltpu.VMEM((rows, block), f32),
            pltpu.VMEM((rows, block), f32),
        ],
        compiler_params=params,
        cost_estimate=pl.CostEstimate(flops=10**7, bytes_accessed=10**7, transcendentals=0),
        name="far_rotations",
    )(orders[:1], high, stored[0], far_gen)
    by_far, by_mid = after(by_far, ffar), after(by_mid, ffar)
    by_both = exchange(by_far, order[-3])
    side_pair = exchange(jnp.concatenate([by_far, by_mid], axis=0), order[-2])
    side_last = exchange(by_both, order[-2])
    x_both = pl.pallas_call(
        far_kernel,
        out_shape=jax.ShapeDtypeStruct((2 * count, rows), jnp.bfloat16),
        in_specs=[full] * 3,
        out_specs=full,
        compiler_params=params,
        name="far_apply",
    )(xs, x_other, ffar)

    stages = [tuple(range(bits)), (0, 2, 1) + tuple(range(3, bits))]

    def slot_of(offset, bits_in_order):
        return sum(((offset >> bit) & 1) << (bits - 1 - n) for n, bit in enumerate(bits_in_order))

    offsets = sorted(range(size), key=lambda o: (1 - (o & 1), slot_of(o, stages[0])))
    slots = [[slot_of(o, bits_in_order) % (size // 2) for o in offsets] for bits_in_order in stages]
    fixed = here.astype(jnp.int32)
    places = jnp.bitwise_xor(fixed, jnp.asarray(np.array(offsets, np.int32)))
    back_places = jnp.bitwise_xor(fixed, jnp.arange(size, dtype=jnp.int32))
    outs = project(x_both, weight, places, slots)

    def stage(keep, got):
        mid = keep.shape[0] // 2
        return keep[mid:] + got[mid:], keep[:mid] + got[:mid]

    outs = [pack(keep, exchange(after(send, by_both, side_pair), 0)) for send, keep in outs]
    gots = [exchange(send, order_[1]) for (send, _), order_ in zip(outs, stages)]
    side_last = after(side_last, *[send for send, _ in outs])
    pieces = jnp.concatenate(
        [pieces, by_far, by_mid, by_both, by_side, side_pair, side_last], axis=0
    )
    gathered = [pieces, exchange(pieces, 0)]
    numbers = jnp.arange(block, dtype=jnp.int32)
    inverse = jnp.sum(
        jnp.where(orders[:, :, None] == numbers[None, None, :], numbers[None, :, None], 0), axis=1
    ).astype(jnp.int32)
    grad_cols, grad_packed = project_back(back_places, gathered, gather_order(order), weight)
    grad_other = exchange_packed(grad_packed, pair_bit)
    gots[0] = after(gots[0], grad_cols)
    gots[-1] = after(gots[-1], grad_cols)
    grad_tokens, grad_gens = pl.pallas_call(
        grads_kernel,
        out_shape=(
            jax.ShapeDtypeStruct((count, rows), f32),
            jax.ShapeDtypeStruct((sections * block, rows), f32),
        ),
        in_specs=[scalars, scalars] + [full] * 9,
        out_specs=(full,) * 2,
        scratch_shapes=[
            pltpu.VMEM((sections * rows, block), f32),
            pltpu.VMEM((sections * rows, block), f32),
            pltpu.VMEM((sections * rows, block), f32),
            pltpu.VMEM(square, f32),
            pltpu.VMEM(square, f32),
            pltpu.VMEM(square, f32),
        ],
        compiler_params=params,
        name="gradients",
    )(inverse, high, grad_cols, grad_other, x_other, tokens, xs, near, bfar, inv_far, inv)
    outs = [unpack(keep, got) for (_, keep), got in zip(outs, gots)]
    for n in range(2, bits - 1):
        gots = [exchange(send, order_[n]) for (send, _), order_ in zip(outs, stages)]
        merge = pack if n == bits - 2 else stage
        outs = [merge(keep, got) for (_, keep), got in zip(outs, gots)]
    lasts = [exchange(send, bits - 1).astype(f32) for send, _ in outs]
    lasts[-1] = after(lasts[-1], grad_tokens, grad_gens)
    outputs = pl.pallas_call(
        last_kernel,
        out_shape=jax.ShapeDtypeStruct((count, cotangent.shape[1]), f32),
        in_specs=[full] * (2 * CHUNKS),
        out_specs=full,
        compiler_params=params,
        name="last_sums",
    )(*[keep for _, keep in outs], *lasts)
    return outputs, grad_tokens, jnp.swapaxes(grad_gens.reshape(sections, block, rows), 1, 2)


def solution(mesh):
    placed = (
        P("groups", "tensor"),
        P("tensor", None),
        P("groups", "tensor", None),
        P(),
        P("groups", "tensor"),
    )
    return jax.shard_map(
        local,
        mesh=mesh,
        in_specs=placed,
        out_specs=(P("groups", "tensor"), P("groups", "tensor"), P("groups", "tensor", None)),
        check_vma=False,
    )
```

```python
import functools

import jax
import jax.numpy as jnp
import numpy as np
from jax import lax
from jax.experimental import pallas as pl
from jax.experimental.pallas import tpu as pltpu
from jax.sharding import PartitionSpec as P

VMEM_LIMIT = 16 * 2**20
WIDE_LIMIT = 46 * 2**20
GROUP = 128
NN = (((1,), (0,)), ((), ()))
NT = (((1,), (1,)), ((), ()))
TN = (((0,), (0,)), ((), ()))
CHUNKS = 2


def exchange(array, bit):
    size = lax.axis_size("tensor")
    return lax.ppermute(array, "tensor", [(i, i ^ (1 << bit)) for i in range(size)])


def parts_of(x):
    first = x.astype(jnp.bfloat16)
    return first, (x - first.astype(jnp.float32)).astype(jnp.bfloat16)


def one_dot(a, b, dims=NN):
    return lax.dot_general(a, b, dims, preferred_element_type=jnp.float32)


def after(value, *earlier):
    return lax.optimization_barrier((value, *earlier))[0]


def dot(a, b, dims=NN):
    a_first, a_rest = parts_of(a)
    b_first, b_rest = parts_of(b)
    return (
        one_dot(a_first, b_first, dims) + one_dot(a_rest, b_first, dims) + one_dot(a_first, b_rest, dims)
    )


def pick(a, chooser):
    first, rest = parts_of(a)
    return one_dot(first, chooser) + one_dot(rest, chooser)


def iota(shape, dim):
    return lax.broadcasted_iota(jnp.int32, shape, dim)


def split_halves(rows_ref, lo_ref, hi_ref, section, rows, half):
    step = half << (section - 1)
    base = section * rows
    for start in range(base, base + rows, 2 * step):
        low = rows_ref[start : start + step, :]
        high = rows_ref[start + step : start + 2 * step, :]
        lo_ref[start : start + step, :] = low
        lo_ref[start + step : start + 2 * step, :] = low
        hi_ref[start : start + step, :] = high
        hi_ref[start + step : start + 2 * step, :] = high


def to_lanes(lo_ref, hi_ref, out_ref, lanes, half, block):
    for a in range(half):
        out_ref[a * block : (a + 1) * block, :] = lo_ref[pl.ds(a, lanes, stride=half), :].T
        out_ref[(half + a) * block : (half + a + 1) * block, :] = hi_ref[
            pl.ds(a, lanes, stride=half), :
        ].T


def by_section(parts, section_of):
    out = parts[-1]
    for k in range(len(parts) - 2, -1, -1):
        out = jnp.where(section_of == k, parts[k], out)
    return out


def lane_facts(shape, per_section, high):
    lane = iota(shape, 1)
    section_of = lane // per_section
    part = lane % per_section
    upper = jnp.bitwise_and(jnp.right_shift(part, jnp.maximum(section_of - 1, 0)), 1)
    return section_of, jnp.where(section_of == 0, high, upper) == 1


def block_masks(section, half):
    row = iota((GROUP, GROUP), 0) // half
    col = iota((GROUP, GROUP), 1) // half
    bit = 1 << (section - 1)
    return col == jnp.bitwise_and(row, ~bit), col == jnp.bitwise_or(row, bit)


def same_mask(half):
    return iota((GROUP, GROUP), 0) // half == iota((GROUP, GROUP), 1) // half


def spreader(offsets, block, half):
    row, col = iota((block, GROUP), 0), iota((block, GROUP), 1) % half
    return jnp.concatenate([(row == at + col).astype(jnp.bfloat16) for at in offsets], axis=1)


def gatherer(offset, block, half):
    row, col = iota((GROUP, block), 0) % half, iota((GROUP, block), 1)
    return (col == offset + row).astype(jnp.bfloat16)


def transpose_to(out_ref, in_ref, block, change=lambda j, t: t):
    for j in range(block):
        out_ref[j * block : (j + 1) * block, :] = change(j, in_ref[pl.ds(j, block, stride=block), :])


def permuted_row(orders_ref, in_ref, i, section_of):
    sections, block = orders_ref.shape
    return by_section(
        [
            in_ref[pl.ds(pl.multiple_of(orders_ref[k, i] * block, block), block), :]
            for k in range(sections)
        ],
        section_of,
    )


def permute_rows(orders_ref, in_ref, out_ref, section_of):
    block = orders_ref.shape[1]
    for i in range(block):
        out_ref[i * block : (i + 1) * block, :] = permuted_row(orders_ref, in_ref, i, section_of)


def invert_blocks(orders_ref, lo_ref, hi_ref, inv_ref, a_ref, b_ref, section_of):
    sections, block = orders_ref.shape
    half = block // 2
    lanes = inv_ref.shape[1]
    to_lanes(lo_ref, hi_ref, a_ref, lanes, half, block)

    transpose_to(b_ref, a_ref, block, lambda j, t: a_ref[j * block : (j + 1) * block, :] - t)
    permute_rows(orders_ref, b_ref, a_ref, section_of)
    transpose_to(b_ref, a_ref, block)
    permute_rows(orders_ref, b_ref, inv_ref, section_of)
    sub = iota((block, lanes), 0)
    for j in range(block):
        inv_ref[j * block : (j + 1) * block, :] += (sub == j).astype(jnp.float32)

    def eliminate(k, _):
        at = pl.multiple_of(k * block, block)
        here = sub == k
        inverse = 1.0 / inv_ref[pl.ds(at + k, 1), :]
        factors = inv_ref[pl.ds(k, block, stride=block), :]
        pivot = jnp.where(here, inverse, inv_ref[pl.ds(at, block), :] * inverse)
        for i in range(block):
            row = inv_ref[i * block : (i + 1) * block, :]
            inv_ref[i * block : (i + 1) * block, :] = (
                jnp.where(here, 0.0, row) - factors[i : i + 1, :] * pivot
            )
        inv_ref[pl.ds(at, block), :] = pivot
        return 0

    lax.fori_loop(0, block, eliminate, 0)


def own_rows(inv_ref, out_ref, half, block, upper):
    lanes = inv_ref.shape[1]
    sub = iota((block, lanes), 0)
    for a in range(half):
        low = 2.0 * inv_ref[a * block : (a + 1) * block, :] - (sub == a).astype(jnp.float32)
        top = 2.0 * inv_ref[(half + a) * block : (half + a + 1) * block, :] - (
            sub == half + a
        ).astype(jnp.float32)
        out_ref[pl.ds(a, lanes, stride=half), :] = jnp.where(upper, top, low).T


def own_cols(inv_ref, out_ref, half, block, upper):
    lanes = inv_ref.shape[1]
    sub = iota((block, lanes), 0)
    for a in range(half):
        low = 2.0 * inv_ref[pl.ds(a, block, stride=block), :] - (sub == a).astype(jnp.float32)
        top = 2.0 * inv_ref[pl.ds(half + a, block, stride=block), :] - (sub == half + a).astype(
            jnp.float32
        )
        out_ref[pl.ds(a, lanes, stride=half), :] = jnp.where(upper, top, low).T


def near_kernel(
    orders_ref, gen_ref, tok_ref, inv_ref, near_ref, xs_ref,
    lo_ref, hi_ref, a_ref, b_ref, row_ref,
):
    sections, block = orders_ref.shape
    half = block // 2
    rows = tok_ref.shape[1]
    lanes = sections * rows // half
    for k in range(sections):
        row_ref[k * rows : (k + 1) * rows, :] = gen_ref[k * block : (k + 1) * block, :].T
    lo_ref[0:rows, :] = row_ref[0:rows, :]
    hi_ref[0:rows, :] = row_ref[0:rows, :]
    for k in range(1, sections):
        split_halves(row_ref, lo_ref, hi_ref, k, rows, half)
    section_of, upper = lane_facts((block, lanes), rows // half, 0)
    invert_blocks(orders_ref, lo_ref, hi_ref, inv_ref, a_ref, b_ref, section_of)
    own_rows(inv_ref, row_ref, half, block, upper)
    spread = spreader((0, half), block, half)
    for k in range(1, sections):
        lo_mask, hi_mask = block_masks(k, half)
        wide = pick(row_ref[k * rows : (k + 1) * rows, :], spread)
        for start in range(0, rows, GROUP):
            part = wide[start : start + GROUP]
            near_ref[k - 1, start : start + GROUP, :] = jnp.where(
                lo_mask, part[:, :GROUP], jnp.where(hi_mask, part[:, GROUP:], 0.0)
            )
    for start in range(0, rows, GROUP):
        stop = start + GROUP
        value = tok_ref[:, start:stop].astype(jnp.float32)
        for k in range(sections - 1, 0, -1):
            value = dot(value, near_ref[k - 1, start:stop, :])
            xs_ref[k - 1, :, start:stop] = value


def far_rotations_kernel(
    orders_ref, high_ref, own_ref, far_ref, inv_ref, ffar_ref, bfar_ref,
    lo_ref, hi_ref, a_ref, b_ref, row_ref, col_ref,
):
    block = orders_ref.shape[1]
    half = block // 2
    rows = far_ref.shape[1]
    high = high_ref[0]
    own = own_ref[...].T
    other = far_ref[...].T
    lo_ref[...] = jnp.where(high == 1, other, own)
    hi_ref[...] = jnp.where(high == 1, own, other)
    invert_blocks(orders_ref, lo_ref, hi_ref, inv_ref, a_ref, b_ref, None)
    upper = high == 1
    own_rows(inv_ref, row_ref, half, block, upper)
    own_cols(inv_ref, col_ref, half, block, upper)
    spread = spreader((half * high, half * (1 - high)), block, half)
    same = same_mask(half)
    for source, target in ((col_ref, ffar_ref), (row_ref, bfar_ref)):
        wide = pick(source[...], spread)
        for start in range(0, rows, GROUP):
            part = wide[start : start + GROUP]
            target[0, start : start + GROUP, :] = jnp.where(same, part[:, :GROUP], 0.0)
            target[1, start : start + GROUP, :] = jnp.where(same, part[:, GROUP:], 0.0)


def write_packed(packed_ref, value):
    count, width = value.shape
    peak = jnp.max(jnp.abs(value), axis=(0, 1), keepdims=True)
    exponent = jnp.ceil(jnp.log2(jnp.maximum(peak, 1e-30))) - 15.0
    packed_ref[0:count, :] = value * jnp.exp2(-exponent)
    packed_ref[count:, :] = jnp.broadcast_to(exponent, (16, width))


def read_packed(packed_ref, start, stop):
    count = packed_ref.shape[0] - 16
    return packed_ref[0:count, start:stop] * jnp.exp2(packed_ref[count : count + 1, 0:1])


def exchange_packed(packed, bit):
    return exchange(packed.astype(jnp.float16), bit).astype(jnp.float32)


def beside(a, b):
    return jnp.concatenate([a, b], axis=1)


def far_kernel(own_ref, oth_ref, far_ref, out_ref):
    count, rows = own_ref.shape[1:]
    for start in range(0, rows, GROUP):
        stop = start + GROUP
        value = dot(
            beside(own_ref[0, :, start:stop], oth_ref[:, start:stop]),
            beside(far_ref[0, start:stop, :], far_ref[1, start:stop, :]),
            NT,
        )
        first = value.astype(jnp.bfloat16)
        out_ref[0:count, start:stop] = first
        out_ref[count : 2 * count, start:stop] = (value - first.astype(jnp.float32)).astype(
            jnp.bfloat16
        )


def project_kernel(slots, places_ref, x_ref, w_ref, *refs):
    *out_refs, held_ref, made_ref, sems, out_sems = refs
    pieces, count, width = made_ref.shape
    half = pieces // 2
    part = width // CHUNKS

    def fetch(p):
        at = pl.multiple_of(places_ref[p] * width, width)
        return pltpu.make_async_copy(w_ref.at[:, pl.ds(at, width)], held_ref.at[p], sems.at[p])

    def leave(p, chunk):
        return pltpu.make_async_copy(
            made_ref.at[p, :, pl.ds(chunk * part, part)],
            out_refs[2 * chunk + p // half].at[slots[chunk][p]],
            out_sems.at[chunk, p],
        )

    for p in range(pieces):
        fetch(p).start()
    for p in range(pieces):
        fetch(p).wait()
        both = one_dot(x_ref[...], held_ref[p])
        made_ref[p] = both[:count] + both[count:]
        for chunk in range(CHUNKS):
            leave(p, chunk).start()
    for p in range(pieces):
        for chunk in range(CHUNKS):
            leave(p, chunk).wait()


def project(x_both, weight, places, slots):
    pieces = places.shape[0]
    count2, rows = x_both.shape
    count = count2 // 2
    width = weight.shape[1] // lax.axis_size("tensor")
    outs = pl.pallas_call(
        functools.partial(project_kernel, slots),
        out_shape=(jax.ShapeDtypeStruct((pieces // 2, count, width // CHUNKS), jnp.float32),)
        * (2 * CHUNKS),
        in_specs=[
            pl.BlockSpec(memory_space=pltpu.SMEM),
            pl.BlockSpec(memory_space=pltpu.VMEM),
            pl.BlockSpec(memory_space=pl.ANY),
        ],
        out_specs=(pl.BlockSpec(memory_space=pl.ANY),) * (2 * CHUNKS),
        scratch_shapes=[
            pltpu.VMEM((pieces, rows, width), weight.dtype),
            pltpu.VMEM((pieces, count, width), jnp.float32),
            pltpu.SemaphoreType.DMA((pieces,)),
            pltpu.SemaphoreType.DMA((CHUNKS, pieces)),
        ],
        compiler_params=pltpu.CompilerParams(vmem_limit_bytes=WIDE_LIMIT),
        cost_estimate=pl.CostEstimate(
            flops=2 * count2 * rows * width * pieces,
            bytes_accessed=pieces * width * (2 * rows + 4 * count),
            transcendentals=0,
        ),
        name="project",
    )(places, x_both, weight)
    return [outs[2 * chunk : 2 * chunk + 2] for chunk in range(CHUNKS)]


def back_kernel(order, places_ref, low_ref, high_ref, w_ref, out_ref, packed_ref, cots_ref, held_ref, cot_sems, sems):
    half, _, width = low_ref.shape

    def fetches(slot):
        at = pl.multiple_of(places_ref[order[slot]] * width, width)
        here = pl.ds(slot * width, width)
        cot = (low_ref if slot < half else high_ref).at[slot % half]
        return (
            pltpu.make_async_copy(cot, cots_ref.at[:, here], cot_sems.at[slot]),
            pltpu.make_async_copy(w_ref.at[:, pl.ds(at, width)], held_ref.at[:, here], sems.at[slot]),
        )

    for slot in range(2 * half):
        for copy in fetches(slot):
            copy.start()
    for slot in range(2 * half):
        for copy in fetches(slot):
            copy.wait()
        here = slice(slot * width, (slot + 1) * width)
        product = one_dot(cots_ref[:, here], held_ref[:, here], NT)
        if slot == 0:
            out_ref[...] = product
        else:
            out_ref[...] += product
    write_packed(packed_ref, out_ref[...])


def project_back(places, gathered, order, weight):
    half, count, width = gathered[0].shape
    steps = half * len(gathered)
    rows = weight.shape[0]
    return pl.pallas_call(
        functools.partial(back_kernel, order),
        out_shape=(
            jax.ShapeDtypeStruct((count, rows), jnp.float32),
            jax.ShapeDtypeStruct((count + 16, rows), jnp.float32),
        ),
        in_specs=[pl.BlockSpec(memory_space=pltpu.SMEM)]
        + [pl.BlockSpec(memory_space=pl.ANY)] * (len(gathered) + 1),
        out_specs=(pl.BlockSpec(memory_space=pltpu.VMEM),) * 2,
        scratch_shapes=[
            pltpu.VMEM((count, steps * width), weight.dtype),
            pltpu.VMEM((rows, steps * width), weight.dtype),
            pltpu.SemaphoreType.DMA((steps,)),
            pltpu.SemaphoreType.DMA((steps,)),
        ],
        compiler_params=pltpu.CompilerParams(vmem_limit_bytes=WIDE_LIMIT),
        cost_estimate=pl.CostEstimate(
            flops=2 * count * rows * width * steps,
            bytes_accessed=steps * width * 2 * (rows + count),
            transcendentals=0,
        ),
        name="project_back",
    )(places, *gathered, weight)


def grow(array, bit):
    return jnp.concatenate([array, exchange(array, bit)], axis=0)


def gather_order(stages):
    order = [0]
    for bit in stages:
        order = order + [n ^ (1 << bit) for n in order]
    return tuple(order)


def lane_matmul(left_ref, right_ref, out_ref, block, lanes):
    step = 4

    def body(t, _):
        first = t * step
        totals = [jnp.zeros((block, lanes), jnp.float32) for _ in range(step)]
        for j in range(block):
            right = right_ref[j * block : (j + 1) * block, :]
            for s in range(step):
                totals[s] += left_ref[pl.ds((first + s) * block + j, 1), :] * right
        for s in range(step):
            out_ref[pl.ds(pl.multiple_of((first + s) * block, block), block), :] = totals[s]
        return 0

    lax.fori_loop(0, block // step, body, 0)


def grads_kernel(
    inverse_ref, high_ref, own_ref, oth_ref, x_oth_ref, tok_ref, xs_ref, near_ref, bfar_ref, inv_far_ref, inv_ref,
    gtok_ref, ggen_ref,
    row_ref, lo_ref, hi_ref, a_ref, b_ref, c_ref,
):
    sections, block = inverse_ref.shape
    half = block // 2
    count, rows = own_ref.shape
    per_section = rows // half
    lanes = sections * per_section
    high = high_ref[0]
    chooser = jnp.concatenate([gatherer(0, block, half), gatherer(half, block, half)], axis=0)
    far_chooser = jnp.concatenate(
        [gatherer(half * high, block, half), gatherer(half * (1 - high), block, half)], axis=0
    )
    same = same_mask(half)
    same = jnp.concatenate([beside(same, same)] * 2, axis=0)
    for start in range(0, rows, GROUP):
        stop = start + GROUP
        x_pair = beside(xs_ref[0, :, start:stop], x_oth_ref[:, start:stop])
        g_pair = beside(own_ref[:, start:stop], read_packed(oth_ref, start, stop))
        both = pick(jnp.where(same, dot(x_pair, g_pair, TN), 0.0), far_chooser)
        mine, theirs = both[:GROUP], both[GROUP:]
        lo_ref[start:stop, :] = jnp.where(high == 1, theirs, mine)
        hi_ref[start:stop, :] = jnp.where(high == 1, mine, theirs)
        grad = dot(g_pair, beside(bfar_ref[0, start:stop, :], bfar_ref[1, start:stop, :]), NT)
        for k in range(1, sections):
            lo_mask, hi_mask = block_masks(k, half)
            if k < sections - 1:
                x = xs_ref[k, :, start:stop]
            else:
                x = tok_ref[:, start:stop].astype(jnp.float32)
            outer = dot(x, grad, TN)
            row_ref[k * rows + start : k * rows + stop, :] = pick(
                beside(jnp.where(lo_mask, outer, 0.0), jnp.where(hi_mask, outer, 0.0)), chooser
            )
            grad = dot(grad, near_ref[k - 1, start:stop, :], NT)
        gtok_ref[:, start:stop] = grad
    for k in range(1, sections):
        split_halves(row_ref, lo_ref, hi_ref, k, rows, half)
    to_lanes(lo_ref, hi_ref, a_ref, lanes, half, block)
    for j in range(block):
        b_ref[j * block : (j + 1) * block, :] = inv_ref[pl.ds(j, block, stride=block), :]
        b_ref[j * block : (j + 1) * block, 0:per_section] = inv_far_ref[
            pl.ds(j, block, stride=block), :
        ]
    lane_matmul(a_ref, b_ref, c_ref, block, lanes)
    lane_matmul(b_ref, c_ref, a_ref, block, lanes)
    section_of, upper = lane_facts((block, lanes), per_section, high)
    transpose_to(c_ref, a_ref, block, lambda j, t: 2.0 * (t - a_ref[j * block : (j + 1) * block, :]))
    permute_rows(inverse_ref, c_ref, b_ref, section_of)
    transpose_to(a_ref, b_ref, block)
    for a in range(half):
        low = permuted_row(inverse_ref, a_ref, a, section_of)
        top = permuted_row(inverse_ref, a_ref, half + a, section_of)
        row_ref[pl.ds(a, lanes, stride=half), :] = jnp.where(upper, top, low).T
    for k in range(sections):
        ggen_ref[k * block : (k + 1) * block, :] = row_ref[k * rows : (k + 1) * rows, :].T


def merge_kernel(got_packed, send_packed, keep_ref, got_ref, send_ref, out_ref):
    half, count, width = out_ref.shape
    if got_packed:
        got_scale = jnp.exp2(got_ref[2 * half * count : 2 * half * count + 1, 0:1])

    def total(p):
        if got_packed:
            return keep_ref[p] + got_ref[p * count : (p + 1) * count, :] * got_scale
        return keep_ref[p] + got_ref[p]

    largest = jnp.zeros((count, width), jnp.float32)
    for p in range(half):
        out_ref[p] = total(p)
        upper = total(half + p)
        if send_packed:
            send_ref[p * count : (p + 1) * count, :] = upper
            largest = jnp.maximum(largest, jnp.abs(upper))
        else:
            send_ref[p] = upper
    if send_packed:
        peak = jnp.max(largest, axis=(0, 1), keepdims=True)
        exponent = jnp.ceil(jnp.log2(jnp.maximum(peak, 1e-30))) - 15.0
        scale = jnp.exp2(-exponent)
        for p in range(half):
            send_ref[p * count : (p + 1) * count, :] *= scale
        send_ref[half * count :, :] = jnp.broadcast_to(exponent, (16, width))


def last_kernel(packed, *refs):
    *in_refs, out_ref = refs
    chunks = len(in_refs) // 2
    width = in_refs[0].shape[2]
    for chunk in range(chunks):
        got_ref = in_refs[chunks + chunk]
        got = read_packed(got_ref, 0, width) if packed[chunk] else got_ref[0]
        out_ref[:, chunk * width : (chunk + 1) * width] = in_refs[chunk][0] + got


def merge(keep, got, got_packed, send_packed):
    pieces, count, width = keep.shape
    half = pieces // 2
    kept = jax.ShapeDtypeStruct((half, count, width), jnp.float32)
    packed = jax.ShapeDtypeStruct((half * count + 16, width), jnp.float32)
    full = pl.BlockSpec(memory_space=pltpu.VMEM)
    send, keep = pl.pallas_call(
        functools.partial(merge_kernel, got_packed, send_packed),
        out_shape=(packed if send_packed else kept, kept),
        in_specs=[full] * 2,
        out_specs=(full,) * 2,
        compiler_params=pltpu.CompilerParams(vmem_limit_bytes=VMEM_LIMIT),
        name="merge",
    )(keep, got.astype(jnp.float32))
    return (send.astype(jnp.float16) if send_packed else send), keep


def local(tokens, weight, generators, orders, cotangent):
    sections, rows, block = generators.shape
    half = block // 2
    count = tokens.shape[0]
    size = lax.axis_size("tensor")
    bits = size.bit_length() - 1
    here = lax.axis_index("tensor")
    pair_bit = bits - 1
    high = jnp.bitwise_and(jnp.right_shift(here, pair_bit), 1).astype(jnp.int32).reshape(1)
    lanes = sections * (rows // half)
    f32 = jnp.float32
    full = pl.BlockSpec(memory_space=pltpu.VMEM)
    scalars = pl.BlockSpec(memory_space=pltpu.SMEM)
    params = pltpu.CompilerParams(vmem_limit_bytes=VMEM_LIMIT)

    stored = jnp.swapaxes(generators, 1, 2)
    far_gen = exchange(stored[0], pair_bit)
    order = list(range(bits - 1, -1, -1))
    pieces = cotangent[None]
    for bit in order[:-4]:
        pieces = grow(pieces, bit)
    firsts = [exchange(pieces, bit) for bit in order[-4:-1]]
    flat = stored.reshape(sections * block, rows)
    square = (block * block, lanes)
    far_square = (block * block, lanes // sections)
    inv, near, xs = pl.pallas_call(
        near_kernel,
        out_shape=(
            jax.ShapeDtypeStruct(square, f32),
            jax.ShapeDtypeStruct((sections - 1, rows, GROUP), f32),
            jax.ShapeDtypeStruct((sections - 1, count, rows), f32),
        ),
        in_specs=[scalars, full, full],
        out_specs=(full,) * 3,
        scratch_shapes=[
            pltpu.VMEM((sections * rows, block), f32),
            pltpu.VMEM((sections * rows, block), f32),
            pltpu.VMEM(square, f32),
            pltpu.VMEM(square, f32),
            pltpu.VMEM((sections * rows, block), f32),
        ],
        compiler_params=params,
        name="near_rotations",
    )(orders, flat, tokens)
    by_far, by_mid, by_side = [after(first, xs) for first in firsts]
    far_gen = after(far_gen, xs, by_side)
    x_other = exchange(xs[0], pair_bit)
    inv_far, ffar, bfar = pl.pallas_call(
        far_rotations_kernel,
        out_shape=(
            jax.ShapeDtypeStruct(far_square, f32),
            jax.ShapeDtypeStruct((2, rows, GROUP), f32),
            jax.ShapeDtypeStruct((2, rows, GROUP), f32),
        ),
        in_specs=[scalars, scalars, full, full],
        out_specs=(full,) * 3,
        scratch_shapes=[
            pltpu.VMEM((rows, block), f32),
            pltpu.VMEM((rows, block), f32),
            pltpu.VMEM(far_square, f32),
            pltpu.VMEM(far_square, f32),
            pltpu.VMEM((rows, block), f32),
            pltpu.VMEM((rows, block), f32),
        ],
        compiler_params=params,
        cost_estimate=pl.CostEstimate(flops=10**7, bytes_accessed=10**7, transcendentals=0),
        name="far_rotations",
    )(orders[:1], high, stored[0], far_gen)
    by_far, by_mid = after(by_far, ffar), after(by_mid, ffar)
    by_both = exchange(by_far, order[-3])
    side_pair = exchange(jnp.concatenate([by_far, by_mid], axis=0), order[-2])
    side_last = exchange(by_both, order[-2])
    x_both = pl.pallas_call(
        far_kernel,
        out_shape=jax.ShapeDtypeStruct((2 * count, rows), jnp.bfloat16),
        in_specs=[full] * 3,
        out_specs=full,
        compiler_params=params,
        name="far_apply",
    )(xs, x_other, ffar)

    stages = [tuple(range(bits)), (0, 2, 1) + tuple(range(3, bits))]

    def slot_of(offset, bits_in_order):
        return sum(((offset >> bit) & 1) << (bits - 1 - n) for n, bit in enumerate(bits_in_order))

    offsets = sorted(range(size), key=lambda o: (1 - (o & 1), slot_of(o, stages[0])))
    slots = [[slot_of(o, bits_in_order) % (size // 2) for o in offsets] for bits_in_order in stages]
    fixed = here.astype(jnp.int32)
    places = jnp.bitwise_xor(fixed, jnp.asarray(np.array(offsets, np.int32)))
    back_places = jnp.bitwise_xor(fixed, jnp.arange(size, dtype=jnp.int32))
    outs = project(x_both, weight, places, slots)

    narrow = [(1, 2), (1, bits - 1)]

    def merged(n, outs, gots):
        return [
            merge(keep, got, n in marks, n + 1 in marks)
            for (_, keep), got, marks in zip(outs, gots, narrow)
        ]

    outs = merged(0, outs, [exchange(after(send, by_both, side_pair), 0) for send, _ in outs])
    gots = [exchange(send, order_[1]) for (send, _), order_ in zip(outs, stages)]
    side_last = after(side_last, *[send for send, _ in outs])
    pieces = jnp.concatenate(
        [pieces, by_far, by_mid, by_both, by_side, side_pair, side_last], axis=0
    )
    gathered = [pieces, exchange(pieces, 0)]
    numbers = jnp.arange(block, dtype=jnp.int32)
    inverse = jnp.sum(
        jnp.where(orders[:, :, None] == numbers[None, None, :], numbers[None, :, None], 0), axis=1
    ).astype(jnp.int32)
    grad_cols, grad_packed = project_back(back_places, gathered, gather_order(order), weight)
    grad_other = exchange_packed(grad_packed, pair_bit)
    gots[0] = after(gots[0], grad_cols)
    gots[-1] = after(gots[-1], grad_cols)
    grad_tokens, grad_gens = pl.pallas_call(
        grads_kernel,
        out_shape=(
            jax.ShapeDtypeStruct((count, rows), f32),
            jax.ShapeDtypeStruct((sections * block, rows), f32),
        ),
        in_specs=[scalars, scalars] + [full] * 9,
        out_specs=(full,) * 2,
        scratch_shapes=[
            pltpu.VMEM((sections * rows, block), f32),
            pltpu.VMEM((sections * rows, block), f32),
            pltpu.VMEM((sections * rows, block), f32),
            pltpu.VMEM(square, f32),
            pltpu.VMEM(square, f32),
            pltpu.VMEM(square, f32),
        ],
        compiler_params=params,
        name="gradients",
    )(inverse, high, grad_cols, grad_other, x_other, tokens, xs, near, bfar, inv_far, inv)
    outs = merged(1, outs, gots)
    for n in range(2, bits - 1):
        gots = [exchange(send, order_[n]) for (send, _), order_ in zip(outs, stages)]
        if n == 2:
            gots[0] = after(gots[0], grad_other)
        outs = merged(n, outs, gots)
    lasts = [exchange(send, bits - 1).astype(f32) for send, _ in outs]
    lasts[-1] = after(lasts[-1], grad_tokens, grad_gens)
    outputs = pl.pallas_call(
        functools.partial(last_kernel, [bits - 1 in marks for marks in narrow]),
        out_shape=jax.ShapeDtypeStruct((count, cotangent.shape[1]), f32),
        in_specs=[full] * (2 * CHUNKS),
        out_specs=full,
        compiler_params=params,
        name="last_sums",
    )(*[keep for _, keep in outs], *lasts)
    return outputs, grad_tokens, jnp.swapaxes(grad_gens.reshape(sections, block, rows), 1, 2)


def solution(mesh):
    placed = (
        P("groups", "tensor"),
        P("tensor", None),
        P("groups", "tensor", None),
        P(),
        P("groups", "tensor"),
    )
    return jax.shard_map(
        local,
        mesh=mesh,
        in_specs=placed,
        out_specs=(P("groups", "tensor"), P("groups", "tensor"), P("groups", "tensor", None)),
        check_vma=False,
    )
```

```python
import functools

import jax
import jax.numpy as jnp
import numpy as np
from jax import lax
from jax.experimental import pallas as pl
from jax.experimental.pallas import tpu as pltpu
from jax.sharding import PartitionSpec as P

VMEM_LIMIT = 16 * 2**20
WIDE_LIMIT = 46 * 2**20
GROUP = 128
NN = (((1,), (0,)), ((), ()))
NT = (((1,), (1,)), ((), ()))
TN = (((0,), (0,)), ((), ()))
CHUNKS = 2


def exchange(array, bit):
    size = lax.axis_size("tensor")
    return lax.ppermute(array, "tensor", [(i, i ^ (1 << bit)) for i in range(size)])


def parts_of(x):
    first = x.astype(jnp.bfloat16)
    return first, (x - first.astype(jnp.float32)).astype(jnp.bfloat16)


def one_dot(a, b, dims=NN):
    return lax.dot_general(a, b, dims, preferred_element_type=jnp.float32)


def after(value, *earlier):
    return lax.optimization_barrier((value, *earlier))[0]


def dot(a, b, dims=NN):
    a_first, a_rest = parts_of(a)
    b_first, b_rest = parts_of(b)
    return (
        one_dot(a_first, b_first, dims) + one_dot(a_rest, b_first, dims) + one_dot(a_first, b_rest, dims)
    )


def pick(a, chooser):
    first, rest = parts_of(a)
    return one_dot(first, chooser) + one_dot(rest, chooser)


def iota(shape, dim):
    return lax.broadcasted_iota(jnp.int32, shape, dim)


def split_halves(rows_ref, lo_ref, hi_ref, section, rows, half):
    step = half << (section - 1)
    base = section * rows
    for start in range(base, base + rows, 2 * step):
        low = rows_ref[start : start + step, :]
        high = rows_ref[start + step : start + 2 * step, :]
        lo_ref[start : start + step, :] = low
        lo_ref[start + step : start + 2 * step, :] = low
        hi_ref[start : start + step, :] = high
        hi_ref[start + step : start + 2 * step, :] = high


def to_lanes(lo_ref, hi_ref, out_ref, lanes, half, block):
    for a in range(half):
        out_ref[a * block : (a + 1) * block, :] = lo_ref[pl.ds(a, lanes, stride=half), :].T
        out_ref[(half + a) * block : (half + a + 1) * block, :] = hi_ref[
            pl.ds(a, lanes, stride=half), :
        ].T


def by_section(parts, section_of):
    out = parts[-1]
    for k in range(len(parts) - 2, -1, -1):
        out = jnp.where(section_of == k, parts[k], out)
    return out


def lane_facts(shape, per_section, high):
    lane = iota(shape, 1)
    section_of = lane // per_section
    part = lane % per_section
    upper = jnp.bitwise_and(jnp.right_shift(part, jnp.maximum(section_of - 1, 0)), 1)
    return section_of, jnp.where(section_of == 0, high, upper) == 1


def block_masks(section, half):
    row = iota((GROUP, GROUP), 0) // half
    col = iota((GROUP, GROUP), 1) // half
    bit = 1 << (section - 1)
    return col == jnp.bitwise_and(row, ~bit), col == jnp.bitwise_or(row, bit)


def same_mask(half):
    return iota((GROUP, GROUP), 0) // half == iota((GROUP, GROUP), 1) // half


def spreader(offsets, block, half):
    row, col = iota((block, GROUP), 0), iota((block, GROUP), 1) % half
    return jnp.concatenate([(row == at + col).astype(jnp.bfloat16) for at in offsets], axis=1)


def gatherer(offset, block, half):
    row, col = iota((GROUP, block), 0) % half, iota((GROUP, block), 1)
    return (col == offset + row).astype(jnp.bfloat16)


def transpose_to(out_ref, in_ref, block, change=lambda j, t: t):
    for j in range(block):
        out_ref[j * block : (j + 1) * block, :] = change(j, in_ref[pl.ds(j, block, stride=block), :])


def permuted_row(orders_ref, in_ref, i, section_of):
    sections, block = orders_ref.shape
    return by_section(
        [
            in_ref[pl.ds(pl.multiple_of(orders_ref[k, i] * block, block), block), :]
            for k in range(sections)
        ],
        section_of,
    )


def permute_rows(orders_ref, in_ref, out_ref, section_of):
    block = orders_ref.shape[1]
    for i in range(block):
        out_ref[i * block : (i + 1) * block, :] = permuted_row(orders_ref, in_ref, i, section_of)


def invert_blocks(orders_ref, lo_ref, hi_ref, inv_ref, a_ref, b_ref, section_of):
    sections, block = orders_ref.shape
    half = block // 2
    lanes = inv_ref.shape[1]
    to_lanes(lo_ref, hi_ref, a_ref, lanes, half, block)

    transpose_to(b_ref, a_ref, block, lambda j, t: a_ref[j * block : (j + 1) * block, :] - t)
    permute_rows(orders_ref, b_ref, a_ref, section_of)
    transpose_to(b_ref, a_ref, block)
    permute_rows(orders_ref, b_ref, inv_ref, section_of)
    sub = iota((block, lanes), 0)
    for j in range(block):
        inv_ref[j * block : (j + 1) * block, :] += (sub == j).astype(jnp.float32)

    def eliminate(k, _):
        at = pl.multiple_of(k * block, block)
        here = sub == k
        inverse = 1.0 / inv_ref[pl.ds(at + k, 1), :]
        factors = inv_ref[pl.ds(k, block, stride=block), :]
        pivot = jnp.where(here, inverse, inv_ref[pl.ds(at, block), :] * inverse)
        for i in range(block):
            row = inv_ref[i * block : (i + 1) * block, :]
            inv_ref[i * block : (i + 1) * block, :] = (
                jnp.where(here, 0.0, row) - factors[i : i + 1, :] * pivot
            )
        inv_ref[pl.ds(at, block), :] = pivot
        return 0

    lax.fori_loop(0, block, eliminate, 0)


def own_rows(inv_ref, out_ref, half, block, upper):
    lanes = inv_ref.shape[1]
    sub = iota((block, lanes), 0)
    for a in range(half):
        low = 2.0 * inv_ref[a * block : (a + 1) * block, :] - (sub == a).astype(jnp.float32)
        top = 2.0 * inv_ref[(half + a) * block : (half + a + 1) * block, :] - (
            sub == half + a
        ).astype(jnp.float32)
        out_ref[pl.ds(a, lanes, stride=half), :] = jnp.where(upper, top, low).T


def own_cols(inv_ref, out_ref, half, block, upper):
    lanes = inv_ref.shape[1]
    sub = iota((block, lanes), 0)
    for a in range(half):
        low = 2.0 * inv_ref[pl.ds(a, block, stride=block), :] - (sub == a).astype(jnp.float32)
        top = 2.0 * inv_ref[pl.ds(half + a, block, stride=block), :] - (sub == half + a).astype(
            jnp.float32
        )
        out_ref[pl.ds(a, lanes, stride=half), :] = jnp.where(upper, top, low).T


def near_kernel(
    orders_ref, gen_ref, tok_ref, inv_ref, near_ref, xs_ref,
    lo_ref, hi_ref, a_ref, b_ref, row_ref,
):
    sections, block = orders_ref.shape
    half = block // 2
    rows = tok_ref.shape[1]
    lanes = sections * rows // half
    for k in range(sections):
        row_ref[k * rows : (k + 1) * rows, :] = gen_ref[k * block : (k + 1) * block, :].T
    lo_ref[0:rows, :] = row_ref[0:rows, :]
    hi_ref[0:rows, :] = row_ref[0:rows, :]
    for k in range(1, sections):
        split_halves(row_ref, lo_ref, hi_ref, k, rows, half)
    section_of, upper = lane_facts((block, lanes), rows // half, 0)
    invert_blocks(orders_ref, lo_ref, hi_ref, inv_ref, a_ref, b_ref, section_of)
    own_rows(inv_ref, row_ref, half, block, upper)
    spread = spreader((0, half), block, half)
    for k in range(1, sections):
        lo_mask, hi_mask = block_masks(k, half)
        wide = pick(row_ref[k * rows : (k + 1) * rows, :], spread)
        for start in range(0, rows, GROUP):
            part = wide[start : start + GROUP]
            near_ref[k - 1, start : start + GROUP, :] = jnp.where(
                lo_mask, part[:, :GROUP], jnp.where(hi_mask, part[:, GROUP:], 0.0)
            )
    for start in range(0, rows, GROUP):
        stop = start + GROUP
        value = tok_ref[:, start:stop].astype(jnp.float32)
        for k in range(sections - 1, 0, -1):
            value = dot(value, near_ref[k - 1, start:stop, :])
            xs_ref[k - 1, :, start:stop] = value


def far_rotations_kernel(
    orders_ref, high_ref, own_ref, far_ref, inv_ref, ffar_ref, bfar_ref,
    lo_ref, hi_ref, a_ref, b_ref, row_ref, col_ref,
):
    block = orders_ref.shape[1]
    half = block // 2
    rows = far_ref.shape[1]
    high = high_ref[0]
    own = own_ref[...].T
    other = far_ref[...].T
    lo_ref[...] = jnp.where(high == 1, other, own)
    hi_ref[...] = jnp.where(high == 1, own, other)
    invert_blocks(orders_ref, lo_ref, hi_ref, inv_ref, a_ref, b_ref, None)
    upper = high == 1
    own_rows(inv_ref, row_ref, half, block, upper)
    own_cols(inv_ref, col_ref, half, block, upper)
    spread = spreader((half * high, half * (1 - high)), block, half)
    same = same_mask(half)
    for source, target in ((col_ref, ffar_ref), (row_ref, bfar_ref)):
        wide = pick(source[...], spread)
        for start in range(0, rows, GROUP):
            part = wide[start : start + GROUP]
            target[0, start : start + GROUP, :] = jnp.where(same, part[:, :GROUP], 0.0)
            target[1, start : start + GROUP, :] = jnp.where(same, part[:, GROUP:], 0.0)


def write_packed(packed_ref, value):
    count, width = value.shape
    peak = jnp.max(jnp.abs(value), axis=(0, 1), keepdims=True)
    exponent = jnp.ceil(jnp.log2(jnp.maximum(peak, 1e-30))) - 15.0
    packed_ref[0:count, :] = value * jnp.exp2(-exponent)
    packed_ref[count:, :] = jnp.broadcast_to(exponent, (16, width))


def read_packed(packed_ref, start, stop):
    count = packed_ref.shape[0] - 16
    return packed_ref[0:count, start:stop] * jnp.exp2(packed_ref[count : count + 1, 0:1])


def exchange_packed(packed, bit):
    return exchange(packed.astype(jnp.float16), bit).astype(jnp.float32)


def beside(a, b):
    return jnp.concatenate([a, b], axis=1)


def far_kernel(own_ref, oth_ref, far_ref, out_ref):
    count, rows = own_ref.shape[1:]
    for start in range(0, rows, GROUP):
        stop = start + GROUP
        value = dot(
            beside(own_ref[0, :, start:stop], oth_ref[:, start:stop]),
            beside(far_ref[0, start:stop, :], far_ref[1, start:stop, :]),
            NT,
        )
        first = value.astype(jnp.bfloat16)
        out_ref[0:count, start:stop] = first
        out_ref[count : 2 * count, start:stop] = (value - first.astype(jnp.float32)).astype(
            jnp.bfloat16
        )


def project_kernel(slots, places_ref, x_ref, w_ref, *refs):
    *out_refs, held_ref, sems = refs
    pieces, _, width = held_ref.shape
    count = x_ref.shape[0] // 2
    half = pieces // 2
    part = width // CHUNKS

    def fetch(p):
        at = pl.multiple_of(places_ref[p] * width, width)
        return pltpu.make_async_copy(w_ref.at[:, pl.ds(at, width)], held_ref.at[p], sems.at[p])

    for p in range(pieces):
        fetch(p).start()
    for p in range(pieces):
        fetch(p).wait()
        both = one_dot(x_ref[...], held_ref[p])
        total = both[:count] + both[count:]
        for chunk in range(CHUNKS):
            out_refs[2 * chunk + p // half][slots[chunk][p]] = total[
                :, chunk * part : (chunk + 1) * part
            ]


def project(x_both, weight, places, slots):
    pieces = places.shape[0]
    count2, rows = x_both.shape
    count = count2 // 2
    width = weight.shape[1] // lax.axis_size("tensor")
    outs = pl.pallas_call(
        functools.partial(project_kernel, slots),
        out_shape=(jax.ShapeDtypeStruct((pieces // 2, count, width // CHUNKS), jnp.float32),)
        * (2 * CHUNKS),
        in_specs=[
            pl.BlockSpec(memory_space=pltpu.SMEM),
            pl.BlockSpec(memory_space=pltpu.VMEM),
            pl.BlockSpec(memory_space=pl.ANY),
        ],
        out_specs=(pl.BlockSpec(memory_space=pltpu.VMEM),) * (2 * CHUNKS),
        scratch_shapes=[
            pltpu.VMEM((pieces, rows, width), weight.dtype),
            pltpu.SemaphoreType.DMA((pieces,)),
        ],
        compiler_params=pltpu.CompilerParams(vmem_limit_bytes=WIDE_LIMIT),
        cost_estimate=pl.CostEstimate(
            flops=2 * count2 * rows * width * pieces,
            bytes_accessed=pieces * width * (2 * rows + 4 * count),
            transcendentals=0,
        ),
        name="project",
    )(places, x_both, weight)
    return [outs[2 * chunk : 2 * chunk + 2] for chunk in range(CHUNKS)]


def back_kernel(order, places_ref, low_ref, high_ref, w_ref, out_ref, packed_ref, cots_ref, held_ref, cot_sems, sems):
    half, _, width = low_ref.shape

    def fetches(slot):
        at = pl.multiple_of(places_ref[order[slot]] * width, width)
        here = pl.ds(slot * width, width)
        cot = (low_ref if slot < half else high_ref).at[slot % half]
        return (
            pltpu.make_async_copy(cot, cots_ref.at[:, here], cot_sems.at[slot]),
            pltpu.make_async_copy(w_ref.at[:, pl.ds(at, width)], held_ref.at[:, here], sems.at[slot]),
        )

    for slot in range(2 * half):
        for copy in fetches(slot):
            copy.start()
    for slot in range(2 * half):
        for copy in fetches(slot):
            copy.wait()
        here = slice(slot * width, (slot + 1) * width)
        product = one_dot(cots_ref[:, here], held_ref[:, here], NT)
        if slot == 0:
            out_ref[...] = product
        else:
            out_ref[...] += product
    write_packed(packed_ref, out_ref[...])


def project_back(places, gathered, order, weight):
    half, count, width = gathered[0].shape
    steps = half * len(gathered)
    rows = weight.shape[0]
    return pl.pallas_call(
        functools.partial(back_kernel, order),
        out_shape=(
            jax.ShapeDtypeStruct((count, rows), jnp.float32),
            jax.ShapeDtypeStruct((count + 16, rows), jnp.float32),
        ),
        in_specs=[pl.BlockSpec(memory_space=pltpu.SMEM)]
        + [pl.BlockSpec(memory_space=pl.ANY)] * (len(gathered) + 1),
        out_specs=(pl.BlockSpec(memory_space=pltpu.VMEM),) * 2,
        scratch_shapes=[
            pltpu.VMEM((count, steps * width), weight.dtype),
            pltpu.VMEM((rows, steps * width), weight.dtype),
            pltpu.SemaphoreType.DMA((steps,)),
            pltpu.SemaphoreType.DMA((steps,)),
        ],
        compiler_params=pltpu.CompilerParams(vmem_limit_bytes=WIDE_LIMIT),
        cost_estimate=pl.CostEstimate(
            flops=2 * count * rows * width * steps,
            bytes_accessed=steps * width * 2 * (rows + count),
            transcendentals=0,
        ),
        name="project_back",
    )(places, *gathered, weight)


def grow(array, bit):
    return jnp.concatenate([array, exchange(array, bit)], axis=0)


def gather_order(stages):
    order = [0]
    for bit in stages:
        order = order + [n ^ (1 << bit) for n in order]
    return tuple(order)


def lane_matmul(left_ref, right_ref, out_ref, block, lanes):
    step = 4

    def body(t, _):
        first = t * step
        totals = [jnp.zeros((block, lanes), jnp.float32) for _ in range(step)]
        for j in range(block):
            right = right_ref[j * block : (j + 1) * block, :]
            for s in range(step):
                totals[s] += left_ref[pl.ds((first + s) * block + j, 1), :] * right
        for s in range(step):
            out_ref[pl.ds(pl.multiple_of((first + s) * block, block), block), :] = totals[s]
        return 0

    lax.fori_loop(0, block // step, body, 0)


def grads_kernel(
    inverse_ref, high_ref, own_ref, oth_ref, x_oth_ref, tok_ref, xs_ref, near_ref, bfar_ref, inv_far_ref, inv_ref,
    gtok_ref, ggen_ref,
    row_ref, lo_ref, hi_ref, a_ref, b_ref, c_ref,
):
    sections, block = inverse_ref.shape
    half = block // 2
    count, rows = own_ref.shape
    per_section = rows // half
    lanes = sections * per_section
    high = high_ref[0]
    chooser = jnp.concatenate([gatherer(0, block, half), gatherer(half, block, half)], axis=0)
    far_chooser = jnp.concatenate(
        [gatherer(half * high, block, half), gatherer(half * (1 - high), block, half)], axis=0
    )
    same = same_mask(half)
    same = jnp.concatenate([beside(same, same)] * 2, axis=0)
    for start in range(0, rows, GROUP):
        stop = start + GROUP
        x_pair = beside(xs_ref[0, :, start:stop], x_oth_ref[:, start:stop])
        g_pair = beside(own_ref[:, start:stop], read_packed(oth_ref, start, stop))
        both = pick(jnp.where(same, dot(x_pair, g_pair, TN), 0.0), far_chooser)
        mine, theirs = both[:GROUP], both[GROUP:]
        lo_ref[start:stop, :] = jnp.where(high == 1, theirs, mine)
        hi_ref[start:stop, :] = jnp.where(high == 1, mine, theirs)
        grad = dot(g_pair, beside(bfar_ref[0, start:stop, :], bfar_ref[1, start:stop, :]), NT)
        for k in range(1, sections):
            lo_mask, hi_mask = block_masks(k, half)
            if k < sections - 1:
                x = xs_ref[k, :, start:stop]
            else:
                x = tok_ref[:, start:stop].astype(jnp.float32)
            outer = dot(x, grad, TN)
            row_ref[k * rows + start : k * rows + stop, :] = pick(
                beside(jnp.where(lo_mask, outer, 0.0), jnp.where(hi_mask, outer, 0.0)), chooser
            )
            grad = dot(grad, near_ref[k - 1, start:stop, :], NT)
        gtok_ref[:, start:stop] = grad
    for k in range(1, sections):
        split_halves(row_ref, lo_ref, hi_ref, k, rows, half)
    to_lanes(lo_ref, hi_ref, a_ref, lanes, half, block)
    for j in range(block):
        b_ref[j * block : (j + 1) * block, :] = inv_ref[pl.ds(j, block, stride=block), :]
        b_ref[j * block : (j + 1) * block, 0:per_section] = inv_far_ref[
            pl.ds(j, block, stride=block), :
        ]
    lane_matmul(a_ref, b_ref, c_ref, block, lanes)
    lane_matmul(b_ref, c_ref, a_ref, block, lanes)
    section_of, upper = lane_facts((block, lanes), per_section, high)
    transpose_to(c_ref, a_ref, block, lambda j, t: 2.0 * (t - a_ref[j * block : (j + 1) * block, :]))
    permute_rows(inverse_ref, c_ref, b_ref, section_of)
    transpose_to(a_ref, b_ref, block)
    for a in range(half):
        low = permuted_row(inverse_ref, a_ref, a, section_of)
        top = permuted_row(inverse_ref, a_ref, half + a, section_of)
        row_ref[pl.ds(a, lanes, stride=half), :] = jnp.where(upper, top, low).T
    for k in range(sections):
        ggen_ref[k * block : (k + 1) * block, :] = row_ref[k * rows : (k + 1) * rows, :].T


def merge_kernel(got_packed, send_packed, keep_ref, got_ref, send_ref, out_ref):
    half, count, width = out_ref.shape
    if got_packed:
        got_scale = jnp.exp2(got_ref[2 * half * count : 2 * half * count + 1, 0:1])

    def total(p):
        if got_packed:
            return keep_ref[p] + got_ref[p * count : (p + 1) * count, :] * got_scale
        return keep_ref[p] + got_ref[p]

    largest = jnp.zeros((count, width), jnp.float32)
    for p in range(half):
        out_ref[p] = total(p)
        upper = total(half + p)
        if send_packed:
            send_ref[p * count : (p + 1) * count, :] = upper
            largest = jnp.maximum(largest, jnp.abs(upper))
        else:
            send_ref[p] = upper
    if send_packed:
        peak = jnp.max(largest, axis=(0, 1), keepdims=True)
        exponent = jnp.ceil(jnp.log2(jnp.maximum(peak, 1e-30))) - 15.0
        scale = jnp.exp2(-exponent)
        for p in range(half):
            send_ref[p * count : (p + 1) * count, :] *= scale
        send_ref[half * count :, :] = jnp.broadcast_to(exponent, (16, width))


def last_kernel(packed, *refs):
    *in_refs, out_ref = refs
    chunks = len(in_refs) // 2
    width = in_refs[0].shape[2]
    for chunk in range(chunks):
        got_ref = in_refs[chunks + chunk]
        got = read_packed(got_ref, 0, width) if packed[chunk] else got_ref[0]
        out_ref[:, chunk * width : (chunk + 1) * width] = in_refs[chunk][0] + got


def merge(keep, got, got_packed, send_packed):
    pieces, count, width = keep.shape
    half = pieces // 2
    kept = jax.ShapeDtypeStruct((half, count, width), jnp.float32)
    packed = jax.ShapeDtypeStruct((half * count + 16, width), jnp.float32)
    full = pl.BlockSpec(memory_space=pltpu.VMEM)
    send, keep = pl.pallas_call(
        functools.partial(merge_kernel, got_packed, send_packed),
        out_shape=(packed if send_packed else kept, kept),
        in_specs=[full] * 2,
        out_specs=(full,) * 2,
        compiler_params=pltpu.CompilerParams(vmem_limit_bytes=VMEM_LIMIT),
        name="merge",
    )(keep, got.astype(jnp.float32))
    return (send.astype(jnp.float16) if send_packed else send), keep


def local(tokens, weight, generators, orders, cotangent):
    sections, rows, block = generators.shape
    half = block // 2
    count = tokens.shape[0]
    size = lax.axis_size("tensor")
    bits = size.bit_length() - 1
    here = lax.axis_index("tensor")
    pair_bit = bits - 1
    high = jnp.bitwise_and(jnp.right_shift(here, pair_bit), 1).astype(jnp.int32).reshape(1)
    lanes = sections * (rows // half)
    f32 = jnp.float32
    full = pl.BlockSpec(memory_space=pltpu.VMEM)
    scalars = pl.BlockSpec(memory_space=pltpu.SMEM)
    params = pltpu.CompilerParams(vmem_limit_bytes=VMEM_LIMIT)

    stored = jnp.swapaxes(generators, 1, 2)
    far_gen = exchange(stored[0], pair_bit)
    order = list(range(bits - 1, -1, -1))
    pieces = cotangent[None]
    for bit in order[:-4]:
        pieces = grow(pieces, bit)
    firsts = [exchange(pieces, bit) for bit in order[-4:-1]]
    flat = stored.reshape(sections * block, rows)
    square = (block * block, lanes)
    far_square = (block * block, lanes // sections)
    inv, near, xs = pl.pallas_call(
        near_kernel,
        out_shape=(
            jax.ShapeDtypeStruct(square, f32),
            jax.ShapeDtypeStruct((sections - 1, rows, GROUP), f32),
            jax.ShapeDtypeStruct((sections - 1, count, rows), f32),
        ),
        in_specs=[scalars, full, full],
        out_specs=(full,) * 3,
        scratch_shapes=[
            pltpu.VMEM((sections * rows, block), f32),
            pltpu.VMEM((sections * rows, block), f32),
            pltpu.VMEM(square, f32),
            pltpu.VMEM(square, f32),
            pltpu.VMEM((sections * rows, block), f32),
        ],
        compiler_params=params,
        name="near_rotations",
    )(orders, flat, tokens)
    by_far, by_mid, by_side = [after(first, xs) for first in firsts]
    far_gen = after(far_gen, xs, by_side)
    x_other = exchange(xs[0], pair_bit)
    inv_far, ffar, bfar = pl.pallas_call(
        far_rotations_kernel,
        out_shape=(
            jax.ShapeDtypeStruct(far_square, f32),
            jax.ShapeDtypeStruct((2, rows, GROUP), f32),
            jax.ShapeDtypeStruct((2, rows, GROUP), f32),
        ),
        in_specs=[scalars, scalars, full, full],
        out_specs=(full,) * 3,
        scratch_shapes=[
            pltpu.VMEM((rows, block), f32),
            pltpu.VMEM((rows, block), f32),
            pltpu.VMEM(far_square, f32),
            pltpu.VMEM(far_square, f32),
            pltpu.VMEM((rows, block), f32),
            pltpu.VMEM((rows, block), f32),
        ],
        compiler_params=params,
        cost_estimate=pl.CostEstimate(flops=10**7, bytes_accessed=10**7, transcendentals=0),
        name="far_rotations",
    )(orders[:1], high, stored[0], far_gen)
    by_far, by_mid = after(by_far, ffar), after(by_mid, ffar)
    by_both = exchange(by_far, order[-3])
    side_pair = exchange(jnp.concatenate([by_far, by_mid], axis=0), order[-2])
    side_last = exchange(by_both, order[-2])
    x_both = pl.pallas_call(
        far_kernel,
        out_shape=jax.ShapeDtypeStruct((2 * count, rows), jnp.bfloat16),
        in_specs=[full] * 3,
        out_specs=full,
        compiler_params=params,
        name="far_apply",
    )(xs, x_other, ffar)

    stages = [tuple(range(bits)), (0, 2, 1) + tuple(range(3, bits))]

    def slot_of(offset, bits_in_order):
        return sum(((offset >> bit) & 1) << (bits - 1 - n) for n, bit in enumerate(bits_in_order))

    offsets = sorted(range(size), key=lambda o: (1 - (o & 1), slot_of(o, stages[0])))
    slots = [[slot_of(o, bits_in_order) % (size // 2) for o in offsets] for bits_in_order in stages]
    fixed = here.astype(jnp.int32)
    places = jnp.bitwise_xor(fixed, jnp.asarray(np.array(offsets, np.int32)))
    back_places = jnp.bitwise_xor(fixed, jnp.arange(size, dtype=jnp.int32))
    outs = project(x_both, weight, places, slots)

    narrow = [(1, 2), (1, bits - 1)]

    def merged(n, outs, gots):
        return [
            merge(keep, got, n in marks, n + 1 in marks)
            for (_, keep), got, marks in zip(outs, gots, narrow)
        ]

    outs = merged(0, outs, [exchange(after(send, by_both, side_pair), 0) for send, _ in outs])
    gots = [exchange(send, order_[1]) for (send, _), order_ in zip(outs, stages)]
    side_last = after(side_last, *[send for send, _ in outs])
    pieces = jnp.concatenate(
        [pieces, by_far, by_mid, by_both, by_side, side_pair, side_last], axis=0
    )
    gathered = [pieces, exchange(pieces, 0)]
    numbers = jnp.arange(block, dtype=jnp.int32)
    inverse = jnp.sum(
        jnp.where(orders[:, :, None] == numbers[None, None, :], numbers[None, :, None], 0), axis=1
    ).astype(jnp.int32)
    grad_cols, grad_packed = project_back(back_places, gathered, gather_order(order), weight)
    grad_other = exchange_packed(grad_packed, pair_bit)
    gots[0] = after(gots[0], grad_cols)
    gots[-1] = after(gots[-1], grad_cols)
    grad_tokens, grad_gens = pl.pallas_call(
        grads_kernel,
        out_shape=(
            jax.ShapeDtypeStruct((count, rows), f32),
            jax.ShapeDtypeStruct((sections * block, rows), f32),
        ),
        in_specs=[scalars, scalars] + [full] * 9,
        out_specs=(full,) * 2,
        scratch_shapes=[
            pltpu.VMEM((sections * rows, block), f32),
            pltpu.VMEM((sections * rows, block), f32),
            pltpu.VMEM((sections * rows, block), f32),
            pltpu.VMEM(square, f32),
            pltpu.VMEM(square, f32),
            pltpu.VMEM(square, f32),
        ],
        compiler_params=params,
        name="gradients",
    )(inverse, high, grad_cols, grad_other, x_other, tokens, xs, near, bfar, inv_far, inv)
    outs = merged(1, outs, gots)
    for n in range(2, bits - 1):
        gots = [exchange(send, order_[n]) for (send, _), order_ in zip(outs, stages)]
        if n == 2:
            gots[0] = after(gots[0], grad_other)
        outs = merged(n, outs, gots)
    lasts = [exchange(send, bits - 1).astype(f32) for send, _ in outs]
    lasts[-1] = after(lasts[-1], grad_tokens, grad_gens)
    outputs = pl.pallas_call(
        functools.partial(last_kernel, [bits - 1 in marks for marks in narrow]),
        out_shape=jax.ShapeDtypeStruct((count, cotangent.shape[1]), f32),
        in_specs=[full] * (2 * CHUNKS),
        out_specs=full,
        compiler_params=params,
        name="last_sums",
    )(*[keep for _, keep in outs], *lasts)
    return outputs, grad_tokens, jnp.swapaxes(grad_gens.reshape(sections, block, rows), 1, 2)


def solution(mesh):
    placed = (
        P("groups", "tensor"),
        P("tensor", None),
        P("groups", "tensor", None),
        P(),
        P("groups", "tensor"),
    )
    return jax.shard_map(
        local,
        mesh=mesh,
        in_specs=placed,
        out_specs=(P("groups", "tensor"), P("groups", "tensor"), P("groups", "tensor", None)),
        check_vma=False,
    )
```

```python
import functools

import jax
import jax.numpy as jnp
import numpy as np
from jax import lax
from jax.experimental import pallas as pl
from jax.experimental.pallas import tpu as pltpu
from jax.sharding import PartitionSpec as P

VMEM_LIMIT = 16 * 2**20
WIDE_LIMIT = 46 * 2**20
DEPTH = 4
GROUP = 128
NN = (((1,), (0,)), ((), ()))
NT = (((1,), (1,)), ((), ()))
TN = (((0,), (0,)), ((), ()))
CHUNKS = 2


def exchange(array, bit):
    size = lax.axis_size("tensor")
    return lax.ppermute(array, "tensor", [(i, i ^ (1 << bit)) for i in range(size)])


def parts_of(x):
    first = x.astype(jnp.bfloat16)
    return first, (x - first.astype(jnp.float32)).astype(jnp.bfloat16)


def one_dot(a, b, dims=NN):
    return lax.dot_general(a, b, dims, preferred_element_type=jnp.float32)


def after(value, *earlier):
    return lax.optimization_barrier((value, *earlier))[0]


def dot(a, b, dims=NN):
    a_first, a_rest = parts_of(a)
    b_first, b_rest = parts_of(b)
    return (
        one_dot(a_first, b_first, dims) + one_dot(a_rest, b_first, dims) + one_dot(a_first, b_rest, dims)
    )


def pick(a, chooser):
    first, rest = parts_of(a)
    return one_dot(first, chooser) + one_dot(rest, chooser)


def iota(shape, dim):
    return lax.broadcasted_iota(jnp.int32, shape, dim)


def split_halves(rows_ref, lo_ref, hi_ref, section, rows, half):
    step = half << (section - 1)
    base = section * rows
    for start in range(base, base + rows, 2 * step):
        low = rows_ref[start : start + step, :]
        high = rows_ref[start + step : start + 2 * step, :]
        lo_ref[start : start + step, :] = low
        lo_ref[start + step : start + 2 * step, :] = low
        hi_ref[start : start + step, :] = high
        hi_ref[start + step : start + 2 * step, :] = high


def to_lanes(lo_ref, hi_ref, out_ref, lanes, half, block):
    for a in range(half):
        out_ref[a * block : (a + 1) * block, :] = lo_ref[pl.ds(a, lanes, stride=half), :].T
        out_ref[(half + a) * block : (half + a + 1) * block, :] = hi_ref[
            pl.ds(a, lanes, stride=half), :
        ].T


def by_section(parts, section_of):
    out = parts[-1]
    for k in range(len(parts) - 2, -1, -1):
        out = jnp.where(section_of == k, parts[k], out)
    return out


def lane_facts(shape, per_section, high):
    lane = iota(shape, 1)
    section_of = lane // per_section
    part = lane % per_section
    upper = jnp.bitwise_and(jnp.right_shift(part, jnp.maximum(section_of - 1, 0)), 1)
    return section_of, jnp.where(section_of == 0, high, upper) == 1


def block_masks(section, half):
    row = iota((GROUP, GROUP), 0) // half
    col = iota((GROUP, GROUP), 1) // half
    bit = 1 << (section - 1)
    return col == jnp.bitwise_and(row, ~bit), col == jnp.bitwise_or(row, bit)


def same_mask(half):
    return iota((GROUP, GROUP), 0) // half == iota((GROUP, GROUP), 1) // half


def spreader(offsets, block, half):
    row, col = iota((block, GROUP), 0), iota((block, GROUP), 1) % half
    return jnp.concatenate([(row == at + col).astype(jnp.bfloat16) for at in offsets], axis=1)


def gatherer(offset, block, half):
    row, col = iota((GROUP, block), 0) % half, iota((GROUP, block), 1)
    return (col == offset + row).astype(jnp.bfloat16)


def transpose_to(out_ref, in_ref, block, change=lambda j, t: t):
    for j in range(block):
        out_ref[j * block : (j + 1) * block, :] = change(j, in_ref[pl.ds(j, block, stride=block), :])


def permuted_row(orders_ref, in_ref, i, section_of):
    sections, block = orders_ref.shape
    return by_section(
        [
            in_ref[pl.ds(pl.multiple_of(orders_ref[k, i] * block, block), block), :]
            for k in range(sections)
        ],
        section_of,
    )


def permute_rows(orders_ref, in_ref, out_ref, section_of):
    block = orders_ref.shape[1]
    for i in range(block):
        out_ref[i * block : (i + 1) * block, :] = permuted_row(orders_ref, in_ref, i, section_of)


def invert_blocks(orders_ref, lo_ref, hi_ref, inv_ref, a_ref, b_ref, section_of):
    sections, block = orders_ref.shape
    half = block // 2
    lanes = inv_ref.shape[1]
    to_lanes(lo_ref, hi_ref, a_ref, lanes, half, block)

    transpose_to(b_ref, a_ref, block, lambda j, t: a_ref[j * block : (j + 1) * block, :] - t)
    permute_rows(orders_ref, b_ref, a_ref, section_of)
    transpose_to(b_ref, a_ref, block)
    permute_rows(orders_ref, b_ref, inv_ref, section_of)
    sub = iota((block, lanes), 0)
    for j in range(block):
        inv_ref[j * block : (j + 1) * block, :] += (sub == j).astype(jnp.float32)

    def eliminate(k, _):
        at = pl.multiple_of(k * block, block)
        here = sub == k
        inverse = 1.0 / inv_ref[pl.ds(at + k, 1), :]
        factors = inv_ref[pl.ds(k, block, stride=block), :]
        pivot = jnp.where(here, inverse, inv_ref[pl.ds(at, block), :] * inverse)
        for i in range(block):
            row = inv_ref[i * block : (i + 1) * block, :]
            inv_ref[i * block : (i + 1) * block, :] = (
                jnp.where(here, 0.0, row) - factors[i : i + 1, :] * pivot
            )
        inv_ref[pl.ds(at, block), :] = pivot
        return 0

    lax.fori_loop(0, block, eliminate, 0)


def own_rows(inv_ref, out_ref, half, block, upper):
    lanes = inv_ref.shape[1]
    sub = iota((block, lanes), 0)
    for a in range(half):
        low = 2.0 * inv_ref[a * block : (a + 1) * block, :] - (sub == a).astype(jnp.float32)
        top = 2.0 * inv_ref[(half + a) * block : (half + a + 1) * block, :] - (
            sub == half + a
        ).astype(jnp.float32)
        out_ref[pl.ds(a, lanes, stride=half), :] = jnp.where(upper, top, low).T


def own_cols(inv_ref, out_ref, half, block, upper):
    lanes = inv_ref.shape[1]
    sub = iota((block, lanes), 0)
    for a in range(half):
        low = 2.0 * inv_ref[pl.ds(a, block, stride=block), :] - (sub == a).astype(jnp.float32)
        top = 2.0 * inv_ref[pl.ds(half + a, block, stride=block), :] - (sub == half + a).astype(
            jnp.float32
        )
        out_ref[pl.ds(a, lanes, stride=half), :] = jnp.where(upper, top, low).T


def near_kernel(
    orders_ref, gen_ref, tok_ref, inv_ref, near_ref, xs_ref,
    lo_ref, hi_ref, a_ref, b_ref, row_ref,
):
    sections, block = orders_ref.shape
    half = block // 2
    rows = tok_ref.shape[1]
    lanes = sections * rows // half
    for k in range(sections):
        row_ref[k * rows : (k + 1) * rows, :] = gen_ref[k * block : (k + 1) * block, :].T
    lo_ref[0:rows, :] = row_ref[0:rows, :]
    hi_ref[0:rows, :] = row_ref[0:rows, :]
    for k in range(1, sections):
        split_halves(row_ref, lo_ref, hi_ref, k, rows, half)
    section_of, upper = lane_facts((block, lanes), rows // half, 0)
    invert_blocks(orders_ref, lo_ref, hi_ref, inv_ref, a_ref, b_ref, section_of)
    own_rows(inv_ref, row_ref, half, block, upper)
    spread = spreader((0, half), block, half)
    for k in range(1, sections):
        lo_mask, hi_mask = block_masks(k, half)
        wide = pick(row_ref[k * rows : (k + 1) * rows, :], spread)
        for start in range(0, rows, GROUP):
            part = wide[start : start + GROUP]
            near_ref[k - 1, start : start + GROUP, :] = jnp.where(
                lo_mask, part[:, :GROUP], jnp.where(hi_mask, part[:, GROUP:], 0.0)
            )
    for start in range(0, rows, GROUP):
        stop = start + GROUP
        value = tok_ref[:, start:stop].astype(jnp.float32)
        for k in range(sections - 1, 0, -1):
            value = dot(value, near_ref[k - 1, start:stop, :])
            xs_ref[k - 1, :, start:stop] = value


def far_rotations_kernel(
    orders_ref, high_ref, own_ref, far_ref, inv_ref, ffar_ref, bfar_ref,
    lo_ref, hi_ref, a_ref, b_ref, row_ref, col_ref,
):
    block = orders_ref.shape[1]
    half = block // 2
    rows = far_ref.shape[1]
    high = high_ref[0]
    own = own_ref[...].T
    other = far_ref[...].T
    lo_ref[...] = jnp.where(high == 1, other, own)
    hi_ref[...] = jnp.where(high == 1, own, other)
    invert_blocks(orders_ref, lo_ref, hi_ref, inv_ref, a_ref, b_ref, None)
    upper = high == 1
    own_rows(inv_ref, row_ref, half, block, upper)
    own_cols(inv_ref, col_ref, half, block, upper)
    spread = spreader((half * high, half * (1 - high)), block, half)
    same = same_mask(half)
    for source, target in ((col_ref, ffar_ref), (row_ref, bfar_ref)):
        wide = pick(source[...], spread)
        for start in range(0, rows, GROUP):
            part = wide[start : start + GROUP]
            target[0, start : start + GROUP, :] = jnp.where(same, part[:, :GROUP], 0.0)
            target[1, start : start + GROUP, :] = jnp.where(same, part[:, GROUP:], 0.0)


def write_packed(packed_ref, value):
    count, width = value.shape
    peak = jnp.max(jnp.abs(value), axis=(0, 1), keepdims=True)
    exponent = jnp.ceil(jnp.log2(jnp.maximum(peak, 1e-30))) - 15.0
    packed_ref[0:count, :] = value * jnp.exp2(-exponent)
    packed_ref[count:, :] = jnp.broadcast_to(exponent, (16, width))


def read_packed(packed_ref, start, stop):
    count = packed_ref.shape[0] - 16
    return packed_ref[0:count, start:stop] * jnp.exp2(packed_ref[count : count + 1, 0:1])


def exchange_packed(packed, bit):
    return exchange(packed.astype(jnp.float16), bit).astype(jnp.float32)


def beside(a, b):
    return jnp.concatenate([a, b], axis=1)


def far_kernel(own_ref, oth_ref, far_ref, out_ref):
    count, rows = own_ref.shape[1:]
    for start in range(0, rows, GROUP):
        stop = start + GROUP
        value = dot(
            beside(own_ref[0, :, start:stop], oth_ref[:, start:stop]),
            beside(far_ref[0, start:stop, :], far_ref[1, start:stop, :]),
            NT,
        )
        first = value.astype(jnp.bfloat16)
        out_ref[0:count, start:stop] = first
        out_ref[count : 2 * count, start:stop] = (value - first.astype(jnp.float32)).astype(
            jnp.bfloat16
        )


def project_kernel(slots, places_ref, x_ref, w_ref, *refs):
    *out_refs, held_ref, sems = refs
    pieces, _, width = held_ref.shape
    count = x_ref.shape[0] // 2
    half = pieces // 2
    part = width // CHUNKS

    def fetch(p):
        at = pl.multiple_of(places_ref[p] * width, width)
        return pltpu.make_async_copy(w_ref.at[:, pl.ds(at, width)], held_ref.at[p], sems.at[p])

    for p in range(min(DEPTH, pieces)):
        fetch(p).start()
    for p in range(pieces):
        fetch(p).wait()
        if p + DEPTH < pieces:
            fetch(p + DEPTH).start()
        both = one_dot(x_ref[...], held_ref[p])
        total = both[:count] + both[count:]
        for chunk in range(CHUNKS):
            out_refs[2 * chunk + p // half][slots[chunk][p]] = total[
                :, chunk * part : (chunk + 1) * part
            ]


def project(x_both, weight, places, slots):
    pieces = places.shape[0]
    count2, rows = x_both.shape
    count = count2 // 2
    width = weight.shape[1] // lax.axis_size("tensor")
    outs = pl.pallas_call(
        functools.partial(project_kernel, slots),
        out_shape=(jax.ShapeDtypeStruct((pieces // 2, count, width // CHUNKS), jnp.float32),)
        * (2 * CHUNKS),
        in_specs=[
            pl.BlockSpec(memory_space=pltpu.SMEM),
            pl.BlockSpec(memory_space=pltpu.VMEM),
            pl.BlockSpec(memory_space=pl.ANY),
        ],
        out_specs=(pl.BlockSpec(memory_space=pltpu.VMEM),) * (2 * CHUNKS),
        scratch_shapes=[
            pltpu.VMEM((pieces, rows, width), weight.dtype),
            pltpu.SemaphoreType.DMA((pieces,)),
        ],
        compiler_params=pltpu.CompilerParams(vmem_limit_bytes=WIDE_LIMIT),
        cost_estimate=pl.CostEstimate(
            flops=2 * count2 * rows * width * pieces,
            bytes_accessed=pieces * width * (2 * rows + 4 * count),
            transcendentals=0,
        ),
        name="project",
    )(places, x_both, weight)
    return [outs[2 * chunk : 2 * chunk + 2] for chunk in range(CHUNKS)]


def back_kernel(order, places_ref, low_ref, high_ref, w_ref, out_ref, packed_ref, cots_ref, held_ref, cot_sems, sems):
    half, _, width = low_ref.shape

    def fetches(slot):
        at = pl.multiple_of(places_ref[order[slot]] * width, width)
        here = pl.ds(slot * width, width)
        cot = (low_ref if slot < half else high_ref).at[slot % half]
        return (
            pltpu.make_async_copy(cot, cots_ref.at[:, here], cot_sems.at[slot]),
            pltpu.make_async_copy(w_ref.at[:, pl.ds(at, width)], held_ref.at[:, here], sems.at[slot]),
        )

    for slot in range(min(DEPTH, 2 * half)):
        for copy in fetches(slot):
            copy.start()
    for slot in range(2 * half):
        for copy in fetches(slot):
            copy.wait()
        if slot + DEPTH < 2 * half:
            for copy in fetches(slot + DEPTH):
                copy.start()
        here = slice(slot * width, (slot + 1) * width)
        product = one_dot(cots_ref[:, here], held_ref[:, here], NT)
        if slot == 0:
            out_ref[...] = product
        else:
            out_ref[...] += product
    write_packed(packed_ref, out_ref[...])


def project_back(places, gathered, order, weight):
    half, count, width = gathered[0].shape
    steps = half * len(gathered)
    rows = weight.shape[0]
    return pl.pallas_call(
        functools.partial(back_kernel, order),
        out_shape=(
            jax.ShapeDtypeStruct((count, rows), jnp.float32),
            jax.ShapeDtypeStruct((count + 16, rows), jnp.float32),
        ),
        in_specs=[pl.BlockSpec(memory_space=pltpu.SMEM)]
        + [pl.BlockSpec(memory_space=pl.ANY)] * (len(gathered) + 1),
        out_specs=(pl.BlockSpec(memory_space=pltpu.VMEM),) * 2,
        scratch_shapes=[
            pltpu.VMEM((count, steps * width), weight.dtype),
            pltpu.VMEM((rows, steps * width), weight.dtype),
            pltpu.SemaphoreType.DMA((steps,)),
            pltpu.SemaphoreType.DMA((steps,)),
        ],
        compiler_params=pltpu.CompilerParams(vmem_limit_bytes=WIDE_LIMIT),
        cost_estimate=pl.CostEstimate(
            flops=2 * count * rows * width * steps,
            bytes_accessed=steps * width * 2 * (rows + count),
            transcendentals=0,
        ),
        name="project_back",
    )(places, *gathered, weight)


def grow(array, bit):
    return jnp.concatenate([array, exchange(array, bit)], axis=0)


def gather_order(stages):
    order = [0]
    for bit in stages:
        order = order + [n ^ (1 << bit) for n in order]
    return tuple(order)


def lane_matmul(left_ref, right_ref, out_ref, block, lanes):
    step = 4

    def body(t, _):
        first = t * step
        totals = [jnp.zeros((block, lanes), jnp.float32) for _ in range(step)]
        for j in range(block):
            right = right_ref[j * block : (j + 1) * block, :]
            for s in range(step):
                totals[s] += left_ref[pl.ds((first + s) * block + j, 1), :] * right
        for s in range(step):
            out_ref[pl.ds(pl.multiple_of((first + s) * block, block), block), :] = totals[s]
        return 0

    lax.fori_loop(0, block // step, body, 0)


def grads_kernel(
    inverse_ref, high_ref, own_ref, oth_ref, x_oth_ref, tok_ref, xs_ref, near_ref, bfar_ref, inv_far_ref, inv_ref,
    gtok_ref, ggen_ref,
    row_ref, lo_ref, hi_ref, a_ref, b_ref, c_ref,
):
    sections, block = inverse_ref.shape
    half = block // 2
    count, rows = own_ref.shape
    per_section = rows // half
    lanes = sections * per_section
    high = high_ref[0]
    chooser = jnp.concatenate([gatherer(0, block, half), gatherer(half, block, half)], axis=0)
    far_chooser = jnp.concatenate(
        [gatherer(half * high, block, half), gatherer(half * (1 - high), block, half)], axis=0
    )
    same = same_mask(half)
    same = jnp.concatenate([beside(same, same)] * 2, axis=0)
    for start in range(0, rows, GROUP):
        stop = start + GROUP
        x_pair = beside(xs_ref[0, :, start:stop], x_oth_ref[:, start:stop])
        g_pair = beside(own_ref[:, start:stop], read_packed(oth_ref, start, stop))
        both = pick(jnp.where(same, dot(x_pair, g_pair, TN), 0.0), far_chooser)
        mine, theirs = both[:GROUP], both[GROUP:]
        lo_ref[start:stop, :] = jnp.where(high == 1, theirs, mine)
        hi_ref[start:stop, :] = jnp.where(high == 1, mine, theirs)
        grad = dot(g_pair, beside(bfar_ref[0, start:stop, :], bfar_ref[1, start:stop, :]), NT)
        for k in range(1, sections):
            lo_mask, hi_mask = block_masks(k, half)
            if k < sections - 1:
                x = xs_ref[k, :, start:stop]
            else:
                x = tok_ref[:, start:stop].astype(jnp.float32)
            outer = dot(x, grad, TN)
            row_ref[k * rows + start : k * rows + stop, :] = pick(
                beside(jnp.where(lo_mask, outer, 0.0), jnp.where(hi_mask, outer, 0.0)), chooser
            )
            grad = dot(grad, near_ref[k - 1, start:stop, :], NT)
        gtok_ref[:, start:stop] = grad
    for k in range(1, sections):
        split_halves(row_ref, lo_ref, hi_ref, k, rows, half)
    to_lanes(lo_ref, hi_ref, a_ref, lanes, half, block)
    for j in range(block):
        b_ref[j * block : (j + 1) * block, :] = inv_ref[pl.ds(j, block, stride=block), :]
        b_ref[j * block : (j + 1) * block, 0:per_section] = inv_far_ref[
            pl.ds(j, block, stride=block), :
        ]
    lane_matmul(a_ref, b_ref, c_ref, block, lanes)
    lane_matmul(b_ref, c_ref, a_ref, block, lanes)
    section_of, upper = lane_facts((block, lanes), per_section, high)
    transpose_to(c_ref, a_ref, block, lambda j, t: 2.0 * (t - a_ref[j * block : (j + 1) * block, :]))
    permute_rows(inverse_ref, c_ref, b_ref, section_of)
    transpose_to(a_ref, b_ref, block)
    for a in range(half):
        low = permuted_row(inverse_ref, a_ref, a, section_of)
        top = permuted_row(inverse_ref, a_ref, half + a, section_of)
        row_ref[pl.ds(a, lanes, stride=half), :] = jnp.where(upper, top, low).T
    for k in range(sections):
        ggen_ref[k * block : (k + 1) * block, :] = row_ref[k * rows : (k + 1) * rows, :].T


def merge_kernel(got_packed, send_packed, keep_ref, got_ref, send_ref, out_ref):
    half, count, width = out_ref.shape
    if got_packed:
        got_scale = jnp.exp2(got_ref[2 * half * count : 2 * half * count + 1, 0:1])

    def total(p):
        if got_packed:
            return keep_ref[p] + got_ref[p * count : (p + 1) * count, :] * got_scale
        return keep_ref[p] + got_ref[p]

    largest = jnp.zeros((count, width), jnp.float32)
    for p in range(half):
        out_ref[p] = total(p)
        upper = total(half + p)
        if send_packed:
            send_ref[p * count : (p + 1) * count, :] = upper
            largest = jnp.maximum(largest, jnp.abs(upper))
        else:
            send_ref[p] = upper
    if send_packed:
        peak = jnp.max(largest, axis=(0, 1), keepdims=True)
        exponent = jnp.ceil(jnp.log2(jnp.maximum(peak, 1e-30))) - 15.0
        scale = jnp.exp2(-exponent)
        for p in range(half):
            send_ref[p * count : (p + 1) * count, :] *= scale
        send_ref[half * count :, :] = jnp.broadcast_to(exponent, (16, width))


def last_kernel(packed, *refs):
    *in_refs, out_ref = refs
    chunks = len(in_refs) // 2
    width = in_refs[0].shape[2]
    for chunk in range(chunks):
        got_ref = in_refs[chunks + chunk]
        got = read_packed(got_ref, 0, width) if packed[chunk] else got_ref[0]
        out_ref[:, chunk * width : (chunk + 1) * width] = in_refs[chunk][0] + got


def merge(keep, got, got_packed, send_packed):
    pieces, count, width = keep.shape
    half = pieces // 2
    kept = jax.ShapeDtypeStruct((half, count, width), jnp.float32)
    packed = jax.ShapeDtypeStruct((half * count + 16, width), jnp.float32)
    full = pl.BlockSpec(memory_space=pltpu.VMEM)
    send, keep = pl.pallas_call(
        functools.partial(merge_kernel, got_packed, send_packed),
        out_shape=(packed if send_packed else kept, kept),
        in_specs=[full] * 2,
        out_specs=(full,) * 2,
        compiler_params=pltpu.CompilerParams(vmem_limit_bytes=VMEM_LIMIT),
        name="merge",
    )(keep, got.astype(jnp.float32))
    return (send.astype(jnp.float16) if send_packed else send), keep


def local(tokens, weight, generators, orders, cotangent):
    sections, rows, block = generators.shape
    half = block // 2
    count = tokens.shape[0]
    size = lax.axis_size("tensor")
    bits = size.bit_length() - 1
    here = lax.axis_index("tensor")
    pair_bit = bits - 1
    high = jnp.bitwise_and(jnp.right_shift(here, pair_bit), 1).astype(jnp.int32).reshape(1)
    lanes = sections * (rows // half)
    f32 = jnp.float32
    full = pl.BlockSpec(memory_space=pltpu.VMEM)
    scalars = pl.BlockSpec(memory_space=pltpu.SMEM)
    params = pltpu.CompilerParams(vmem_limit_bytes=VMEM_LIMIT)

    stored = jnp.swapaxes(generators, 1, 2)
    far_gen = exchange(stored[0], pair_bit)
    order = list(range(bits - 1, -1, -1))
    pieces = cotangent[None]
    for bit in order[:-4]:
        pieces = grow(pieces, bit)
    firsts = [exchange(pieces, bit) for bit in order[-4:-1]]
    flat = stored.reshape(sections * block, rows)
    square = (block * block, lanes)
    far_square = (block * block, lanes // sections)
    inv, near, xs = pl.pallas_call(
        near_kernel,
        out_shape=(
            jax.ShapeDtypeStruct(square, f32),
            jax.ShapeDtypeStruct((sections - 1, rows, GROUP), f32),
            jax.ShapeDtypeStruct((sections - 1, count, rows), f32),
        ),
        in_specs=[scalars, full, full],
        out_specs=(full,) * 3,
        scratch_shapes=[
            pltpu.VMEM((sections * rows, block), f32),
            pltpu.VMEM((sections * rows, block), f32),
            pltpu.VMEM(square, f32),
            pltpu.VMEM(square, f32),
            pltpu.VMEM((sections * rows, block), f32),
        ],
        compiler_params=params,
        name="near_rotations",
    )(orders, flat, tokens)
    by_far, by_mid, by_side = [after(first, xs) for first in firsts]
    far_gen = after(far_gen, xs, by_side)
    x_other = exchange(xs[0], pair_bit)
    inv_far, ffar, bfar = pl.pallas_call(
        far_rotations_kernel,
        out_shape=(
            jax.ShapeDtypeStruct(far_square, f32),
            jax.ShapeDtypeStruct((2, rows, GROUP), f32),
            jax.ShapeDtypeStruct((2, rows, GROUP), f32),
        ),
        in_specs=[scalars, scalars, full, full],
        out_specs=(full,) * 3,
        scratch_shapes=[
            pltpu.VMEM((rows, block), f32),
            pltpu.VMEM((rows, block), f32),
            pltpu.VMEM(far_square, f32),
            pltpu.VMEM(far_square, f32),
            pltpu.VMEM((rows, block), f32),
            pltpu.VMEM((rows, block), f32),
        ],
        compiler_params=params,
        cost_estimate=pl.CostEstimate(flops=10**7, bytes_accessed=10**7, transcendentals=0),
        name="far_rotations",
    )(orders[:1], high, stored[0], far_gen)
    by_far, by_mid = after(by_far, ffar), after(by_mid, ffar)
    by_both = exchange(by_far, order[-3])
    side_pair = exchange(jnp.concatenate([by_far, by_mid], axis=0), order[-2])
    side_last = exchange(by_both, order[-2])
    x_both = pl.pallas_call(
        far_kernel,
        out_shape=jax.ShapeDtypeStruct((2 * count, rows), jnp.bfloat16),
        in_specs=[full] * 3,
        out_specs=full,
        compiler_params=params,
        name="far_apply",
    )(xs, x_other, ffar)

    stages = [tuple(range(bits)), (0, 2, 1) + tuple(range(3, bits))]

    def slot_of(offset, bits_in_order):
        return sum(((offset >> bit) & 1) << (bits - 1 - n) for n, bit in enumerate(bits_in_order))

    offsets = sorted(range(size), key=lambda o: (1 - (o & 1), slot_of(o, stages[0])))
    slots = [[slot_of(o, bits_in_order) % (size // 2) for o in offsets] for bits_in_order in stages]
    fixed = here.astype(jnp.int32)
    places = jnp.bitwise_xor(fixed, jnp.asarray(np.array(offsets, np.int32)))
    back_places = jnp.bitwise_xor(fixed, jnp.arange(size, dtype=jnp.int32))
    outs = project(x_both, weight, places, slots)

    narrow = [(1, 2), (1, bits - 1)]

    def merged(n, outs, gots):
        return [
            merge(keep, got, n in marks, n + 1 in marks)
            for (_, keep), got, marks in zip(outs, gots, narrow)
        ]

    outs = merged(0, outs, [exchange(after(send, by_both, side_pair), 0) for send, _ in outs])
    gots = [exchange(send, order_[1]) for (send, _), order_ in zip(outs, stages)]
    side_last = after(side_last, *[send for send, _ in outs])
    pieces = jnp.concatenate(
        [pieces, by_far, by_mid, by_both, by_side, side_pair, side_last], axis=0
    )
    gathered = [pieces, exchange(pieces, 0)]
    numbers = jnp.arange(block, dtype=jnp.int32)
    inverse = jnp.sum(
        jnp.where(orders[:, :, None] == numbers[None, None, :], numbers[None, :, None], 0), axis=1
    ).astype(jnp.int32)
    grad_cols, grad_packed = project_back(back_places, gathered, gather_order(order), weight)
    grad_other = exchange_packed(grad_packed, pair_bit)
    gots[0] = after(gots[0], grad_cols)
    gots[-1] = after(gots[-1], grad_cols)
    grad_tokens, grad_gens = pl.pallas_call(
        grads_kernel,
        out_shape=(
            jax.ShapeDtypeStruct((count, rows), f32),
            jax.ShapeDtypeStruct((sections * block, rows), f32),
        ),
        in_specs=[scalars, scalars] + [full] * 9,
        out_specs=(full,) * 2,
        scratch_shapes=[
            pltpu.VMEM((sections * rows, block), f32),
            pltpu.VMEM((sections * rows, block), f32),
            pltpu.VMEM((sections * rows, block), f32),
            pltpu.VMEM(square, f32),
            pltpu.VMEM(square, f32),
            pltpu.VMEM(square, f32),
        ],
        compiler_params=params,
        name="gradients",
    )(inverse, high, grad_cols, grad_other, x_other, tokens, xs, near, bfar, inv_far, inv)
    outs = merged(1, outs, gots)
    for n in range(2, bits - 1):
        gots = [exchange(send, order_[n]) for (send, _), order_ in zip(outs, stages)]
        if n == 2:
            gots[0] = after(gots[0], grad_other)
        outs = merged(n, outs, gots)
    lasts = [exchange(send, bits - 1).astype(f32) for send, _ in outs]
    lasts[-1] = after(lasts[-1], grad_tokens, grad_gens)
    outputs = pl.pallas_call(
        functools.partial(last_kernel, [bits - 1 in marks for marks in narrow]),
        out_shape=jax.ShapeDtypeStruct((count, cotangent.shape[1]), f32),
        in_specs=[full] * (2 * CHUNKS),
        out_specs=full,
        compiler_params=params,
        name="last_sums",
    )(*[keep for _, keep in outs], *lasts)
    return outputs, grad_tokens, jnp.swapaxes(grad_gens.reshape(sections, block, rows), 1, 2)


def solution(mesh):
    placed = (
        P("groups", "tensor"),
        P("tensor", None),
        P("groups", "tensor", None),
        P(),
        P("groups", "tensor"),
    )
    return jax.shard_map(
        local,
        mesh=mesh,
        in_specs=placed,
        out_specs=(P("groups", "tensor"), P("groups", "tensor"), P("groups", "tensor", None)),
        check_vma=False,
    )
```

```python
import functools

import jax
import jax.numpy as jnp
import numpy as np
from jax import lax
from jax.experimental import pallas as pl
from jax.experimental.pallas import tpu as pltpu
from jax.sharding import PartitionSpec as P

VMEM_LIMIT = 16 * 2**20
WIDE_LIMIT = 46 * 2**20
GROUP = 128
NN = (((1,), (0,)), ((), ()))
NT = (((1,), (1,)), ((), ()))
TN = (((0,), (0,)), ((), ()))
CHUNKS = 2


def exchange(array, bit):
    size = lax.axis_size("tensor")
    return lax.ppermute(array, "tensor", [(i, i ^ (1 << bit)) for i in range(size)])


def parts_of(x):
    first = x.astype(jnp.bfloat16)
    return first, (x - first.astype(jnp.float32)).astype(jnp.bfloat16)


def one_dot(a, b, dims=NN):
    return lax.dot_general(a, b, dims, preferred_element_type=jnp.float32)


def after(value, *earlier):
    return lax.optimization_barrier((value, *earlier))[0]


def dot(a, b, dims=NN):
    a_first, a_rest = parts_of(a)
    b_first, b_rest = parts_of(b)
    return (
        one_dot(a_first, b_first, dims) + one_dot(a_rest, b_first, dims) + one_dot(a_first, b_rest, dims)
    )


def pick(a, chooser):
    first, rest = parts_of(a)
    return one_dot(first, chooser) + one_dot(rest, chooser)


def iota(shape, dim):
    return lax.broadcasted_iota(jnp.int32, shape, dim)


def split_halves(rows_ref, lo_ref, hi_ref, section, rows, half):
    step = half << (section - 1)
    base = section * rows
    for start in range(base, base + rows, 2 * step):
        low = rows_ref[start : start + step, :]
        high = rows_ref[start + step : start + 2 * step, :]
        lo_ref[start : start + step, :] = low
        lo_ref[start + step : start + 2 * step, :] = low
        hi_ref[start : start + step, :] = high
        hi_ref[start + step : start + 2 * step, :] = high


def to_lanes(lo_ref, hi_ref, out_ref, lanes, half, block):
    for a in range(half):
        out_ref[a * block : (a + 1) * block, :] = lo_ref[pl.ds(a, lanes, stride=half), :].T
        out_ref[(half + a) * block : (half + a + 1) * block, :] = hi_ref[
            pl.ds(a, lanes, stride=half), :
        ].T


def by_section(parts, section_of):
    out = parts[-1]
    for k in range(len(parts) - 2, -1, -1):
        out = jnp.where(section_of == k, parts[k], out)
    return out


def lane_facts(shape, per_section, high):
    lane = iota(shape, 1)
    section_of = lane // per_section
    part = lane % per_section
    upper = jnp.bitwise_and(jnp.right_shift(part, jnp.maximum(section_of - 1, 0)), 1)
    return section_of, jnp.where(section_of == 0, high, upper) == 1


def block_masks(section, half):
    row = iota((GROUP, GROUP), 0) // half
    col = iota((GROUP, GROUP), 1) // half
    bit = 1 << (section - 1)
    return col == jnp.bitwise_and(row, ~bit), col == jnp.bitwise_or(row, bit)


def same_mask(half):
    return iota((GROUP, GROUP), 0) // half == iota((GROUP, GROUP), 1) // half


def spreader(offsets, block, half):
    row, col = iota((block, GROUP), 0), iota((block, GROUP), 1) % half
    return jnp.concatenate([(row == at + col).astype(jnp.bfloat16) for at in offsets], axis=1)


def gatherer(offset, block, half):
    row, col = iota((GROUP, block), 0) % half, iota((GROUP, block), 1)
    return (col == offset + row).astype(jnp.bfloat16)


def transpose_to(out_ref, in_ref, block, change=lambda j, t: t):
    for j in range(block):
        out_ref[j * block : (j + 1) * block, :] = change(j, in_ref[pl.ds(j, block, stride=block), :])


def permuted_row(orders_ref, in_ref, i, section_of):
    sections, block = orders_ref.shape
    return by_section(
        [
            in_ref[pl.ds(pl.multiple_of(orders_ref[k, i] * block, block), block), :]
            for k in range(sections)
        ],
        section_of,
    )


def permute_rows(orders_ref, in_ref, out_ref, section_of):
    block = orders_ref.shape[1]
    for i in range(block):
        out_ref[i * block : (i + 1) * block, :] = permuted_row(orders_ref, in_ref, i, section_of)


def invert_blocks(orders_ref, lo_ref, hi_ref, inv_ref, a_ref, b_ref, section_of):
    sections, block = orders_ref.shape
    half = block // 2
    lanes = inv_ref.shape[1]
    to_lanes(lo_ref, hi_ref, a_ref, lanes, half, block)

    transpose_to(b_ref, a_ref, block, lambda j, t: a_ref[j * block : (j + 1) * block, :] - t)
    permute_rows(orders_ref, b_ref, a_ref, section_of)
    transpose_to(b_ref, a_ref, block)
    permute_rows(orders_ref, b_ref, inv_ref, section_of)
    sub = iota((block, lanes), 0)
    for j in range(block):
        inv_ref[j * block : (j + 1) * block, :] += (sub == j).astype(jnp.float32)

    def eliminate(k, _):
        at = pl.multiple_of(k * block, block)
        here = sub == k
        inverse = 1.0 / inv_ref[pl.ds(at + k, 1), :]
        factors = inv_ref[pl.ds(k, block, stride=block), :]
        pivot = jnp.where(here, inverse, inv_ref[pl.ds(at, block), :] * inverse)
        for i in range(block):
            row = inv_ref[i * block : (i + 1) * block, :]
            inv_ref[i * block : (i + 1) * block, :] = (
                jnp.where(here, 0.0, row) - factors[i : i + 1, :] * pivot
            )
        inv_ref[pl.ds(at, block), :] = pivot
        return 0

    lax.fori_loop(0, block, eliminate, 0)


def own_rows(inv_ref, out_ref, half, block, upper):
    lanes = inv_ref.shape[1]
    sub = iota((block, lanes), 0)
    for a in range(half):
        low = 2.0 * inv_ref[a * block : (a + 1) * block, :] - (sub == a).astype(jnp.float32)
        top = 2.0 * inv_ref[(half + a) * block : (half + a + 1) * block, :] - (
            sub == half + a
        ).astype(jnp.float32)
        out_ref[pl.ds(a, lanes, stride=half), :] = jnp.where(upper, top, low).T


def own_cols(inv_ref, out_ref, half, block, upper):
    lanes = inv_ref.shape[1]
    sub = iota((block, lanes), 0)
    for a in range(half):
        low = 2.0 * inv_ref[pl.ds(a, block, stride=block), :] - (sub == a).astype(jnp.float32)
        top = 2.0 * inv_ref[pl.ds(half + a, block, stride=block), :] - (sub == half + a).astype(
            jnp.float32
        )
        out_ref[pl.ds(a, lanes, stride=half), :] = jnp.where(upper, top, low).T


def near_kernel(
    orders_ref, gen_ref, tok_ref, inv_ref, near_ref, xs_ref,
    lo_ref, hi_ref, a_ref, b_ref, row_ref,
):
    sections, block = orders_ref.shape
    half = block // 2
    rows = tok_ref.shape[1]
    lanes = sections * rows // half
    for k in range(sections):
        row_ref[k * rows : (k + 1) * rows, :] = gen_ref[k * block : (k + 1) * block, :].T
    lo_ref[0:rows, :] = row_ref[0:rows, :]
    hi_ref[0:rows, :] = row_ref[0:rows, :]
    for k in range(1, sections):
        split_halves(row_ref, lo_ref, hi_ref, k, rows, half)
    section_of, upper = lane_facts((block, lanes), rows // half, 0)
    invert_blocks(orders_ref, lo_ref, hi_ref, inv_ref, a_ref, b_ref, section_of)
    own_rows(inv_ref, row_ref, half, block, upper)
    spread = spreader((0, half), block, half)
    for k in range(1, sections):
        lo_mask, hi_mask = block_masks(k, half)
        wide = pick(row_ref[k * rows : (k + 1) * rows, :], spread)
        for start in range(0, rows, GROUP):
            part = wide[start : start + GROUP]
            near_ref[k - 1, start : start + GROUP, :] = jnp.where(
                lo_mask, part[:, :GROUP], jnp.where(hi_mask, part[:, GROUP:], 0.0)
            )
    for start in range(0, rows, GROUP):
        stop = start + GROUP
        value = tok_ref[:, start:stop].astype(jnp.float32)
        for k in range(sections - 1, 0, -1):
            value = dot(value, near_ref[k - 1, start:stop, :])
            xs_ref[k - 1, :, start:stop] = value


def far_rotations_kernel(
    orders_ref, high_ref, own_ref, far_ref, inv_ref, ffar_ref, bfar_ref,
    lo_ref, hi_ref, a_ref, b_ref, row_ref, col_ref,
):
    block = orders_ref.shape[1]
    half = block // 2
    rows = far_ref.shape[1]
    high = high_ref[0]
    own = own_ref[...].T
    other = far_ref[...].T
    lo_ref[...] = jnp.where(high == 1, other, own)
    hi_ref[...] = jnp.where(high == 1, own, other)
    invert_blocks(orders_ref, lo_ref, hi_ref, inv_ref, a_ref, b_ref, None)
    upper = high == 1
    own_rows(inv_ref, row_ref, half, block, upper)
    own_cols(inv_ref, col_ref, half, block, upper)
    spread = spreader((half * high, half * (1 - high)), block, half)
    same = same_mask(half)
    for source, target in ((col_ref, ffar_ref), (row_ref, bfar_ref)):
        wide = pick(source[...], spread)
        for start in range(0, rows, GROUP):
            part = wide[start : start + GROUP]
            target[0, start : start + GROUP, :] = jnp.where(same, part[:, :GROUP], 0.0)
            target[1, start : start + GROUP, :] = jnp.where(same, part[:, GROUP:], 0.0)


def write_packed(packed_ref, value):
    count, width = value.shape
    peak = jnp.max(jnp.abs(value), axis=(0, 1), keepdims=True)
    exponent = jnp.ceil(jnp.log2(jnp.maximum(peak, 1e-30))) - 15.0
    packed_ref[0:count, :] = value * jnp.exp2(-exponent)
    packed_ref[count:, :] = jnp.broadcast_to(exponent, (16, width))


def read_packed(packed_ref, start, stop):
    count = packed_ref.shape[0] - 16
    return packed_ref[0:count, start:stop] * jnp.exp2(packed_ref[count : count + 1, 0:1])


def exchange_packed(packed, bit):
    return exchange(packed.astype(jnp.float16), bit).astype(jnp.float32)


def beside(a, b):
    return jnp.concatenate([a, b], axis=1)


def far_kernel(own_ref, oth_ref, far_ref, out_ref):
    count, rows = own_ref.shape[1:]
    for start in range(0, rows, GROUP):
        stop = start + GROUP
        value = dot(
            beside(own_ref[0, :, start:stop], oth_ref[:, start:stop]),
            beside(far_ref[0, start:stop, :], far_ref[1, start:stop, :]),
            NT,
        )
        first = value.astype(jnp.bfloat16)
        out_ref[0:count, start:stop] = first
        out_ref[count : 2 * count, start:stop] = (value - first.astype(jnp.float32)).astype(
            jnp.bfloat16
        )


def project_kernel(slots, places_ref, x_ref, w_ref, *refs):
    *out_refs, held_ref, sems = refs
    pieces, _, width = held_ref.shape
    count = x_ref.shape[0] // 2
    half = pieces // 2
    part = width // CHUNKS

    def fetch(p):
        at = pl.multiple_of(places_ref[p] * width, width)
        return pltpu.make_async_copy(w_ref.at[:, pl.ds(at, width)], held_ref.at[p], sems.at[p])

    for p in range(pieces):
        fetch(p).start()
    for p in range(pieces):
        fetch(p).wait()
        both = one_dot(x_ref[...], held_ref[p])
        total = both[:count] + both[count:]
        for chunk in range(CHUNKS):
            out_refs[2 * chunk + p // half][slots[chunk][p]] = total[
                :, chunk * part : (chunk + 1) * part
            ]


def project(x_both, weight, places, slots):
    pieces = places.shape[0]
    count2, rows = x_both.shape
    count = count2 // 2
    width = weight.shape[1] // lax.axis_size("tensor")
    outs = pl.pallas_call(
        functools.partial(project_kernel, slots),
        out_shape=(jax.ShapeDtypeStruct((pieces // 2, count, width // CHUNKS), jnp.float32),)
        * (2 * CHUNKS),
        in_specs=[
            pl.BlockSpec(memory_space=pltpu.SMEM),
            pl.BlockSpec(memory_space=pltpu.VMEM),
            pl.BlockSpec(memory_space=pl.ANY),
        ],
        out_specs=(pl.BlockSpec(memory_space=pltpu.VMEM),) * (2 * CHUNKS),
        scratch_shapes=[
            pltpu.VMEM((pieces, rows, width), weight.dtype),
            pltpu.SemaphoreType.DMA((pieces,)),
        ],
        compiler_params=pltpu.CompilerParams(vmem_limit_bytes=WIDE_LIMIT),
        cost_estimate=pl.CostEstimate(
            flops=2 * count2 * rows * width * pieces,
            bytes_accessed=pieces * width * (2 * rows + 4 * count),
            transcendentals=0,
        ),
        name="project",
    )(places, x_both, weight)
    return [outs[2 * chunk : 2 * chunk + 2] for chunk in range(CHUNKS)]


def back_kernel(order, places_ref, low_ref, high_ref, w_ref, out_ref, packed_ref, cots_ref, held_ref, cot_sems, sems):
    half, _, width = low_ref.shape

    def fetches(slot):
        at = pl.multiple_of(places_ref[order[slot]] * width, width)
        here = pl.ds(slot * width, width)
        cot = (low_ref if slot < half else high_ref).at[slot % half]
        return (
            pltpu.make_async_copy(cot, cots_ref.at[:, here], cot_sems.at[slot]),
            pltpu.make_async_copy(w_ref.at[:, pl.ds(at, width)], held_ref.at[:, here], sems.at[slot]),
        )

    for slot in range(2 * half):
        for copy in fetches(slot):
            copy.start()
    for slot in range(2 * half):
        for copy in fetches(slot):
            copy.wait()
        here = slice(slot * width, (slot + 1) * width)
        product = one_dot(cots_ref[:, here], held_ref[:, here], NT)
        if slot == 0:
            out_ref[...] = product
        else:
            out_ref[...] += product
    write_packed(packed_ref, out_ref[...])


def project_back(places, gathered, order, weight):
    half, count, width = gathered[0].shape
    steps = half * len(gathered)
    rows = weight.shape[0]
    return pl.pallas_call(
        functools.partial(back_kernel, order),
        out_shape=(
            jax.ShapeDtypeStruct((count, rows), jnp.float32),
            jax.ShapeDtypeStruct((count + 16, rows), jnp.float32),
        ),
        in_specs=[pl.BlockSpec(memory_space=pltpu.SMEM)]
        + [pl.BlockSpec(memory_space=pl.ANY)] * (len(gathered) + 1),
        out_specs=(pl.BlockSpec(memory_space=pltpu.VMEM),) * 2,
        scratch_shapes=[
            pltpu.VMEM((count, steps * width), weight.dtype),
            pltpu.VMEM((rows, steps * width), weight.dtype),
            pltpu.SemaphoreType.DMA((steps,)),
            pltpu.SemaphoreType.DMA((steps,)),
        ],
        compiler_params=pltpu.CompilerParams(vmem_limit_bytes=WIDE_LIMIT),
        cost_estimate=pl.CostEstimate(
            flops=2 * count * rows * width * steps,
            bytes_accessed=steps * width * 2 * (rows + count),
            transcendentals=0,
        ),
        name="project_back",
    )(places, *gathered, weight)


def grow(array, bit):
    return jnp.concatenate([array, exchange(array, bit)], axis=0)


def gather_order(stages):
    order = [0]
    for bit in stages:
        order = order + [n ^ (1 << bit) for n in order]
    return tuple(order)


def lane_matmul(left_ref, right_ref, out_ref, block, lanes):
    step = 4

    def body(t, _):
        first = t * step
        totals = [jnp.zeros((block, lanes), jnp.float32) for _ in range(step)]
        for j in range(block):
            right = right_ref[j * block : (j + 1) * block, :]
            for s in range(step):
                totals[s] += left_ref[pl.ds((first + s) * block + j, 1), :] * right
        for s in range(step):
            out_ref[pl.ds(pl.multiple_of((first + s) * block, block), block), :] = totals[s]
        return 0

    lax.fori_loop(0, block // step, body, 0)


def grads_kernel(
    inverse_ref, high_ref, own_ref, oth_ref, x_oth_ref, tok_ref, xs_ref, near_ref, bfar_ref, inv_far_ref, inv_ref,
    gtok_ref, ggen_ref,
    row_ref, lo_ref, hi_ref, a_ref, b_ref, c_ref,
):
    sections, block = inverse_ref.shape
    half = block // 2
    count, rows = own_ref.shape
    per_section = rows // half
    lanes = sections * per_section
    high = high_ref[0]
    chooser = jnp.concatenate([gatherer(0, block, half), gatherer(half, block, half)], axis=0)
    far_chooser = jnp.concatenate(
        [gatherer(half * high, block, half), gatherer(half * (1 - high), block, half)], axis=0
    )
    same = same_mask(half)
    same = jnp.concatenate([beside(same, same)] * 2, axis=0)
    for start in range(0, rows, GROUP):
        stop = start + GROUP
        x_pair = beside(xs_ref[0, :, start:stop], x_oth_ref[:, start:stop])
        g_pair = beside(own_ref[:, start:stop], read_packed(oth_ref, start, stop))
        both = pick(jnp.where(same, dot(x_pair, g_pair, TN), 0.0), far_chooser)
        mine, theirs = both[:GROUP], both[GROUP:]
        lo_ref[start:stop, :] = jnp.where(high == 1, theirs, mine)
        hi_ref[start:stop, :] = jnp.where(high == 1, mine, theirs)
        grad = dot(g_pair, beside(bfar_ref[0, start:stop, :], bfar_ref[1, start:stop, :]), NT)
        for k in range(1, sections):
            lo_mask, hi_mask = block_masks(k, half)
            if k < sections - 1:
                x = xs_ref[k, :, start:stop]
            else:
                x = tok_ref[:, start:stop].astype(jnp.float32)
            outer = dot(x, grad, TN)
            row_ref[k * rows + start : k * rows + stop, :] = pick(
                beside(jnp.where(lo_mask, outer, 0.0), jnp.where(hi_mask, outer, 0.0)), chooser
            )
            grad = dot(grad, near_ref[k - 1, start:stop, :], NT)
        gtok_ref[:, start:stop] = grad
    for k in range(1, sections):
        split_halves(row_ref, lo_ref, hi_ref, k, rows, half)
    to_lanes(lo_ref, hi_ref, a_ref, lanes, half, block)
    for j in range(block):
        b_ref[j * block : (j + 1) * block, :] = inv_ref[pl.ds(j, block, stride=block), :]
        b_ref[j * block : (j + 1) * block, 0:per_section] = inv_far_ref[
            pl.ds(j, block, stride=block), :
        ]
    lane_matmul(a_ref, b_ref, c_ref, block, lanes)
    lane_matmul(b_ref, c_ref, a_ref, block, lanes)
    section_of, upper = lane_facts((block, lanes), per_section, high)
    transpose_to(c_ref, a_ref, block, lambda j, t: 2.0 * (t - a_ref[j * block : (j + 1) * block, :]))
    permute_rows(inverse_ref, c_ref, b_ref, section_of)
    transpose_to(a_ref, b_ref, block)
    for a in range(half):
        low = permuted_row(inverse_ref, a_ref, a, section_of)
        top = permuted_row(inverse_ref, a_ref, half + a, section_of)
        row_ref[pl.ds(a, lanes, stride=half), :] = jnp.where(upper, top, low).T
    for k in range(sections):
        ggen_ref[k * block : (k + 1) * block, :] = row_ref[k * rows : (k + 1) * rows, :].T


def merge_kernel(got_packed, send_packed, keep_ref, got_ref, send_ref, out_ref):
    half, count, width = out_ref.shape
    if got_packed:
        got_scale = jnp.exp2(got_ref[2 * half * count : 2 * half * count + 1, 0:1])

    def total(p):
        if got_packed:
            return keep_ref[p] + got_ref[p * count : (p + 1) * count, :] * got_scale
        return keep_ref[p] + got_ref[p]

    largest = jnp.zeros((count, width), jnp.float32)
    for p in range(half):
        out_ref[p] = total(p)
        upper = total(half + p)
        if send_packed:
            send_ref[p * count : (p + 1) * count, :] = upper
            largest = jnp.maximum(largest, jnp.abs(upper))
        else:
            send_ref[p] = upper
    if send_packed:
        peak = jnp.max(largest, axis=(0, 1), keepdims=True)
        exponent = jnp.ceil(jnp.log2(jnp.maximum(peak, 1e-30))) - 15.0
        scale = jnp.exp2(-exponent)
        for p in range(half):
            send_ref[p * count : (p + 1) * count, :] *= scale
        send_ref[half * count :, :] = jnp.broadcast_to(exponent, (16, width))


def last_kernel(packed, *refs):
    *in_refs, out_ref = refs
    chunks = len(in_refs) // 2
    width = in_refs[0].shape[2]
    for chunk in range(chunks):
        got_ref = in_refs[chunks + chunk]
        got = read_packed(got_ref, 0, width) if packed[chunk] else got_ref[0]
        out_ref[:, chunk * width : (chunk + 1) * width] = in_refs[chunk][0] + got


def merge(keep, got, got_packed, send_packed):
    pieces, count, width = keep.shape
    half = pieces // 2
    kept = jax.ShapeDtypeStruct((half, count, width), jnp.float32)
    packed = jax.ShapeDtypeStruct((half * count + 16, width), jnp.float32)
    full = pl.BlockSpec(memory_space=pltpu.VMEM)
    send, keep = pl.pallas_call(
        functools.partial(merge_kernel, got_packed, send_packed),
        out_shape=(packed if send_packed else kept, kept),
        in_specs=[full] * 2,
        out_specs=(full,) * 2,
        compiler_params=pltpu.CompilerParams(vmem_limit_bytes=VMEM_LIMIT),
        name="merge",
    )(keep, got.astype(jnp.float32))
    return (send.astype(jnp.float16) if send_packed else send), keep


def local(tokens, weight, generators, orders, cotangent):
    sections, rows, block = generators.shape
    half = block // 2
    count = tokens.shape[0]
    size = lax.axis_size("tensor")
    bits = size.bit_length() - 1
    here = lax.axis_index("tensor")
    pair_bit = bits - 1
    high = jnp.bitwise_and(jnp.right_shift(here, pair_bit), 1).astype(jnp.int32).reshape(1)
    lanes = sections * (rows // half)
    f32 = jnp.float32
    full = pl.BlockSpec(memory_space=pltpu.VMEM)
    scalars = pl.BlockSpec(memory_space=pltpu.SMEM)
    params = pltpu.CompilerParams(vmem_limit_bytes=VMEM_LIMIT)

    stored = jnp.swapaxes(generators, 1, 2)
    far_gen = exchange(stored[0], pair_bit)
    order = list(range(bits - 1, -1, -1))
    pieces = cotangent[None]
    for bit in order[:-4]:
        pieces = grow(pieces, bit)
    firsts = [exchange(pieces, bit) for bit in order[-4:-1]]
    flat = stored.reshape(sections * block, rows)
    square = (block * block, lanes)
    far_square = (block * block, lanes // sections)
    inv, near, xs = pl.pallas_call(
        near_kernel,
        out_shape=(
            jax.ShapeDtypeStruct(square, f32),
            jax.ShapeDtypeStruct((sections - 1, rows, GROUP), f32),
            jax.ShapeDtypeStruct((sections - 1, count, rows), f32),
        ),
        in_specs=[scalars, full, full],
        out_specs=(full,) * 3,
        scratch_shapes=[
            pltpu.VMEM((sections * rows, block), f32),
            pltpu.VMEM((sections * rows, block), f32),
            pltpu.VMEM(square, f32),
            pltpu.VMEM(square, f32),
            pltpu.VMEM((sections * rows, block), f32),
        ],
        compiler_params=params,
        name="near_rotations",
    )(orders, flat, tokens)
    by_far, by_mid, by_side = [after(first, xs) for first in firsts]
    far_gen = after(far_gen, xs, by_side)
    x_other = exchange(xs[0], pair_bit)
    inv_far, ffar, bfar = pl.pallas_call(
        far_rotations_kernel,
        out_shape=(
            jax.ShapeDtypeStruct(far_square, f32),
            jax.ShapeDtypeStruct((2, rows, GROUP), f32),
            jax.ShapeDtypeStruct((2, rows, GROUP), f32),
        ),
        in_specs=[scalars, scalars, full, full],
        out_specs=(full,) * 3,
        scratch_shapes=[
            pltpu.VMEM((rows, block), f32),
            pltpu.VMEM((rows, block), f32),
            pltpu.VMEM(far_square, f32),
            pltpu.VMEM(far_square, f32),
            pltpu.VMEM((rows, block), f32),
            pltpu.VMEM((rows, block), f32),
        ],
        compiler_params=params,
        cost_estimate=pl.CostEstimate(flops=10**7, bytes_accessed=10**7, transcendentals=0),
        name="far_rotations",
    )(orders[:1], high, stored[0], far_gen)
    by_far, by_mid = after(by_far, ffar), after(by_mid, ffar)
    by_both = exchange(by_far, order[-3])
    side_pair = exchange(jnp.concatenate([by_far, by_mid], axis=0), order[-2])
    side_last = exchange(by_both, order[-2])
    x_both = pl.pallas_call(
        far_kernel,
        out_shape=jax.ShapeDtypeStruct((2 * count, rows), jnp.bfloat16),
        in_specs=[full] * 3,
        out_specs=full,
        compiler_params=params,
        name="far_apply",
    )(xs, x_other, ffar)

    stages = [tuple(range(bits)), (0, 2, 1) + tuple(range(3, bits))]

    def slot_of(offset, bits_in_order):
        return sum(((offset >> bit) & 1) << (bits - 1 - n) for n, bit in enumerate(bits_in_order))

    offsets = sorted(range(size), key=lambda o: (1 - (o & 1), slot_of(o, stages[0])))
    slots = [[slot_of(o, bits_in_order) % (size // 2) for o in offsets] for bits_in_order in stages]
    fixed = here.astype(jnp.int32)
    places = jnp.bitwise_xor(fixed, jnp.asarray(np.array(offsets, np.int32)))
    back_places = jnp.bitwise_xor(fixed, jnp.arange(size, dtype=jnp.int32))
    outs = project(x_both, weight, places, slots)

    narrow = [(1, 2), (1, bits - 1)]

    def merged(n, outs, gots):
        return [
            merge(keep, got, n in marks, n + 1 in marks)
            for (_, keep), got, marks in zip(outs, gots, narrow)
        ]

    outs = merged(0, outs, [exchange(after(send, by_both, side_pair), 0) for send, _ in outs])
    gots = [exchange(send, order_[1]) for (send, _), order_ in zip(outs, stages)]
    side_last = after(side_last, *[send for send, _ in outs])
    pieces = jnp.concatenate(
        [pieces, by_far, by_mid, by_both, by_side, side_pair, side_last], axis=0
    )
    gathered = [pieces, exchange(pieces, 0)]
    numbers = jnp.arange(block, dtype=jnp.int32)
    inverse = jnp.sum(
        jnp.where(orders[:, :, None] == numbers[None, None, :], numbers[None, :, None], 0), axis=1
    ).astype(jnp.int32)
    grad_cols, grad_packed = project_back(back_places, gathered, gather_order(order), weight)
    grad_other = exchange_packed(grad_packed, pair_bit)
    gots[0] = after(gots[0], grad_cols)
    gots[-1] = after(gots[-1], grad_cols)
    grad_tokens, grad_gens = pl.pallas_call(
        grads_kernel,
        out_shape=(
            jax.ShapeDtypeStruct((count, rows), f32),
            jax.ShapeDtypeStruct((sections * block, rows), f32),
        ),
        in_specs=[scalars, scalars] + [full] * 9,
        out_specs=(full,) * 2,
        scratch_shapes=[
            pltpu.VMEM((sections * rows, block), f32),
            pltpu.VMEM((sections * rows, block), f32),
            pltpu.VMEM((sections * rows, block), f32),
            pltpu.VMEM(square, f32),
            pltpu.VMEM(square, f32),
            pltpu.VMEM(square, f32),
        ],
        compiler_params=params,
        name="gradients",
    )(inverse, high, grad_cols, grad_other, x_other, tokens, xs, near, bfar, inv_far, inv)
    ahead = merge(outs[0][1], gots[0], True, 2 in narrow[0])
    gots = [gots[0]] + [after(got, ahead[0]) for got in gots[1:]]
    outs = [ahead] + merged(1, outs, gots)[1:]
    for n in range(2, bits - 1):
        gots = [exchange(send, order_[n]) for (send, _), order_ in zip(outs, stages)]
        if n == 2:
            gots[0] = after(gots[0], grad_other)
        outs = merged(n, outs, gots)
    lasts = [exchange(send, bits - 1).astype(f32) for send, _ in outs]
    lasts[-1] = after(lasts[-1], grad_tokens, grad_gens)
    outputs = pl.pallas_call(
        functools.partial(last_kernel, [bits - 1 in marks for marks in narrow]),
        out_shape=jax.ShapeDtypeStruct((count, cotangent.shape[1]), f32),
        in_specs=[full] * (2 * CHUNKS),
        out_specs=full,
        compiler_params=params,
        name="last_sums",
    )(*[keep for _, keep in outs], *lasts)
    return outputs, grad_tokens, jnp.swapaxes(grad_gens.reshape(sections, block, rows), 1, 2)


def solution(mesh):
    placed = (
        P("groups", "tensor"),
        P("tensor", None),
        P("groups", "tensor", None),
        P(),
        P("groups", "tensor"),
    )
    return jax.shard_map(
        local,
        mesh=mesh,
        in_specs=placed,
        out_specs=(P("groups", "tensor"), P("groups", "tensor"), P("groups", "tensor", None)),
        check_vma=False,
    )
```
